32 devices in a mesh: grp: 4 (over z), dp: 8 (over y, x, core).
Axes of the slice: x: 2, y: 2, z: 4, core: 2. Of those that a mesh axis runs over, the one named last changes fastest.
Arguments:
- hidden: bfloat16 [8, 4, 320, 2048], P('dp', 'grp'), may hold values from -6 to 6
- cotangent: bfloat16 [8, 4, 320, 2048], P('dp', 'grp'), may hold values from -6 to 6
- segment_ids: int32 [8, 1024], P('dp'), may hold values from 0 to 3, never falling along the last dimension, each value on 1 to 512 neighbouring positions
- continuation_prompt: int32 [8, 4], P('dp', 'grp'), may hold values from 0 to 3
- gain_master: float32 [2, 2048], P(None, ('grp', 'dp')), may hold values from 0.5 to 1.5
- gain_first: float32 [2, 2048], P(None, ('grp', 'dp')), may hold values from -96 to 96
- gain_second: float32 [2, 2048], P(None, ('grp', 'dp')), may hold values from 100 to 10000
- attention_master: float32 [2048, 4096], P(('grp', 'dp')), may hold values from -0.125 to 0.125
- attention_first: float32 [2048, 4096], P(('grp', 'dp')), may hold values from -80 to 80
- attention_second: float32 [2048, 4096], P(('grp', 'dp')), may hold values from 80 to 8000
- merge_master: float32 [2048, 2048], P(('grp', 'dp')), may hold values from -1 to 1
- merge_first: float32 [2048, 2048], P(('grp', 'dp')), may hold values from -6 to 6
- merge_second: float32 [2048, 2048], P(('grp', 'dp')), may hold values from 2 to 120
- feedforward_master: float32 [2048, 24576], P(('grp', 'dp')), may hold values from -0.125 to 0.125
- feedforward_first: float32 [2048, 24576], P(('grp', 'dp')), may hold values from -48 to 48
- feedforward_second: float32 [2048, 24576], P(('grp', 'dp')), may hold values from 30 to 2000
Outputs:
- block_output: bfloat16 [8, 4, 320, 2048], P('dp', 'grp')
- input_grad: float32 [8, 4, 320, 2048], P('dp', 'grp')
- gain_grad: float32 [2, 2048], P(None, ('grp', 'dp'))
- gain_update: float32 [2, 2048], P(None, ('grp', 'dp'))
- gain_first_new: float32 [2, 2048], P(None, ('grp', 'dp'))
- gain_second_new: float32 [2, 2048], P(None, ('grp', 'dp'))
- attention_grad: float32 [2048, 4096], P(('grp', 'dp'))
- attention_update: float32 [2048, 4096], P(('grp', 'dp'))
- attention_first_new: float32 [2048, 4096], P(('grp', 'dp'))
- attention_second_new: float32 [2048, 4096], P(('grp', 'dp'))
- merge_grad: float32 [2048, 2048], P(('grp', 'dp'))
- merge_update: float32 [2048, 2048], P(('grp', 'dp'))
- merge_first_new: float32 [2048, 2048], P(('grp', 'dp'))
- merge_second_new: float32 [2048, 2048], P(('grp', 'dp'))
- feedforward_grad: float32 [2048, 24576], P(('grp', 'dp'))
- feedforward_update: float32 [2048, 24576], P(('grp', 'dp'))
- feedforward_first_new: float32 [2048, 24576], P(('grp', 'dp'))
- feedforward_second_new: float32 [2048, 24576], P(('grp', 'dp'))
The draws below stay inside these ranges and needn't reach their ends.
Inputs may be any that keep to these rules, and one draw needn't show every extreme that they name: `segment_ids`: along a group's prompt the ids never fall; each of the 4 ids covers 1 to 512 positions, and one covers exactly 512.
All inputs are finite; a program needn't handle non-finite values.
Results may differ from the reference program's by a relative error of at most 0.025.
The reference program's roundings to bfloat16 on the way count: a program that leaves them out, or rounds other values in their place, can miss the bound.
Values may be sent and summed in bfloat16 or wider, within the bound.
A program may use at most 896 MiB of HBM per device.

```python
import math
import jax
import jax.numpy as jnp
import numpy as np
from jax import lax

D = 2048
FF = 8192
HQ = 8
HK = 4
HD = 256
PROMPT_LEN = 1024
PROMPTS = 4
CONT = 64
STEP = 10
GROUPS = 8
ROWS_DEV = 320
QKV = 4096
AO = 2048
N_GRP = 4


def set_ends(array, stream_key, least, largest):
    spot = [jax.random.randint(jax.random.fold_in(stream_key, axis), (), 0, length) for axis, length in enumerate(array.shape)]
    longest = array.shape.index(max(array.shape))
    beside = spot[:longest] + [(spot[longest] + 1) % array.shape[longest]] + spot[longest + 1:]
    return array.at[tuple(spot)].set(least).at[tuple(beside)].set(largest)


def levels(rng, dims, cuts, least, top_value):
    level, own = 1.0, jax.random.fold_in(rng, 6)
    for axis_at, parts in cuts:
        steps = jnp.exp(jax.random.uniform(jax.random.fold_in(own, axis_at), (parts,), jnp.float32, least / len(cuts), top_value / len(cuts)))
        level = level * jnp.repeat(steps, dims[axis_at] // parts).reshape([-1 if axis == axis_at else 1 for axis in range(len(dims))])
    return level


def length_profile(amount, total, most, lean):
    portions = [(1 << 20) // math.isqrt(grade ** lean) + 1 for grade in range(2, amount + 1)]
    rest, counts = total - most - (amount - 1), [1] * (amount - 1)
    while rest > 0:
        candidates = [i for i in range(amount - 1) if counts[i] < most]
        mass, budget = sum([portions[i] for i in candidates]), rest
        for i in candidates:
            addition = min(most - counts[i], max(1, budget * portions[i] // mass), rest)
            counts[i] = counts[i] + addition
            rest = rest - addition
    return np.array([most] + counts)


def uneven_parts(stream_key, count, total, bound, slope):
    if count == 2:
        one = jax.random.randint(stream_key, (), max(1, total - bound), min(bound, total - 1) + 1)
        return jnp.stack([one, total - one])
    tallies = jnp.asarray(length_profile(count, total, bound, slope), jnp.int32)
    couples = (count - 1) // 2
    donor, receiver = tallies[1:1 + 2 * couples:2], tallies[2:2 + 2 * couples:2]
    margin = jnp.minimum(donor - 1, bound - receiver)
    passed = jax.random.randint(jax.random.fold_in(stream_key, 1), (couples,), 0, 1 << 20) % (margin + 1)
    tallies = tallies.at[1:1 + 2 * couples:2].set(donor - passed).at[2:2 + 2 * couples:2].set(receiver + passed)
    return tallies[jax.random.permutation(jax.random.fold_in(stream_key, 2), count)]


def scatter_about(rng, extent, width, limit, split=(), held_as=jnp.bfloat16):
    drawn = width * jax.random.normal(rng, extent, jnp.float32)
    if split:
        drawn = drawn * levels(rng, extent, split, -0.22, 0.18)
    return jnp.clip(drawn, -limit, limit).astype(held_as)


def setup_inputs(seed: int = 0) -> dict:
    seeds = jax.random.split(jax.random.key(seed), 17)
    return {
        "hidden": scatter_about(seeds[0], (GROUPS, N_GRP, ROWS_DEV, D), 1.0, 6.0, ((0, 8), (1, 4))),
        "cotangent": scatter_about(seeds[1], (GROUPS, N_GRP, ROWS_DEV, D), 1.0, 6.0, ((0, 8), (1, 4))),
        "segment_ids": jax.vmap(lambda own: jnp.searchsorted(jnp.cumsum(uneven_parts(own, PROMPTS, PROMPT_LEN, PROMPT_LEN // 2, 1)), jnp.arange(PROMPT_LEN), side="right"))(jax.random.split(seeds[2], GROUPS)).reshape((GROUPS, PROMPT_LEN)).astype(jnp.int32),
        "continuation_prompt": set_ends(jax.random.randint(seeds[3], (GROUPS, N_GRP), 0, PROMPTS), jax.random.fold_in(seeds[3], 1), 0, PROMPTS - 1).astype(jnp.int32),
        "gain_master": jnp.clip(1.0 + 0.1 * jax.random.normal(seeds[4], (2, D), jnp.float32), 0.5, 1.5),
        "gain_first": scatter_about(seeds[5], (2, D), 17.0, 96.0, ((1, 32),), jnp.float32),
        "gain_second": jnp.clip(jnp.exp(math.log(10000.0) - 4.6051702 * jax.random.uniform(seeds[6], (2, D), jnp.float32) ** levels(seeds[6], (2, D), ((1, 32),), -0.2, 0.2)), 100.0, 10000.0),
        "attention_master": scatter_about(seeds[7], (D, QKV), D ** -0.5, 0.125, ((0, 32),), jnp.float32),
        "attention_first": scatter_about(seeds[8], (D, QKV), 14.0, 80.0, ((0, 32),), jnp.float32),
        "attention_second": jnp.clip(jnp.exp(math.log(8000.0) - 4.6051702 * jax.random.uniform(seeds[9], (D, QKV), jnp.float32) ** levels(seeds[9], (D, QKV), ((0, 32),), -0.2, 0.2)), 80.0, 8000.0),
        "merge_master": scatter_about(seeds[10], (D, AO), (AO // 64) ** -0.5, 1.0, ((0, 32),), jnp.float32),
        "merge_first": scatter_about(seeds[11], (D, AO), 1.7, 6.0, ((0, 32),), jnp.float32),
        "merge_second": jnp.clip(jnp.exp(math.log(120.0) - 4.0943446 * jax.random.uniform(seeds[12], (D, AO), jnp.float32) ** levels(seeds[12], (D, AO), ((0, 32),), -0.2, 0.2)), 2.0, 120.0),
        "feedforward_master": scatter_about(seeds[13], (D, 3 * FF), D ** -0.5, 0.125, ((0, 32),), jnp.float32),
        "feedforward_first": scatter_about(seeds[14], (D, 3 * FF), 8.0, 48.0, ((0, 32),), jnp.float32),
        "feedforward_second": jnp.clip(jnp.exp(math.log(2000.0) - 4.199705 * jax.random.uniform(seeds[15], (D, 3 * FF), jnp.float32) ** levels(seeds[15], (D, 3 * FF), ((0, 32),), -0.2, 0.2)), 30.0, 2000.0),
    }


EPS_NORM = 1e-06
ROPE_THETA = 1000042.0
MASK_FILL = -1e+30
BETA_ONE = 0.9
BETA_TWO = 0.95
ADAM_EPS = 1e-08
LEARN_RATE = 0.02
WEIGHT_DECAY = 0.1

@jax.custom_vjp
def low(v):
    return lax.optimization_barrier(v.astype(jnp.bfloat16)).astype(jnp.float32)

@jax.custom_vjp
def low_back(v):
    return v

def low_keep(v):
    return (low(v), None)

def low_pass(kept, grad):
    return (grad,)

def back_keep(v):
    return (v, None)

def back_low(kept, grad):
    return (low(grad),)
low.defvjp(low_keep, low_pass)
low_back.defvjp(back_keep, back_low)

def norm_rows(values, gain_row):
    return values * lax.rsqrt(lax.optimization_barrier(jnp.mean(values * values, axis=-1, keepdims=True)) + EPS_NORM) * gain_row

def rotate(values, cosine, sine_part):
    half_width = values.shape[-1] // 2
    front_half = values[..., :half_width]
    back_half = values[..., half_width:]
    return jnp.concatenate([front_half * cosine - back_half * sine_part, back_half * cosine + front_half * sine_part], axis=-1)

def angle_table(positions):
    inverse_rate = ROPE_THETA ** (-(jnp.arange(HD // 2, dtype=jnp.float32) * 2.0) / HD)
    angles = positions.astype(jnp.float32)[..., None] * inverse_rate
    return (jnp.cos(angles), jnp.sin(angles))

def segment_positions(segment_row, source_row):
    labels = jnp.arange(PROMPTS, dtype=jnp.int32)
    member = (segment_row[None, :] == labels[:, None]).astype(jnp.int32)
    lengths = lax.optimization_barrier(jnp.sum(member, axis=1, dtype=jnp.int32))
    starts = jnp.cumsum(lengths, dtype=jnp.int32) - lengths
    prompt_index = jnp.arange(segment_row.shape[0], dtype=jnp.int32)
    prompt_positions = prompt_index - lax.optimization_barrier(jnp.sum(member * starts[:, None], axis=0, dtype=jnp.int32))
    source_length = lax.optimization_barrier(jnp.sum((source_row[:, None] == labels[None, :]).astype(jnp.int32) * lengths[None, :], axis=1, dtype=jnp.int32))
    follow_positions = source_length[:, None] + jnp.arange(CONT, dtype=jnp.int32)[None, :]
    return (prompt_positions, follow_positions)

def visibility(segment_row, source_row, device_count, prompt_rows):
    row_count = prompt_rows + CONT
    row_index = jnp.arange(row_count, dtype=jnp.int32)
    is_prompt = row_index < prompt_rows
    global_row = jnp.arange(device_count, dtype=jnp.int32)[:, None] * prompt_rows + jnp.minimum(row_index, prompt_rows - 1)[None, :]
    query_segment = jnp.where(is_prompt[None, :], segment_row[global_row], source_row[:, None])
    key_index = jnp.arange(PROMPT_LEN, dtype=jnp.int32)
    prompt_seen = (segment_row[None, None, :] == query_segment[:, :, None]) & ((key_index[None, None, :] <= global_row[:, :, None]) | ~is_prompt[None, :, None])
    follow_seen = (~is_prompt)[:, None] & (jnp.arange(CONT, dtype=jnp.int32)[None, :] <= (row_index - prompt_rows)[:, None])
    return jnp.concatenate([prompt_seen, jnp.broadcast_to(follow_seen, (device_count,) + follow_seen.shape)], axis=2)

def group_forward(weights, group_rows, segment_row, source_row):
    gain_copy, attention_copy, merge_copy, feedforward_copy = weights
    device_count = group_rows.shape[0]
    row_count = group_rows.shape[1]
    prompt_rows = PROMPT_LEN // device_count
    query_width = HQ * HD
    key_width = HK * HD
    prompt_positions, follow_positions = segment_positions(segment_row, source_row)
    positions = jnp.concatenate([prompt_positions.reshape(device_count, prompt_rows), follow_positions], axis=1)
    cosine, sine_part = angle_table(positions)
    cosine = cosine[:, :, None, :]
    sine_part = sine_part[:, :, None, :]
    highest = lax.Precision.HIGHEST
    normed = low(norm_rows(group_rows, gain_copy[0]))
    project = low_back(jnp.einsum('nrd,de->nre', normed, attention_copy, precision=highest))
    queries = low(rotate(project[..., :query_width].reshape(device_count, row_count, HQ, HD), cosine, sine_part))
    key_rows = low(rotate(project[..., query_width:query_width + key_width].reshape(device_count, row_count, HK, HD), cosine, sine_part))
    value_rows = low(project[..., query_width + key_width:].reshape(device_count, row_count, HK, HD))
    prompt_keys = key_rows[:, :prompt_rows].reshape(PROMPT_LEN, HK, HD)
    prompt_values = value_rows[:, :prompt_rows].reshape(PROMPT_LEN, HK, HD)
    all_keys = jnp.concatenate([jnp.broadcast_to(prompt_keys, (device_count,) + prompt_keys.shape), key_rows[:, prompt_rows:]], axis=1)
    all_values = jnp.concatenate([jnp.broadcast_to(prompt_values, (device_count,) + prompt_values.shape), value_rows[:, prompt_rows:]], axis=1)
    visible = visibility(segment_row, source_row, device_count, prompt_rows)
    head_queries = queries.reshape(device_count, row_count, HK, HQ // HK, HD)
    raw_scores = jnp.einsum('nrkgd,nskd->nkgrs', head_queries, all_keys, precision=highest) * HD ** (-0.5)
    scores = low_back(raw_scores)
    masked = jnp.where(visible[:, None, None], scores, MASK_FILL)
    row_peak = lax.optimization_barrier(jnp.max(masked, axis=-1, keepdims=True))
    unnormed = jnp.exp(masked - row_peak)
    probabilities = low(unnormed / lax.optimization_barrier(jnp.sum(unnormed, axis=-1, keepdims=True)))
    attended = jnp.einsum('nkgrs,nskd->nrkgd', probabilities, all_values, precision=highest).reshape(device_count, row_count, query_width)
    attended = low(low_back(attended))
    branch = low_back(jnp.einsum('nre,de->nrd', attended, merge_copy, precision=highest))
    middle = group_rows + branch
    normed_two = low(norm_rows(middle, gain_copy[1]))
    gate_up = low_back(jnp.einsum('nrd,de->nre', normed_two, feedforward_copy[:, :2 * FF], precision=highest))
    activated = low(jax.nn.silu(gate_up[..., :FF]) * gate_up[..., FF:])
    down_out = low_back(jnp.einsum('nrf,df->nrd', activated, feedforward_copy[:, 2 * FF:], precision=highest))
    return middle + down_out

def adam_step(master, first_moment, second_moment, gradient, decay_rate):
    first_new = BETA_ONE * first_moment + (1.0 - BETA_ONE) * gradient
    second_new = BETA_TWO * second_moment + (1.0 - BETA_TWO) * gradient * gradient
    correct_one = 1.0 - BETA_ONE ** STEP
    correct_two = 1.0 - BETA_TWO ** STEP
    update = first_new / correct_one / (jnp.sqrt(second_new / correct_two) + ADAM_EPS)
    return (-LEARN_RATE * (update + decay_rate * master), first_new, second_new)

def reference(hidden, cotangent, segment_ids, continuation_prompt, gain_master, gain_first, gain_second, attention_master, attention_first, attention_second, merge_master, merge_first, merge_second, feedforward_master, feedforward_first, feedforward_second):

    def forward(gain_param, attention_param, merge_param, feedforward_param, inputs):
        weights = (low(gain_param), low(attention_param), low(merge_param), low(feedforward_param))

        def one_group(group_items):
            return group_forward(weights, group_items[0], group_items[1], group_items[2])
        return lax.map(jax.checkpoint(one_group), (inputs, segment_ids, continuation_prompt))
    result, pullback = jax.vjp(forward, gain_master, attention_master, merge_master, feedforward_master, hidden.astype(jnp.float32))
    gain_grad, attention_grad, merge_grad, feedforward_grad, input_grad = pullback(cotangent.astype(jnp.float32))
    gain_new = adam_step(gain_master, gain_first, gain_second, gain_grad, 0.0)
    attention_new = adam_step(attention_master, attention_first, attention_second, attention_grad, WEIGHT_DECAY)
    merge_new = adam_step(merge_master, merge_first, merge_second, merge_grad, WEIGHT_DECAY)
    feedforward_new = adam_step(feedforward_master, feedforward_first, feedforward_second, feedforward_grad, WEIGHT_DECAY)
    return (result.astype(jnp.bfloat16), input_grad, gain_grad, gain_new[0], gain_new[1], gain_new[2], attention_grad, attention_new[0], attention_new[1], attention_new[2], merge_grad, merge_new[0], merge_new[1], merge_new[2], feedforward_grad, feedforward_new[0], feedforward_new[1], feedforward_new[2])
```

```python
import jax
import jax.numpy as jnp
from jax import lax
from jax.sharding import PartitionSpec as P

D = 2048
FF = 8192
HQ = 8
HK = 4
HD = 256
PROMPT_LEN = 1024
PROMPTS = 4
CONT = 64
STEP = 10


EPS_NORM = 1e-06
ROPE_THETA = 1000042.0
MASK_FILL = -1e30
BETA_ONE = 0.9
BETA_TWO = 0.95
ADAM_EPS = 1e-08
LEARN_RATE = 0.02
WEIGHT_DECAY = 0.1


def contract(left, right, left_axis, right_axis):
    return lax.dot_general(
        left, right, (((left_axis,), (right_axis,)), ((), ())), preferred_element_type=jnp.float32
    )


def rotate(values, cosine, sine_part):
    half_width = values.shape[-1] // 2
    front_half = values[..., :half_width]
    back_half = values[..., half_width:]
    return jnp.concatenate(
        [front_half * cosine - back_half * sine_part, back_half * cosine + front_half * sine_part],
        axis=-1,
    )


def angle_table(positions):
    inverse_rate = ROPE_THETA ** (-(jnp.arange(HD // 2, dtype=jnp.float32) * 2.0) / HD)
    angles = positions.astype(jnp.float32)[..., None] * inverse_rate
    return (jnp.cos(angles), jnp.sin(angles))


def segment_positions(segment_row, source_row):
    labels = jnp.arange(PROMPTS, dtype=jnp.int32)
    member = (segment_row[None, :] == labels[:, None]).astype(jnp.int32)
    lengths = jnp.sum(member, axis=1, dtype=jnp.int32)
    starts = jnp.sum(
        jnp.where(labels[None, :] < labels[:, None], lengths[None, :], 0), axis=1, dtype=jnp.int32
    )
    prompt_index = jnp.arange(segment_row.shape[0], dtype=jnp.int32)
    prompt_positions = prompt_index - jnp.sum(member * starts[:, None], axis=0, dtype=jnp.int32)
    source_length = jnp.sum(
        (source_row[:, None] == labels[None, :]).astype(jnp.int32) * lengths[None, :],
        axis=1,
        dtype=jnp.int32,
    )
    follow_positions = source_length[:, None] + jnp.arange(CONT, dtype=jnp.int32)[None, :]
    return (prompt_positions, follow_positions)


def norm_scale(values):
    return lax.rsqrt(jnp.mean(values * values, axis=-1, keepdims=True) + EPS_NORM)


def norm_back(values, row_scale, gain_row, normed_grad):
    scaled = normed_grad * gain_row
    return row_scale * scaled - values * row_scale**3 * jnp.mean(
        scaled * values, axis=-1, keepdims=True
    )


def masked_scores(head_queries, all_keys, visible, score_scale):
    raw_scores = (
        jnp.einsum("rkgd,skd->kgrs", head_queries, all_keys, preferred_element_type=jnp.float32)
        * score_scale
    )
    return jnp.where(visible, raw_scores, MASK_FILL)


def adam_step(master, first_moment, second_moment, gradient, decay_rate):
    first_new = BETA_ONE * first_moment + (1.0 - BETA_ONE) * gradient
    second_new = BETA_TWO * second_moment + (1.0 - BETA_TWO) * gradient * gradient
    correct_one = 1.0 - BETA_ONE**STEP
    correct_two = 1.0 - BETA_TWO**STEP
    update = first_new / correct_one / (jnp.sqrt(second_new / correct_two) + ADAM_EPS)
    return (-LEARN_RATE * (update + decay_rate * master), first_new, second_new)


def gate_parts(gate_values, up_values):
    gate_sigmoid = jax.nn.sigmoid(gate_values)
    gate_silu = gate_values * gate_sigmoid
    return (gate_sigmoid, gate_silu, (gate_silu * up_values).astype(jnp.bfloat16))


def gate_backward(activated_grad, gate_values, up_values, gate_sigmoid, gate_silu):
    gate_grad = (
        activated_grad * up_values * gate_sigmoid * (1.0 + gate_values * (1.0 - gate_sigmoid))
    ).astype(jnp.bfloat16)
    up_grad = (activated_grad * gate_silu).astype(jnp.bfloat16)
    return (gate_grad, up_grad)


def body(
    hidden,
    cotangent,
    segment_ids,
    continuation_prompt,
    gain_master,
    gain_first,
    gain_second,
    attention_master,
    attention_first,
    attention_second,
    merge_master,
    merge_first,
    merge_second,
    feedforward_master,
    feedforward_first,
    feedforward_second,
):
    group_index = lax.axis_index("grp")
    row_count = hidden.shape[2]
    prompt_rows = row_count - CONT
    query_width = HQ * HD
    key_width = HK * HD
    group_heads = HQ // HK
    score_scale = HD ** (-0.5)
    key_count = PROMPT_LEN + CONT
    gain_low = gain_master.astype(jnp.bfloat16)
    attention_low = attention_master.astype(jnp.bfloat16)
    merge_low = merge_master.astype(jnp.bfloat16)
    dp_size = lax.axis_size("dp")
    own_rows = feedforward_master.shape[0]
    own_hidden = FF // dp_size
    gain_rows, attention_weight, merge_weight = (
        lax.all_gather(gain_low, ("grp", "dp"), axis=1, tiled=True),
        lax.all_gather(attention_low, ("grp", "dp"), axis=0, tiled=True),
        lax.all_gather(merge_low, ("grp", "dp"), axis=0, tiled=True),
    )
    feedforward_low = jnp.transpose(
        feedforward_master.astype(jnp.bfloat16).reshape(own_rows, 3, dp_size, own_hidden),
        (2, 0, 1, 3),
    ).reshape(dp_size * own_rows, 3 * own_hidden)
    feedforward_weight = lax.all_gather(
        lax.all_to_all(feedforward_low, "dp", 0, 0, tiled=True), "grp", axis=0, tiled=True
    )
    gate_weight = feedforward_weight[:, : 2 * own_hidden]
    down_weight = feedforward_weight[:, 2 * own_hidden :]
    down_grad = lax.all_gather(cotangent.reshape(-1, D), "dp", axis=0, tiled=True)
    gain_float = gain_rows.astype(jnp.float32)
    segment_row = segment_ids[0]
    source_row = continuation_prompt[0]
    prompt_positions, follow_positions = segment_positions(segment_row, source_row)
    own_positions = jnp.concatenate(
        [
            lax.dynamic_slice_in_dim(prompt_positions, group_index * prompt_rows, prompt_rows),
            follow_positions[0],
        ]
    )
    cosine, sine_part = angle_table(own_positions)
    cosine = cosine[:, None, :]
    sine_part = sine_part[:, None, :]
    inputs = hidden.reshape(row_count, D).astype(jnp.float32)
    first_scale = norm_scale(inputs)
    normed = (inputs * first_scale * gain_float[0]).astype(jnp.bfloat16)
    project = jnp.dot(normed, attention_weight, preferred_element_type=jnp.float32)
    queries = rotate(project[:, :query_width].reshape(row_count, HQ, HD), cosine, sine_part).astype(
        jnp.bfloat16
    )
    key_rows = (
        rotate(
            project[:, query_width : query_width + key_width].reshape(row_count, HK, HD),
            cosine,
            sine_part,
        )
        .astype(jnp.bfloat16)
        .reshape(row_count, key_width)
    )
    value_rows = project[:, query_width + key_width :].astype(jnp.bfloat16)
    prompt_pairs = jnp.concatenate([key_rows[:prompt_rows], value_rows[:prompt_rows]], axis=1)
    gathered = lax.all_gather(prompt_pairs, "grp", axis=0, tiled=True)
    all_keys = jnp.concatenate([gathered[:, :key_width], key_rows[prompt_rows:]], axis=0).reshape(
        key_count, HK, HD
    )
    all_values = jnp.concatenate(
        [gathered[:, key_width:], value_rows[prompt_rows:]], axis=0
    ).reshape(key_count, HK, HD)
    row_index = jnp.arange(row_count, dtype=jnp.int32)
    is_prompt = row_index < prompt_rows
    global_row = group_index * prompt_rows + jnp.minimum(row_index, prompt_rows - 1)
    own_segment = lax.dynamic_slice_in_dim(segment_row, group_index * prompt_rows, prompt_rows)
    query_segment = jnp.concatenate([own_segment, jnp.broadcast_to(source_row, (CONT,))])
    key_index = jnp.arange(PROMPT_LEN, dtype=jnp.int32)
    prompt_seen = (segment_row[None, :] == query_segment[:, None]) & (
        (key_index[None, :] <= global_row[:, None]) | ~is_prompt[:, None]
    )
    follow_seen = (~is_prompt)[:, None] & (
        jnp.arange(CONT, dtype=jnp.int32)[None, :] <= (row_index - prompt_rows)[:, None]
    )
    visible = jnp.concatenate([prompt_seen, follow_seen], axis=1)
    head_queries = queries.reshape(row_count, HK, group_heads, HD)
    scores = masked_scores(head_queries, all_keys, visible, score_scale)
    row_peak = jnp.max(scores, axis=-1, keepdims=True)
    unnormed = jnp.exp(scores - row_peak)
    row_total = jnp.sum(unnormed, axis=-1, keepdims=True)
    probability_low = (unnormed / row_total).astype(jnp.bfloat16)
    row_logsum = row_peak + jnp.log(row_total)
    attended = (
        jnp.einsum(
            "kgrs,skd->rkgd", probability_low, all_values, preferred_element_type=jnp.float32
        )
        .reshape(row_count, query_width)
        .astype(jnp.bfloat16)
    )
    middle = inputs + contract(attended, merge_weight, 1, 1)
    second_scale = norm_scale(middle)
    normed_two = (middle * second_scale * gain_float[1]).astype(jnp.bfloat16)
    grad_rows = cotangent.reshape(row_count, D).astype(jnp.float32)
    normed_all = lax.all_gather(normed_two, "dp", axis=0, tiled=True)
    gate_up = jnp.dot(normed_all, gate_weight, preferred_element_type=jnp.float32)
    gate_values = gate_up[:, :own_hidden]
    up_values = gate_up[:, own_hidden:]
    gate_sigmoid, gate_silu, activated = gate_parts(gate_values, up_values)
    down_part = contract(activated, down_weight, 1, 1).astype(jnp.bfloat16)
    activated_grad = contract(down_grad, down_weight, 1, 0)
    gate_grad, up_grad = gate_backward(
        activated_grad, gate_values, up_values, gate_sigmoid, gate_silu
    )
    gate_up_grad = jnp.concatenate([gate_grad, up_grad], axis=1)
    normed_two_part = contract(gate_up_grad, gate_weight, 1, 1).astype(jnp.bfloat16)
    normed_two_grad = lax.psum_scatter(
        normed_two_part, "dp", scatter_dimension=0, tiled=True
    ).astype(jnp.float32)
    result = middle + lax.psum_scatter(
        down_part, "dp", scatter_dimension=0, tiled=True
    ).astype(jnp.float32)

    def to_owner(left, right):
        part = lax.psum_scatter(
            contract(left, right, 0, 0).astype(jnp.bfloat16),
            "grp",
            scatter_dimension=0,
            tiled=True,
        )
        spread = lax.all_to_all(part, "dp", 0, 0, tiled=True)
        width = right.shape[1] // own_hidden
        return (
            jnp.transpose(spread.reshape(dp_size, own_rows, width, own_hidden), (1, 2, 0, 3))
            .reshape(own_rows, width * FF)
            .astype(jnp.float32)
        )

    feedforward_grad = jnp.concatenate(
        [to_owner(normed_all, gate_up_grad), to_owner(down_grad, activated)], axis=1
    )
    block_output = result.astype(jnp.bfloat16).reshape(hidden.shape)
    middle_grad = grad_rows + norm_back(middle, second_scale, gain_float[1], normed_two_grad)
    gain_two_part = jnp.sum(normed_two_grad * middle * second_scale, axis=0)
    branch_grad = middle_grad.astype(jnp.bfloat16)
    merge_term = contract(branch_grad, attended, 0, 0)
    attended_grad = (
        contract(branch_grad, merge_weight, 1, 0)
        .astype(jnp.bfloat16)
        .reshape(row_count, HK, group_heads, HD)
    )
    scores = masked_scores(head_queries, all_keys, visible, score_scale)
    probabilities = jnp.exp(scores - row_logsum)
    probability_grad = jnp.einsum(
        "rkgd,skd->kgrs", attended_grad, all_values, preferred_element_type=jnp.float32
    )
    row_delta = jnp.sum(probabilities * probability_grad, axis=-1, keepdims=True)
    score_grad = (probabilities * (probability_grad - row_delta)).astype(jnp.bfloat16)
    query_grad = (
        jnp.einsum("kgrs,skd->rkgd", score_grad, all_keys, preferred_element_type=jnp.float32)
        * score_scale
    )
    key_grad = (
        jnp.einsum("kgrs,rkgd->skd", score_grad, head_queries, preferred_element_type=jnp.float32)
        * score_scale
    )
    value_grad = jnp.einsum(
        "kgrs,rkgd->skd",
        probabilities.astype(jnp.bfloat16),
        attended_grad,
        preferred_element_type=jnp.float32,
    )
    prompt_grads = jnp.concatenate(
        [
            key_grad[:PROMPT_LEN].reshape(PROMPT_LEN, key_width),
            value_grad[:PROMPT_LEN].reshape(PROMPT_LEN, key_width),
        ],
        axis=1,
    )
    summed = lax.psum_scatter(
        prompt_grads.astype(jnp.bfloat16), "grp", scatter_dimension=0, tiled=True
    ).astype(jnp.float32)
    key_local = jnp.concatenate(
        [summed[:, :key_width], key_grad[PROMPT_LEN:].reshape(CONT, key_width)], axis=0
    ).reshape(row_count, HK, HD)
    value_local = jnp.concatenate(
        [summed[:, key_width:], value_grad[PROMPT_LEN:].reshape(CONT, key_width)], axis=0
    )
    project_grad = jnp.concatenate(
        [
            rotate(query_grad.reshape(row_count, HQ, HD), cosine, -sine_part).reshape(
                row_count, query_width
            ),
            rotate(key_local, cosine, -sine_part).reshape(row_count, key_width),
            value_local,
        ],
        axis=1,
    ).astype(jnp.bfloat16)
    attention_term = contract(normed, project_grad, 0, 0)
    normed_grad = contract(project_grad, attention_weight, 1, 1)
    input_grad = (middle_grad + norm_back(inputs, first_scale, gain_float[0], normed_grad)).reshape(
        hidden.shape
    )
    gain_one_part = jnp.sum(normed_grad * inputs * first_scale, axis=0)
    gain_term = jnp.stack([gain_one_part, gain_two_part])
    gain_grad, attention_grad, merge_grad = (
        lax.psum_scatter(gain_term, ("grp", "dp"), scatter_dimension=1, tiled=True),
        lax.psum_scatter(
            attention_term.astype(jnp.bfloat16), ("grp", "dp"), scatter_dimension=0, tiled=True
        ).astype(jnp.float32),
        lax.psum_scatter(
            merge_term.astype(jnp.bfloat16), ("grp", "dp"), scatter_dimension=0, tiled=True
        ).astype(jnp.float32),
    )
    gain_new = adam_step(gain_master, gain_first, gain_second, gain_grad, 0.0)
    attention_new = adam_step(
        attention_master, attention_first, attention_second, attention_grad, WEIGHT_DECAY
    )
    merge_new = adam_step(merge_master, merge_first, merge_second, merge_grad, WEIGHT_DECAY)
    feedforward_new = adam_step(
        feedforward_master, feedforward_first, feedforward_second, feedforward_grad, WEIGHT_DECAY
    )
    return (
        block_output,
        input_grad,
        gain_grad,
        gain_new[0],
        gain_new[1],
        gain_new[2],
        attention_grad,
        attention_new[0],
        attention_new[1],
        attention_new[2],
        merge_grad,
        merge_new[0],
        merge_new[1],
        merge_new[2],
        feedforward_grad,
        feedforward_new[0],
        feedforward_new[1],
        feedforward_new[2],
    )


def solution(mesh):
    placed = (
        P("dp", "grp", None, None),
        P("dp", "grp", None, None),
        P("dp", None),
        P("dp", "grp"),
        P(None, ("grp", "dp")),
        P(None, ("grp", "dp")),
        P(None, ("grp", "dp")),
        P(("grp", "dp"), None),
        P(("grp", "dp"), None),
        P(("grp", "dp"), None),
        P(("grp", "dp"), None),
        P(("grp", "dp"), None),
        P(("grp", "dp"), None),
        P(("grp", "dp"), None),
        P(("grp", "dp"), None),
        P(("grp", "dp"), None),
    )
    return jax.shard_map(
        body,
        mesh=mesh,
        in_specs=placed,
        out_specs=(
            P("dp", "grp", None, None),
            P("dp", "grp", None, None),
            P(None, ("grp", "dp")),
            P(None, ("grp", "dp")),
            P(None, ("grp", "dp")),
            P(None, ("grp", "dp")),
            P(("grp", "dp"), None),
            P(("grp", "dp"), None),
            P(("grp", "dp"), None),
            P(("grp", "dp"), None),
            P(("grp", "dp"), None),
            P(("grp", "dp"), None),
            P(("grp", "dp"), None),
            P(("grp", "dp"), None),
            P(("grp", "dp"), None),
            P(("grp", "dp"), None),
            P(("grp", "dp"), None),
            P(("grp", "dp"), None),
        ),
        check_vma=False,
    )
```

```python
import functools

import jax
import jax.numpy as jnp
from jax import lax
from jax.experimental import pallas as pl
from jax.experimental.pallas import tpu as pltpu
from jax.sharding import PartitionSpec as P

D = 2048
FF = 8192
HQ = 8
HK = 4
HD = 256
PROMPT_LEN = 1024
PROMPTS = 4
CONT = 64
STEP = 10
GAIN_PAD = 128

EPS_NORM = 1e-06
ROPE_THETA = 1000042.0
MASK_FILL = -1e30
BETA_ONE = 0.9
BETA_TWO = 0.95
ADAM_EPS = 1e-08
LEARN_RATE = 0.02
WEIGHT_DECAY = 0.1
LOW = jnp.bfloat16
FULL = jnp.float32
MESH = pl.DeviceIdType.MESH


def contract(left, right, left_axis, right_axis):
    return lax.dot_general(
        left, right, (((left_axis,), (right_axis,)), ((), ())), preferred_element_type=FULL
    )


def rotate(values, cosine, sine_part):
    half_width = values.shape[-1] // 2
    front_half = values[..., :half_width]
    back_half = values[..., half_width:]
    return jnp.concatenate(
        [front_half * cosine - back_half * sine_part, back_half * cosine + front_half * sine_part],
        axis=-1,
    )


def angle_table(positions):
    inverse_rate = ROPE_THETA ** (-(jnp.arange(HD // 2, dtype=FULL) * 2.0) / HD)
    angles = positions.astype(FULL)[..., None] * inverse_rate
    return (jnp.cos(angles), jnp.sin(angles))


def segment_positions(segment_row, source_row):
    labels = jnp.arange(PROMPTS, dtype=jnp.int32)
    member = (segment_row[None, :] == labels[:, None]).astype(jnp.int32)
    lengths = jnp.sum(member, axis=1, dtype=jnp.int32)
    starts = jnp.sum(
        jnp.where(labels[None, :] < labels[:, None], lengths[None, :], 0), axis=1, dtype=jnp.int32
    )
    prompt_index = jnp.arange(segment_row.shape[0], dtype=jnp.int32)
    prompt_positions = prompt_index - jnp.sum(member * starts[:, None], axis=0, dtype=jnp.int32)
    source_length = jnp.sum(
        (source_row[:, None] == labels[None, :]).astype(jnp.int32) * lengths[None, :],
        axis=1,
        dtype=jnp.int32,
    )
    follow_positions = source_length[:, None] + jnp.arange(CONT, dtype=jnp.int32)[None, :]
    return (prompt_positions, follow_positions)


def norm_scale(values):
    return lax.rsqrt(jnp.mean(values * values, axis=-1, keepdims=True) + EPS_NORM)


def norm_back(values, row_scale, gain_row, normed_grad):
    scaled = normed_grad * gain_row
    return row_scale * scaled - values * row_scale**3 * jnp.mean(
        scaled * values, axis=-1, keepdims=True
    )


def masked_scores(head_queries, all_keys, visible, score_scale):
    raw_scores = (
        jnp.einsum("rkgd,skd->kgrs", head_queries, all_keys, preferred_element_type=FULL)
        * score_scale
    )
    return jnp.where(visible, raw_scores, MASK_FILL)


def adam_step(master, first_moment, second_moment, gradient, decay_rate):
    first_new = BETA_ONE * first_moment + (1.0 - BETA_ONE) * gradient
    second_new = BETA_TWO * second_moment + (1.0 - BETA_TWO) * gradient * gradient
    correct_one = 1.0 - BETA_ONE**STEP
    correct_two = 1.0 - BETA_TWO**STEP
    update = first_new / correct_one / (jnp.sqrt(second_new / correct_two) + ADAM_EPS)
    return (-LEARN_RATE * (update + decay_rate * master), first_new, second_new)


def gate_parts(gate_values, up_values):
    gate_sigmoid = jax.nn.sigmoid(gate_values)
    gate_silu = gate_values * gate_sigmoid
    return (gate_sigmoid, gate_silu, (gate_silu * up_values).astype(LOW))


def gate_backward(activated_grad, gate_values, up_values, gate_sigmoid, gate_silu):
    gate_grad = (
        activated_grad * up_values * gate_sigmoid * (1.0 + gate_values * (1.0 - gate_sigmoid))
    ).astype(LOW)
    up_grad = (activated_grad * gate_silu).astype(LOW)
    return (gate_grad, up_grad)


def flip(index, bits):
    bit = 1
    while bit <= bits:
        if bits & bit:
            index = index + bit - 2 * bit * lax.rem(index // bit, 2)
        bit *= 2
    return index


def remote(source, target, send, recv, there):
    return pltpu.make_async_remote_copy(
        src_ref=source,
        dst_ref=target,
        send_sem=send,
        recv_sem=recv,
        device_id=there,
        device_id_type=MESH,
    )


def gather_kernel(
    lines,
    plane,
    prompt_rows,
    weight_ref,
    hidden_ref,
    forward_ref,
    weights_ref,
    rows_ref,
    gate_ref,
    down_ref,
    local_sem,
    line_send,
    line_recv,
    rows_send,
    rows_recv,
    near_send,
    near_recv,
    half_send,
    half_recv,
    core_send,
    core_recv,
    swap_send,
    swap_recv,
):
    g = lax.axis_index("grp")
    d = lax.axis_index("dp")
    evens = range(0, plane, 2)
    forward_halves = plane == 8
    near = (2, 4) if forward_halves else tuple(evens[1:])
    width = weight_ref.shape[1]
    cut = (width // 256) * 128

    barrier = pltpu.get_barrier_semaphore()
    for offset in range(1, plane):
        pl.semaphore_signal(barrier, inc=1, device_id=(g, flip(d, offset)), device_id_type=MESH)

    for step in range(1, lines):
        there = lax.rem(g + step, lines)
        pl.semaphore_signal(barrier, inc=1, device_id=(there, d), device_id_type=MESH)
    pl.semaphore_wait(barrier, plane + lines - 2)

    copy = remote
    own_rows = hidden_ref.at[pl.ds(0, prompt_rows)]

    def line_weight(way, step):
        block = g - step + 1 if way == 0 else g + step - 1
        source = weight_ref if step == 1 else weights_ref.at[block, d]
        return copy(
            source,
            weights_ref.at[block, d],
            line_send.at[way, step],
            line_recv.at[way, step],
            (g + 1 if way == 0 else g - 1, d),
        )

    def line_rows(way, step):
        block = g - step + 1 if way == 0 else g + step - 1
        source = own_rows if step == 1 else rows_ref.at[block]
        return copy(
            source,
            rows_ref.at[block],
            rows_send.at[way, step],
            rows_recv.at[way, step],
            (g + 1 if way == 0 else g - 1, d),
        )

    def sends(way, step):
        if way == 0:
            return (g < lines - 1) & (g >= step - 1)
        return (g > 0) & (g + step - 1 < lines)

    def receives(way, step):
        return g >= step if way == 0 else g + step < lines

    def near_copy(block, offset, own):
        source = weight_ref if own else weights_ref.at[block, d]
        at = near.index(offset)
        return copy(
            source,
            weights_ref.at[block, d],
            near_send.at[block, at],
            near_recv.at[block, at],
            (g, flip(d, offset)),
        )

    def half_copy(block, part):
        columns = pl.ds(0, cut) if part == 0 else pl.ds(cut, width - cut)
        origin = flip(d, 2) if part == 0 else flip(d, 4)
        there = flip(d, 4) if part == 0 else flip(d, 2)
        piece = weights_ref.at[block, origin, :, columns]
        return copy(
            piece, piece, half_send.at[block, part], half_recv.at[block, part], (g, there)
        )

    def core_copy(block, offset, own=False):
        source = weight_ref if own else weights_ref.at[block, flip(d, offset)]
        return copy(
            source,
            weights_ref.at[block, flip(d, offset)],
            core_send.at[block, offset // 2],
            core_recv.at[block, offset // 2],
            (g, flip(d, 1)),
        )

    own_hidden = down_ref.shape[2]

    def swap_piece(owner, part, source_index):
        source = forward_ref.at[:, pl.ds(part * FF + owner * own_hidden, own_hidden)]
        if part == 2:
            return source, down_ref.at[source_index]
        return source, gate_ref.at[source_index, :, pl.ds(part * own_hidden, own_hidden)]

    def swap_copy(offset, part):
        source, target = swap_piece(flip(d, offset), part, d)
        return copy(
            source,
            target,
            swap_send.at[offset, part],
            swap_recv.at[offset, part],
            (g, flip(d, offset)),
        )

    locals_ = (
        pltpu.make_async_copy(weight_ref, weights_ref.at[g, d], local_sem.at[0]),
        pltpu.make_async_copy(own_rows, rows_ref.at[g], local_sem.at[1]),
        *(
            pltpu.make_async_copy(*swap_piece(d, part, d), local_sem.at[2 + part])
            for part in range(3)
        ),
    )

    def launch(block, own):
        for offset in near:
            near_copy(block, offset, own).start()
        core_copy(block, 0, own).start()

    def relay(block):
        for offset in near:
            near_copy(block, offset, False).wait_recv()
            core_copy(block, offset).start()
        if forward_halves:
            half_copy(block, 0).start()
            half_copy(block, 1).start()

    def finish(block):
        if forward_halves:
            half_copy(block, 0).wait_recv()
            half_copy(block, 1).wait_recv()
            core_copy(block, 6).start()

    for way in (0, 1):
        pl.when(sends(way, 1))(lambda way=way: line_weight(way, 1).start())
    launch(g, True)
    for one in locals_:
        one.start()
    for offset in range(1, plane):
        for part in range(3):
            swap_copy(offset, part).start()

    for step in range(1, lines):
        for way in (0, 1):

            @pl.when(receives(way, step))
            def _(way=way, step=step):
                line_weight(way, step).wait_recv()

            if step + 1 < lines:
                pl.when(sends(way, step + 1))(
                    lambda way=way, step=step: line_weight(way, step + 1).start()
                )
            else:
                pl.when(sends(way, 1))(lambda way=way: line_rows(way, 1).start())

            @pl.when(receives(way, step))
            def _(way=way, step=step):
                launch(g - step if way == 0 else g + step, False)

        if step == 1:
            relay(g)
        else:
            for way in (0, 1):
                pl.when(receives(way, step - 1))(
                    lambda way=way, step=step: relay(
                        g - step + 1 if way == 0 else g + step - 1
                    )
                )
    for step in range(1, lines):
        for way in (0, 1):

            @pl.when(receives(way, step))
            def _(way=way, step=step):
                line_rows(way, step).wait_recv()

            if step + 1 < lines:
                pl.when(sends(way, step + 1))(
                    lambda way=way, step=step: line_rows(way, step + 1).start()
                )
        if step == 1:
            for way in (0, 1):
                pl.when(receives(way, lines - 1))(
                    lambda way=way: relay(g - lines + 1 if way == 0 else g + lines - 1)
                )
            finish(g)
    for step in range(1, lines):
        for way in (0, 1):
            pl.when(receives(way, step))(
                lambda way=way, step=step: finish(g - step if way == 0 else g + step)
            )

    def drain(block):
        for offset in evens:
            core_copy(block, offset).wait()
        for offset in near:
            near_copy(block, offset, False).wait_send()
        if forward_halves:
            half_copy(block, 0).wait_send()
            half_copy(block, 1).wait_send()

    drain(g)
    for step in range(1, lines):
        for way in (0, 1):
            pl.when(receives(way, step))(
                lambda way=way, step=step: drain(g - step if way == 0 else g + step)
            )

            @pl.when(sends(way, step))
            def _(way=way, step=step):
                line_weight(way, step).wait_send()
                line_rows(way, step).wait_send()

    for offset in range(1, plane):
        for part in range(3):
            swap_copy(offset, part).wait()
    for one in locals_:
        one.wait()


def gather_start(weight, hidden, forward):
    lines, plane = lax.axis_size("grp"), lax.axis_size("dp")
    prompt_rows = PROMPT_LEN // lines
    own_rows, width = weight.shape
    anywhere = pl.BlockSpec(memory_space=pl.ANY)
    dma = pltpu.SemaphoreType.DMA
    near_count = 2 if plane == 8 else plane // 2 - 1
    pairs = (
        (2, lines),
        (2, lines),
        (2, lines),
        (2, lines),
        (lines, near_count),
        (lines, near_count),
        (lines, 2),
        (lines, 2),
        (lines, plane // 2),
        (lines, plane // 2),
        (plane, 3),
        (plane, 3),
    )
    own_hidden = FF // plane
    return pl.pallas_call(
        functools.partial(gather_kernel, lines, plane, prompt_rows),
        out_shape=(
            jax.ShapeDtypeStruct((lines, plane, own_rows, width), weight.dtype),
            jax.ShapeDtypeStruct((lines, prompt_rows, D), hidden.dtype),
            jax.ShapeDtypeStruct((plane, own_rows, 2 * own_hidden), forward.dtype),
            jax.ShapeDtypeStruct((plane, own_rows, own_hidden), forward.dtype),
        ),
        in_specs=[anywhere] * 3,
        out_specs=(anywhere,) * 4,
        scratch_shapes=[dma((5,))] + [dma(shape) for shape in pairs],
        compiler_params=pltpu.CompilerParams(collective_id=0, has_side_effects=True),
        name="gather_start",
    )(weight, hidden, forward)


def plane_swap(block, offset):
    size = lax.axis_size("dp")
    return lax.ppermute(block, "dp", [(i, i ^ offset) for i in range(size)])


def plane_gather(block):
    mine = [block] + [plane_swap(block, o) for o in range(2, lax.axis_size("dp"), 2)]
    pairs = [(one, plane_swap(one, 1)) for one in mine]
    return jnp.concatenate([one for pair in pairs for one in pair], axis=0)


def plane_scatter(part_of):
    size = lax.axis_size("dp")
    sums = {}
    for offset in list(range(size - 2, 0, -2)) + [0]:
        arrived = plane_swap(part_of(offset + 1).astype(LOW), 1)
        sums[offset] = part_of(offset).astype(FULL) + arrived.astype(FULL)
        if offset:
            sums[offset] = plane_swap(sums[offset].astype(LOW), offset)
    total = sums[0]
    for offset in range(2, size, 2):
        total = total + sums[offset].astype(FULL)
    return total


def plane_rows(term):
    lines, plane = lax.axis_size("grp"), lax.axis_size("dp")
    d = lax.axis_index("dp")
    blocks = term.reshape(lines, plane, -1, term.shape[1])
    mine = plane_scatter(
        lambda offset: lax.dynamic_index_in_dim(blocks, d ^ offset, 1, keepdims=False)
    )
    return mine.astype(LOW).reshape(-1, term.shape[1])


def line_scatter(term):
    return lax.psum_scatter(term, "grp", scatter_dimension=0, tiled=True)


def finish_kernel(
    lines,
    plane,
    query_ref,
    pair_ref,
    gain_ref,
    gate_ref,
    down_ref,
    a_master,
    a_first,
    a_second,
    f_master,
    f_first,
    f_second,
    a_grad,
    a_update,
    a_first_new,
    a_second_new,
    gain_out,
    f_grad,
    f_update,
    f_first_new,
    f_second_new,
    mine,
    core_in,
    plane_in,
    line_in,
    gate_in,
    down_in,
    state,
    made,
    a_state,
    a_made,
    gain_made,
    mine_sem,
    core_send,
    core_recv,
    plane_send,
    plane_recv,
    line_send,
    line_recv,
    swap_send,
    swap_recv,
    own_sem,
    state_sem,
    made_sem,
    a_sem,
    gain_sem,
):
    g = lax.axis_index("grp")
    d = lax.axis_index("dp")
    chips = plane // 2
    chip, core = lax.div(d, 2), lax.rem(d, 2)
    partner = d + 1 - 2 * core
    rows = a_master.shape[0]
    own_hidden = down_ref.shape[2]
    query_width, pair_width = query_ref.shape[4], pair_ref.shape[4]
    width = core_in.shape[3]
    parts = (
        (query_ref, pl.ds(0, query_width)),
        (pair_ref, pl.ds(query_width, pair_width)),
        (gain_ref, pl.ds(query_width + pair_width, GAIN_PAD)),
    )

    barrier = pltpu.get_barrier_semaphore()
    for step in range(1, plane):
        there = lax.rem(d + step, plane)
        pl.semaphore_signal(barrier, inc=1, device_id=(g, there), device_id_type=MESH)
    for step in range(1, lines):
        there = lax.rem(g + step, lines)
        pl.semaphore_signal(barrier, inc=1, device_id=(there, d), device_id_type=MESH)
    pl.semaphore_wait(barrier, plane + lines - 2)

    def line_at(turn):
        return lax.rem(g + turn + 1, lines)

    def core_copy(turn, part):
        line = line_at(turn)
        ref, columns = parts[part]
        return remote(
            ref.at[line, :, 1 - core],
            core_in.at[line, :, :, columns],
            core_send.at[turn, part],
            core_recv.at[turn, part],
            (g, partner),
        )

    def mine_copy(turn, part):
        line = line_at(turn)
        ref, columns = parts[part]
        return pltpu.make_async_copy(
            ref.at[line, :, core], mine.at[line, :, :, columns], mine_sem.at[turn, part]
        )

    def plane_copy(turn, step):
        line = line_at(turn)
        there = lax.rem(chip + step, chips)
        return remote(
            core_in.at[line, there],
            plane_in.at[line, chip],
            plane_send.at[turn, step],
            plane_recv.at[turn, step],
            (g, 2 * there + core),
        )

    def line_copy(turn):
        line = line_at(turn)
        return remote(
            core_in.at[line, chip],
            line_in.at[g],
            line_send.at[turn],
            line_recv.at[turn],
            (line, d),
        )

    def swap_copy(step, part):
        there = lax.rem(d + step, plane)
        source, target = (gate_ref, gate_in) if part == 0 else (down_ref, down_in)
        return remote(
            source.at[there],
            target.at[d],
            swap_send.at[step, part],
            swap_recv.at[step, part],
            (g, there),
        )

    own_swap = (
        pltpu.make_async_copy(gate_ref.at[d], gate_in.at[d], own_sem.at[0]),
        pltpu.make_async_copy(down_ref.at[d], down_in.at[d], own_sem.at[1]),
    )

    def state_copy(turn, part, which):
        source = (f_master, f_first, f_second)[which]
        block = lax.rem(d + turn, plane)
        slot = lax.rem(turn, 2)
        return pltpu.make_async_copy(
            source.at[:, pl.ds(part * FF + block * own_hidden, own_hidden)],
            state.at[slot, part, which],
            state_sem.at[slot, part, which],
        )

    def made_copy(turn, part, which):
        target = (f_grad, f_update, f_first_new, f_second_new)[which]
        block = lax.rem(d + turn, plane)
        slot = lax.rem(turn, 2)
        return pltpu.make_async_copy(
            made.at[slot, part, which],
            target.at[:, pl.ds(part * FF + block * own_hidden, own_hidden)],
            made_sem.at[slot, part, which],
        )

    def a_state_copy(which):
        return pltpu.make_async_copy(
            (a_master, a_first, a_second)[which], a_state.at[which], a_sem.at[which]
        )

    def a_made_copy(which):
        return pltpu.make_async_copy(
            a_made.at[which],
            (a_grad, a_update, a_first_new, a_second_new)[which],
            a_sem.at[3 + which],
        )

    for turn in range(lines):
        for part in range(3):
            core_copy(turn, part).start()
            mine_copy(turn, part).start()
    for step in range(1, plane):
        for part in range(2):
            swap_copy(step, part).start()
    for one in own_swap:
        one.start()
    for part in range(3):
        for which in range(3):
            state_copy(0, part, which).start()
    for which in range(3):
        a_state_copy(which).start()

    tile = 384 if width % 384 == 0 else 128
    tiles = width // tile

    for turn in range(lines):
        line = line_at(turn)
        for part in range(3):
            core_copy(turn, part).wait_recv()
            mine_copy(turn, part).wait()
        for step in range(1, chips):
            there = lax.rem(chip + step, chips)

            @pl.loop(0, tiles)
            def _(at, line=line, there=there):
                columns = pl.ds(pl.multiple_of(at * tile, tile), tile)
                total = mine[line, there, :, columns].astype(FULL) + core_in[
                    line, there, :, columns
                ].astype(FULL)
                core_in[line, there, :, columns] = total.astype(LOW)

            plane_copy(turn, step).start()

    def step_rows(slot, part, at, gradient):
        rows_at = pl.ds(pl.multiple_of(at * 16, 16), 16)
        update, first_new, second_new = adam_step(
            state[slot, part, 0, rows_at],
            state[slot, part, 1, rows_at],
            state[slot, part, 2, rows_at],
            gradient,
            WEIGHT_DECAY,
        )
        made[slot, part, 0, rows_at] = gradient
        made[slot, part, 1, rows_at] = update
        made[slot, part, 2, rows_at] = first_new
        made[slot, part, 3, rows_at] = second_new

    def forward_turn(turn):
        slot = lax.rem(turn, 2)
        block = lax.rem(d + turn, plane)

        @pl.when(turn + 1 < plane)
        def _():
            for part in range(3):
                for which in range(3):
                    state_copy(turn + 1, part, which).start()

        @pl.when(turn > 1)
        def _():
            for part in range(3):
                for which in range(4):
                    made_copy(turn - 2, part, which).wait()

        for part in range(3):
            for which in range(3):
                state_copy(turn, part, which).wait()

            @pl.loop(0, rows // 16)
            def _(at, part=part):
                rows_at = pl.ds(pl.multiple_of(at * 16, 16), 16)
                if part < 2:
                    gradient = gate_in[
                        block, rows_at, pl.ds(part * own_hidden, own_hidden)
                    ].astype(FULL)
                else:
                    gradient = down_in[block, rows_at].astype(FULL)
                step_rows(slot, part, at, gradient)

            for which in range(4):
                made_copy(turn, part, which).start()

    for one in own_swap:
        one.wait()
    for step in range(1, plane):
        for part in range(2):
            swap_copy(step, part).wait_recv()
    each = plane // lines
    for turn in range(lines):
        lax.fori_loop(turn * each, (turn + 1) * each, lambda k, c: (forward_turn(k), c)[1], 0)
        line = line_at(turn)
        for step in range(1, chips):
            plane_copy(turn, step).wait_recv()

        @pl.loop(0, tiles)
        def _(at, line=line):
            columns = pl.ds(pl.multiple_of(at * tile, tile), tile)
            total = mine[line, chip, :, columns].astype(FULL) + core_in[
                line, chip, :, columns
            ].astype(FULL)
            for step in range(1, chips):
                total = total + plane_in[line, lax.rem(chip + step, chips), :, columns].astype(FULL)
            core_in[line, chip, :, columns] = total.astype(LOW)

        if turn < lines - 1:
            line_copy(turn).start()

    for part in range(3):
        for which in range(4):
            for turn in (plane - 2, plane - 1):
                made_copy(turn, part, which).wait()
    for turn in range(lines - 1):
        line_copy(turn).wait_recv()
    for which in range(3):
        a_state_copy(which).wait()

    def owned(columns):
        total = core_in[g, chip, :, columns].astype(FULL)
        for step in range(1, lines):
            total = total + line_in[lax.rem(g + step, lines), :, columns].astype(FULL)
        return total

    @pl.loop(0, (query_width + pair_width) // 256)
    def _(at):
        columns = pl.ds(pl.multiple_of(at * 256, 256), 256)
        gradient = owned(columns)
        update, first_new, second_new = adam_step(
            a_state[0, :, columns],
            a_state[1, :, columns],
            a_state[2, :, columns],
            gradient,
            WEIGHT_DECAY,
        )
        a_made[0, :, columns] = gradient
        a_made[1, :, columns] = update
        a_made[2, :, columns] = first_new
        a_made[3, :, columns] = second_new

    for which in range(4):
        a_made_copy(which).start()
    gain_made[...] = owned(pl.ds(query_width + pair_width, GAIN_PAD))
    gain_copy = pltpu.make_async_copy(gain_made, gain_out, gain_sem.at[0])
    gain_copy.start()
    for turn in range(lines):
        for part in range(3):
            core_copy(turn, part).wait_send()
        for step in range(1, chips):
            plane_copy(turn, step).wait_send()
        if turn < lines - 1:
            line_copy(turn).wait_send()
    for step in range(1, plane):
        for part in range(2):
            swap_copy(step, part).wait_send()
    for which in range(4):
        a_made_copy(which).wait()
    gain_copy.wait()


def finish(query_term, pair_term, gain_term, gate_part, down_part, attention, forward):
    lines, plane = lax.axis_size("grp"), lax.axis_size("dp")
    chips = plane // 2
    rows, a_width = attention[0].shape
    f_width = forward[0].shape[1]
    own_hidden = down_part.shape[1]
    width = a_width + GAIN_PAD
    anywhere = pl.BlockSpec(memory_space=pl.ANY)
    dma = pltpu.SemaphoreType.DMA
    vmem = pltpu.VMEM

    def by_device(term):
        return term.reshape(lines, chips, 2, rows, term.shape[1])

    a_shape = jax.ShapeDtypeStruct((rows, a_width), FULL)
    f_shape = jax.ShapeDtypeStruct((rows, f_width), FULL)
    return pl.pallas_call(
        functools.partial(finish_kernel, lines, plane),
        out_shape=(a_shape,) * 4
        + (jax.ShapeDtypeStruct((rows, GAIN_PAD), FULL),)
        + (f_shape,) * 4,
        in_specs=[anywhere] * 11,
        out_specs=(anywhere,) * 9,
        scratch_shapes=[
            vmem((lines, chips, rows, width), LOW),
            vmem((lines, chips, rows, width), LOW),
            vmem((lines, chips, rows, width), LOW),
            vmem((lines, rows, width), LOW),
            vmem((plane, rows, 2 * own_hidden), LOW),
            vmem((plane, rows, own_hidden), LOW),
            vmem((2, 3, 3, rows, own_hidden), FULL),
            vmem((2, 3, 4, rows, own_hidden), FULL),
            vmem((3, rows, a_width), FULL),
            vmem((4, rows, a_width), FULL),
            vmem((rows, GAIN_PAD), FULL),
            dma((lines, 3)),
            dma((lines, 3)),
            dma((lines, 3)),
            dma((lines, chips)),
            dma((lines, chips)),
            dma((lines,)),
            dma((lines,)),
            dma((plane, 2)),
            dma((plane, 2)),
            dma((2,)),
            dma((2, 3, 3)),
            dma((2, 3, 4)),
            dma((7,)),
            dma((1,)),
        ],
        compiler_params=pltpu.CompilerParams(
            collective_id=1, has_side_effects=True, vmem_limit_bytes=60 * 2**20
        ),
        name="finish",
    )(
        by_device(query_term),
        by_device(pair_term),
        by_device(gain_term),
        gate_part.reshape(plane, rows, -1),
        down_part.reshape(plane, rows, -1),
        *attention,
        *forward,
    )


def body(
    hidden,
    cotangent,
    segment_ids,
    continuation_prompt,
    gain_master,
    gain_first,
    gain_second,
    attention_master,
    attention_first,
    attention_second,
    merge_master,
    merge_first,
    merge_second,
    feedforward_master,
    feedforward_first,
    feedforward_second,
):
    group_index = lax.axis_index("grp")
    dp_size = lax.axis_size("dp")
    row_count = hidden.shape[2]
    prompt_rows = row_count - CONT
    query_width = HQ * HD
    key_width = HK * HD
    qkv_width = query_width + 2 * key_width
    group_heads = HQ // HK
    score_scale = HD ** (-0.5)
    key_count = PROMPT_LEN + CONT
    own_rows = feedforward_master.shape[0]
    own_hidden = FF // dp_size
    own_inputs = hidden.reshape(row_count, D)

    gain_columns = jnp.pad(gain_master.T, ((0, 0), (0, GAIN_PAD - 2)))
    weight_low = jnp.concatenate(
        [attention_master.astype(LOW), merge_master.astype(LOW), gain_columns.astype(LOW)], axis=1
    )
    weights, group_rows, gate_rows, down_rows = gather_start(
        weight_low, own_inputs, feedforward_master.astype(LOW)
    )
    weights, late_cotangent = lax.optimization_barrier((weights, cotangent))
    weights = weights.reshape(D, -1)
    attention_weight = weights[:, :qkv_width]
    merge_weight = weights[:, qkv_width : qkv_width + D]
    gain_float = weights[:, qkv_width + D : qkv_width + D + 2].astype(FULL).T
    gate_weight = lax.all_gather(
        gate_rows.reshape(dp_size * own_rows, 2 * own_hidden), "grp", axis=0, tiled=True
    )
    gate_weight, down_rows = lax.optimization_barrier((gate_weight, down_rows))
    down_weight = lax.all_gather(
        down_rows.reshape(dp_size * own_rows, own_hidden), "grp", axis=0, tiled=True
    )
    down_grad = plane_gather(late_cotangent.reshape(row_count, D))

    segment_row = segment_ids[0]
    source_row = continuation_prompt[0]
    prompt_positions, follow_positions = segment_positions(segment_row, source_row)
    cosine, sine_part = angle_table(jnp.concatenate([prompt_positions, follow_positions[0]]))

    def own_part(table):
        return jnp.concatenate(
            [
                lax.dynamic_slice_in_dim(table, group_index * prompt_rows, prompt_rows),
                table[PROMPT_LEN:],
            ]
        )

    own_cosine = own_part(cosine)[:, None, :]
    own_sine = own_part(sine_part)[:, None, :]
    cosine = cosine[:, None, :]
    sine_part = sine_part[:, None, :]

    inputs = own_inputs.astype(FULL)
    first_scale = norm_scale(inputs)
    normed = (inputs * first_scale * gain_float[0]).astype(LOW)
    key_inputs = jnp.concatenate(
        [group_rows.reshape(PROMPT_LEN, D), own_inputs[prompt_rows:]], axis=0
    ).astype(FULL)
    key_scale = norm_scale(key_inputs)
    key_normed = (key_inputs * key_scale * gain_float[0]).astype(LOW)
    query_weight = attention_weight[:, :query_width]
    pair_weight = attention_weight[:, query_width:]
    queries = rotate(
        jnp.dot(normed, query_weight, preferred_element_type=FULL).reshape(row_count, HQ, HD),
        own_cosine,
        own_sine,
    ).astype(LOW)
    pairs = jnp.dot(key_normed, pair_weight, preferred_element_type=FULL)
    all_keys = rotate(
        pairs[:, :key_width].reshape(key_count, HK, HD), cosine, sine_part
    ).astype(LOW)
    all_values = pairs[:, key_width:].astype(LOW).reshape(key_count, HK, HD)

    row_index = jnp.arange(row_count, dtype=jnp.int32)
    is_prompt = row_index < prompt_rows
    global_row = group_index * prompt_rows + jnp.minimum(row_index, prompt_rows - 1)
    own_segment = lax.dynamic_slice_in_dim(segment_row, group_index * prompt_rows, prompt_rows)
    query_segment = jnp.concatenate([own_segment, jnp.broadcast_to(source_row, (CONT,))])
    key_index = jnp.arange(PROMPT_LEN, dtype=jnp.int32)
    prompt_seen = (segment_row[None, :] == query_segment[:, None]) & (
        (key_index[None, :] <= global_row[:, None]) | ~is_prompt[:, None]
    )
    follow_seen = (~is_prompt)[:, None] & (
        jnp.arange(CONT, dtype=jnp.int32)[None, :] <= (row_index - prompt_rows)[:, None]
    )
    visible = jnp.concatenate([prompt_seen, follow_seen], axis=1)
    head_queries = queries.reshape(row_count, HK, group_heads, HD)
    scores = masked_scores(head_queries, all_keys, visible, score_scale)
    row_peak = jnp.max(scores, axis=-1, keepdims=True)
    unnormed = jnp.exp(scores - row_peak)
    row_total = jnp.sum(unnormed, axis=-1, keepdims=True)
    probability_low = (unnormed / row_total).astype(LOW)
    row_logsum = row_peak + jnp.log(row_total)
    attended = (
        jnp.einsum("kgrs,skd->rkgd", probability_low, all_values, preferred_element_type=FULL)
        .reshape(row_count, query_width)
        .astype(LOW)
    )
    middle = inputs + contract(attended, merge_weight, 1, 1)
    second_scale = norm_scale(middle)
    normed_two = (middle * second_scale * gain_float[1]).astype(LOW)
    grad_rows = cotangent.reshape(row_count, D).astype(FULL)

    normed_two, down_grad = lax.optimization_barrier((normed_two, down_grad))
    normed_all = plane_gather(normed_two)
    gate_up = jnp.dot(normed_all, gate_weight, preferred_element_type=FULL)
    gate_values = gate_up[:, :own_hidden]
    up_values = gate_up[:, own_hidden:]
    gate_sigmoid, gate_silu, activated = gate_parts(gate_values, up_values)
    activated_grad = contract(down_grad, down_weight, 1, 0)
    gate_grad, up_grad = gate_backward(
        activated_grad, gate_values, up_values, gate_sigmoid, gate_silu
    )
    gate_up_grad = jnp.concatenate([gate_grad, up_grad], axis=1)

    def by_offset(left, right, right_axis):
        chunks = {}
        for offset in range(0, dp_size, 2):
            rows = left[offset * row_count : (offset + 2) * row_count]
            chunks[offset] = contract(rows, right, 1, right_axis).astype(LOW)
        return lambda offset: chunks[offset - offset % 2][
            (offset % 2) * row_count : (offset % 2 + 1) * row_count
        ]

    down_term = contract(down_grad, activated, 0, 0).astype(LOW)
    back_parts = by_offset(gate_up_grad, gate_weight, 1)
    gate_term = contract(normed_all, gate_up_grad, 0, 0).astype(LOW)
    normed_two_grad = plane_scatter(back_parts)
    down_part = line_scatter(down_term)
    gate_term, down_part = lax.optimization_barrier((gate_term, down_part))
    gate_part = line_scatter(gate_term)
    normed_two_grad, activated = lax.optimization_barrier((normed_two_grad, activated))
    result = middle + plane_scatter(by_offset(activated, down_weight, 1))
    block_output = result.astype(LOW).reshape(hidden.shape)
    middle_grad = grad_rows + norm_back(middle, second_scale, gain_float[1], normed_two_grad)
    gain_two_part = jnp.sum(normed_two_grad * middle * second_scale, axis=0)
    branch_grad = middle_grad.astype(LOW)
    merge_part = plane_rows(contract(branch_grad, attended, 0, 0).astype(LOW))
    merge_part, gate_part = lax.optimization_barrier((merge_part, gate_part))
    merge_grad = line_scatter(merge_part).astype(FULL)
    attended_grad = (
        contract(branch_grad, merge_weight, 1, 0)
        .astype(LOW)
        .reshape(row_count, HK, group_heads, HD)
    )
    scores = masked_scores(head_queries, all_keys, visible, score_scale)
    probabilities = jnp.exp(scores - row_logsum)
    probability_grad = jnp.einsum(
        "rkgd,skd->kgrs", attended_grad, all_values, preferred_element_type=FULL
    )
    row_delta = jnp.sum(probabilities * probability_grad, axis=-1, keepdims=True)
    score_grad = (probabilities * (probability_grad - row_delta)).astype(LOW)
    query_grad = (
        jnp.einsum("kgrs,skd->rkgd", score_grad, all_keys, preferred_element_type=FULL)
        * score_scale
    )
    key_grad = (
        jnp.einsum("kgrs,rkgd->skd", score_grad, head_queries, preferred_element_type=FULL)
        * score_scale
    )
    value_grad = jnp.einsum(
        "kgrs,rkgd->skd", probabilities.astype(LOW), attended_grad, preferred_element_type=FULL
    )
    query_project = (
        rotate(query_grad.reshape(row_count, HQ, HD), own_cosine, -own_sine)
        .reshape(row_count, query_width)
        .astype(LOW)
    )
    pair_project = jnp.concatenate(
        [
            rotate(key_grad, cosine, -sine_part).reshape(key_count, key_width),
            value_grad.reshape(key_count, key_width),
        ],
        axis=1,
    ).astype(LOW)
    query_back = contract(query_project, query_weight, 1, 1)
    pair_back = contract(pair_project, pair_weight, 1, 1)
    gain_one_part = jnp.sum(query_back * inputs * first_scale, axis=0) + jnp.sum(
        pair_back * key_inputs * key_scale, axis=0
    )
    gain_term = jnp.pad(
        jnp.stack([gain_one_part, gain_two_part], axis=1), ((0, 0), (0, GAIN_PAD - 2))
    )
    pair_low = pair_back[:PROMPT_LEN].astype(LOW)
    pair_low, merge_grad = lax.optimization_barrier((pair_low, merge_grad))
    finished = finish(
        contract(normed, query_project, 0, 0).astype(LOW),
        contract(key_normed, pair_project, 0, 0).astype(LOW),
        gain_term.astype(LOW),
        gate_part,
        down_part,
        (attention_master, attention_first, attention_second),
        (feedforward_master, feedforward_first, feedforward_second),
    )
    gain_grad = finished[4][:, :2].T
    pair_sum = lax.psum_scatter(
        pair_low, "grp", scatter_dimension=0, tiled=True
    ).astype(FULL)
    normed_grad = query_back + jnp.concatenate([pair_sum, pair_back[PROMPT_LEN:]], axis=0)
    input_grad = (middle_grad + norm_back(inputs, first_scale, gain_float[0], normed_grad)).reshape(
        hidden.shape
    )
    gain_new = adam_step(gain_master, gain_first, gain_second, gain_grad, 0.0)
    merge_new = adam_step(merge_master, merge_first, merge_second, merge_grad, WEIGHT_DECAY)
    return (
        block_output,
        input_grad,
        gain_grad,
        *gain_new,
        *finished[:4],
        merge_grad,
        *merge_new,
        *finished[5:],
    )


def solution(mesh):
    tokens = P("dp", "grp", None, None)
    gains = P(None, ("grp", "dp"))
    matrix = P(("grp", "dp"), None)
    return jax.shard_map(
        body,
        mesh=mesh,
        in_specs=(tokens, tokens, P("dp", None), P("dp", "grp")) + (gains,) * 3 + (matrix,) * 9,
        out_specs=(tokens, tokens) + (gains,) * 4 + (matrix,) * 12,
        check_vma=False,
    )
```

```python
import functools

import jax
import jax.numpy as jnp
from jax import lax
from jax.experimental import pallas as pl
from jax.experimental.pallas import tpu as pltpu
from jax.sharding import PartitionSpec as P

D = 2048
FF = 8192
HQ = 8
HK = 4
HD = 256
PROMPT_LEN = 1024
PROMPTS = 4
CONT = 64
STEP = 10
GAIN_PAD = 128

EPS_NORM = 1e-06
ROPE_THETA = 1000042.0
MASK_FILL = -1e30
BETA_ONE = 0.9
BETA_TWO = 0.95
ADAM_EPS = 1e-08
LEARN_RATE = 0.02
WEIGHT_DECAY = 0.1
LOW = jnp.bfloat16
FULL = jnp.float32
MESH = pl.DeviceIdType.MESH


def contract(left, right, left_axis, right_axis):
    return lax.dot_general(
        left, right, (((left_axis,), (right_axis,)), ((), ())), preferred_element_type=FULL
    )


def angle_table(positions):
    inverse_rate = ROPE_THETA ** (-(jnp.arange(HD // 2, dtype=FULL) * 2.0) / HD)
    angles = positions.astype(FULL)[..., None] * inverse_rate
    return (jnp.cos(angles), jnp.sin(angles))


def segment_positions(segment_row, source_row):
    labels = jnp.arange(PROMPTS, dtype=jnp.int32)
    member = (segment_row[None, :] == labels[:, None]).astype(jnp.int32)
    lengths = jnp.sum(member, axis=1, dtype=jnp.int32)
    starts = jnp.sum(
        jnp.where(labels[None, :] < labels[:, None], lengths[None, :], 0), axis=1, dtype=jnp.int32
    )
    prompt_index = jnp.arange(segment_row.shape[0], dtype=jnp.int32)
    prompt_positions = prompt_index - jnp.sum(member * starts[:, None], axis=0, dtype=jnp.int32)
    source_length = jnp.sum(
        (source_row[:, None] == labels[None, :]).astype(jnp.int32) * lengths[None, :],
        axis=1,
        dtype=jnp.int32,
    )
    follow_positions = source_length[:, None] + jnp.arange(CONT, dtype=jnp.int32)[None, :]
    return (prompt_positions, follow_positions)


def norm_scale(values):
    return lax.rsqrt(jnp.mean(values * values, axis=-1, keepdims=True) + EPS_NORM)


def norm_back(values, row_scale, gain_row, normed_grad):
    scaled = normed_grad * gain_row
    return row_scale * scaled - values * row_scale**3 * jnp.mean(
        scaled * values, axis=-1, keepdims=True
    )


def adam_step(master, first_moment, second_moment, gradient, decay_rate):
    first_new = BETA_ONE * first_moment + (1.0 - BETA_ONE) * gradient
    second_new = BETA_TWO * second_moment + (1.0 - BETA_TWO) * gradient * gradient
    correct_one = 1.0 - BETA_ONE**STEP
    correct_two = 1.0 - BETA_TWO**STEP
    update = first_new / correct_one / (jnp.sqrt(second_new / correct_two) + ADAM_EPS)
    return (-LEARN_RATE * (update + decay_rate * master), first_new, second_new)


def gate_parts(gate_values, up_values):
    gate_sigmoid = jax.nn.sigmoid(gate_values)
    gate_silu = gate_values * gate_sigmoid
    return (gate_sigmoid, gate_silu, (gate_silu * up_values).astype(LOW))


def gate_backward(activated_grad, gate_values, up_values, gate_sigmoid, gate_silu):
    gate_grad = (
        activated_grad * up_values * gate_sigmoid * (1.0 + gate_values * (1.0 - gate_sigmoid))
    ).astype(LOW)
    up_grad = (activated_grad * gate_silu).astype(LOW)
    return (gate_grad, up_grad)


def flip(index, bits):
    bit = 1
    while bit <= bits:
        if bits & bit:
            index = index + bit - 2 * bit * lax.rem(index // bit, 2)
        bit *= 2
    return index


def remote(source, target, send, recv, there):
    return pltpu.make_async_remote_copy(
        src_ref=source,
        dst_ref=target,
        send_sem=send,
        recv_sem=recv,
        device_id=there,
        device_id_type=MESH,
    )


def gather_kernel(
    lines,
    plane,
    prompt_rows,
    weight_ref,
    hidden_ref,
    forward_ref,
    weights_ref,
    rows_ref,
    gate_ref,
    down_ref,
    local_sem,
    line_send,
    line_recv,
    rows_send,
    rows_recv,
    near_send,
    near_recv,
    half_send,
    half_recv,
    core_send,
    core_recv,
    swap_send,
    swap_recv,
):
    g = lax.axis_index("grp")
    d = lax.axis_index("dp")
    evens = range(0, plane, 2)
    forward_halves = plane == 8
    near = (2, 4) if forward_halves else tuple(evens[1:])
    width = weight_ref.shape[1]
    cut = (width // 256) * 128

    barrier = pltpu.get_barrier_semaphore()
    for offset in range(1, plane):
        pl.semaphore_signal(barrier, inc=1, device_id=(g, flip(d, offset)), device_id_type=MESH)

    for step in range(1, lines):
        there = lax.rem(g + step, lines)
        pl.semaphore_signal(barrier, inc=1, device_id=(there, d), device_id_type=MESH)
    pl.semaphore_wait(barrier, plane + lines - 2)

    copy = remote
    own_rows = hidden_ref.at[pl.ds(0, prompt_rows)]

    def line_weight(way, step):
        block = g - step + 1 if way == 0 else g + step - 1
        source = weight_ref if step == 1 else weights_ref.at[block, d]
        return copy(
            source,
            weights_ref.at[block, d],
            line_send.at[way, step],
            line_recv.at[way, step],
            (g + 1 if way == 0 else g - 1, d),
        )

    def line_rows(way, step):
        block = g - step + 1 if way == 0 else g + step - 1
        source = own_rows if step == 1 else rows_ref.at[block]
        return copy(
            source,
            rows_ref.at[block],
            rows_send.at[way, step],
            rows_recv.at[way, step],
            (g + 1 if way == 0 else g - 1, d),
        )

    def sends(way, step):
        if way == 0:
            return (g < lines - 1) & (g >= step - 1)
        return (g > 0) & (g + step - 1 < lines)

    def receives(way, step):
        return g >= step if way == 0 else g + step < lines

    def near_copy(block, offset, own):
        source = weight_ref if own else weights_ref.at[block, d]
        at = near.index(offset)
        return copy(
            source,
            weights_ref.at[block, d],
            near_send.at[block, at],
            near_recv.at[block, at],
            (g, flip(d, offset)),
        )

    def half_copy(block, part):
        columns = pl.ds(0, cut) if part == 0 else pl.ds(cut, width - cut)
        origin = flip(d, 2) if part == 0 else flip(d, 4)
        there = flip(d, 4) if part == 0 else flip(d, 2)
        piece = weights_ref.at[block, origin, :, columns]
        return copy(
            piece, piece, half_send.at[block, part], half_recv.at[block, part], (g, there)
        )

    def core_copy(block, offset, own=False):
        source = weight_ref if own else weights_ref.at[block, flip(d, offset)]
        return copy(
            source,
            weights_ref.at[block, flip(d, offset)],
            core_send.at[block, offset // 2],
            core_recv.at[block, offset // 2],
            (g, flip(d, 1)),
        )

    own_hidden = down_ref.shape[2]

    def swap_piece(owner, part, source_index):
        source = forward_ref.at[:, pl.ds(part * FF + owner * own_hidden, own_hidden)]
        if part == 2:
            return source, down_ref.at[source_index]
        return source, gate_ref.at[source_index, :, pl.ds(part * own_hidden, own_hidden)]

    def swap_copy(offset, part):
        source, target = swap_piece(flip(d, offset), part, d)
        return copy(
            source,
            target,
            swap_send.at[offset, part],
            swap_recv.at[offset, part],
            (g, flip(d, offset)),
        )

    locals_ = (
        pltpu.make_async_copy(weight_ref, weights_ref.at[g, d], local_sem.at[0]),
        pltpu.make_async_copy(own_rows, rows_ref.at[g], local_sem.at[1]),
        *(
            pltpu.make_async_copy(*swap_piece(d, part, d), local_sem.at[2 + part])
            for part in range(3)
        ),
    )

    def launch(block, own):
        for offset in near:
            near_copy(block, offset, own).start()
        core_copy(block, 0, own).start()

    def relay(block):
        for offset in near:
            near_copy(block, offset, False).wait_recv()
            core_copy(block, offset).start()
        if forward_halves:
            half_copy(block, 0).start()
            half_copy(block, 1).start()

    def finish(block):
        if forward_halves:
            half_copy(block, 0).wait_recv()
            half_copy(block, 1).wait_recv()
            core_copy(block, 6).start()

    for way in (0, 1):
        pl.when(sends(way, 1))(lambda way=way: line_weight(way, 1).start())
    launch(g, True)
    for one in locals_:
        one.start()
    for offset in range(1, plane):
        for part in range(3):
            swap_copy(offset, part).start()

    for step in range(1, lines):
        for way in (0, 1):

            @pl.when(receives(way, step))
            def _(way=way, step=step):
                line_weight(way, step).wait_recv()

            if step + 1 < lines:
                pl.when(sends(way, step + 1))(
                    lambda way=way, step=step: line_weight(way, step + 1).start()
                )
            else:
                pl.when(sends(way, 1))(lambda way=way: line_rows(way, 1).start())

            @pl.when(receives(way, step))
            def _(way=way, step=step):
                launch(g - step if way == 0 else g + step, False)

        if step == 1:
            relay(g)
        else:
            for way in (0, 1):
                pl.when(receives(way, step - 1))(
                    lambda way=way, step=step: relay(
                        g - step + 1 if way == 0 else g + step - 1
                    )
                )
    for step in range(1, lines):
        for way in (0, 1):

            @pl.when(receives(way, step))
            def _(way=way, step=step):
                line_rows(way, step).wait_recv()

            if step + 1 < lines:
                pl.when(sends(way, step + 1))(
                    lambda way=way, step=step: line_rows(way, step + 1).start()
                )
        if step == 1:
            for way in (0, 1):
                pl.when(receives(way, lines - 1))(
                    lambda way=way: relay(g - lines + 1 if way == 0 else g + lines - 1)
                )
            finish(g)
    for step in range(1, lines):
        for way in (0, 1):
            pl.when(receives(way, step))(
                lambda way=way, step=step: finish(g - step if way == 0 else g + step)
            )

    def drain(block):
        for offset in evens:
            core_copy(block, offset).wait()
        for offset in near:
            near_copy(block, offset, False).wait_send()
        if forward_halves:
            half_copy(block, 0).wait_send()
            half_copy(block, 1).wait_send()

    drain(g)
    for step in range(1, lines):
        for way in (0, 1):
            pl.when(receives(way, step))(
                lambda way=way, step=step: drain(g - step if way == 0 else g + step)
            )

            @pl.when(sends(way, step))
            def _(way=way, step=step):
                line_weight(way, step).wait_send()
                line_rows(way, step).wait_send()

    for offset in range(1, plane):
        for part in range(3):
            swap_copy(offset, part).wait()
    for one in locals_:
        one.wait()


def gather_start(weight, hidden, forward):
    lines, plane = lax.axis_size("grp"), lax.axis_size("dp")
    prompt_rows = PROMPT_LEN // lines
    own_rows, width = weight.shape
    anywhere = pl.BlockSpec(memory_space=pl.ANY)
    dma = pltpu.SemaphoreType.DMA
    near_count = 2 if plane == 8 else plane // 2 - 1
    pairs = (
        (2, lines),
        (2, lines),
        (2, lines),
        (2, lines),
        (lines, near_count),
        (lines, near_count),
        (lines, 2),
        (lines, 2),
        (lines, plane // 2),
        (lines, plane // 2),
        (plane, 3),
        (plane, 3),
    )
    own_hidden = FF // plane
    return pl.pallas_call(
        functools.partial(gather_kernel, lines, plane, prompt_rows),
        out_shape=(
            jax.ShapeDtypeStruct((lines, plane, own_rows, width), weight.dtype),
            jax.ShapeDtypeStruct((lines, prompt_rows, D), hidden.dtype),
            jax.ShapeDtypeStruct((plane, own_rows, 2 * own_hidden), forward.dtype),
            jax.ShapeDtypeStruct((plane, own_rows, own_hidden), forward.dtype),
        ),
        in_specs=[anywhere] * 3,
        out_specs=(anywhere,) * 4,
        scratch_shapes=[dma((5,))] + [dma(shape) for shape in pairs],
        compiler_params=pltpu.CompilerParams(collective_id=0, has_side_effects=True),
        name="gather_start",
    )(weight, hidden, forward)


def project_kernel(
    place_ref,
    group_ref,
    own_ref,
    gain_ref,
    cosine_ref,
    sine_ref,
    weight_ref,
    query_ref,
    pair_ref,
    normed_ref,
    own_normed_ref,
    scale_ref,
):
    step = pl.program_id(0)
    own_rows = own_ref.shape[0]
    prompt_rows = own_rows - CONT
    start = pl.multiple_of(place_ref[0] * prompt_rows, 16)
    tile = 32

    def norm_tile(values, at):
        values = values.astype(FULL)
        scale = lax.rsqrt(jnp.mean(values * values, axis=-1, keepdims=True) + EPS_NORM)
        normed_ref[pl.ds(at, tile)] = (values * scale * gain_ref[...]).astype(LOW)
        scale_ref[pl.ds(at, tile)] = jnp.broadcast_to(scale, (tile, 128))

    @pl.when(step == 0)
    def _():
        @pl.loop(0, PROMPT_LEN // tile)
        def _(at):
            first = pl.multiple_of(at * tile, tile)
            norm_tile(group_ref[pl.ds(first, tile)], first)

        for at in range(0, CONT, tile):
            norm_tile(own_ref[prompt_rows + at : prompt_rows + at + tile], PROMPT_LEN + at)
        own_normed_ref[:prompt_rows] = normed_ref[pl.ds(start, prompt_rows)]
        own_normed_ref[prompt_rows:] = normed_ref[PROMPT_LEN:]

    def turn(values, cosine, sine_part):
        front, back = values[:, : HD // 2], values[:, HD // 2 :]
        return front * cosine - back * sine_part, back * cosine + front * sine_part

    def project(rows):
        return jnp.dot(rows, weight_ref[...], preferred_element_type=FULL)

    @pl.when(step < HQ)
    def _():
        for first, count, table in ((0, prompt_rows, start), (prompt_rows, CONT, PROMPT_LEN)):
            values = project(own_normed_ref[first : first + count])
            front, back = turn(
                values, cosine_ref[pl.ds(table, count)], sine_ref[pl.ds(table, count)]
            )
            query_ref[first : first + count, : HD // 2] = front.astype(LOW)
            query_ref[first : first + count, HD // 2 :] = back.astype(LOW)

    key_count = PROMPT_LEN + CONT
    part = key_count // 4

    @pl.when((step >= HQ) & (step < HQ + HK))
    def _():
        @pl.loop(0, 4)
        def _(at):
            rows = pl.ds(pl.multiple_of(at * part, 16), part)
            front, back = turn(project(normed_ref[rows]), cosine_ref[rows], sine_ref[rows])
            pair_ref[rows, : HD // 2] = front.astype(LOW)
            pair_ref[rows, HD // 2 :] = back.astype(LOW)

    @pl.when(step >= HQ + HK)
    def _():
        @pl.loop(0, 4)
        def _(at):
            rows = pl.ds(pl.multiple_of(at * part, 16), part)
            pair_ref[rows] = project(normed_ref[rows]).astype(LOW)


VMEM_LIMIT = 60 * 2**20


def project_heads(place, group_rows, own_inputs, gain_row, cosine, sine_part, weights):
    own_rows = own_inputs.shape[0]
    key_count = PROMPT_LEN + CONT
    whole = lambda shape: pl.BlockSpec(shape, lambda j, p: (0, 0))
    return pl.pallas_call(
        project_kernel,
        grid_spec=pltpu.PrefetchScalarGridSpec(
            num_scalar_prefetch=1,
            grid=(HQ + 2 * HK,),
            in_specs=[
                whole((PROMPT_LEN, D)),
                whole((own_rows, D)),
                whole((1, D)),
                whole((key_count, HD // 2)),
                whole((key_count, HD // 2)),
                pl.BlockSpec((D, HD), lambda j, p: (0, j)),
            ],
            out_specs=[
                pl.BlockSpec((own_rows, HD), lambda j, p: (0, jnp.minimum(j, HQ - 1))),
                pl.BlockSpec((key_count, HD), lambda j, p: (0, jnp.maximum(j - HQ, 0))),
                whole((key_count, D)),
                whole((own_rows, D)),
                whole((key_count, 128)),
            ],
        ),
        out_shape=[
            jax.ShapeDtypeStruct((own_rows, HQ * HD), LOW),
            jax.ShapeDtypeStruct((key_count, 2 * HK * HD), LOW),
            jax.ShapeDtypeStruct((key_count, D), LOW),
            jax.ShapeDtypeStruct((own_rows, D), LOW),
            jax.ShapeDtypeStruct((key_count, 128), FULL),
        ],
        compiler_params=pltpu.CompilerParams(vmem_limit_bytes=VMEM_LIMIT),
        name="project_heads",
    )(place, group_rows, own_inputs, gain_row, cosine, sine_part, weights)


def across(left, right):
    return lax.dot_general(left, right, (((1,), (1,)), ((), ())), preferred_element_type=FULL)


def along(left, right):
    return lax.dot_general(left, right, (((0,), (0,)), ((), ())), preferred_element_type=FULL)


def attend_kernel(query_ref, key_ref, value_ref, seen_ref, attended_ref, logsum_ref):
    group_heads = HQ // HK
    for head in range(group_heads):
        columns = slice(head * HD, (head + 1) * HD)
        scores = across(query_ref[:, columns], key_ref[...]) * HD ** (-0.5)
        scores = jnp.where(seen_ref[...] > 0, scores, MASK_FILL)
        peak = jnp.max(scores, axis=-1, keepdims=True)
        unnormed = jnp.exp(scores - peak)
        total = jnp.sum(unnormed, axis=-1, keepdims=True)
        low = (unnormed / total).astype(LOW)
        attended_ref[:, columns] = jnp.dot(
            low, value_ref[...], preferred_element_type=FULL
        ).astype(LOW)
        logsum_ref[:, head * 128 : (head + 1) * 128] = jnp.broadcast_to(
            peak + jnp.log(total), (query_ref.shape[0], 128)
        )


def attend(queries, pairs, seen):
    rows, key_count = seen.shape
    group_heads = HQ // HK
    return pl.pallas_call(
        attend_kernel,
        grid=(HK,),
        in_specs=[
            pl.BlockSpec((rows, group_heads * HD), lambda j: (0, j)),
            pl.BlockSpec((key_count, HD), lambda j: (0, j)),
            pl.BlockSpec((key_count, HD), lambda j: (0, HK + j)),
            pl.BlockSpec((rows, key_count), lambda j: (0, 0)),
        ],
        out_specs=[
            pl.BlockSpec((rows, group_heads * HD), lambda j: (0, j)),
            pl.BlockSpec((rows, group_heads * 128), lambda j: (0, j)),
        ],
        out_shape=[
            jax.ShapeDtypeStruct((rows, HQ * HD), LOW),
            jax.ShapeDtypeStruct((rows, HQ * 128), FULL),
        ],
        compiler_params=pltpu.CompilerParams(vmem_limit_bytes=VMEM_LIMIT),
        name="attend",
    )(queries, pairs, pairs, seen)


def attend_back_kernel(
    place_ref,
    query_ref,
    key_ref,
    value_ref,
    seen_ref,
    logsum_ref,
    grad_ref,
    cosine_ref,
    sine_ref,
    query_out,
    pair_out,
):
    step = pl.program_id(0)
    group_heads = HQ // HK
    rows = query_ref.shape[0]
    prompt_rows = rows - CONT
    start = pl.multiple_of(place_ref[0] * prompt_rows, 16)
    score_scale = HD ** (-0.5)
    key_grad = value_grad = 0.0

    def turn_back(values, cosine, sine_part):
        front, back = values[:, : HD // 2], values[:, HD // 2 :]
        return jnp.concatenate(
            [front * cosine + back * sine_part, back * cosine - front * sine_part], axis=1
        ).astype(LOW)

    for head in range(group_heads):
        columns = slice(head * HD, (head + 1) * HD)
        scores = across(query_ref[:, columns], key_ref[...]) * score_scale
        scores = jnp.where(seen_ref[...] > 0, scores, MASK_FILL)
        probabilities = jnp.exp(scores - logsum_ref[:, head * 128 : head * 128 + 1])
        grads = grad_ref[:, columns]
        probability_grad = across(grads, value_ref[...])
        delta = jnp.sum(probabilities * probability_grad, axis=-1, keepdims=True)
        score_grad = (probabilities * (probability_grad - delta)).astype(LOW)
        query_grad = jnp.dot(score_grad, key_ref[...], preferred_element_type=FULL) * score_scale
        key_grad = key_grad + along(score_grad, query_ref[:, columns])
        value_grad = value_grad + along(probabilities.astype(LOW), grads)
        query_out[:prompt_rows, columns] = turn_back(
            query_grad[:prompt_rows],
            cosine_ref[pl.ds(start, prompt_rows)],
            sine_ref[pl.ds(start, prompt_rows)],
        )
        query_out[prompt_rows:, columns] = turn_back(
            query_grad[prompt_rows:], cosine_ref[PROMPT_LEN:], sine_ref[PROMPT_LEN:]
        )
    pair_out[:, pl.ds(pl.multiple_of(step * HD, HD), HD)] = turn_back(
        key_grad * score_scale, cosine_ref[...], sine_ref[...]
    )
    pair_out[:, pl.ds(pl.multiple_of((HK + step) * HD, HD), HD)] = value_grad.astype(LOW)


def attend_back(place, queries, pairs, seen, logsum, grads, cosine, sine_part):
    rows, key_count = seen.shape
    group_heads = HQ // HK
    whole = lambda shape: pl.BlockSpec(shape, lambda j, p: (0, 0))
    return pl.pallas_call(
        attend_back_kernel,
        grid_spec=pltpu.PrefetchScalarGridSpec(
            num_scalar_prefetch=1,
            grid=(HK,),
            in_specs=[
                pl.BlockSpec((rows, group_heads * HD), lambda j, p: (0, j)),
                pl.BlockSpec((key_count, HD), lambda j, p: (0, j)),
                pl.BlockSpec((key_count, HD), lambda j, p: (0, HK + j)),
                whole((rows, key_count)),
                pl.BlockSpec((rows, group_heads * 128), lambda j, p: (0, j)),
                pl.BlockSpec((rows, group_heads * HD), lambda j, p: (0, j)),
                whole((key_count, HD // 2)),
                whole((key_count, HD // 2)),
            ],
            out_specs=[
                pl.BlockSpec((rows, group_heads * HD), lambda j, p: (0, j)),
                whole((key_count, 2 * HK * HD)),
            ],
        ),
        out_shape=[
            jax.ShapeDtypeStruct((rows, HQ * HD), LOW),
            jax.ShapeDtypeStruct((key_count, 2 * HK * HD), LOW),
        ],
        compiler_params=pltpu.CompilerParams(vmem_limit_bytes=VMEM_LIMIT),
        name="attend_back",
    )(place, queries, pairs, pairs, seen, logsum, grads, cosine, sine_part)


def weights_back_kernel(
    place_ref,
    query_ref,
    pair_ref,
    branch_ref,
    attended_ref,
    normed_ref,
    own_normed_ref,
    group_ref,
    own_ref,
    scale_ref,
    query_weight_ref,
    pair_weight_ref,
    query_term,
    pair_term,
    merge_term,
    back_out,
    pair_back_out,
    gain_out,
):
    rows = query_ref.shape[0]
    prompt_rows = rows - CONT
    start = pl.multiple_of(place_ref[0] * prompt_rows, 16)
    query_term[...] = along(own_normed_ref[...], query_ref[...]).astype(LOW)
    pair_term[...] = along(normed_ref[...], pair_ref[...]).astype(LOW)
    merge_term[...] = along(branch_ref[...], attended_ref[...]).astype(LOW)
    query_back = across(query_ref[...], query_weight_ref[...])
    pair_back = across(pair_ref[...], pair_weight_ref[...])
    own_values = own_ref[prompt_rows:].astype(FULL) * scale_ref[PROMPT_LEN:, :1]
    tail = query_back[prompt_rows:] + pair_back[PROMPT_LEN:]
    group_values = group_ref[...].astype(FULL) * scale_ref[:PROMPT_LEN, :1]
    own_prompt = own_ref[:prompt_rows].astype(FULL) * scale_ref[pl.ds(start, prompt_rows), :1]
    gain_out[...] = (
        jnp.sum(pair_back[:PROMPT_LEN] * group_values, axis=0, keepdims=True)
        + jnp.sum(query_back[:prompt_rows] * own_prompt, axis=0, keepdims=True)
        + jnp.sum(tail * own_values, axis=0, keepdims=True)
    )
    back_out[:prompt_rows] = query_back[:prompt_rows]
    back_out[prompt_rows:] = tail
    pair_back_out[...] = pair_back[:PROMPT_LEN].astype(LOW)


def weights_back(
    place, queries, pairs, branch, attended, normed, own_normed, group_rows, own_inputs, scale, weights
):
    rows, key_count = queries.shape[0], pairs.shape[0]
    wide, tile = HQ * HD, 256
    whole = lambda shape: pl.BlockSpec(shape, lambda j, p: (0, 0))
    tall = lambda count: pl.BlockSpec((count, tile), lambda j, p: (0, j))
    flat = lambda at: pl.BlockSpec((tile, wide), lambda j, p: (j, at))
    return pl.pallas_call(
        weights_back_kernel,
        grid_spec=pltpu.PrefetchScalarGridSpec(
            num_scalar_prefetch=1,
            grid=(D // tile,),
            in_specs=[
                whole((rows, wide)),
                whole((key_count, wide)),
                tall(rows),
                whole((rows, wide)),
                tall(key_count),
                tall(rows),
                tall(PROMPT_LEN),
                tall(rows),
                whole((key_count, 128)),
                flat(0),
                flat(1),
            ],
            out_specs=[flat(0), flat(0), flat(0), tall(rows), tall(PROMPT_LEN), tall(1)],
        ),
        out_shape=[
            jax.ShapeDtypeStruct((D, wide), LOW),
            jax.ShapeDtypeStruct((D, wide), LOW),
            jax.ShapeDtypeStruct((D, wide), LOW),
            jax.ShapeDtypeStruct((rows, D), FULL),
            jax.ShapeDtypeStruct((PROMPT_LEN, D), LOW),
            jax.ShapeDtypeStruct((1, D), FULL),
        ],
        compiler_params=pltpu.CompilerParams(vmem_limit_bytes=VMEM_LIMIT),
        name="weights_back",
    )(
        place,
        queries,
        pairs,
        branch,
        attended,
        normed,
        own_normed,
        group_rows,
        own_inputs,
        scale,
        weights,
        weights,
    )


def plane_swap(block, offset):
    size = lax.axis_size("dp")
    return lax.ppermute(block, "dp", [(i, i ^ offset) for i in range(size)])


def plane_gather(block):
    mine = [block] + [plane_swap(block, o) for o in range(2, lax.axis_size("dp"), 2)]
    pairs = [(one, plane_swap(one, 1)) for one in mine]
    return jnp.concatenate([one for pair in pairs for one in pair], axis=0)


def plane_scatter(part_of):
    size = lax.axis_size("dp")
    sums = {}
    for offset in list(range(size - 2, 0, -2)) + [0]:
        arrived = plane_swap(part_of(offset + 1).astype(LOW), 1)
        sums[offset] = part_of(offset).astype(FULL) + arrived.astype(FULL)
        if offset:
            sums[offset] = plane_swap(sums[offset].astype(LOW), offset)
    total = sums[0]
    for offset in range(2, size, 2):
        total = total + sums[offset].astype(FULL)
    return total


def line_scatter(term):
    return lax.psum_scatter(term, "grp", scatter_dimension=0, tiled=True)


def finish_kernel(
    lines,
    plane,
    query_ref,
    pair_ref,
    merge_ref,
    gain_ref,
    gate_ref,
    down_ref,
    back_ref,
    a_master,
    a_first,
    a_second,
    m_master,
    m_first,
    m_second,
    f_master,
    f_first,
    f_second,
    a_grad,
    a_update,
    a_first_new,
    a_second_new,
    m_grad,
    m_update,
    m_first_new,
    m_second_new,
    gain_out,
    back_out,
    f_grad,
    f_update,
    f_first_new,
    f_second_new,
    mine,
    core_in,
    plane_in,
    line_in,
    gate_in,
    down_in,
    state,
    made,
    a_state,
    a_made,
    gain_made,
    mine_sem,
    core_send,
    core_recv,
    plane_send,
    plane_recv,
    line_send,
    line_recv,
    swap_send,
    swap_recv,
    own_sem,
    state_sem,
    made_sem,
    a_sem,
    gain_sem,
    back_send,
    back_recv,
):
    g = lax.axis_index("grp")
    d = lax.axis_index("dp")
    chips = plane // 2
    chip, core = lax.div(d, 2), lax.rem(d, 2)
    partner = d + 1 - 2 * core
    rows = a_master.shape[0]
    own_hidden = down_ref.shape[2]
    width = core_in.shape[3]
    a_width, m_width = a_master.shape[1], m_master.shape[1]
    parts, begin = [], 0
    for ref in (query_ref, pair_ref, merge_ref, gain_ref):
        parts.append((ref, pl.ds(begin, ref.shape[4])))
        begin += ref.shape[4]
    prompt_rows = back_out.shape[1]

    barrier = pltpu.get_barrier_semaphore()
    for step in range(1, plane):
        there = lax.rem(d + step, plane)
        pl.semaphore_signal(barrier, inc=1, device_id=(g, there), device_id_type=MESH)
    for step in range(1, lines):
        there = lax.rem(g + step, lines)
        pl.semaphore_signal(barrier, inc=1, device_id=(there, d), device_id_type=MESH)
    pl.semaphore_wait(barrier, plane + lines - 2)

    def line_at(turn):
        return lax.rem(g + turn + 1, lines)

    def core_copy(turn, part):
        line = line_at(turn)
        ref, columns = parts[part]
        return remote(
            ref.at[line, :, 1 - core],
            core_in.at[line, :, :, columns],
            core_send.at[turn, part],
            core_recv.at[turn, part],
            (g, partner),
        )

    def mine_copy(turn, part):
        line = line_at(turn)
        ref, columns = parts[part]
        return pltpu.make_async_copy(
            ref.at[line, :, core], mine.at[turn % 2, :, :, columns], mine_sem.at[turn, part]
        )

    def plane_copy(turn, step):
        line = line_at(turn)
        there = lax.rem(chip + step, chips)
        return remote(
            core_in.at[line, there],
            plane_in.at[line, chip],
            plane_send.at[turn, step],
            plane_recv.at[turn, step],
            (g, 2 * there + core),
        )

    def line_copy(turn):
        line = line_at(turn)
        return remote(
            core_in.at[line, chip],
            line_in.at[g],
            line_send.at[turn],
            line_recv.at[turn],
            (line, d),
        )

    def swap_copy(step, part):
        there = lax.rem(d + step, plane)
        source, target = (gate_ref, gate_in) if part == 0 else (down_ref, down_in)
        return remote(
            source.at[there],
            target.at[d],
            swap_send.at[step, part],
            swap_recv.at[step, part],
            (g, there),
        )

    own_swap = (
        pltpu.make_async_copy(gate_ref.at[d], gate_in.at[d], own_sem.at[0]),
        pltpu.make_async_copy(down_ref.at[d], down_in.at[d], own_sem.at[1]),
    )

    def f_columns(turn):
        block = lax.rem(d + lax.div(turn, 3), plane)
        return pl.ds(
            pl.multiple_of(lax.rem(turn, 3) * FF + block * own_hidden, own_hidden), own_hidden
        )

    def state_copy(turn, which):
        slot = lax.rem(turn, 2)
        return pltpu.make_async_copy(
            (f_master, f_first, f_second)[which].at[:, f_columns(turn)],
            state.at[slot, which],
            state_sem.at[slot, which],
        )

    def made_copy(turn, which):
        slot = lax.rem(turn, 2)
        return pltpu.make_async_copy(
            made.at[slot, which],
            (f_grad, f_update, f_first_new, f_second_new)[which].at[:, f_columns(turn)],
            made_sem.at[slot, which],
        )

    def back_copy(step):
        there = lax.rem(g + step, lines)
        return remote(
            back_ref.at[there],
            back_out.at[g],
            back_send.at[step],
            back_recv.at[step],
            (there, d),
        )

    own_back = pltpu.make_async_copy(back_ref.at[g], back_out.at[g], own_sem.at[2])

    slabs = (pl.ds(0, a_width), pl.ds(a_width, m_width))

    def a_state_copy(which, slab):
        source = ((a_master, a_first, a_second), (m_master, m_first, m_second))[slab][which]
        return pltpu.make_async_copy(
            source, a_state.at[which, :, slabs[slab]], a_sem.at[slab, which]
        )

    def a_made_copy(which, slab):
        target = (
            (a_grad, a_update, a_first_new, a_second_new),
            (m_grad, m_update, m_first_new, m_second_new),
        )[slab][which]
        return pltpu.make_async_copy(
            a_made.at[which, :, slabs[slab]], target, a_sem.at[slab, 3 + which]
        )

    every = range(len(parts))
    for turn in range(lines):
        for part in every:
            core_copy(turn, part).start()
            if turn < 2:
                mine_copy(turn, part).start()
    for step in range(1, lines):
        back_copy(step).start()
    for step in range(1, plane):
        for part in range(2):
            swap_copy(step, part).start()
    for one in own_swap:
        one.start()
    own_back.start()
    for which in range(3):
        state_copy(0, which).start()
        for slab in range(2):
            a_state_copy(which, slab).start()

    tile = 896 if width % 896 == 0 else 128
    tiles = width // tile

    for turn in range(lines):
        line = line_at(turn)
        for part in every:
            core_copy(turn, part).wait_recv()
            mine_copy(turn, part).wait()
        for step in range(1, chips + 1):
            there = lax.rem(chip + step, chips)

            @pl.loop(0, tiles)
            def _(at, line=line, there=there, turn=turn):
                columns = pl.ds(pl.multiple_of(at * tile, tile), tile)
                total = mine[turn % 2, there, :, columns].astype(FULL) + core_in[
                    line, there, :, columns
                ].astype(FULL)
                core_in[line, there, :, columns] = total.astype(LOW)

            if step < chips:
                plane_copy(turn, step).start()
        if turn + 2 < lines:
            for part in every:
                mine_copy(turn + 2, part).start()

    def forward_turn(turn):
        slot = lax.rem(turn, 2)
        block = lax.rem(d + lax.div(turn, 3), plane)
        part = lax.rem(turn, 3)

        @pl.when(turn + 1 < 3 * plane)
        def _():
            for which in range(3):
                state_copy(turn + 1, which).start()

        @pl.when(turn > 1)
        def _():
            for which in range(4):
                made_copy(turn - 2, which).wait()

        for which in range(3):
            state_copy(turn, which).wait()

        def rows_step(read):
            @pl.loop(0, rows // 16)
            def _(at):
                rows_at = pl.ds(pl.multiple_of(at * 16, 16), 16)
                gradient = read(rows_at).astype(FULL)
                update, first_new, second_new = adam_step(
                    state[slot, 0, rows_at],
                    state[slot, 1, rows_at],
                    state[slot, 2, rows_at],
                    gradient,
                    WEIGHT_DECAY,
                )
                made[slot, 0, rows_at] = gradient
                made[slot, 1, rows_at] = update
                made[slot, 2, rows_at] = first_new
                made[slot, 3, rows_at] = second_new

        for own in range(2):
            pl.when(part == own)(
                lambda own=own: rows_step(
                    lambda at: gate_in[block, at, pl.ds(own * own_hidden, own_hidden)]
                )
            )
        pl.when(part == 2)(lambda: rows_step(lambda at: down_in[block, at]))
        for which in range(4):
            made_copy(turn, which).start()

    for one in own_swap:
        one.wait()
    for step in range(1, plane):
        for part in range(2):
            swap_copy(step, part).wait_recv()
    each = 3 * plane // lines
    for turn in range(lines):
        lax.fori_loop(turn * each, (turn + 1) * each, lambda k, c: (forward_turn(k), c)[1], 0)
        line = line_at(turn)
        for step in range(1, chips):
            plane_copy(turn, step).wait_recv()

        @pl.loop(0, tiles)
        def _(at, line=line):
            columns = pl.ds(pl.multiple_of(at * tile, tile), tile)
            total = core_in[line, chip, :, columns].astype(FULL)
            for step in range(1, chips):
                total = total + plane_in[line, lax.rem(chip + step, chips), :, columns].astype(FULL)
            core_in[line, chip, :, columns] = total.astype(LOW)

        if turn < lines - 1:
            line_copy(turn).start()

    for which in range(4):
        for turn in (3 * plane - 2, 3 * plane - 1):
            made_copy(turn, which).wait()
    for turn in range(lines - 1):
        line_copy(turn).wait_recv()
    for which in range(3):
        for slab in range(2):
            a_state_copy(which, slab).wait()

    def owned(columns):
        total = core_in[g, chip, :, columns].astype(FULL)
        for step in range(1, lines):
            total = total + line_in[lax.rem(g + step, lines), :, columns].astype(FULL)
        return total

    @pl.loop(0, (a_width + m_width) // 256)
    def _(at):
        columns = pl.ds(pl.multiple_of(at * 256, 256), 256)
        gradient = owned(columns)
        update, first_new, second_new = adam_step(
            a_state[0, :, columns],
            a_state[1, :, columns],
            a_state[2, :, columns],
            gradient,
            WEIGHT_DECAY,
        )
        a_made[0, :, columns] = gradient
        a_made[1, :, columns] = update
        a_made[2, :, columns] = first_new
        a_made[3, :, columns] = second_new

    for which in range(4):
        for slab in range(2):
            a_made_copy(which, slab).start()
    gain_made[...] = owned(pl.ds(a_width + m_width, GAIN_PAD))
    gain_copy = pltpu.make_async_copy(gain_made, gain_out, gain_sem.at[0])
    gain_copy.start()
    for turn in range(lines):
        for part in every:
            core_copy(turn, part).wait_send()
        for step in range(1, chips):
            plane_copy(turn, step).wait_send()
        if turn < lines - 1:
            line_copy(turn).wait_send()
    for step in range(1, plane):
        for part in range(2):
            swap_copy(step, part).wait_send()
    for step in range(1, lines):
        back_copy(step).wait()
    own_back.wait()
    for which in range(4):
        for slab in range(2):
            a_made_copy(which, slab).wait()
    gain_copy.wait()


def finish(terms, gate_part, down_part, pair_back, attention, merge, forward):
    lines, plane = lax.axis_size("grp"), lax.axis_size("dp")
    chips = plane // 2
    rows, a_width = attention[0].shape
    m_width = merge[0].shape[1]
    own_hidden = down_part.shape[1]
    width = a_width + m_width + GAIN_PAD
    anywhere = pl.BlockSpec(memory_space=pl.ANY)
    dma = pltpu.SemaphoreType.DMA
    vmem = pltpu.VMEM
    back = pair_back.reshape(lines, PROMPT_LEN // lines, D)

    def like(array):
        return jax.ShapeDtypeStruct(array.shape, array.dtype)

    return pl.pallas_call(
        functools.partial(finish_kernel, lines, plane),
        out_shape=(like(attention[0]),) * 4
        + (like(merge[0]),) * 4
        + (jax.ShapeDtypeStruct((rows, GAIN_PAD), FULL), like(back))
        + (like(forward[0]),) * 4,
        in_specs=[anywhere] * 16,
        out_specs=(anywhere,) * 14,
        scratch_shapes=[
            vmem((2, chips, rows, width), LOW),
            vmem((lines, chips, rows, width), LOW),
            vmem((lines, chips, rows, width), LOW),
            vmem((lines, rows, width), LOW),
            vmem((plane, rows, 2 * own_hidden), LOW),
            vmem((plane, rows, own_hidden), LOW),
            vmem((2, 3, rows, own_hidden), FULL),
            vmem((2, 4, rows, own_hidden), FULL),
            vmem((3, rows, a_width + m_width), FULL),
            vmem((4, rows, a_width + m_width), FULL),
            vmem((rows, GAIN_PAD), FULL),
            dma((lines, 4)),
            dma((lines, 4)),
            dma((lines, 4)),
            dma((lines, chips)),
            dma((lines, chips)),
            dma((lines,)),
            dma((lines,)),
            dma((plane, 2)),
            dma((plane, 2)),
            dma((3,)),
            dma((2, 3)),
            dma((2, 4)),
            dma((2, 7)),
            dma((1,)),
            dma((lines,)),
            dma((lines,)),
        ],
        compiler_params=pltpu.CompilerParams(
            collective_id=1, has_side_effects=True, vmem_limit_bytes=VMEM_LIMIT
        ),
        name="finish",
    )(
        *(term.reshape(lines, chips, 2, rows, term.shape[1]) for term in terms),
        gate_part.reshape(plane, rows, -1),
        down_part.reshape(plane, rows, -1),
        back,
        *attention,
        *merge,
        *forward,
    )


def body(
    hidden,
    cotangent,
    segment_ids,
    continuation_prompt,
    gain_master,
    gain_first,
    gain_second,
    attention_master,
    attention_first,
    attention_second,
    merge_master,
    merge_first,
    merge_second,
    feedforward_master,
    feedforward_first,
    feedforward_second,
):
    group_index = lax.axis_index("grp")
    dp_size = lax.axis_size("dp")
    row_count = hidden.shape[2]
    prompt_rows = row_count - CONT
    qkv_width = (HQ + 2 * HK) * HD
    own_rows = feedforward_master.shape[0]
    own_hidden = FF // dp_size
    own_inputs = hidden.reshape(row_count, D)

    gain_columns = jnp.pad(gain_master.T, ((0, 0), (0, GAIN_PAD - 2)))
    weight_low = jnp.concatenate(
        [attention_master.astype(LOW), merge_master.astype(LOW), gain_columns.astype(LOW)], axis=1
    )
    weights, group_rows, gate_rows, down_rows = gather_start(
        weight_low, own_inputs, feedforward_master.astype(LOW)
    )
    weights, late_cotangent = lax.optimization_barrier((weights, cotangent))
    weights = weights.reshape(D, -1)
    merge_weight = weights[:, qkv_width : qkv_width + D]
    gain_float = weights[:, qkv_width + D : qkv_width + D + 2].astype(FULL).T
    gate_weight = lax.all_gather(
        gate_rows.reshape(dp_size * own_rows, 2 * own_hidden), "grp", axis=0, tiled=True
    )
    gate_weight, down_rows = lax.optimization_barrier((gate_weight, down_rows))
    down_weight = lax.all_gather(
        down_rows.reshape(dp_size * own_rows, own_hidden), "grp", axis=0, tiled=True
    )
    down_grad = plane_gather(late_cotangent.reshape(row_count, D))

    segment_row = segment_ids[0]
    source_row = continuation_prompt[0]
    prompt_positions, follow_positions = segment_positions(segment_row, source_row)
    cosine, sine_part = angle_table(jnp.concatenate([prompt_positions, follow_positions[0]]))

    place = jnp.reshape(group_index, (1,)).astype(jnp.int32)
    group_rows = group_rows.reshape(PROMPT_LEN, D)
    queries, pairs, key_normed, normed, key_scale = project_heads(
        place, group_rows, own_inputs, gain_float[:1], cosine, sine_part, weights
    )
    inputs = own_inputs.astype(FULL)
    first_scale = norm_scale(inputs)

    row_index = jnp.arange(row_count, dtype=jnp.int32)
    is_prompt = row_index < prompt_rows
    global_row = group_index * prompt_rows + jnp.minimum(row_index, prompt_rows - 1)
    own_segment = lax.dynamic_slice_in_dim(segment_row, group_index * prompt_rows, prompt_rows)
    query_segment = jnp.concatenate([own_segment, jnp.broadcast_to(source_row, (CONT,))])
    key_index = jnp.arange(PROMPT_LEN, dtype=jnp.int32)
    prompt_seen = (segment_row[None, :] == query_segment[:, None]) & (
        (key_index[None, :] <= global_row[:, None]) | ~is_prompt[:, None]
    )
    follow_seen = (~is_prompt)[:, None] & (
        jnp.arange(CONT, dtype=jnp.int32)[None, :] <= (row_index - prompt_rows)[:, None]
    )
    visible = jnp.concatenate([prompt_seen, follow_seen], axis=1)
    seen = visible.astype(FULL)
    attended, row_logsum = attend(queries, pairs, seen)
    middle = inputs + contract(attended, merge_weight, 1, 1)
    second_scale = norm_scale(middle)
    normed_two = (middle * second_scale * gain_float[1]).astype(LOW)
    grad_rows = cotangent.reshape(row_count, D).astype(FULL)

    def by_offset(left, right, right_axis):
        chunks = {}
        for offset in range(0, dp_size, 2):
            rows = left[offset * row_count : (offset + 2) * row_count]
            chunks[offset] = contract(rows, right, 1, right_axis).astype(LOW)
        return lambda offset: chunks[offset - offset % 2][
            (offset % 2) * row_count : (offset % 2 + 1) * row_count
        ]

    normed_two, down_grad = lax.optimization_barrier((normed_two, down_grad))
    normed_all = plane_gather(normed_two)
    gate_up = jnp.dot(normed_all, gate_weight, preferred_element_type=FULL)
    gate_values = gate_up[:, :own_hidden]
    up_values = gate_up[:, own_hidden:]
    gate_sigmoid, gate_silu, activated = gate_parts(gate_values, up_values)
    down_term = contract(down_grad, activated, 0, 0).astype(LOW)
    down_term, down_weight = lax.optimization_barrier((down_term, down_weight))
    out_parts = by_offset(activated, down_weight, 1)
    out_chunks = [out_parts(offset) for offset in range(dp_size)]
    out_chunks, down_grad = lax.optimization_barrier((out_chunks, down_grad))
    out_sum = plane_scatter(lambda offset: out_chunks[offset])
    activated_grad = contract(down_grad, down_weight, 1, 0)
    gate_grad, up_grad = gate_backward(
        activated_grad, gate_values, up_values, gate_sigmoid, gate_silu
    )
    gate_up_grad = jnp.concatenate([gate_grad, up_grad], axis=1)

    back_parts = by_offset(gate_up_grad, gate_weight, 1)
    normed_two_grad = plane_scatter(back_parts)
    down_part = line_scatter(down_term)
    gate_term = contract(normed_all, gate_up_grad, 0, 0).astype(LOW)
    normed_two_grad, gate_term = lax.optimization_barrier((normed_two_grad, gate_term))
    gate_term, down_part = lax.optimization_barrier((gate_term, down_part))
    gate_part = line_scatter(gate_term)
    result = middle + out_sum
    block_output = result.astype(LOW).reshape(hidden.shape)
    middle_grad = grad_rows + norm_back(middle, second_scale, gain_float[1], normed_two_grad)
    gain_two_part = jnp.sum(normed_two_grad * middle * second_scale, axis=0)
    branch_grad = middle_grad.astype(LOW)
    attended_grad = contract(branch_grad, merge_weight, 1, 0).astype(LOW)
    query_project, pair_project = attend_back(
        place, queries, pairs, seen, row_logsum, attended_grad, cosine, sine_part
    )
    query_term, pair_term, merge_term, normed_grad, pair_back, gain_one_part = weights_back(
        place,
        query_project,
        pair_project,
        branch_grad,
        attended,
        key_normed,
        normed,
        group_rows,
        own_inputs,
        key_scale,
        weights,
    )
    gain_term = jnp.pad(
        jnp.stack([gain_one_part[0], gain_two_part], axis=1), ((0, 0), (0, GAIN_PAD - 2))
    )
    finished = finish(
        (query_term, pair_term, merge_term, gain_term.astype(LOW)),
        gate_part,
        down_part,
        pair_back,
        (attention_master, attention_first, attention_second),
        (merge_master, merge_first, merge_second),
        (feedforward_master, feedforward_first, feedforward_second),
    )
    gain_grad = finished[8][:, :2].T
    pair_sum = jnp.sum(finished[9].astype(FULL), axis=0)
    normed_grad = normed_grad + jnp.pad(pair_sum, ((0, CONT), (0, 0)))
    input_grad = (middle_grad + norm_back(inputs, first_scale, gain_float[0], normed_grad)).reshape(
        hidden.shape
    )
    gain_new = adam_step(gain_master, gain_first, gain_second, gain_grad, 0.0)
    return (
        block_output,
        input_grad,
        gain_grad,
        *gain_new,
        *finished[:8],
        *finished[10:],
    )


def solution(mesh):
    tokens = P("dp", "grp", None, None)
    gains = P(None, ("grp", "dp"))
    matrix = P(("grp", "dp"), None)
    return jax.shard_map(
        body,
        mesh=mesh,
        in_specs=(tokens, tokens, P("dp", None), P("dp", "grp")) + (gains,) * 3 + (matrix,) * 9,
        out_specs=(tokens, tokens) + (gains,) * 4 + (matrix,) * 12,
        check_vma=False,
    )
```

```python
import functools

import jax
import jax.numpy as jnp
from jax import lax
from jax.experimental import pallas as pl
from jax.experimental.pallas import tpu as pltpu
from jax.sharding import PartitionSpec as P

D = 2048
FF = 8192
HQ = 8
HK = 4
HD = 256
PROMPT_LEN = 1024
PROMPTS = 4
CONT = 64
STEP = 10
GAIN_PAD = 128

EPS_NORM = 1e-06
ROPE_THETA = 1000042.0
MASK_FILL = -1e30
BETA_ONE = 0.9
BETA_TWO = 0.95
ADAM_EPS = 1e-08
LEARN_RATE = 0.02
WEIGHT_DECAY = 0.1
LOW = jnp.bfloat16
FULL = jnp.float32
MESH = pl.DeviceIdType.MESH


def contract(left, right, left_axis, right_axis):
    return lax.dot_general(
        left, right, (((left_axis,), (right_axis,)), ((), ())), preferred_element_type=FULL
    )


def angle_table(positions):
    inverse_rate = ROPE_THETA ** (-(jnp.arange(HD // 2, dtype=FULL) * 2.0) / HD)
    angles = positions.astype(FULL)[..., None] * inverse_rate
    return (jnp.cos(angles), jnp.sin(angles))


def segment_positions(segment_row, source_row):
    labels = jnp.arange(PROMPTS, dtype=jnp.int32)
    member = (segment_row[None, :] == labels[:, None]).astype(jnp.int32)
    lengths = jnp.sum(member, axis=1, dtype=jnp.int32)
    starts = jnp.sum(
        jnp.where(labels[None, :] < labels[:, None], lengths[None, :], 0), axis=1, dtype=jnp.int32
    )
    prompt_index = jnp.arange(segment_row.shape[0], dtype=jnp.int32)
    prompt_positions = prompt_index - jnp.sum(member * starts[:, None], axis=0, dtype=jnp.int32)
    source_length = jnp.sum(
        (source_row[:, None] == labels[None, :]).astype(jnp.int32) * lengths[None, :],
        axis=1,
        dtype=jnp.int32,
    )
    follow_positions = source_length[:, None] + jnp.arange(CONT, dtype=jnp.int32)[None, :]
    return (prompt_positions, follow_positions)


def norm_scale(values):
    return lax.rsqrt(jnp.mean(values * values, axis=-1, keepdims=True) + EPS_NORM)


def norm_back(values, row_scale, gain_row, normed_grad):
    scaled = normed_grad * gain_row
    return row_scale * scaled - values * row_scale**3 * jnp.mean(
        scaled * values, axis=-1, keepdims=True
    )


def adam_step(master, first_moment, second_moment, gradient, decay_rate):
    first_new = BETA_ONE * first_moment + (1.0 - BETA_ONE) * gradient
    second_new = BETA_TWO * second_moment + (1.0 - BETA_TWO) * gradient * gradient
    correct_one = 1.0 - BETA_ONE**STEP
    correct_two = 1.0 - BETA_TWO**STEP
    update = first_new / correct_one / (jnp.sqrt(second_new / correct_two) + ADAM_EPS)
    return (-LEARN_RATE * (update + decay_rate * master), first_new, second_new)


def gate_parts(gate_values, up_values):
    gate_sigmoid = jax.nn.sigmoid(gate_values)
    gate_silu = gate_values * gate_sigmoid
    return (gate_sigmoid, gate_silu, (gate_silu * up_values).astype(LOW))


def gate_backward(activated_grad, gate_values, up_values, gate_sigmoid, gate_silu):
    gate_grad = (
        activated_grad * up_values * gate_sigmoid * (1.0 + gate_values * (1.0 - gate_sigmoid))
    ).astype(LOW)
    up_grad = (activated_grad * gate_silu).astype(LOW)
    return (gate_grad, up_grad)


def flip(index, bits):
    bit = 1
    while bit <= bits:
        if bits & bit:
            index = index + bit - 2 * bit * lax.rem(index // bit, 2)
        bit *= 2
    return index


def remote(source, target, send, recv, there):
    return pltpu.make_async_remote_copy(
        src_ref=source,
        dst_ref=target,
        send_sem=send,
        recv_sem=recv,
        device_id=there,
        device_id_type=MESH,
    )


def gather_kernel(
    lines,
    plane,
    prompt_rows,
    weight_ref,
    hidden_ref,
    forward_ref,
    weights_ref,
    rows_ref,
    gate_ref,
    down_ref,
    local_sem,
    line_send,
    line_recv,
    rows_send,
    rows_recv,
    near_send,
    near_recv,
    half_send,
    half_recv,
    core_send,
    core_recv,
    swap_send,
    swap_recv,
):
    g = lax.axis_index("grp")
    d = lax.axis_index("dp")
    evens = range(0, plane, 2)
    forward_halves = plane == 8
    near = (2, 4) if forward_halves else tuple(evens[1:])
    width = weight_ref.shape[1]
    cut = (width // 256) * 128

    barrier = pltpu.get_barrier_semaphore()
    for offset in range(1, plane):
        pl.semaphore_signal(barrier, inc=1, device_id=(g, flip(d, offset)), device_id_type=MESH)

    for step in range(1, lines):
        there = lax.rem(g + step, lines)
        pl.semaphore_signal(barrier, inc=1, device_id=(there, d), device_id_type=MESH)
    pl.semaphore_wait(barrier, plane + lines - 2)

    copy = remote
    own_rows = hidden_ref.at[pl.ds(0, prompt_rows)]

    def line_weight(way, step):
        block = g - step + 1 if way == 0 else g + step - 1
        source = weight_ref if step == 1 else weights_ref.at[block, d]
        return copy(
            source,
            weights_ref.at[block, d],
            line_send.at[way, step],
            line_recv.at[way, step],
            (g + 1 if way == 0 else g - 1, d),
        )

    def line_rows(way, step):
        block = g - step + 1 if way == 0 else g + step - 1
        source = own_rows if step == 1 else rows_ref.at[block]
        return copy(
            source,
            rows_ref.at[block],
            rows_send.at[way, step],
            rows_recv.at[way, step],
            (g + 1 if way == 0 else g - 1, d),
        )

    def sends(way, step):
        if way == 0:
            return (g < lines - 1) & (g >= step - 1)
        return (g > 0) & (g + step - 1 < lines)

    def receives(way, step):
        return g >= step if way == 0 else g + step < lines

    def near_copy(block, offset, own):
        source = weight_ref if own else weights_ref.at[block, d]
        at = near.index(offset)
        return copy(
            source,
            weights_ref.at[block, d],
            near_send.at[block, at],
            near_recv.at[block, at],
            (g, flip(d, offset)),
        )

    def half_copy(block, part):
        columns = pl.ds(0, cut) if part == 0 else pl.ds(cut, width - cut)
        origin = flip(d, 2) if part == 0 else flip(d, 4)
        there = flip(d, 4) if part == 0 else flip(d, 2)
        piece = weights_ref.at[block, origin, :, columns]
        return copy(
            piece, piece, half_send.at[block, part], half_recv.at[block, part], (g, there)
        )

    def core_copy(block, offset, own=False):
        source = weight_ref if own else weights_ref.at[block, flip(d, offset)]
        return copy(
            source,
            weights_ref.at[block, flip(d, offset)],
            core_send.at[block, offset // 2],
            core_recv.at[block, offset // 2],
            (g, flip(d, 1)),
        )

    own_hidden = down_ref.shape[2]

    def swap_piece(owner, part, source_index):
        source = forward_ref.at[:, pl.ds(part * FF + owner * own_hidden, own_hidden)]
        if part == 2:
            return source, down_ref.at[source_index]
        return source, gate_ref.at[source_index, :, pl.ds(part * own_hidden, own_hidden)]

    def swap_copy(offset, part):
        source, target = swap_piece(flip(d, offset), part, d)
        return copy(
            source,
            target,
            swap_send.at[offset, part],
            swap_recv.at[offset, part],
            (g, flip(d, offset)),
        )

    locals_ = (
        pltpu.make_async_copy(weight_ref, weights_ref.at[g, d], local_sem.at[0]),
        pltpu.make_async_copy(own_rows, rows_ref.at[g], local_sem.at[1]),
        *(
            pltpu.make_async_copy(*swap_piece(d, part, d), local_sem.at[2 + part])
            for part in range(3)
        ),
    )

    def launch(block, own):
        for offset in near:
            near_copy(block, offset, own).start()
        core_copy(block, 0, own).start()

    def relay(block):
        for offset in near:
            near_copy(block, offset, False).wait_recv()
            core_copy(block, offset).start()
        if forward_halves:
            half_copy(block, 0).start()
            half_copy(block, 1).start()

    def finish(block):
        if forward_halves:
            half_copy(block, 0).wait_recv()
            half_copy(block, 1).wait_recv()
            core_copy(block, 6).start()

    def both(step, act):
        for way in (0, 1):
            pl.when(receives(way, step))(
                lambda way=way: act(g - step if way == 0 else g + step)
            )

    def take_rows(step):
        for way in (0, 1):

            @pl.when(receives(way, step))
            def _(way=way):
                line_rows(way, step).wait_recv()

            if step + 1 < lines:
                pl.when(sends(way, step + 1))(
                    lambda way=way: line_rows(way, step + 1).start()
                )

    for way in (0, 1):
        pl.when(sends(way, 1))(lambda way=way: line_weight(way, 1).start())
    launch(g, True)
    for one in locals_:
        one.start()
    for step in range(1, lines):
        for way in (0, 1):

            @pl.when(receives(way, step))
            def _(way=way, step=step):
                line_weight(way, step).wait_recv()

            if step + 1 < lines:
                pl.when(sends(way, step + 1))(
                    lambda way=way, step=step: line_weight(way, step + 1).start()
                )
            else:
                pl.when(sends(way, 1))(lambda way=way: line_rows(way, 1).start())

        both(step, lambda block: launch(block, False))
        if step == 1:
            relay(g)
            for offset in range(1, plane):
                for part in range(3):
                    swap_copy(offset, part).start()
    for step in range(1, lines):
        take_rows(step)
        both(step, relay)
        if step == 1:
            finish(g)
        else:
            both(step - 1, finish)
    both(lines - 1, finish)

    def drain(block):
        for offset in evens:
            core_copy(block, offset).wait()
        for offset in near:
            near_copy(block, offset, False).wait_send()
        if forward_halves:
            half_copy(block, 0).wait_send()
            half_copy(block, 1).wait_send()

    drain(g)
    for step in range(1, lines):
        for way in (0, 1):
            pl.when(receives(way, step))(
                lambda way=way, step=step: drain(g - step if way == 0 else g + step)
            )

            @pl.when(sends(way, step))
            def _(way=way, step=step):
                line_weight(way, step).wait_send()
                line_rows(way, step).wait_send()

    for offset in range(1, plane):
        for part in range(3):
            swap_copy(offset, part).wait()
    for one in locals_:
        one.wait()


def gather_start(weight, hidden, forward):
    lines, plane = lax.axis_size("grp"), lax.axis_size("dp")
    prompt_rows = PROMPT_LEN // lines
    own_rows, width = weight.shape
    anywhere = pl.BlockSpec(memory_space=pl.ANY)
    dma = pltpu.SemaphoreType.DMA
    near_count = 2 if plane == 8 else plane // 2 - 1
    pairs = (
        (2, lines),
        (2, lines),
        (2, lines),
        (2, lines),
        (lines, near_count),
        (lines, near_count),
        (lines, 2),
        (lines, 2),
        (lines, plane // 2),
        (lines, plane // 2),
        (plane, 3),
        (plane, 3),
    )
    own_hidden = FF // plane
    return pl.pallas_call(
        functools.partial(gather_kernel, lines, plane, prompt_rows),
        out_shape=(
            jax.ShapeDtypeStruct((lines, plane, own_rows, width), weight.dtype),
            jax.ShapeDtypeStruct((lines, prompt_rows, D), hidden.dtype),
            jax.ShapeDtypeStruct((plane, own_rows, 2 * own_hidden), forward.dtype),
            jax.ShapeDtypeStruct((plane, own_rows, own_hidden), forward.dtype),
        ),
        in_specs=[anywhere] * 3,
        out_specs=(anywhere,) * 4,
        scratch_shapes=[dma((5,))] + [dma(shape) for shape in pairs],
        compiler_params=pltpu.CompilerParams(collective_id=0, has_side_effects=True),
        name="gather_start",
    )(weight, hidden, forward)


def project_kernel(
    place_ref,
    group_ref,
    own_ref,
    gain_ref,
    cosine_ref,
    sine_ref,
    weight_ref,
    query_ref,
    pair_ref,
    normed_ref,
    own_normed_ref,
    scale_ref,
):
    step = pl.program_id(0)
    own_rows = own_ref.shape[0]
    prompt_rows = own_rows - CONT
    start = pl.multiple_of(place_ref[0] * prompt_rows, 16)
    tile = 32

    def norm_tile(values, at):
        values = values.astype(FULL)
        scale = lax.rsqrt(jnp.mean(values * values, axis=-1, keepdims=True) + EPS_NORM)
        normed_ref[pl.ds(at, tile)] = (values * scale * gain_ref[...]).astype(LOW)
        scale_ref[pl.ds(at, tile)] = jnp.broadcast_to(scale, (tile, 128))

    @pl.when(step == 0)
    def _():
        @pl.loop(0, PROMPT_LEN // tile)
        def _(at):
            first = pl.multiple_of(at * tile, tile)
            norm_tile(group_ref[pl.ds(first, tile)], first)

        for at in range(0, CONT, tile):
            norm_tile(own_ref[prompt_rows + at : prompt_rows + at + tile], PROMPT_LEN + at)
        own_normed_ref[:prompt_rows] = normed_ref[pl.ds(start, prompt_rows)]
        own_normed_ref[prompt_rows:] = normed_ref[PROMPT_LEN:]

    def turn(values, cosine, sine_part):
        front, back = values[:, : HD // 2], values[:, HD // 2 :]
        return front * cosine - back * sine_part, back * cosine + front * sine_part

    def project(rows):
        return jnp.dot(rows, weight_ref[...], preferred_element_type=FULL)

    @pl.when(step < HQ)
    def _():
        for first, count, table in ((0, prompt_rows, start), (prompt_rows, CONT, PROMPT_LEN)):
            values = project(own_normed_ref[first : first + count])
            front, back = turn(
                values, cosine_ref[pl.ds(table, count)], sine_ref[pl.ds(table, count)]
            )
            query_ref[first : first + count, : HD // 2] = front.astype(LOW)
            query_ref[first : first + count, HD // 2 :] = back.astype(LOW)

    key_count = PROMPT_LEN + CONT
    part = key_count // 4

    @pl.when((step >= HQ) & (step < HQ + HK))
    def _():
        @pl.loop(0, 4)
        def _(at):
            rows = pl.ds(pl.multiple_of(at * part, 16), part)
            front, back = turn(project(normed_ref[rows]), cosine_ref[rows], sine_ref[rows])
            pair_ref[rows, : HD // 2] = front.astype(LOW)
            pair_ref[rows, HD // 2 :] = back.astype(LOW)

    @pl.when(step >= HQ + HK)
    def _():
        @pl.loop(0, 4)
        def _(at):
            rows = pl.ds(pl.multiple_of(at * part, 16), part)
            pair_ref[rows] = project(normed_ref[rows]).astype(LOW)


VMEM_LIMIT = 60 * 2**20


def project_heads(place, group_rows, own_inputs, gain_row, cosine, sine_part, weights):
    own_rows = own_inputs.shape[0]
    key_count = PROMPT_LEN + CONT
    whole = lambda shape: pl.BlockSpec(shape, lambda j, p: (0, 0))
    return pl.pallas_call(
        project_kernel,
        grid_spec=pltpu.PrefetchScalarGridSpec(
            num_scalar_prefetch=1,
            grid=(HQ + 2 * HK,),
            in_specs=[
                whole((PROMPT_LEN, D)),
                whole((own_rows, D)),
                whole((1, D)),
                whole((key_count, HD // 2)),
                whole((key_count, HD // 2)),
                pl.BlockSpec((D, HD), lambda j, p: (0, j)),
            ],
            out_specs=[
                pl.BlockSpec((own_rows, HD), lambda j, p: (0, jnp.minimum(j, HQ - 1))),
                pl.BlockSpec((key_count, HD), lambda j, p: (0, jnp.maximum(j - HQ, 0))),
                whole((key_count, D)),
                whole((own_rows, D)),
                whole((key_count, 128)),
            ],
        ),
        out_shape=[
            jax.ShapeDtypeStruct((own_rows, HQ * HD), LOW),
            jax.ShapeDtypeStruct((key_count, 2 * HK * HD), LOW),
            jax.ShapeDtypeStruct((key_count, D), LOW),
            jax.ShapeDtypeStruct((own_rows, D), LOW),
            jax.ShapeDtypeStruct((key_count, 128), FULL),
        ],
        compiler_params=pltpu.CompilerParams(vmem_limit_bytes=VMEM_LIMIT),
        name="project_heads",
    )(place, group_rows, own_inputs, gain_row, cosine, sine_part, weights)


def across(left, right):
    return lax.dot_general(left, right, (((1,), (1,)), ((), ())), preferred_element_type=FULL)


def along(left, right):
    return lax.dot_general(left, right, (((0,), (0,)), ((), ())), preferred_element_type=FULL)


def attend_kernel(query_ref, key_ref, value_ref, seen_ref, attended_ref, logsum_ref):
    group_heads = HQ // HK
    for head in range(group_heads):
        columns = slice(head * HD, (head + 1) * HD)
        scores = across(query_ref[:, columns], key_ref[...]) * HD ** (-0.5)
        scores = jnp.where(seen_ref[...] > 0, scores, MASK_FILL)
        peak = jnp.max(scores, axis=-1, keepdims=True)
        unnormed = jnp.exp(scores - peak)
        total = jnp.sum(unnormed, axis=-1, keepdims=True)
        low = (unnormed / total).astype(LOW)
        attended_ref[:, columns] = jnp.dot(
            low, value_ref[...], preferred_element_type=FULL
        ).astype(LOW)
        logsum_ref[:, head * 128 : (head + 1) * 128] = jnp.broadcast_to(
            peak + jnp.log(total), (query_ref.shape[0], 128)
        )


def attend(queries, pairs, seen):
    rows, key_count = seen.shape
    group_heads = HQ // HK
    return pl.pallas_call(
        attend_kernel,
        grid=(HK,),
        in_specs=[
            pl.BlockSpec((rows, group_heads * HD), lambda j: (0, j)),
            pl.BlockSpec((key_count, HD), lambda j: (0, j)),
            pl.BlockSpec((key_count, HD), lambda j: (0, HK + j)),
            pl.BlockSpec((rows, key_count), lambda j: (0, 0)),
        ],
        out_specs=[
            pl.BlockSpec((rows, group_heads * HD), lambda j: (0, j)),
            pl.BlockSpec((rows, group_heads * 128), lambda j: (0, j)),
        ],
        out_shape=[
            jax.ShapeDtypeStruct((rows, HQ * HD), LOW),
            jax.ShapeDtypeStruct((rows, HQ * 128), FULL),
        ],
        compiler_params=pltpu.CompilerParams(vmem_limit_bytes=VMEM_LIMIT),
        name="attend",
    )(queries, pairs, pairs, seen)


def attend_back_kernel(
    place_ref,
    query_ref,
    key_ref,
    value_ref,
    seen_ref,
    logsum_ref,
    grad_ref,
    cosine_ref,
    sine_ref,
    query_out,
    pair_out,
):
    step = pl.program_id(0)
    group_heads = HQ // HK
    rows = query_ref.shape[0]
    prompt_rows = rows - CONT
    start = pl.multiple_of(place_ref[0] * prompt_rows, 16)
    score_scale = HD ** (-0.5)
    key_grad = value_grad = 0.0

    def turn_back(values, cosine, sine_part):
        front, back = values[:, : HD // 2], values[:, HD // 2 :]
        return jnp.concatenate(
            [front * cosine + back * sine_part, back * cosine - front * sine_part], axis=1
        ).astype(LOW)

    for head in range(group_heads):
        columns = slice(head * HD, (head + 1) * HD)
        scores = across(query_ref[:, columns], key_ref[...]) * score_scale
        scores = jnp.where(seen_ref[...] > 0, scores, MASK_FILL)
        probabilities = jnp.exp(scores - logsum_ref[:, head * 128 : head * 128 + 1])
        grads = grad_ref[:, columns]
        probability_grad = across(grads, value_ref[...])
        delta = jnp.sum(probabilities * probability_grad, axis=-1, keepdims=True)
        score_grad = (probabilities * (probability_grad - delta)).astype(LOW)
        query_grad = jnp.dot(score_grad, key_ref[...], preferred_element_type=FULL) * score_scale
        key_grad = key_grad + along(score_grad, query_ref[:, columns])
        value_grad = value_grad + along(probabilities.astype(LOW), grads)
        query_out[:prompt_rows, columns] = turn_back(
            query_grad[:prompt_rows],
            cosine_ref[pl.ds(start, prompt_rows)],
            sine_ref[pl.ds(start, prompt_rows)],
        )
        query_out[prompt_rows:, columns] = turn_back(
            query_grad[prompt_rows:], cosine_ref[PROMPT_LEN:], sine_ref[PROMPT_LEN:]
        )
    pair_out[:, pl.ds(pl.multiple_of(step * HD, HD), HD)] = turn_back(
        key_grad * score_scale, cosine_ref[...], sine_ref[...]
    )
    pair_out[:, pl.ds(pl.multiple_of((HK + step) * HD, HD), HD)] = value_grad.astype(LOW)


def attend_back(place, queries, pairs, seen, logsum, grads, cosine, sine_part):
    rows, key_count = seen.shape
    group_heads = HQ // HK
    whole = lambda shape: pl.BlockSpec(shape, lambda j, p: (0, 0))
    return pl.pallas_call(
        attend_back_kernel,
        grid_spec=pltpu.PrefetchScalarGridSpec(
            num_scalar_prefetch=1,
            grid=(HK,),
            in_specs=[
                pl.BlockSpec((rows, group_heads * HD), lambda j, p: (0, j)),
                pl.BlockSpec((key_count, HD), lambda j, p: (0, j)),
                pl.BlockSpec((key_count, HD), lambda j, p: (0, HK + j)),
                whole((rows, key_count)),
                pl.BlockSpec((rows, group_heads * 128), lambda j, p: (0, j)),
                pl.BlockSpec((rows, group_heads * HD), lambda j, p: (0, j)),
                whole((key_count, HD // 2)),
                whole((key_count, HD // 2)),
            ],
            out_specs=[
                pl.BlockSpec((rows, group_heads * HD), lambda j, p: (0, j)),
                whole((key_count, 2 * HK * HD)),
            ],
        ),
        out_shape=[
            jax.ShapeDtypeStruct((rows, HQ * HD), LOW),
            jax.ShapeDtypeStruct((key_count, 2 * HK * HD), LOW),
        ],
        compiler_params=pltpu.CompilerParams(vmem_limit_bytes=VMEM_LIMIT),
        name="attend_back",
    )(place, queries, pairs, pairs, seen, logsum, grads, cosine, sine_part)


def weights_back_kernel(
    place_ref,
    query_ref,
    pair_ref,
    branch_ref,
    attended_ref,
    normed_ref,
    own_normed_ref,
    group_ref,
    own_ref,
    scale_ref,
    query_weight_ref,
    pair_weight_ref,
    query_term,
    pair_term,
    merge_term,
    back_out,
    pair_back_out,
    gain_out,
):
    rows = query_ref.shape[0]
    prompt_rows = rows - CONT
    start = pl.multiple_of(place_ref[0] * prompt_rows, 16)
    query_term[...] = along(own_normed_ref[...], query_ref[...]).astype(LOW)
    pair_term[...] = along(normed_ref[...], pair_ref[...]).astype(LOW)
    merge_term[...] = along(branch_ref[...], attended_ref[...]).astype(LOW)
    query_back = across(query_ref[...], query_weight_ref[...])
    pair_back = across(pair_ref[...], pair_weight_ref[...])
    own_values = own_ref[prompt_rows:].astype(FULL) * scale_ref[PROMPT_LEN:, :1]
    tail = query_back[prompt_rows:] + pair_back[PROMPT_LEN:]
    group_values = group_ref[...].astype(FULL) * scale_ref[:PROMPT_LEN, :1]
    own_prompt = own_ref[:prompt_rows].astype(FULL) * scale_ref[pl.ds(start, prompt_rows), :1]
    gain_out[...] = (
        jnp.sum(pair_back[:PROMPT_LEN] * group_values, axis=0, keepdims=True)
        + jnp.sum(query_back[:prompt_rows] * own_prompt, axis=0, keepdims=True)
        + jnp.sum(tail * own_values, axis=0, keepdims=True)
    )
    back_out[:prompt_rows] = query_back[:prompt_rows]
    back_out[prompt_rows:] = tail
    pair_back_out[...] = pair_back[:PROMPT_LEN].astype(LOW)


def weights_back(
    place, queries, pairs, branch, attended, normed, own_normed, group_rows, own_inputs, scale, weights
):
    rows, key_count = queries.shape[0], pairs.shape[0]
    wide, tile = HQ * HD, 256
    whole = lambda shape: pl.BlockSpec(shape, lambda j, p: (0, 0))
    tall = lambda count: pl.BlockSpec((count, tile), lambda j, p: (0, j))
    flat = lambda at: pl.BlockSpec((tile, wide), lambda j, p: (j, at))
    return pl.pallas_call(
        weights_back_kernel,
        grid_spec=pltpu.PrefetchScalarGridSpec(
            num_scalar_prefetch=1,
            grid=(D // tile,),
            in_specs=[
                whole((rows, wide)),
                whole((key_count, wide)),
                tall(rows),
                whole((rows, wide)),
                tall(key_count),
                tall(rows),
                tall(PROMPT_LEN),
                tall(rows),
                whole((key_count, 128)),
                flat(0),
                flat(1),
            ],
            out_specs=[flat(0), flat(0), flat(0), tall(rows), tall(PROMPT_LEN), tall(1)],
        ),
        out_shape=[
            jax.ShapeDtypeStruct((D, wide), LOW),
            jax.ShapeDtypeStruct((D, wide), LOW),
            jax.ShapeDtypeStruct((D, wide), LOW),
            jax.ShapeDtypeStruct((rows, D), FULL),
            jax.ShapeDtypeStruct((PROMPT_LEN, D), LOW),
            jax.ShapeDtypeStruct((1, D), FULL),
        ],
        compiler_params=pltpu.CompilerParams(vmem_limit_bytes=VMEM_LIMIT),
        name="weights_back",
    )(
        place,
        queries,
        pairs,
        branch,
        attended,
        normed,
        own_normed,
        group_rows,
        own_inputs,
        scale,
        weights,
        weights,
    )


def plane_swap(block, offset):
    size = lax.axis_size("dp")
    return lax.ppermute(block, "dp", [(i, i ^ offset) for i in range(size)])


def plane_gather(block):
    mine = [block] + [plane_swap(block, o) for o in range(2, lax.axis_size("dp"), 2)]
    pairs = [(one, plane_swap(one, 1)) for one in mine]
    return jnp.concatenate([one for pair in pairs for one in pair], axis=0)


def plane_scatter(part_of):
    size = lax.axis_size("dp")
    sums = {}
    for offset in list(range(size - 2, 0, -2)) + [0]:
        arrived = plane_swap(part_of(offset + 1).astype(LOW), 1)
        sums[offset] = part_of(offset).astype(FULL) + arrived.astype(FULL)
        if offset:
            sums[offset] = plane_swap(sums[offset].astype(LOW), offset)
    total = sums[0]
    for offset in range(2, size, 2):
        total = total + sums[offset].astype(FULL)
    return total


def line_scatter(term):
    return lax.psum_scatter(term, "grp", scatter_dimension=0, tiled=True)


def finish_kernel(
    lines,
    plane,
    query_ref,
    pair_ref,
    merge_ref,
    gain_ref,
    gate_ref,
    up_ref,
    down_ref,
    back_ref,
    a_master,
    a_first,
    a_second,
    m_master,
    m_first,
    m_second,
    f_master,
    f_first,
    f_second,
    a_grad,
    a_update,
    a_first_new,
    a_second_new,
    m_grad,
    m_update,
    m_first_new,
    m_second_new,
    gain_out,
    back_out,
    f_grad,
    f_update,
    f_first_new,
    f_second_new,
    mine,
    core_in,
    plane_in,
    line_in,
    swap_in,
    state,
    made,
    a_state,
    a_made,
    gain_made,
    mine_sem,
    core_send,
    core_recv,
    plane_send,
    plane_recv,
    line_send,
    line_recv,
    swap_send,
    swap_recv,
    own_sem,
    state_sem,
    made_sem,
    a_sem,
    gain_sem,
    back_send,
    back_recv,
):
    g = lax.axis_index("grp")
    d = lax.axis_index("dp")
    chips = plane // 2
    chip, core = lax.div(d, 2), lax.rem(d, 2)
    partner = d + 1 - 2 * core
    rows = a_master.shape[0]
    own_hidden = gate_ref.shape[2]
    width = core_in.shape[3]
    a_width, m_width = a_master.shape[1], m_master.shape[1]
    parts, begin = [], 0
    for ref in (query_ref, pair_ref, merge_ref, gain_ref):
        parts.append((ref, pl.ds(begin, ref.shape[4])))
        begin += ref.shape[4]
    prompt_rows = back_out.shape[1]

    barrier = pltpu.get_barrier_semaphore()
    for step in range(1, plane):
        there = lax.rem(d + step, plane)
        pl.semaphore_signal(barrier, inc=1, device_id=(g, there), device_id_type=MESH)
    for step in range(1, lines):
        there = lax.rem(g + step, lines)
        pl.semaphore_signal(barrier, inc=1, device_id=(there, d), device_id_type=MESH)
    pl.semaphore_wait(barrier, plane + lines - 2)

    def line_at(turn):
        return lax.rem(g + turn + 1, lines)

    def core_copy(turn, part):
        line = line_at(turn)
        ref, columns = parts[part]
        return remote(
            ref.at[line, :, 1 - core],
            core_in.at[line, :, :, columns],
            core_send.at[turn, part],
            core_recv.at[turn, part],
            (g, partner),
        )

    def mine_copy(turn, part):
        line = line_at(turn)
        ref, columns = parts[part]
        return pltpu.make_async_copy(
            ref.at[line, :, core], mine.at[turn % 2, :, :, columns], mine_sem.at[turn, part]
        )

    cut = width // 256 * 128
    columns_of = (pl.ds(0, cut), pl.ds(cut, width - cut))

    def plane_copy(turn, step):
        line = line_at(turn)
        there = lax.rem(chip + step, chips)
        return remote(
            core_in.at[line, there],
            plane_in.at[line, chip],
            plane_send.at[turn, step],
            plane_recv.at[turn, step],
            (g, 2 * there + core),
        )

    def near_copy(turn, part, relayed):
        line = line_at(turn)
        there = flip(chip, part + 1)
        owner = flip(chip, 3) if relayed else there
        return remote(
            core_in.at[line, owner, :, columns_of[part]],
            plane_in.at[line, 1 if relayed else 0, :, columns_of[part]],
            plane_send.at[turn, 2 * relayed + part],
            plane_recv.at[turn, 2 * relayed + part],
            (g, 2 * there + core),
        )

    def relay_copy(turn, part):
        line = line_at(turn)
        there = flip(chip, 2 - part)
        return remote(
            core_in.at[line, there, :, columns_of[part]],
            plane_in.at[line, 2, :, columns_of[part]],
            plane_send.at[turn, 4 + part],
            plane_recv.at[turn, 4 + part],
            (g, 2 * there + core),
        )

    def line_copy(turn):
        line = line_at(turn)
        return remote(
            core_in.at[line, chip],
            line_in.at[g],
            line_send.at[turn],
            line_recv.at[turn],
            (line, d),
        )

    forward_refs = (gate_ref, up_ref, down_ref)

    def swap_copy(step, part):
        there = lax.rem(d + step, plane)
        return remote(
            forward_refs[part].at[there],
            swap_in.at[part, d],
            swap_send.at[step, part],
            swap_recv.at[step, part],
            (g, there),
        )

    own_swap = [
        pltpu.make_async_copy(forward_refs[part].at[d], swap_in.at[part, d], own_sem.at[part])
        for part in range(3)
    ]

    def f_columns(turn):
        block = lax.rem(d + lax.div(turn, 3), plane)
        return pl.ds(
            pl.multiple_of(lax.rem(turn, 3) * FF + block * own_hidden, own_hidden), own_hidden
        )

    def state_copy(turn, which):
        slot = lax.rem(turn, 2)
        return pltpu.make_async_copy(
            (f_master, f_first, f_second)[which].at[:, f_columns(turn)],
            state.at[slot, which],
            state_sem.at[slot, which],
        )

    def made_copy(turn, which):
        slot = lax.rem(turn, 2)
        return pltpu.make_async_copy(
            made.at[slot, which],
            (f_grad, f_update, f_first_new, f_second_new)[which].at[:, f_columns(turn)],
            made_sem.at[slot, which],
        )

    def back_copy(step):
        there = lax.rem(g + step, lines)
        return remote(
            back_ref.at[there],
            back_out.at[g],
            back_send.at[step],
            back_recv.at[step],
            (there, d),
        )

    own_back = pltpu.make_async_copy(back_ref.at[g], back_out.at[g], own_sem.at[3])

    slabs = (pl.ds(0, a_width), pl.ds(a_width, m_width))

    def a_state_copy(which, slab):
        source = ((a_master, a_first, a_second), (m_master, m_first, m_second))[slab][which]
        return pltpu.make_async_copy(
            source, a_state.at[which, :, slabs[slab]], a_sem.at[slab, which]
        )

    def a_made_copy(which, slab):
        target = (
            (a_grad, a_update, a_first_new, a_second_new),
            (m_grad, m_update, m_first_new, m_second_new),
        )[slab][which]
        return pltpu.make_async_copy(
            a_made.at[which, :, slabs[slab]], target, a_sem.at[slab, 3 + which]
        )

    every = range(len(parts))
    for turn in range(lines):
        for part in every:
            core_copy(turn, part).start()
            if turn < 2:
                mine_copy(turn, part).start()
    for step in range(1, lines):
        back_copy(step).start()
    for step in range(1, plane):
        for part in range(3):
            swap_copy(step, part).start()
    for one in own_swap:
        one.start()
    own_back.start()
    for which in range(3):
        state_copy(0, which).start()
        for slab in range(2):
            a_state_copy(which, slab).start()

    tile = 896 if width % 896 == 0 else 128
    halves = plane == 8

    def add_into(line, there, other, columns=None):
        first, count = (0, width) if columns is None else columns
        step = tile if columns is None else 128

        @pl.loop(0, count // step)
        def _(at):
            here = pl.ds(pl.multiple_of(first + at * step, 128), step)
            total = core_in[line, there, :, here].astype(FULL) + other(here).astype(FULL)
            core_in[line, there, :, here] = total.astype(LOW)

    for turn in range(lines):
        line = line_at(turn)
        for part in every:
            core_copy(turn, part).wait_recv()
            mine_copy(turn, part).wait()
        order = (3, 1, 2, 0) if halves else tuple(range(1, chips + 1))
        for step in order:
            there = flip(chip, step) if halves else lax.rem(chip + step, chips)
            add_into(
                line, there, lambda here, there=there, turn=turn: mine[turn % 2, there, :, here]
            )
            if halves and step == 3:
                for part in range(2):
                    near_copy(turn, part, True).start()
            elif halves and step:
                near_copy(turn, step - 1, False).start()
            elif not halves and step < chips:
                plane_copy(turn, step).start()
        if turn + 2 < lines:
            for part in every:
                mine_copy(turn + 2, part).start()

    def pass_on(turn):
        line = line_at(turn)
        for part, columns in enumerate(((0, cut), (cut, width - cut))):
            near_copy(turn, part, True).wait_recv()
            add_into(
                line,
                flip(chip, 2 - part),
                lambda here, line=line: plane_in[line, 1, :, here],
                columns,
            )
            relay_copy(turn, part).start()

    def forward_turn(turn):
        slot = lax.rem(turn, 2)
        block = lax.rem(d + lax.div(turn, 3), plane)
        part = lax.rem(turn, 3)

        @pl.when(turn + 1 < 3 * plane)
        def _():
            for which in range(3):
                state_copy(turn + 1, which).start()

        @pl.when(turn > 1)
        def _():
            for which in range(4):
                made_copy(turn - 2, which).wait()

        for which in range(3):
            state_copy(turn, which).wait()

        @pl.loop(0, rows // 16)
        def _(at):
            rows_at = pl.ds(pl.multiple_of(at * 16, 16), 16)
            gradient = swap_in[part, block, rows_at].astype(FULL)
            update, first_new, second_new = adam_step(
                state[slot, 0, rows_at],
                state[slot, 1, rows_at],
                state[slot, 2, rows_at],
                gradient,
                WEIGHT_DECAY,
            )
            made[slot, 0, rows_at] = gradient
            made[slot, 1, rows_at] = update
            made[slot, 2, rows_at] = first_new
            made[slot, 3, rows_at] = second_new

        for which in range(4):
            made_copy(turn, which).start()

    if halves:
        pass_on(0)
    for one in own_swap:
        one.wait()
    for step in range(1, plane):
        for part in range(3):
            swap_copy(step, part).wait_recv()
    each = 3 * plane // lines
    for turn in range(lines):
        lax.fori_loop(turn * each, (turn + 1) * each, lambda k, c: (forward_turn(k), c)[1], 0)
        line = line_at(turn)
        if halves:
            if turn + 1 < lines:
                pass_on(turn + 1)
            for part in range(2):
                near_copy(turn, part, False).wait_recv()
                relay_copy(turn, part).wait_recv()
            arrived = (0, 2)
        else:
            for step in range(1, chips):
                plane_copy(turn, step).wait_recv()
            arrived = tuple(lax.rem(chip + step, chips) for step in range(1, chips))

        @pl.loop(0, width // tile)
        def _(at, line=line, arrived=arrived):
            columns = pl.ds(pl.multiple_of(at * tile, tile), tile)
            total = core_in[line, chip, :, columns].astype(FULL)
            for block in arrived:
                total = total + plane_in[line, block, :, columns].astype(FULL)
            core_in[line, chip, :, columns] = total.astype(LOW)

        if turn < lines - 1:
            line_copy(turn).start()

    for which in range(4):
        for turn in (3 * plane - 2, 3 * plane - 1):
            made_copy(turn, which).wait()
    for turn in range(lines - 1):
        line_copy(turn).wait_recv()
    for which in range(3):
        for slab in range(2):
            a_state_copy(which, slab).wait()

    def owned(columns):
        total = core_in[g, chip, :, columns].astype(FULL)
        for step in range(1, lines):
            total = total + line_in[lax.rem(g + step, lines), :, columns].astype(FULL)
        return total

    @pl.loop(0, (a_width + m_width) // 256)
    def _(at):
        columns = pl.ds(pl.multiple_of(at * 256, 256), 256)
        gradient = owned(columns)
        update, first_new, second_new = adam_step(
            a_state[0, :, columns],
            a_state[1, :, columns],
            a_state[2, :, columns],
            gradient,
            WEIGHT_DECAY,
        )
        a_made[0, :, columns] = gradient
        a_made[1, :, columns] = update
        a_made[2, :, columns] = first_new
        a_made[3, :, columns] = second_new

    for which in range(4):
        for slab in range(2):
            a_made_copy(which, slab).start()
    gain_made[...] = owned(pl.ds(a_width + m_width, GAIN_PAD))
    gain_copy = pltpu.make_async_copy(gain_made, gain_out, gain_sem.at[0])
    gain_copy.start()
    for turn in range(lines):
        for part in every:
            core_copy(turn, part).wait_send()
        if halves:
            for part in range(2):
                near_copy(turn, part, False).wait_send()
                near_copy(turn, part, True).wait_send()
                relay_copy(turn, part).wait_send()
        else:
            for step in range(1, chips):
                plane_copy(turn, step).wait_send()
        if turn < lines - 1:
            line_copy(turn).wait_send()
    for step in range(1, plane):
        for part in range(3):
            swap_copy(step, part).wait_send()
    for step in range(1, lines):
        back_copy(step).wait()
    own_back.wait()
    for which in range(4):
        for slab in range(2):
            a_made_copy(which, slab).wait()
    gain_copy.wait()


def finish(terms, forward_parts, pair_back, attention, merge, forward):
    lines, plane = lax.axis_size("grp"), lax.axis_size("dp")
    chips = plane // 2
    rows, a_width = attention[0].shape
    m_width = merge[0].shape[1]
    own_hidden = forward_parts[0].shape[1]
    width = a_width + m_width + GAIN_PAD
    anywhere = pl.BlockSpec(memory_space=pl.ANY)
    dma = pltpu.SemaphoreType.DMA
    vmem = pltpu.VMEM
    back = pair_back.reshape(lines, PROMPT_LEN // lines, D)

    def like(array):
        return jax.ShapeDtypeStruct(array.shape, array.dtype)

    return pl.pallas_call(
        functools.partial(finish_kernel, lines, plane),
        out_shape=(like(attention[0]),) * 4
        + (like(merge[0]),) * 4
        + (jax.ShapeDtypeStruct((rows, GAIN_PAD), FULL), like(back))
        + (like(forward[0]),) * 4,
        in_specs=[anywhere] * 17,
        out_specs=(anywhere,) * 14,
        scratch_shapes=[
            vmem((2, chips, rows, width), LOW),
            vmem((lines, chips, rows, width), LOW),
            vmem((lines, 3 if plane == 8 else chips, rows, width), LOW),
            vmem((lines, rows, width), LOW),
            vmem((3, plane, rows, own_hidden), LOW),
            vmem((2, 3, rows, own_hidden), FULL),
            vmem((2, 4, rows, own_hidden), FULL),
            vmem((3, rows, a_width + m_width), FULL),
            vmem((4, rows, a_width + m_width), FULL),
            vmem((rows, GAIN_PAD), FULL),
            dma((lines, 4)),
            dma((lines, 4)),
            dma((lines, 4)),
            dma((lines, max(6, chips))),
            dma((lines, max(6, chips))),
            dma((lines,)),
            dma((lines,)),
            dma((plane, 3)),
            dma((plane, 3)),
            dma((4,)),
            dma((2, 3)),
            dma((2, 4)),
            dma((2, 7)),
            dma((1,)),
            dma((lines,)),
            dma((lines,)),
        ],
        compiler_params=pltpu.CompilerParams(
            collective_id=1, has_side_effects=True, vmem_limit_bytes=VMEM_LIMIT
        ),
        name="finish",
    )(
        *(term.reshape(lines, chips, 2, rows, term.shape[1]) for term in terms),
        *(part.reshape(plane, rows, -1) for part in forward_parts),
        back,
        *attention,
        *merge,
        *forward,
    )


def body(
    hidden,
    cotangent,
    segment_ids,
    continuation_prompt,
    gain_master,
    gain_first,
    gain_second,
    attention_master,
    attention_first,
    attention_second,
    merge_master,
    merge_first,
    merge_second,
    feedforward_master,
    feedforward_first,
    feedforward_second,
):
    group_index = lax.axis_index("grp")
    dp_size = lax.axis_size("dp")
    row_count = hidden.shape[2]
    prompt_rows = row_count - CONT
    qkv_width = (HQ + 2 * HK) * HD
    own_rows = feedforward_master.shape[0]
    own_hidden = FF // dp_size
    own_inputs = hidden.reshape(row_count, D)

    gain_columns = jnp.pad(gain_master.T, ((0, 0), (0, GAIN_PAD - 2)))
    weight_low = jnp.concatenate(
        [attention_master.astype(LOW), merge_master.astype(LOW), gain_columns.astype(LOW)], axis=1
    )
    weights, group_rows, gate_rows, down_rows = gather_start(
        weight_low, own_inputs, feedforward_master.astype(LOW)
    )
    weights, late_cotangent = lax.optimization_barrier((weights, cotangent))
    weights = weights.reshape(D, -1)
    merge_weight = weights[:, qkv_width : qkv_width + D]
    gain_float = weights[:, qkv_width + D : qkv_width + D + 2].astype(FULL).T
    gate_weight = lax.all_gather(
        gate_rows.reshape(dp_size * own_rows, 2 * own_hidden), "grp", axis=0, tiled=True
    )
    gate_weight, down_rows = lax.optimization_barrier((gate_weight, down_rows))
    down_weight = lax.all_gather(
        down_rows.reshape(dp_size * own_rows, own_hidden), "grp", axis=0, tiled=True
    )
    down_grad = plane_gather(late_cotangent.reshape(row_count, D))

    segment_row = segment_ids[0]
    source_row = continuation_prompt[0]
    prompt_positions, follow_positions = segment_positions(segment_row, source_row)
    cosine, sine_part = angle_table(jnp.concatenate([prompt_positions, follow_positions[0]]))

    place = jnp.reshape(group_index, (1,)).astype(jnp.int32)
    group_rows = group_rows.reshape(PROMPT_LEN, D)
    queries, pairs, key_normed, normed, key_scale = project_heads(
        place, group_rows, own_inputs, gain_float[:1], cosine, sine_part, weights
    )
    inputs = own_inputs.astype(FULL)
    first_scale = norm_scale(inputs)

    row_index = jnp.arange(row_count, dtype=jnp.int32)
    is_prompt = row_index < prompt_rows
    global_row = group_index * prompt_rows + jnp.minimum(row_index, prompt_rows - 1)
    own_segment = lax.dynamic_slice_in_dim(segment_row, group_index * prompt_rows, prompt_rows)
    query_segment = jnp.concatenate([own_segment, jnp.broadcast_to(source_row, (CONT,))])
    key_index = jnp.arange(PROMPT_LEN, dtype=jnp.int32)
    prompt_seen = (segment_row[None, :] == query_segment[:, None]) & (
        (key_index[None, :] <= global_row[:, None]) | ~is_prompt[:, None]
    )
    follow_seen = (~is_prompt)[:, None] & (
        jnp.arange(CONT, dtype=jnp.int32)[None, :] <= (row_index - prompt_rows)[:, None]
    )
    visible = jnp.concatenate([prompt_seen, follow_seen], axis=1)
    seen = visible.astype(FULL)
    attended, row_logsum = attend(queries, pairs, seen)
    middle = inputs + contract(attended, merge_weight, 1, 1)
    second_scale = norm_scale(middle)
    normed_two = (middle * second_scale * gain_float[1]).astype(LOW)
    grad_rows = cotangent.reshape(row_count, D).astype(FULL)

    def by_offset(left, right, right_axis, after=None):
        chunks = {}
        for offset in list(range(2, dp_size, 2)) + [0]:
            rows = left[offset * row_count : (offset + 2) * row_count]
            if offset == 0 and after is not None:
                rows, _ = lax.optimization_barrier((rows, after))
            chunks[offset] = contract(rows, right, 1, right_axis).astype(LOW)
        return lambda offset: chunks[offset - offset % 2][
            (offset % 2) * row_count : (offset % 2 + 1) * row_count
        ]

    normed_two, down_grad = lax.optimization_barrier((normed_two, down_grad))
    normed_all = plane_gather(normed_two)
    gate_up = jnp.dot(normed_all, gate_weight, preferred_element_type=FULL)
    gate_values = gate_up[:, :own_hidden]
    up_values = gate_up[:, own_hidden:]
    gate_sigmoid, gate_silu, activated = gate_parts(gate_values, up_values)
    down_term = contract(down_grad, activated, 0, 0).astype(LOW)
    down_term, down_weight = lax.optimization_barrier((down_term, down_weight))
    out_parts = by_offset(activated, down_weight, 1)
    out_chunks = [out_parts(offset) for offset in range(dp_size)]
    out_chunks, down_grad = lax.optimization_barrier((out_chunks, down_grad))
    out_swapped = [plane_swap(out_chunks[offset + 1], 1) for offset in range(0, dp_size, 2)]
    activated_grad = contract(down_grad, down_weight, 1, 0)
    gate_grad, up_grad = gate_backward(
        activated_grad, gate_values, up_values, gate_sigmoid, gate_silu
    )
    gate_up_grad = jnp.concatenate([gate_grad, up_grad], axis=1)

    gate_up_grad, out_swapped = lax.optimization_barrier((gate_up_grad, out_swapped))
    out_sums = [
        out_chunks[2 * at].astype(FULL) + one.astype(FULL) for at, one in enumerate(out_swapped)
    ]
    out_arrived = [plane_swap(one.astype(LOW), 2 * at) for at, one in enumerate(out_sums) if at]
    down_part = line_scatter(down_term)
    back_parts = by_offset(gate_up_grad, gate_weight, 1, down_part)
    normed_two_grad = plane_scatter(back_parts)
    gate_term = contract(normed_all, gate_up_grad[:, :own_hidden], 0, 0).astype(LOW)
    normed_all, out_arrived = lax.optimization_barrier((normed_all, out_arrived))
    up_term = contract(normed_all, gate_up_grad[:, own_hidden:], 0, 0).astype(LOW)
    gate_part = line_scatter(gate_term)
    normed_two_grad, gate_term, up_term = lax.optimization_barrier(
        (normed_two_grad, gate_term, up_term)
    )
    result = middle + out_sums[0]
    for one in out_arrived:
        result = result + one.astype(FULL)
    block_output = result.astype(LOW).reshape(hidden.shape)
    middle_grad = grad_rows + norm_back(middle, second_scale, gain_float[1], normed_two_grad)
    gain_two_part = jnp.sum(normed_two_grad * middle * second_scale, axis=0)
    branch_grad = middle_grad.astype(LOW)
    attended_grad = contract(branch_grad, merge_weight, 1, 0).astype(LOW)
    attended_grad, gate_part = lax.optimization_barrier((attended_grad, gate_part))
    up_part = line_scatter(up_term)
    query_project, pair_project = attend_back(
        place, queries, pairs, seen, row_logsum, attended_grad, cosine, sine_part
    )
    query_term, pair_term, merge_term, normed_grad, pair_back, gain_one_part = weights_back(
        place,
        query_project,
        pair_project,
        branch_grad,
        attended,
        key_normed,
        normed,
        group_rows,
        own_inputs,
        key_scale,
        weights,
    )
    gain_term = jnp.pad(
        jnp.stack([gain_one_part[0], gain_two_part], axis=1), ((0, 0), (0, GAIN_PAD - 2))
    )
    finished = finish(
        (query_term, pair_term, merge_term, gain_term.astype(LOW)),
        (gate_part, up_part, down_part),
        pair_back,
        (attention_master, attention_first, attention_second),
        (merge_master, merge_first, merge_second),
        (feedforward_master, feedforward_first, feedforward_second),
    )
    gain_grad = finished[8][:, :2].T
    pair_sum = jnp.sum(finished[9].astype(FULL), axis=0)
    normed_grad = normed_grad + jnp.pad(pair_sum, ((0, CONT), (0, 0)))
    input_grad = (middle_grad + norm_back(inputs, first_scale, gain_float[0], normed_grad)).reshape(
        hidden.shape
    )
    gain_new = adam_step(gain_master, gain_first, gain_second, gain_grad, 0.0)
    return (
        block_output,
        input_grad,
        gain_grad,
        *gain_new,
        *finished[:8],
        *finished[10:],
    )


def solution(mesh):
    tokens = P("dp", "grp", None, None)
    gains = P(None, ("grp", "dp"))
    matrix = P(("grp", "dp"), None)
    return jax.shard_map(
        body,
        mesh=mesh,
        in_specs=(tokens, tokens, P("dp", None), P("dp", "grp")) + (gains,) * 3 + (matrix,) * 9,
        out_specs=(tokens, tokens) + (gains,) * 4 + (matrix,) * 12,
        check_vma=False,
    )
```

```python
import functools

import jax
import jax.numpy as jnp
from jax import lax
from jax.experimental import pallas as pl
from jax.experimental.pallas import tpu as pltpu
from jax.sharding import PartitionSpec as P

D = 2048
FF = 8192
HQ = 8
HK = 4
HD = 256
PROMPT_LEN = 1024
PROMPTS = 4
CONT = 64
STEP = 10
GAIN_PAD = 128

EPS_NORM = 1e-06
ROPE_THETA = 1000042.0
MASK_FILL = -1e30
BETA_ONE = 0.9
BETA_TWO = 0.95
ADAM_EPS = 1e-08
LEARN_RATE = 0.02
WEIGHT_DECAY = 0.1
LOW = jnp.bfloat16
FULL = jnp.float32
MESH = pl.DeviceIdType.MESH


def contract(left, right, left_axis, right_axis):
    return lax.dot_general(
        left, right, (((left_axis,), (right_axis,)), ((), ())), preferred_element_type=FULL
    )


def angle_table(positions):
    inverse_rate = ROPE_THETA ** (-(jnp.arange(HD // 2, dtype=FULL) * 2.0) / HD)
    angles = positions.astype(FULL)[..., None] * inverse_rate
    return (jnp.cos(angles), jnp.sin(angles))


def segment_positions(segment_row, source_row):
    labels = jnp.arange(PROMPTS, dtype=jnp.int32)
    member = (segment_row[None, :] == labels[:, None]).astype(jnp.int32)
    lengths = jnp.sum(member, axis=1, dtype=jnp.int32)
    starts = jnp.sum(
        jnp.where(labels[None, :] < labels[:, None], lengths[None, :], 0), axis=1, dtype=jnp.int32
    )
    prompt_index = jnp.arange(segment_row.shape[0], dtype=jnp.int32)
    prompt_positions = prompt_index - jnp.sum(member * starts[:, None], axis=0, dtype=jnp.int32)
    source_length = jnp.sum(
        (source_row[:, None] == labels[None, :]).astype(jnp.int32) * lengths[None, :],
        axis=1,
        dtype=jnp.int32,
    )
    follow_positions = source_length[:, None] + jnp.arange(CONT, dtype=jnp.int32)[None, :]
    return (prompt_positions, follow_positions)


def norm_scale(values):
    return lax.rsqrt(jnp.mean(values * values, axis=-1, keepdims=True) + EPS_NORM)


def norm_back(values, row_scale, gain_row, normed_grad):
    scaled = normed_grad * gain_row
    return row_scale * scaled - values * row_scale**3 * jnp.mean(
        scaled * values, axis=-1, keepdims=True
    )


def adam_step(master, first_moment, second_moment, gradient, decay_rate):
    first_new = BETA_ONE * first_moment + (1.0 - BETA_ONE) * gradient
    second_new = BETA_TWO * second_moment + (1.0 - BETA_TWO) * gradient * gradient
    correct_one = 1.0 - BETA_ONE**STEP
    correct_two = 1.0 - BETA_TWO**STEP
    update = first_new / correct_one / (jnp.sqrt(second_new / correct_two) + ADAM_EPS)
    return (-LEARN_RATE * (update + decay_rate * master), first_new, second_new)


def gate_parts(gate_values, up_values):
    gate_sigmoid = jax.nn.sigmoid(gate_values)
    gate_silu = gate_values * gate_sigmoid
    return (gate_sigmoid, gate_silu, (gate_silu * up_values).astype(LOW))


def gate_backward(activated_grad, gate_values, up_values, gate_sigmoid, gate_silu):
    gate_grad = (
        activated_grad * up_values * gate_sigmoid * (1.0 + gate_values * (1.0 - gate_sigmoid))
    ).astype(LOW)
    up_grad = (activated_grad * gate_silu).astype(LOW)
    return (gate_grad, up_grad)


def flip(index, bits):
    bit = 1
    while bit <= bits:
        if bits & bit:
            index = index + bit - 2 * bit * lax.rem(index // bit, 2)
        bit *= 2
    return index


def remote(source, target, send, recv, there):
    return pltpu.make_async_remote_copy(
        src_ref=source,
        dst_ref=target,
        send_sem=send,
        recv_sem=recv,
        device_id=there,
        device_id_type=MESH,
    )


def gather_kernel(
    lines,
    plane,
    prompt_rows,
    weight_ref,
    hidden_ref,
    forward_ref,
    weights_ref,
    rows_ref,
    gate_ref,
    down_ref,
    local_sem,
    line_send,
    line_recv,
    rows_send,
    rows_recv,
    near_send,
    near_recv,
    half_send,
    half_recv,
    core_send,
    core_recv,
    swap_send,
    swap_recv,
):
    g = lax.axis_index("grp")
    d = lax.axis_index("dp")
    evens = range(0, plane, 2)
    forward_halves = plane == 8
    near = (2, 4) if forward_halves else tuple(evens[1:])
    width = weight_ref.shape[1]
    cut = (width // 256) * 128

    barrier = pltpu.get_barrier_semaphore()
    for offset in range(1, plane):
        pl.semaphore_signal(barrier, inc=1, device_id=(g, flip(d, offset)), device_id_type=MESH)

    for step in range(1, lines):
        there = lax.rem(g + step, lines)
        pl.semaphore_signal(barrier, inc=1, device_id=(there, d), device_id_type=MESH)
    pl.semaphore_wait(barrier, plane + lines - 2)

    copy = remote
    own_rows = hidden_ref.at[pl.ds(0, prompt_rows)]

    def line_weight(way, step):
        block = g - step + 1 if way == 0 else g + step - 1
        source = weight_ref if step == 1 else weights_ref.at[block, d]
        return copy(
            source,
            weights_ref.at[block, d],
            line_send.at[way, step],
            line_recv.at[way, step],
            (g + 1 if way == 0 else g - 1, d),
        )

    def line_rows(way, step):
        block = g - step + 1 if way == 0 else g + step - 1
        source = own_rows if step == 1 else rows_ref.at[block]
        return copy(
            source,
            rows_ref.at[block],
            rows_send.at[way, step],
            rows_recv.at[way, step],
            (g + 1 if way == 0 else g - 1, d),
        )

    def sends(way, step):
        if way == 0:
            return (g < lines - 1) & (g >= step - 1)
        return (g > 0) & (g + step - 1 < lines)

    def receives(way, step):
        return g >= step if way == 0 else g + step < lines

    def near_copy(block, offset, own):
        source = weight_ref if own else weights_ref.at[block, d]
        at = near.index(offset)
        return copy(
            source,
            weights_ref.at[block, d],
            near_send.at[block, at],
            near_recv.at[block, at],
            (g, flip(d, offset)),
        )

    def half_copy(block, part):
        columns = pl.ds(0, cut) if part == 0 else pl.ds(cut, width - cut)
        origin = flip(d, 2) if part == 0 else flip(d, 4)
        there = flip(d, 4) if part == 0 else flip(d, 2)
        piece = weights_ref.at[block, origin, :, columns]
        return copy(
            piece, piece, half_send.at[block, part], half_recv.at[block, part], (g, there)
        )

    def core_copy(block, offset, own=False):
        source = weight_ref if own else weights_ref.at[block, flip(d, offset)]
        return copy(
            source,
            weights_ref.at[block, flip(d, offset)],
            core_send.at[block, offset // 2],
            core_recv.at[block, offset // 2],
            (g, flip(d, 1)),
        )

    own_hidden = down_ref.shape[2]

    def swap_piece(owner, part, source_index):
        source = forward_ref.at[:, pl.ds(part * FF + owner * own_hidden, own_hidden)]
        if part == 2:
            return source, down_ref.at[source_index]
        return source, gate_ref.at[source_index, :, pl.ds(part * own_hidden, own_hidden)]

    def swap_copy(offset, part):
        source, target = swap_piece(flip(d, offset), part, d)
        return copy(
            source,
            target,
            swap_send.at[offset, part],
            swap_recv.at[offset, part],
            (g, flip(d, offset)),
        )

    locals_ = (
        pltpu.make_async_copy(weight_ref, weights_ref.at[g, d], local_sem.at[0]),
        pltpu.make_async_copy(own_rows, rows_ref.at[g], local_sem.at[1]),
        *(
            pltpu.make_async_copy(*swap_piece(d, part, d), local_sem.at[2 + part])
            for part in range(3)
        ),
    )

    def launch(block, own):
        for offset in near:
            near_copy(block, offset, own).start()
        core_copy(block, 0, own).start()

    def relay(block):
        for offset in near:
            near_copy(block, offset, False).wait_recv()
            core_copy(block, offset).start()
        if forward_halves:
            half_copy(block, 0).start()
            half_copy(block, 1).start()

    def finish(block):
        if forward_halves:
            half_copy(block, 0).wait_recv()
            half_copy(block, 1).wait_recv()
            core_copy(block, 6).start()

    def both(step, act):
        for way in (0, 1):
            pl.when(receives(way, step))(
                lambda way=way: act(g - step if way == 0 else g + step)
            )

    def take_rows(step):
        for way in (0, 1):

            @pl.when(receives(way, step))
            def _(way=way):
                line_rows(way, step).wait_recv()

            if step + 1 < lines:
                pl.when(sends(way, step + 1))(
                    lambda way=way: line_rows(way, step + 1).start()
                )

    for way in (0, 1):
        pl.when(sends(way, 1))(lambda way=way: line_weight(way, 1).start())
    launch(g, True)
    for one in locals_:
        one.start()
    for step in range(1, lines):
        for way in (0, 1):

            @pl.when(receives(way, step))
            def _(way=way, step=step):
                line_weight(way, step).wait_recv()

            if step + 1 < lines:
                pl.when(sends(way, step + 1))(
                    lambda way=way, step=step: line_weight(way, step + 1).start()
                )
            else:
                pl.when(sends(way, 1))(lambda way=way: line_rows(way, 1).start())

        both(step, lambda block: launch(block, False))
        if step == 1:
            relay(g)
            for offset in range(1, plane):
                for part in range(3):
                    swap_copy(offset, part).start()
    for step in range(1, lines):
        take_rows(step)
        both(step, relay)
        if step == 1:
            finish(g)
        else:
            both(step - 1, finish)
    both(lines - 1, finish)

    def drain(block):
        for offset in evens:
            core_copy(block, offset).wait()
        for offset in near:
            near_copy(block, offset, False).wait_send()
        if forward_halves:
            half_copy(block, 0).wait_send()
            half_copy(block, 1).wait_send()

    drain(g)
    for step in range(1, lines):
        for way in (0, 1):
            pl.when(receives(way, step))(
                lambda way=way, step=step: drain(g - step if way == 0 else g + step)
            )

            @pl.when(sends(way, step))
            def _(way=way, step=step):
                line_weight(way, step).wait_send()
                line_rows(way, step).wait_send()

    for offset in range(1, plane):
        for part in range(3):
            swap_copy(offset, part).wait()
    for one in locals_:
        one.wait()


def gather_start(weight, hidden, forward):
    lines, plane = lax.axis_size("grp"), lax.axis_size("dp")
    prompt_rows = PROMPT_LEN // lines
    own_rows, width = weight.shape
    anywhere = pl.BlockSpec(memory_space=pl.ANY)
    dma = pltpu.SemaphoreType.DMA
    near_count = 2 if plane == 8 else plane // 2 - 1
    pairs = (
        (2, lines),
        (2, lines),
        (2, lines),
        (2, lines),
        (lines, near_count),
        (lines, near_count),
        (lines, 2),
        (lines, 2),
        (lines, plane // 2),
        (lines, plane // 2),
        (plane, 3),
        (plane, 3),
    )
    own_hidden = FF // plane
    return pl.pallas_call(
        functools.partial(gather_kernel, lines, plane, prompt_rows),
        out_shape=(
            jax.ShapeDtypeStruct((lines, plane, own_rows, width), weight.dtype),
            jax.ShapeDtypeStruct((lines, prompt_rows, D), hidden.dtype),
            jax.ShapeDtypeStruct((plane, own_rows, 2 * own_hidden), forward.dtype),
            jax.ShapeDtypeStruct((plane, own_rows, own_hidden), forward.dtype),
        ),
        in_specs=[anywhere] * 3,
        out_specs=(anywhere,) * 4,
        scratch_shapes=[dma((5,))] + [dma(shape) for shape in pairs],
        compiler_params=pltpu.CompilerParams(collective_id=0, has_side_effects=True),
        name="gather_start",
    )(weight, hidden, forward)


def project_kernel(
    place_ref,
    group_ref,
    own_ref,
    gain_ref,
    cosine_ref,
    sine_ref,
    weight_ref,
    query_ref,
    pair_ref,
    normed_ref,
    own_normed_ref,
    scale_ref,
):
    step = pl.program_id(0)
    own_rows = own_ref.shape[0]
    prompt_rows = own_rows - CONT
    start = pl.multiple_of(place_ref[0] * prompt_rows, 16)
    tile = 32

    def norm_tile(values, at):
        values = values.astype(FULL)
        scale = lax.rsqrt(jnp.mean(values * values, axis=-1, keepdims=True) + EPS_NORM)
        normed_ref[pl.ds(at, tile)] = (values * scale * gain_ref[...]).astype(LOW)
        scale_ref[pl.ds(at, tile)] = jnp.broadcast_to(scale, (tile, 128))

    @pl.when(step == 0)
    def _():
        @pl.loop(0, PROMPT_LEN // tile)
        def _(at):
            first = pl.multiple_of(at * tile, tile)
            norm_tile(group_ref[pl.ds(first, tile)], first)

        for at in range(0, CONT, tile):
            norm_tile(own_ref[prompt_rows + at : prompt_rows + at + tile], PROMPT_LEN + at)
        own_normed_ref[:prompt_rows] = normed_ref[pl.ds(start, prompt_rows)]
        own_normed_ref[prompt_rows:] = normed_ref[PROMPT_LEN:]

    def turn(values, cosine, sine_part):
        front, back = values[:, : HD // 2], values[:, HD // 2 :]
        return front * cosine - back * sine_part, back * cosine + front * sine_part

    def project(rows):
        return jnp.dot(rows, weight_ref[...], preferred_element_type=FULL)

    @pl.when(step < HQ)
    def _():
        for first, count, table in ((0, prompt_rows, start), (prompt_rows, CONT, PROMPT_LEN)):
            values = project(own_normed_ref[first : first + count])
            front, back = turn(
                values, cosine_ref[pl.ds(table, count)], sine_ref[pl.ds(table, count)]
            )
            query_ref[first : first + count, : HD // 2] = front.astype(LOW)
            query_ref[first : first + count, HD // 2 :] = back.astype(LOW)

    key_count = PROMPT_LEN + CONT
    part = key_count // 4

    @pl.when((step >= HQ) & (step < HQ + HK))
    def _():
        @pl.loop(0, 4)
        def _(at):
            rows = pl.ds(pl.multiple_of(at * part, 16), part)
            front, back = turn(project(normed_ref[rows]), cosine_ref[rows], sine_ref[rows])
            pair_ref[rows, : HD // 2] = front.astype(LOW)
            pair_ref[rows, HD // 2 :] = back.astype(LOW)

    @pl.when(step >= HQ + HK)
    def _():
        @pl.loop(0, 4)
        def _(at):
            rows = pl.ds(pl.multiple_of(at * part, 16), part)
            pair_ref[rows] = project(normed_ref[rows]).astype(LOW)


VMEM_LIMIT = 60 * 2**20


def project_heads(place, group_rows, own_inputs, gain_row, cosine, sine_part, weights):
    own_rows = own_inputs.shape[0]
    key_count = PROMPT_LEN + CONT
    whole = lambda shape: pl.BlockSpec(shape, lambda j, p: (0, 0))
    return pl.pallas_call(
        project_kernel,
        grid_spec=pltpu.PrefetchScalarGridSpec(
            num_scalar_prefetch=1,
            grid=(HQ + 2 * HK,),
            in_specs=[
                whole((PROMPT_LEN, D)),
                whole((own_rows, D)),
                whole((1, D)),
                whole((key_count, HD // 2)),
                whole((key_count, HD // 2)),
                pl.BlockSpec((D, HD), lambda j, p: (0, j)),
            ],
            out_specs=[
                pl.BlockSpec((own_rows, HD), lambda j, p: (0, jnp.minimum(j, HQ - 1))),
                pl.BlockSpec((key_count, HD), lambda j, p: (0, jnp.maximum(j - HQ, 0))),
                whole((key_count, D)),
                whole((own_rows, D)),
                whole((key_count, 128)),
            ],
        ),
        out_shape=[
            jax.ShapeDtypeStruct((own_rows, HQ * HD), LOW),
            jax.ShapeDtypeStruct((key_count, 2 * HK * HD), LOW),
            jax.ShapeDtypeStruct((key_count, D), LOW),
            jax.ShapeDtypeStruct((own_rows, D), LOW),
            jax.ShapeDtypeStruct((key_count, 128), FULL),
        ],
        compiler_params=pltpu.CompilerParams(vmem_limit_bytes=VMEM_LIMIT),
        name="project_heads",
    )(place, group_rows, own_inputs, gain_row, cosine, sine_part, weights)


def across(left, right):
    return lax.dot_general(left, right, (((1,), (1,)), ((), ())), preferred_element_type=FULL)


def along(left, right):
    return lax.dot_general(left, right, (((0,), (0,)), ((), ())), preferred_element_type=FULL)


def attend_kernel(query_ref, key_ref, value_ref, seen_ref, attended_ref, logsum_ref):
    group_heads = HQ // HK
    for head in range(group_heads):
        columns = slice(head * HD, (head + 1) * HD)
        scores = across(query_ref[:, columns], key_ref[...]) * HD ** (-0.5)
        scores = jnp.where(seen_ref[...] > 0, scores, MASK_FILL)
        peak = jnp.max(scores, axis=-1, keepdims=True)
        unnormed = jnp.exp(scores - peak)
        total = jnp.sum(unnormed, axis=-1, keepdims=True)
        low = (unnormed / total).astype(LOW)
        attended_ref[:, columns] = jnp.dot(
            low, value_ref[...], preferred_element_type=FULL
        ).astype(LOW)
        logsum_ref[:, head * 128 : (head + 1) * 128] = jnp.broadcast_to(
            peak + jnp.log(total), (query_ref.shape[0], 128)
        )


def attend(queries, pairs, seen):
    rows, key_count = seen.shape
    group_heads = HQ // HK
    return pl.pallas_call(
        attend_kernel,
        grid=(HK,),
        in_specs=[
            pl.BlockSpec((rows, group_heads * HD), lambda j: (0, j)),
            pl.BlockSpec((key_count, HD), lambda j: (0, j)),
            pl.BlockSpec((key_count, HD), lambda j: (0, HK + j)),
            pl.BlockSpec((rows, key_count), lambda j: (0, 0)),
        ],
        out_specs=[
            pl.BlockSpec((rows, group_heads * HD), lambda j: (0, j)),
            pl.BlockSpec((rows, group_heads * 128), lambda j: (0, j)),
        ],
        out_shape=[
            jax.ShapeDtypeStruct((rows, HQ * HD), LOW),
            jax.ShapeDtypeStruct((rows, HQ * 128), FULL),
        ],
        compiler_params=pltpu.CompilerParams(vmem_limit_bytes=VMEM_LIMIT),
        name="attend",
    )(queries, pairs, pairs, seen)


def attend_back_kernel(
    place_ref,
    query_ref,
    key_ref,
    value_ref,
    seen_ref,
    logsum_ref,
    grad_ref,
    cosine_ref,
    sine_ref,
    query_out,
    pair_out,
):
    step = pl.program_id(0)
    group_heads = HQ // HK
    rows = query_ref.shape[0]
    prompt_rows = rows - CONT
    start = pl.multiple_of(place_ref[0] * prompt_rows, 16)
    score_scale = HD ** (-0.5)
    key_grad = value_grad = 0.0

    def turn_back(values, cosine, sine_part):
        front, back = values[:, : HD // 2], values[:, HD // 2 :]
        return jnp.concatenate(
            [front * cosine + back * sine_part, back * cosine - front * sine_part], axis=1
        ).astype(LOW)

    for head in range(group_heads):
        columns = slice(head * HD, (head + 1) * HD)
        scores = across(query_ref[:, columns], key_ref[...]) * score_scale
        scores = jnp.where(seen_ref[...] > 0, scores, MASK_FILL)
        probabilities = jnp.exp(scores - logsum_ref[:, head * 128 : head * 128 + 1])
        grads = grad_ref[:, columns]
        probability_grad = across(grads, value_ref[...])
        delta = jnp.sum(probabilities * probability_grad, axis=-1, keepdims=True)
        score_grad = (probabilities * (probability_grad - delta)).astype(LOW)
        query_grad = jnp.dot(score_grad, key_ref[...], preferred_element_type=FULL) * score_scale
        key_grad = key_grad + along(score_grad, query_ref[:, columns])
        value_grad = value_grad + along(probabilities.astype(LOW), grads)
        query_out[:prompt_rows, columns] = turn_back(
            query_grad[:prompt_rows],
            cosine_ref[pl.ds(start, prompt_rows)],
            sine_ref[pl.ds(start, prompt_rows)],
        )
        query_out[prompt_rows:, columns] = turn_back(
            query_grad[prompt_rows:], cosine_ref[PROMPT_LEN:], sine_ref[PROMPT_LEN:]
        )
    pair_out[:, pl.ds(pl.multiple_of(step * HD, HD), HD)] = turn_back(
        key_grad * score_scale, cosine_ref[...], sine_ref[...]
    )
    pair_out[:, pl.ds(pl.multiple_of((HK + step) * HD, HD), HD)] = value_grad.astype(LOW)


def attend_back(place, queries, pairs, seen, logsum, grads, cosine, sine_part):
    rows, key_count = seen.shape
    group_heads = HQ // HK
    whole = lambda shape: pl.BlockSpec(shape, lambda j, p: (0, 0))
    return pl.pallas_call(
        attend_back_kernel,
        grid_spec=pltpu.PrefetchScalarGridSpec(
            num_scalar_prefetch=1,
            grid=(HK,),
            in_specs=[
                pl.BlockSpec((rows, group_heads * HD), lambda j, p: (0, j)),
                pl.BlockSpec((key_count, HD), lambda j, p: (0, j)),
                pl.BlockSpec((key_count, HD), lambda j, p: (0, HK + j)),
                whole((rows, key_count)),
                pl.BlockSpec((rows, group_heads * 128), lambda j, p: (0, j)),
                pl.BlockSpec((rows, group_heads * HD), lambda j, p: (0, j)),
                whole((key_count, HD // 2)),
                whole((key_count, HD // 2)),
            ],
            out_specs=[
                pl.BlockSpec((rows, group_heads * HD), lambda j, p: (0, j)),
                whole((key_count, 2 * HK * HD)),
            ],
        ),
        out_shape=[
            jax.ShapeDtypeStruct((rows, HQ * HD), LOW),
            jax.ShapeDtypeStruct((key_count, 2 * HK * HD), LOW),
        ],
        compiler_params=pltpu.CompilerParams(vmem_limit_bytes=VMEM_LIMIT),
        name="attend_back",
    )(place, queries, pairs, pairs, seen, logsum, grads, cosine, sine_part)


def weights_back_kernel(
    place_ref,
    query_ref,
    pair_ref,
    branch_ref,
    attended_ref,
    normed_ref,
    own_normed_ref,
    group_ref,
    own_ref,
    scale_ref,
    query_weight_ref,
    pair_weight_ref,
    query_term,
    pair_term,
    merge_term,
    back_out,
    pair_back_out,
    gain_out,
):
    rows = query_ref.shape[0]
    prompt_rows = rows - CONT
    start = pl.multiple_of(place_ref[0] * prompt_rows, 16)
    query_term[...] = along(own_normed_ref[...], query_ref[...]).astype(LOW)
    pair_term[...] = along(normed_ref[...], pair_ref[...]).astype(LOW)
    merge_term[...] = along(branch_ref[...], attended_ref[...]).astype(LOW)
    query_back = across(query_ref[...], query_weight_ref[...])
    pair_back = across(pair_ref[...], pair_weight_ref[...])
    own_values = own_ref[prompt_rows:].astype(FULL) * scale_ref[PROMPT_LEN:, :1]
    tail = query_back[prompt_rows:] + pair_back[PROMPT_LEN:]
    group_values = group_ref[...].astype(FULL) * scale_ref[:PROMPT_LEN, :1]
    own_prompt = own_ref[:prompt_rows].astype(FULL) * scale_ref[pl.ds(start, prompt_rows), :1]
    gain_out[...] = (
        jnp.sum(pair_back[:PROMPT_LEN] * group_values, axis=0, keepdims=True)
        + jnp.sum(query_back[:prompt_rows] * own_prompt, axis=0, keepdims=True)
        + jnp.sum(tail * own_values, axis=0, keepdims=True)
    )
    back_out[:prompt_rows] = query_back[:prompt_rows]
    back_out[prompt_rows:] = tail
    pair_back_out[...] = pair_back[:PROMPT_LEN].astype(LOW)


def weights_back(
    place, queries, pairs, branch, attended, normed, own_normed, group_rows, own_inputs, scale, weights
):
    rows, key_count = queries.shape[0], pairs.shape[0]
    wide, tile = HQ * HD, 256
    whole = lambda shape: pl.BlockSpec(shape, lambda j, p: (0, 0))
    tall = lambda count: pl.BlockSpec((count, tile), lambda j, p: (0, j))
    flat = lambda at: pl.BlockSpec((tile, wide), lambda j, p: (j, at))
    return pl.pallas_call(
        weights_back_kernel,
        grid_spec=pltpu.PrefetchScalarGridSpec(
            num_scalar_prefetch=1,
            grid=(D // tile,),
            in_specs=[
                whole((rows, wide)),
                whole((key_count, wide)),
                tall(rows),
                whole((rows, wide)),
                tall(key_count),
                tall(rows),
                tall(PROMPT_LEN),
                tall(rows),
                whole((key_count, 128)),
                flat(0),
                flat(1),
            ],
            out_specs=[flat(0), flat(0), flat(0), tall(rows), tall(PROMPT_LEN), tall(1)],
        ),
        out_shape=[
            jax.ShapeDtypeStruct((D, wide), LOW),
            jax.ShapeDtypeStruct((D, wide), LOW),
            jax.ShapeDtypeStruct((D, wide), LOW),
            jax.ShapeDtypeStruct((rows, D), FULL),
            jax.ShapeDtypeStruct((PROMPT_LEN, D), LOW),
            jax.ShapeDtypeStruct((1, D), FULL),
        ],
        compiler_params=pltpu.CompilerParams(vmem_limit_bytes=VMEM_LIMIT),
        name="weights_back",
    )(
        place,
        queries,
        pairs,
        branch,
        attended,
        normed,
        own_normed,
        group_rows,
        own_inputs,
        scale,
        weights,
        weights,
    )


def plane_swap(block, offset):
    size = lax.axis_size("dp")
    return lax.ppermute(block, "dp", [(i, i ^ offset) for i in range(size)])


def plane_gather(block):
    mine = [block] + [plane_swap(block, o) for o in range(2, lax.axis_size("dp"), 2)]
    pairs = [(one, plane_swap(one, 1)) for one in mine]
    return jnp.concatenate([one for pair in pairs for one in pair], axis=0)


def plane_scatter(part_of):
    size = lax.axis_size("dp")
    sums = {}
    for offset in list(range(size - 2, 0, -2)) + [0]:
        arrived = plane_swap(part_of(offset + 1).astype(LOW), 1)
        sums[offset] = part_of(offset).astype(FULL) + arrived.astype(FULL)
        if offset:
            sums[offset] = plane_swap(sums[offset].astype(LOW), offset)
    total = sums[0]
    for offset in range(2, size, 2):
        total = total + sums[offset].astype(FULL)
    return total


def line_scatter(term):
    return lax.psum_scatter(term, "grp", scatter_dimension=0, tiled=True)


def finish_kernel(
    lines,
    plane,
    query_ref,
    pair_ref,
    merge_ref,
    gain_ref,
    gate_ref,
    up_ref,
    down_ref,
    a_master,
    a_first,
    a_second,
    m_master,
    m_first,
    m_second,
    f_master,
    f_first,
    f_second,
    a_grad,
    a_update,
    a_first_new,
    a_second_new,
    m_grad,
    m_update,
    m_first_new,
    m_second_new,
    gain_out,
    f_grad,
    f_update,
    f_first_new,
    f_second_new,
    mine,
    core_in,
    plane_in,
    line_in,
    swap_in,
    state,
    made,
    a_state,
    a_made,
    gain_made,
    mine_sem,
    core_send,
    core_recv,
    plane_send,
    plane_recv,
    line_send,
    line_recv,
    swap_send,
    swap_recv,
    own_sem,
    state_sem,
    made_sem,
    a_sem,
    gain_sem,
):
    g = lax.axis_index("grp")
    d = lax.axis_index("dp")
    chips = plane // 2
    chip, core = lax.div(d, 2), lax.rem(d, 2)
    partner = d + 1 - 2 * core
    rows = a_master.shape[0]
    own_hidden = gate_ref.shape[2]
    width = core_in.shape[3]
    a_width, m_width = a_master.shape[1], m_master.shape[1]
    parts, begin = [], 0
    for ref in (query_ref, pair_ref, merge_ref, gain_ref):
        parts.append((ref, pl.ds(begin, ref.shape[4])))
        begin += ref.shape[4]

    barrier = pltpu.get_barrier_semaphore()
    for step in range(1, plane):
        there = lax.rem(d + step, plane)
        pl.semaphore_signal(barrier, inc=1, device_id=(g, there), device_id_type=MESH)
    for step in range(1, lines):
        there = lax.rem(g + step, lines)
        pl.semaphore_signal(barrier, inc=1, device_id=(there, d), device_id_type=MESH)
    pl.semaphore_wait(barrier, plane + lines - 2)

    def line_at(turn):
        return lax.rem(g + turn + 1, lines)

    def core_copy(turn, part):
        line = line_at(turn)
        ref, columns = parts[part]
        return remote(
            ref.at[line, :, 1 - core],
            core_in.at[line, :, :, columns],
            core_send.at[turn, part],
            core_recv.at[turn, part],
            (g, partner),
        )

    def mine_copy(turn, part):
        line = line_at(turn)
        ref, columns = parts[part]
        return pltpu.make_async_copy(
            ref.at[line, :, core], mine.at[turn % 2, :, :, columns], mine_sem.at[turn, part]
        )

    cut = width // 256 * 128
    columns_of = (pl.ds(0, cut), pl.ds(cut, width - cut))

    def plane_copy(turn, step):
        line = line_at(turn)
        there = lax.rem(chip + step, chips)
        return remote(
            core_in.at[line, there],
            plane_in.at[line, chip],
            plane_send.at[turn, step],
            plane_recv.at[turn, step],
            (g, 2 * there + core),
        )

    def near_copy(turn, part, relayed):
        line = line_at(turn)
        there = flip(chip, part + 1)
        owner = flip(chip, 3) if relayed else there
        return remote(
            core_in.at[line, owner, :, columns_of[part]],
            plane_in.at[line, 1 if relayed else 0, :, columns_of[part]],
            plane_send.at[turn, 2 * relayed + part],
            plane_recv.at[turn, 2 * relayed + part],
            (g, 2 * there + core),
        )

    def relay_copy(turn, part):
        line = line_at(turn)
        there = flip(chip, 2 - part)
        return remote(
            core_in.at[line, there, :, columns_of[part]],
            plane_in.at[line, 2, :, columns_of[part]],
            plane_send.at[turn, 4 + part],
            plane_recv.at[turn, 4 + part],
            (g, 2 * there + core),
        )

    def line_copy(turn):
        line = line_at(turn)
        return remote(
            core_in.at[line, chip],
            line_in.at[g],
            line_send.at[turn],
            line_recv.at[turn],
            (line, d),
        )

    forward_refs = (gate_ref, up_ref, down_ref)

    def swap_copy(step, part):
        there = lax.rem(d + step, plane)
        return remote(
            forward_refs[part].at[there],
            swap_in.at[part, d],
            swap_send.at[step, part],
            swap_recv.at[step, part],
            (g, there),
        )

    own_swap = [
        pltpu.make_async_copy(forward_refs[part].at[d], swap_in.at[part, d], own_sem.at[part])
        for part in range(3)
    ]

    def f_columns(turn):
        block = lax.rem(d + lax.div(turn, 3), plane)
        return pl.ds(
            pl.multiple_of(lax.rem(turn, 3) * FF + block * own_hidden, own_hidden), own_hidden
        )

    def state_copy(turn, which):
        slot = lax.rem(turn, 2)
        return pltpu.make_async_copy(
            (f_master, f_first, f_second)[which].at[:, f_columns(turn)],
            state.at[slot, which],
            state_sem.at[slot, which],
        )

    def made_copy(turn, which):
        slot = lax.rem(turn, 2)
        return pltpu.make_async_copy(
            made.at[slot, which],
            (f_grad, f_update, f_first_new, f_second_new)[which].at[:, f_columns(turn)],
            made_sem.at[slot, which],
        )

    slabs = (pl.ds(0, a_width), pl.ds(a_width, m_width))

    def a_state_copy(which, slab):
        source = ((a_master, a_first, a_second), (m_master, m_first, m_second))[slab][which]
        return pltpu.make_async_copy(
            source, a_state.at[which, :, slabs[slab]], a_sem.at[slab, which]
        )

    def a_made_copy(which, slab):
        target = (
            (a_grad, a_update, a_first_new, a_second_new),
            (m_grad, m_update, m_first_new, m_second_new),
        )[slab][which]
        return pltpu.make_async_copy(
            a_made.at[which, :, slabs[slab]], target, a_sem.at[slab, 3 + which]
        )

    every = range(len(parts))
    for turn in range(lines):
        for part in every:
            core_copy(turn, part).start()
            if turn < 2:
                mine_copy(turn, part).start()
    for step in range(1, plane):
        for part in range(3):
            swap_copy(step, part).start()
    for one in own_swap:
        one.start()
    for which in range(3):
        state_copy(0, which).start()
        for slab in range(2):
            a_state_copy(which, slab).start()

    tile = 896 if width % 896 == 0 else 128
    halves = plane == 8

    def add_into(line, there, other, columns=None):
        first, count = (0, width) if columns is None else columns
        step = tile if columns is None else 128

        @pl.loop(0, count // step)
        def _(at):
            here = pl.ds(pl.multiple_of(first + at * step, 128), step)
            total = core_in[line, there, :, here].astype(FULL) + other(here).astype(FULL)
            core_in[line, there, :, here] = total.astype(LOW)

    for turn in range(lines):
        line = line_at(turn)
        for part in every:
            core_copy(turn, part).wait_recv()
            mine_copy(turn, part).wait()
        order = (3, 1, 2, 0) if halves else tuple(range(1, chips + 1))
        for step in order:
            there = flip(chip, step) if halves else lax.rem(chip + step, chips)
            add_into(
                line, there, lambda here, there=there, turn=turn: mine[turn % 2, there, :, here]
            )
            if halves and step == 3:
                for part in range(2):
                    near_copy(turn, part, True).start()
            elif halves and step:
                near_copy(turn, step - 1, False).start()
            elif not halves and step < chips:
                plane_copy(turn, step).start()
        if turn + 2 < lines:
            for part in every:
                mine_copy(turn + 2, part).start()

    def pass_on(turn):
        line = line_at(turn)
        for part, columns in enumerate(((0, cut), (cut, width - cut))):
            near_copy(turn, part, True).wait_recv()
            add_into(
                line,
                flip(chip, 2 - part),
                lambda here, line=line: plane_in[line, 1, :, here],
                columns,
            )
            relay_copy(turn, part).start()

    def forward_turn(turn):
        slot = lax.rem(turn, 2)
        block = lax.rem(d + lax.div(turn, 3), plane)
        part = lax.rem(turn, 3)

        @pl.when(turn + 1 < 3 * plane)
        def _():
            for which in range(3):
                state_copy(turn + 1, which).start()

        @pl.when(turn > 1)
        def _():
            for which in range(4):
                made_copy(turn - 2, which).wait()

        for which in range(3):
            state_copy(turn, which).wait()

        @pl.loop(0, rows // 16)
        def _(at):
            rows_at = pl.ds(pl.multiple_of(at * 16, 16), 16)
            gradient = swap_in[part, block, rows_at].astype(FULL)
            update, first_new, second_new = adam_step(
                state[slot, 0, rows_at],
                state[slot, 1, rows_at],
                state[slot, 2, rows_at],
                gradient,
                WEIGHT_DECAY,
            )
            made[slot, 0, rows_at] = gradient
            made[slot, 1, rows_at] = update
            made[slot, 2, rows_at] = first_new
            made[slot, 3, rows_at] = second_new

        for which in range(4):
            made_copy(turn, which).start()

    if halves:
        pass_on(0)
    for one in own_swap:
        one.wait()
    for step in range(1, plane):
        for part in range(3):
            swap_copy(step, part).wait_recv()
    each = 3 * plane // lines
    for turn in range(lines):
        lax.fori_loop(turn * each, (turn + 1) * each, lambda k, c: (forward_turn(k), c)[1], 0)
        line = line_at(turn)
        if halves:
            if turn + 1 < lines:
                pass_on(turn + 1)
            for part in range(2):
                near_copy(turn, part, False).wait_recv()
                relay_copy(turn, part).wait_recv()
            arrived = (0, 2)
        else:
            for step in range(1, chips):
                plane_copy(turn, step).wait_recv()
            arrived = tuple(lax.rem(chip + step, chips) for step in range(1, chips))

        @pl.loop(0, width // tile)
        def _(at, line=line, arrived=arrived):
            columns = pl.ds(pl.multiple_of(at * tile, tile), tile)
            total = core_in[line, chip, :, columns].astype(FULL)
            for block in arrived:
                total = total + plane_in[line, block, :, columns].astype(FULL)
            core_in[line, chip, :, columns] = total.astype(LOW)

        if turn < lines - 1:
            line_copy(turn).start()

    for which in range(4):
        for turn in (3 * plane - 2, 3 * plane - 1):
            made_copy(turn, which).wait()
    for turn in range(lines - 1):
        line_copy(turn).wait_recv()
    for which in range(3):
        for slab in range(2):
            a_state_copy(which, slab).wait()

    def owned(columns):
        total = core_in[g, chip, :, columns].astype(FULL)
        for step in range(1, lines):
            total = total + line_in[lax.rem(g + step, lines), :, columns].astype(FULL)
        return total

    @pl.loop(0, (a_width + m_width) // 256)
    def _(at):
        columns = pl.ds(pl.multiple_of(at * 256, 256), 256)
        gradient = owned(columns)
        update, first_new, second_new = adam_step(
            a_state[0, :, columns],
            a_state[1, :, columns],
            a_state[2, :, columns],
            gradient,
            WEIGHT_DECAY,
        )
        a_made[0, :, columns] = gradient
        a_made[1, :, columns] = update
        a_made[2, :, columns] = first_new
        a_made[3, :, columns] = second_new

    for which in range(4):
        for slab in range(2):
            a_made_copy(which, slab).start()
    gain_made[...] = owned(pl.ds(a_width + m_width, GAIN_PAD))
    gain_copy = pltpu.make_async_copy(gain_made, gain_out, gain_sem.at[0])
    gain_copy.start()
    for turn in range(lines):
        for part in every:
            core_copy(turn, part).wait_send()
        if halves:
            for part in range(2):
                near_copy(turn, part, False).wait_send()
                near_copy(turn, part, True).wait_send()
                relay_copy(turn, part).wait_send()
        else:
            for step in range(1, chips):
                plane_copy(turn, step).wait_send()
        if turn < lines - 1:
            line_copy(turn).wait_send()
    for step in range(1, plane):
        for part in range(3):
            swap_copy(step, part).wait_send()
    for which in range(4):
        for slab in range(2):
            a_made_copy(which, slab).wait()
    gain_copy.wait()


def finish(terms, forward_parts, attention, merge, forward):
    lines, plane = lax.axis_size("grp"), lax.axis_size("dp")
    chips = plane // 2
    rows, a_width = attention[0].shape
    m_width = merge[0].shape[1]
    own_hidden = forward_parts[0].shape[1]
    width = a_width + m_width + GAIN_PAD
    anywhere = pl.BlockSpec(memory_space=pl.ANY)
    dma = pltpu.SemaphoreType.DMA
    vmem = pltpu.VMEM

    def like(array):
        return jax.ShapeDtypeStruct(array.shape, array.dtype)

    return pl.pallas_call(
        functools.partial(finish_kernel, lines, plane),
        out_shape=(like(attention[0]),) * 4
        + (like(merge[0]),) * 4
        + (jax.ShapeDtypeStruct((rows, GAIN_PAD), FULL),)
        + (like(forward[0]),) * 4,
        in_specs=[anywhere] * 16,
        out_specs=(anywhere,) * 13,
        scratch_shapes=[
            vmem((2, chips, rows, width), LOW),
            vmem((lines, chips, rows, width), LOW),
            vmem((lines, 3 if plane == 8 else chips, rows, width), LOW),
            vmem((lines, rows, width), LOW),
            vmem((3, plane, rows, own_hidden), LOW),
            vmem((2, 3, rows, own_hidden), FULL),
            vmem((2, 4, rows, own_hidden), FULL),
            vmem((3, rows, a_width + m_width), FULL),
            vmem((4, rows, a_width + m_width), FULL),
            vmem((rows, GAIN_PAD), FULL),
            dma((lines, 4)),
            dma((lines, 4)),
            dma((lines, 4)),
            dma((lines, max(6, chips))),
            dma((lines, max(6, chips))),
            dma((lines,)),
            dma((lines,)),
            dma((plane, 3)),
            dma((plane, 3)),
            dma((3,)),
            dma((2, 3)),
            dma((2, 4)),
            dma((2, 7)),
            dma((1,)),
        ],
        compiler_params=pltpu.CompilerParams(
            collective_id=1, has_side_effects=True, vmem_limit_bytes=VMEM_LIMIT
        ),
        name="finish",
    )(
        *(term.reshape(lines, chips, 2, rows, term.shape[1]) for term in terms),
        *(part.reshape(plane, rows, -1) for part in forward_parts),
        *attention,
        *merge,
        *forward,
    )


def body(
    hidden,
    cotangent,
    segment_ids,
    continuation_prompt,
    gain_master,
    gain_first,
    gain_second,
    attention_master,
    attention_first,
    attention_second,
    merge_master,
    merge_first,
    merge_second,
    feedforward_master,
    feedforward_first,
    feedforward_second,
):
    group_index = lax.axis_index("grp")
    dp_size = lax.axis_size("dp")
    row_count = hidden.shape[2]
    prompt_rows = row_count - CONT
    qkv_width = (HQ + 2 * HK) * HD
    own_rows = feedforward_master.shape[0]
    own_hidden = FF // dp_size
    own_inputs = hidden.reshape(row_count, D)

    gain_columns = jnp.pad(gain_master.T, ((0, 0), (0, GAIN_PAD - 2)))
    weight_low = jnp.concatenate(
        [attention_master.astype(LOW), merge_master.astype(LOW), gain_columns.astype(LOW)], axis=1
    )
    weights, group_rows, gate_rows, down_rows = gather_start(
        weight_low, own_inputs, feedforward_master.astype(LOW)
    )
    weights, late_cotangent = lax.optimization_barrier((weights, cotangent))
    weights = weights.reshape(D, -1)
    merge_weight = weights[:, qkv_width : qkv_width + D]
    gain_float = weights[:, qkv_width + D : qkv_width + D + 2].astype(FULL).T
    gate_weight = lax.all_gather(
        gate_rows.reshape(dp_size * own_rows, 2 * own_hidden), "grp", axis=0, tiled=True
    )
    gate_weight, down_rows = lax.optimization_barrier((gate_weight, down_rows))
    down_weight = lax.all_gather(
        down_rows.reshape(dp_size * own_rows, own_hidden), "grp", axis=0, tiled=True
    )
    down_grad = plane_gather(late_cotangent.reshape(row_count, D))

    segment_row = segment_ids[0]
    source_row = continuation_prompt[0]
    prompt_positions, follow_positions = segment_positions(segment_row, source_row)
    cosine, sine_part = angle_table(jnp.concatenate([prompt_positions, follow_positions[0]]))

    place = jnp.reshape(group_index, (1,)).astype(jnp.int32)
    group_rows = group_rows.reshape(PROMPT_LEN, D)
    queries, pairs, key_normed, normed, key_scale = project_heads(
        place, group_rows, own_inputs, gain_float[:1], cosine, sine_part, weights
    )
    inputs = own_inputs.astype(FULL)
    first_scale = norm_scale(inputs)

    row_index = jnp.arange(row_count, dtype=jnp.int32)
    is_prompt = row_index < prompt_rows
    global_row = group_index * prompt_rows + jnp.minimum(row_index, prompt_rows - 1)
    own_segment = lax.dynamic_slice_in_dim(segment_row, group_index * prompt_rows, prompt_rows)
    query_segment = jnp.concatenate([own_segment, jnp.broadcast_to(source_row, (CONT,))])
    key_index = jnp.arange(PROMPT_LEN, dtype=jnp.int32)
    prompt_seen = (segment_row[None, :] == query_segment[:, None]) & (
        (key_index[None, :] <= global_row[:, None]) | ~is_prompt[:, None]
    )
    follow_seen = (~is_prompt)[:, None] & (
        jnp.arange(CONT, dtype=jnp.int32)[None, :] <= (row_index - prompt_rows)[:, None]
    )
    visible = jnp.concatenate([prompt_seen, follow_seen], axis=1)
    seen = visible.astype(FULL)
    attended, row_logsum = attend(queries, pairs, seen)
    middle = inputs + contract(attended, merge_weight, 1, 1)
    second_scale = norm_scale(middle)
    normed_two = (middle * second_scale * gain_float[1]).astype(LOW)
    grad_rows = cotangent.reshape(row_count, D).astype(FULL)

    def by_offset(left, right, right_axis, after=None):
        chunks = {}
        for offset in list(range(2, dp_size, 2)) + [0]:
            rows = left[offset * row_count : (offset + 2) * row_count]
            if offset == 0 and after is not None:
                rows, _ = lax.optimization_barrier((rows, after))
            chunks[offset] = contract(rows, right, 1, right_axis).astype(LOW)
        return lambda offset: chunks[offset - offset % 2][
            (offset % 2) * row_count : (offset % 2 + 1) * row_count
        ]

    normed_two, down_grad = lax.optimization_barrier((normed_two, down_grad))
    normed_all = plane_gather(normed_two)
    gate_up = jnp.dot(normed_all, gate_weight, preferred_element_type=FULL)
    gate_values = gate_up[:, :own_hidden]
    up_values = gate_up[:, own_hidden:]
    gate_sigmoid, gate_silu, activated = gate_parts(gate_values, up_values)
    down_term = contract(down_grad, activated, 0, 0).astype(LOW)
    down_term, down_weight = lax.optimization_barrier((down_term, down_weight))
    out_parts = by_offset(activated, down_weight, 1)
    out_chunks = [out_parts(offset) for offset in range(dp_size)]
    out_chunks, down_grad = lax.optimization_barrier((out_chunks, down_grad))
    out_swapped = [plane_swap(out_chunks[offset + 1], 1) for offset in range(0, dp_size, 2)]
    activated_grad = contract(down_grad, down_weight, 1, 0)
    gate_grad, up_grad = gate_backward(
        activated_grad, gate_values, up_values, gate_sigmoid, gate_silu
    )
    gate_up_grad = jnp.concatenate([gate_grad, up_grad], axis=1)

    gate_up_grad, out_swapped = lax.optimization_barrier((gate_up_grad, out_swapped))
    out_sums = [
        out_chunks[2 * at].astype(FULL) + one.astype(FULL) for at, one in enumerate(out_swapped)
    ]
    out_arrived = [plane_swap(one.astype(LOW), 2 * at) for at, one in enumerate(out_sums) if at]
    down_part = line_scatter(down_term)
    back_parts = by_offset(gate_up_grad, gate_weight, 1, down_part)
    normed_two_grad = plane_scatter(back_parts)
    gate_term = contract(normed_all, gate_up_grad[:, :own_hidden], 0, 0).astype(LOW)
    normed_all, out_arrived = lax.optimization_barrier((normed_all, out_arrived))
    up_term = contract(normed_all, gate_up_grad[:, own_hidden:], 0, 0).astype(LOW)
    gate_part = line_scatter(gate_term)
    normed_two_grad, gate_term, up_term = lax.optimization_barrier(
        (normed_two_grad, gate_term, up_term)
    )
    result = middle + out_sums[0]
    for one in out_arrived:
        result = result + one.astype(FULL)
    block_output = result.astype(LOW).reshape(hidden.shape)
    middle_grad = grad_rows + norm_back(middle, second_scale, gain_float[1], normed_two_grad)
    gain_two_part = jnp.sum(normed_two_grad * middle * second_scale, axis=0)
    branch_grad = middle_grad.astype(LOW)
    attended_grad = contract(branch_grad, merge_weight, 1, 0).astype(LOW)
    attended_grad, gate_part = lax.optimization_barrier((attended_grad, gate_part))
    up_part = line_scatter(up_term)
    query_project, pair_project = attend_back(
        place, queries, pairs, seen, row_logsum, attended_grad, cosine, sine_part
    )
    query_term, pair_term, merge_term, normed_grad, pair_back, gain_one_part = weights_back(
        place,
        query_project,
        pair_project,
        branch_grad,
        attended,
        key_normed,
        normed,
        group_rows,
        own_inputs,
        key_scale,
        weights,
    )
    gain_term = jnp.pad(
        jnp.stack([gain_one_part[0], gain_two_part], axis=1), ((0, 0), (0, GAIN_PAD - 2))
    )
    pair_back, up_part = lax.optimization_barrier((pair_back, up_part))
    pair_sum = line_scatter(pair_back)
    finished = finish(
        (query_term, pair_term, merge_term, gain_term.astype(LOW)),
        (gate_part, up_part, down_part),
        (attention_master, attention_first, attention_second),
        (merge_master, merge_first, merge_second),
        (feedforward_master, feedforward_first, feedforward_second),
    )
    gain_grad = finished[8][:, :2].T
    pair_sum, gain_grad = lax.optimization_barrier((pair_sum, gain_grad))
    pair_sum = pair_sum.astype(FULL)
    normed_grad = normed_grad + jnp.pad(pair_sum, ((0, CONT), (0, 0)))
    input_grad = (middle_grad + norm_back(inputs, first_scale, gain_float[0], normed_grad)).reshape(
        hidden.shape
    )
    gain_new = adam_step(gain_master, gain_first, gain_second, gain_grad, 0.0)
    return (
        block_output,
        input_grad,
        gain_grad,
        *gain_new,
        *finished[:8],
        *finished[9:],
    )


def solution(mesh):
    tokens = P("dp", "grp", None, None)
    gains = P(None, ("grp", "dp"))
    matrix = P(("grp", "dp"), None)
    return jax.shard_map(
        body,
        mesh=mesh,
        in_specs=(tokens, tokens, P("dp", None), P("dp", "grp")) + (gains,) * 3 + (matrix,) * 9,
        out_specs=(tokens, tokens) + (gains,) * 4 + (matrix,) * 12,
        check_vma=False,
    )
```

```python
import functools

import jax
import jax.numpy as jnp
from jax import lax
from jax.experimental import pallas as pl
from jax.experimental.pallas import tpu as pltpu
from jax.sharding import PartitionSpec as P

D = 2048
FF = 8192
HQ = 8
HK = 4
HD = 256
PROMPT_LEN = 1024
PROMPTS = 4
CONT = 64
STEP = 10
GAIN_PAD = 128

EPS_NORM = 1e-06
ROPE_THETA = 1000042.0
MASK_FILL = -1e30
BETA_ONE = 0.9
BETA_TWO = 0.95
ADAM_EPS = 1e-08
LEARN_RATE = 0.02
WEIGHT_DECAY = 0.1
LOW = jnp.bfloat16
FULL = jnp.float32
MESH = pl.DeviceIdType.MESH


def contract(left, right, left_axis, right_axis):
    return lax.dot_general(
        left, right, (((left_axis,), (right_axis,)), ((), ())), preferred_element_type=FULL
    )


def angle_table(positions):
    inverse_rate = ROPE_THETA ** (-(jnp.arange(HD // 2, dtype=FULL) * 2.0) / HD)
    angles = positions.astype(FULL)[..., None] * inverse_rate
    return (jnp.cos(angles), jnp.sin(angles))


def segment_positions(segment_row, source_row):
    labels = jnp.arange(PROMPTS, dtype=jnp.int32)
    member = (segment_row[None, :] == labels[:, None]).astype(jnp.int32)
    lengths = jnp.sum(member, axis=1, dtype=jnp.int32)
    starts = jnp.sum(
        jnp.where(labels[None, :] < labels[:, None], lengths[None, :], 0), axis=1, dtype=jnp.int32
    )
    prompt_index = jnp.arange(segment_row.shape[0], dtype=jnp.int32)
    prompt_positions = prompt_index - jnp.sum(member * starts[:, None], axis=0, dtype=jnp.int32)
    source_length = jnp.sum(
        (source_row[:, None] == labels[None, :]).astype(jnp.int32) * lengths[None, :],
        axis=1,
        dtype=jnp.int32,
    )
    follow_positions = source_length[:, None] + jnp.arange(CONT, dtype=jnp.int32)[None, :]
    return (prompt_positions, follow_positions)


def norm_scale(values):
    return lax.rsqrt(jnp.mean(values * values, axis=-1, keepdims=True) + EPS_NORM)


def norm_back(values, row_scale, gain_row, normed_grad):
    scaled = normed_grad * gain_row
    return row_scale * scaled - values * row_scale**3 * jnp.mean(
        scaled * values, axis=-1, keepdims=True
    )


def adam_step(master, first_moment, second_moment, gradient, decay_rate):
    first_new = BETA_ONE * first_moment + (1.0 - BETA_ONE) * gradient
    second_new = BETA_TWO * second_moment + (1.0 - BETA_TWO) * gradient * gradient
    correct_one = 1.0 - BETA_ONE**STEP
    correct_two = 1.0 - BETA_TWO**STEP
    update = first_new / correct_one / (jnp.sqrt(second_new / correct_two) + ADAM_EPS)
    return (-LEARN_RATE * (update + decay_rate * master), first_new, second_new)


def gate_parts(gate_values, up_values):
    gate_sigmoid = jax.nn.sigmoid(gate_values)
    gate_silu = gate_values * gate_sigmoid
    return (gate_sigmoid, gate_silu, (gate_silu * up_values).astype(LOW))


def gate_backward(activated_grad, gate_values, up_values, gate_sigmoid, gate_silu):
    gate_grad = (
        activated_grad * up_values * gate_sigmoid * (1.0 + gate_values * (1.0 - gate_sigmoid))
    ).astype(LOW)
    up_grad = (activated_grad * gate_silu).astype(LOW)
    return (gate_grad, up_grad)


def flip(index, bits):
    bit = 1
    while bit <= bits:
        if bits & bit:
            index = index + bit - 2 * bit * lax.rem(index // bit, 2)
        bit *= 2
    return index


def remote(source, target, send, recv, there):
    return pltpu.make_async_remote_copy(
        src_ref=source,
        dst_ref=target,
        send_sem=send,
        recv_sem=recv,
        device_id=there,
        device_id_type=MESH,
    )


def gather_kernel(
    lines,
    plane,
    prompt_rows,
    weight_ref,
    hidden_ref,
    forward_ref,
    weights_ref,
    rows_ref,
    gate_ref,
    down_ref,
    local_sem,
    line_send,
    line_recv,
    rows_send,
    rows_recv,
    near_send,
    near_recv,
    half_send,
    half_recv,
    core_send,
    core_recv,
    swap_send,
    swap_recv,
):
    g = lax.axis_index("grp")
    d = lax.axis_index("dp")
    evens = range(0, plane, 2)
    forward_halves = plane == 8
    near = (2, 4) if forward_halves else tuple(evens[1:])
    width = weight_ref.shape[1]
    cut = (width // 256) * 128

    barrier = pltpu.get_barrier_semaphore()
    for offset in range(1, plane):
        pl.semaphore_signal(barrier, inc=1, device_id=(g, flip(d, offset)), device_id_type=MESH)

    for step in range(1, lines):
        there = lax.rem(g + step, lines)
        pl.semaphore_signal(barrier, inc=1, device_id=(there, d), device_id_type=MESH)
    pl.semaphore_wait(barrier, plane + lines - 2)

    copy = remote
    own_rows = hidden_ref.at[pl.ds(0, prompt_rows)]

    def line_weight(way, step):
        block = g - step + 1 if way == 0 else g + step - 1
        source = weight_ref if step == 1 else weights_ref.at[block, d]
        return copy(
            source,
            weights_ref.at[block, d],
            line_send.at[way, step],
            line_recv.at[way, step],
            (g + 1 if way == 0 else g - 1, d),
        )

    def line_rows(way, step):
        block = g - step + 1 if way == 0 else g + step - 1
        source = own_rows if step == 1 else rows_ref.at[block]
        return copy(
            source,
            rows_ref.at[block],
            rows_send.at[way, step],
            rows_recv.at[way, step],
            (g + 1 if way == 0 else g - 1, d),
        )

    def sends(way, step):
        if way == 0:
            return (g < lines - 1) & (g >= step - 1)
        return (g > 0) & (g + step - 1 < lines)

    def receives(way, step):
        return g >= step if way == 0 else g + step < lines

    def near_copy(block, offset, own):
        source = weight_ref if own else weights_ref.at[block, d]
        at = near.index(offset)
        return copy(
            source,
            weights_ref.at[block, d],
            near_send.at[block, at],
            near_recv.at[block, at],
            (g, flip(d, offset)),
        )

    def half_copy(block, part):
        columns = pl.ds(0, cut) if part == 0 else pl.ds(cut, width - cut)
        origin = flip(d, 2) if part == 0 else flip(d, 4)
        there = flip(d, 4) if part == 0 else flip(d, 2)
        piece = weights_ref.at[block, origin, :, columns]
        return copy(
            piece, piece, half_send.at[block, part], half_recv.at[block, part], (g, there)
        )

    def core_copy(block, offset, own=False):
        source = weight_ref if own else weights_ref.at[block, flip(d, offset)]
        return copy(
            source,
            weights_ref.at[block, flip(d, offset)],
            core_send.at[block, offset // 2],
            core_recv.at[block, offset // 2],
            (g, flip(d, 1)),
        )

    own_hidden = down_ref.shape[2]

    def swap_piece(owner, part, source_index):
        source = forward_ref.at[:, pl.ds(part * FF + owner * own_hidden, own_hidden)]
        if part == 2:
            return source, down_ref.at[source_index]
        return source, gate_ref.at[source_index, :, pl.ds(part * own_hidden, own_hidden)]

    def swap_copy(offset, part):
        source, target = swap_piece(flip(d, offset), part, d)
        return copy(
            source,
            target,
            swap_send.at[offset, part],
            swap_recv.at[offset, part],
            (g, flip(d, offset)),
        )

    locals_ = (
        pltpu.make_async_copy(weight_ref, weights_ref.at[g, d], local_sem.at[0]),
        pltpu.make_async_copy(own_rows, rows_ref.at[g], local_sem.at[1]),
        *(
            pltpu.make_async_copy(*swap_piece(d, part, d), local_sem.at[2 + part])
            for part in range(3)
        ),
    )

    def launch(block, own):
        for offset in near:
            near_copy(block, offset, own).start()
        core_copy(block, 0, own).start()

    def relay(block):
        for offset in near:
            near_copy(block, offset, False).wait_recv()
            core_copy(block, offset).start()
        if forward_halves:
            half_copy(block, 0).start()
            half_copy(block, 1).start()

    def finish(block):
        if forward_halves:
            half_copy(block, 0).wait_recv()
            half_copy(block, 1).wait_recv()
            core_copy(block, 6).start()

    def both(step, act):
        for way in (0, 1):
            pl.when(receives(way, step))(
                lambda way=way: act(g - step if way == 0 else g + step)
            )

    def take_rows(step):
        for way in (0, 1):

            @pl.when(receives(way, step))
            def _(way=way):
                line_rows(way, step).wait_recv()

            if step + 1 < lines:
                pl.when(sends(way, step + 1))(
                    lambda way=way: line_rows(way, step + 1).start()
                )

    for way in (0, 1):
        pl.when(sends(way, 1))(lambda way=way: line_weight(way, 1).start())
    launch(g, True)
    for one in locals_:
        one.start()
    for step in range(1, lines):
        for way in (0, 1):

            @pl.when(receives(way, step))
            def _(way=way, step=step):
                line_weight(way, step).wait_recv()

            if step + 1 < lines:
                pl.when(sends(way, step + 1))(
                    lambda way=way, step=step: line_weight(way, step + 1).start()
                )
            else:
                pl.when(sends(way, 1))(lambda way=way: line_rows(way, 1).start())

        both(step, lambda block: launch(block, False))
        if step == 1:
            relay(g)
            for offset in range(1, plane):
                for part in range(3):
                    swap_copy(offset, part).start()
    for step in range(1, lines):
        take_rows(step)
        both(step, relay)
        if step == 1:
            finish(g)
        else:
            both(step - 1, finish)
    both(lines - 1, finish)

    def drain(block):
        for offset in evens:
            core_copy(block, offset).wait()
        for offset in near:
            near_copy(block, offset, False).wait_send()
        if forward_halves:
            half_copy(block, 0).wait_send()
            half_copy(block, 1).wait_send()

    drain(g)
    for step in range(1, lines):
        for way in (0, 1):
            pl.when(receives(way, step))(
                lambda way=way, step=step: drain(g - step if way == 0 else g + step)
            )

            @pl.when(sends(way, step))
            def _(way=way, step=step):
                line_weight(way, step).wait_send()
                line_rows(way, step).wait_send()

    for offset in range(1, plane):
        for part in range(3):
            swap_copy(offset, part).wait()
    for one in locals_:
        one.wait()


def gather_start(weight, hidden, forward):
    lines, plane = lax.axis_size("grp"), lax.axis_size("dp")
    prompt_rows = PROMPT_LEN // lines
    own_rows, width = weight.shape
    anywhere = pl.BlockSpec(memory_space=pl.ANY)
    dma = pltpu.SemaphoreType.DMA
    near_count = 2 if plane == 8 else plane // 2 - 1
    pairs = (
        (2, lines),
        (2, lines),
        (2, lines),
        (2, lines),
        (lines, near_count),
        (lines, near_count),
        (lines, 2),
        (lines, 2),
        (lines, plane // 2),
        (lines, plane // 2),
        (plane, 3),
        (plane, 3),
    )
    own_hidden = FF // plane
    return pl.pallas_call(
        functools.partial(gather_kernel, lines, plane, prompt_rows),
        out_shape=(
            jax.ShapeDtypeStruct((lines, plane, own_rows, width), weight.dtype),
            jax.ShapeDtypeStruct((lines, prompt_rows, D), hidden.dtype),
            jax.ShapeDtypeStruct((plane, own_rows, 2 * own_hidden), forward.dtype),
            jax.ShapeDtypeStruct((plane, own_rows, own_hidden), forward.dtype),
        ),
        in_specs=[anywhere] * 3,
        out_specs=(anywhere,) * 4,
        scratch_shapes=[dma((5,))] + [dma(shape) for shape in pairs],
        compiler_params=pltpu.CompilerParams(collective_id=0, has_side_effects=True),
        name="gather_start",
    )(weight, hidden, forward)


def project_kernel(
    place_ref,
    group_ref,
    own_ref,
    gain_ref,
    cosine_ref,
    sine_ref,
    weight_ref,
    query_ref,
    pair_ref,
    normed_ref,
    own_normed_ref,
    scale_ref,
):
    step = pl.program_id(0)
    own_rows = own_ref.shape[0]
    prompt_rows = own_rows - CONT
    start = pl.multiple_of(place_ref[0] * prompt_rows, 16)
    tile = 32

    def norm_tile(values, at):
        values = values.astype(FULL)
        scale = lax.rsqrt(jnp.mean(values * values, axis=-1, keepdims=True) + EPS_NORM)
        normed_ref[pl.ds(at, tile)] = (values * scale * gain_ref[...]).astype(LOW)
        scale_ref[pl.ds(at, tile)] = jnp.broadcast_to(scale, (tile, 128))

    @pl.when(step == 0)
    def _():
        @pl.loop(0, PROMPT_LEN // tile)
        def _(at):
            first = pl.multiple_of(at * tile, tile)
            norm_tile(group_ref[pl.ds(first, tile)], first)

        for at in range(0, CONT, tile):
            norm_tile(own_ref[prompt_rows + at : prompt_rows + at + tile], PROMPT_LEN + at)
        own_normed_ref[:prompt_rows] = normed_ref[pl.ds(start, prompt_rows)]
        own_normed_ref[prompt_rows:] = normed_ref[PROMPT_LEN:]

    def turn(values, cosine, sine_part):
        front, back = values[:, : HD // 2], values[:, HD // 2 :]
        return front * cosine - back * sine_part, back * cosine + front * sine_part

    def project(rows):
        return jnp.dot(rows, weight_ref[...], preferred_element_type=FULL)

    @pl.when(step < HQ)
    def _():
        for first, count, table in ((0, prompt_rows, start), (prompt_rows, CONT, PROMPT_LEN)):
            values = project(own_normed_ref[first : first + count])
            front, back = turn(
                values, cosine_ref[pl.ds(table, count)], sine_ref[pl.ds(table, count)]
            )
            query_ref[first : first + count, : HD // 2] = front.astype(LOW)
            query_ref[first : first + count, HD // 2 :] = back.astype(LOW)

    key_count = PROMPT_LEN + CONT
    part = key_count // 4

    @pl.when((step >= HQ) & (step < HQ + HK))
    def _():
        @pl.loop(0, 4)
        def _(at):
            rows = pl.ds(pl.multiple_of(at * part, 16), part)
            front, back = turn(project(normed_ref[rows]), cosine_ref[rows], sine_ref[rows])
            pair_ref[rows, : HD // 2] = front.astype(LOW)
            pair_ref[rows, HD // 2 :] = back.astype(LOW)

    @pl.when(step >= HQ + HK)
    def _():
        @pl.loop(0, 4)
        def _(at):
            rows = pl.ds(pl.multiple_of(at * part, 16), part)
            pair_ref[rows] = project(normed_ref[rows]).astype(LOW)


VMEM_LIMIT = 60 * 2**20


def project_heads(place, group_rows, own_inputs, gain_row, cosine, sine_part, weights):
    own_rows = own_inputs.shape[0]
    key_count = PROMPT_LEN + CONT
    whole = lambda shape: pl.BlockSpec(shape, lambda j, p: (0, 0))
    return pl.pallas_call(
        project_kernel,
        grid_spec=pltpu.PrefetchScalarGridSpec(
            num_scalar_prefetch=1,
            grid=(HQ + 2 * HK,),
            in_specs=[
                whole((PROMPT_LEN, D)),
                whole((own_rows, D)),
                whole((1, D)),
                whole((key_count, HD // 2)),
                whole((key_count, HD // 2)),
                pl.BlockSpec((D, HD), lambda j, p: (0, j)),
            ],
            out_specs=[
                pl.BlockSpec((own_rows, HD), lambda j, p: (0, jnp.minimum(j, HQ - 1))),
                pl.BlockSpec((key_count, HD), lambda j, p: (0, jnp.maximum(j - HQ, 0))),
                whole((key_count, D)),
                whole((own_rows, D)),
                whole((key_count, 128)),
            ],
        ),
        out_shape=[
            jax.ShapeDtypeStruct((own_rows, HQ * HD), LOW),
            jax.ShapeDtypeStruct((key_count, 2 * HK * HD), LOW),
            jax.ShapeDtypeStruct((key_count, D), LOW),
            jax.ShapeDtypeStruct((own_rows, D), LOW),
            jax.ShapeDtypeStruct((key_count, 128), FULL),
        ],
        compiler_params=pltpu.CompilerParams(vmem_limit_bytes=VMEM_LIMIT),
        name="project_heads",
    )(place, group_rows, own_inputs, gain_row, cosine, sine_part, weights)


def across(left, right):
    return lax.dot_general(left, right, (((1,), (1,)), ((), ())), preferred_element_type=FULL)


def along(left, right):
    return lax.dot_general(left, right, (((0,), (0,)), ((), ())), preferred_element_type=FULL)


def attend_kernel(query_ref, key_ref, value_ref, seen_ref, attended_ref, logsum_ref):
    group_heads = HQ // HK
    for head in range(group_heads):
        columns = slice(head * HD, (head + 1) * HD)
        scores = across(query_ref[:, columns], key_ref[...]) * HD ** (-0.5)
        scores = jnp.where(seen_ref[...] > 0, scores, MASK_FILL)
        peak = jnp.max(scores, axis=-1, keepdims=True)
        unnormed = jnp.exp(scores - peak)
        total = jnp.sum(unnormed, axis=-1, keepdims=True)
        low = (unnormed / total).astype(LOW)
        attended_ref[:, columns] = jnp.dot(
            low, value_ref[...], preferred_element_type=FULL
        ).astype(LOW)
        logsum_ref[:, head * 128 : (head + 1) * 128] = jnp.broadcast_to(
            peak + jnp.log(total), (query_ref.shape[0], 128)
        )


def attend(queries, pairs, seen):
    rows, key_count = seen.shape
    group_heads = HQ // HK
    return pl.pallas_call(
        attend_kernel,
        grid=(HK,),
        in_specs=[
            pl.BlockSpec((rows, group_heads * HD), lambda j: (0, j)),
            pl.BlockSpec((key_count, HD), lambda j: (0, j)),
            pl.BlockSpec((key_count, HD), lambda j: (0, HK + j)),
            pl.BlockSpec((rows, key_count), lambda j: (0, 0)),
        ],
        out_specs=[
            pl.BlockSpec((rows, group_heads * HD), lambda j: (0, j)),
            pl.BlockSpec((rows, group_heads * 128), lambda j: (0, j)),
        ],
        out_shape=[
            jax.ShapeDtypeStruct((rows, HQ * HD), LOW),
            jax.ShapeDtypeStruct((rows, HQ * 128), FULL),
        ],
        compiler_params=pltpu.CompilerParams(vmem_limit_bytes=VMEM_LIMIT),
        name="attend",
    )(queries, pairs, pairs, seen)


def attend_back_kernel(
    place_ref,
    query_ref,
    key_ref,
    value_ref,
    seen_ref,
    logsum_ref,
    grad_ref,
    cosine_ref,
    sine_ref,
    query_out,
    pair_out,
):
    step = pl.program_id(0)
    group_heads = HQ // HK
    rows = query_ref.shape[0]
    prompt_rows = rows - CONT
    start = pl.multiple_of(place_ref[0] * prompt_rows, 16)
    score_scale = HD ** (-0.5)
    key_grad = value_grad = 0.0

    def turn_back(values, cosine, sine_part):
        front, back = values[:, : HD // 2], values[:, HD // 2 :]
        return jnp.concatenate(
            [front * cosine + back * sine_part, back * cosine - front * sine_part], axis=1
        ).astype(LOW)

    for head in range(group_heads):
        columns = slice(head * HD, (head + 1) * HD)
        scores = across(query_ref[:, columns], key_ref[...]) * score_scale
        scores = jnp.where(seen_ref[...] > 0, scores, MASK_FILL)
        probabilities = jnp.exp(scores - logsum_ref[:, head * 128 : head * 128 + 1])
        grads = grad_ref[:, columns]
        probability_grad = across(grads, value_ref[...])
        delta = jnp.sum(probabilities * probability_grad, axis=-1, keepdims=True)
        score_grad = (probabilities * (probability_grad - delta)).astype(LOW)
        query_grad = jnp.dot(score_grad, key_ref[...], preferred_element_type=FULL) * score_scale
        key_grad = key_grad + along(score_grad, query_ref[:, columns])
        value_grad = value_grad + along(probabilities.astype(LOW), grads)
        query_out[:prompt_rows, columns] = turn_back(
            query_grad[:prompt_rows],
            cosine_ref[pl.ds(start, prompt_rows)],
            sine_ref[pl.ds(start, prompt_rows)],
        )
        query_out[prompt_rows:, columns] = turn_back(
            query_grad[prompt_rows:], cosine_ref[PROMPT_LEN:], sine_ref[PROMPT_LEN:]
        )
    pair_out[:, pl.ds(pl.multiple_of(step * HD, HD), HD)] = turn_back(
        key_grad * score_scale, cosine_ref[...], sine_ref[...]
    )
    pair_out[:, pl.ds(pl.multiple_of((HK + step) * HD, HD), HD)] = value_grad.astype(LOW)


def attend_back(place, queries, pairs, seen, logsum, grads, cosine, sine_part):
    rows, key_count = seen.shape
    group_heads = HQ // HK
    whole = lambda shape: pl.BlockSpec(shape, lambda j, p: (0, 0))
    return pl.pallas_call(
        attend_back_kernel,
        grid_spec=pltpu.PrefetchScalarGridSpec(
            num_scalar_prefetch=1,
            grid=(HK,),
            in_specs=[
                pl.BlockSpec((rows, group_heads * HD), lambda j, p: (0, j)),
                pl.BlockSpec((key_count, HD), lambda j, p: (0, j)),
                pl.BlockSpec((key_count, HD), lambda j, p: (0, HK + j)),
                whole((rows, key_count)),
                pl.BlockSpec((rows, group_heads * 128), lambda j, p: (0, j)),
                pl.BlockSpec((rows, group_heads * HD), lambda j, p: (0, j)),
                whole((key_count, HD // 2)),
                whole((key_count, HD // 2)),
            ],
            out_specs=[
                pl.BlockSpec((rows, group_heads * HD), lambda j, p: (0, j)),
                whole((key_count, 2 * HK * HD)),
            ],
        ),
        out_shape=[
            jax.ShapeDtypeStruct((rows, HQ * HD), LOW),
            jax.ShapeDtypeStruct((key_count, 2 * HK * HD), LOW),
        ],
        compiler_params=pltpu.CompilerParams(vmem_limit_bytes=VMEM_LIMIT),
        name="attend_back",
    )(place, queries, pairs, pairs, seen, logsum, grads, cosine, sine_part)


def weights_back_kernel(
    place_ref,
    query_ref,
    pair_ref,
    branch_ref,
    attended_ref,
    normed_ref,
    own_normed_ref,
    group_ref,
    own_ref,
    scale_ref,
    query_weight_ref,
    pair_weight_ref,
    query_term,
    pair_term,
    merge_term,
    back_out,
    pair_back_out,
    gain_out,
):
    rows = query_ref.shape[0]
    prompt_rows = rows - CONT
    start = pl.multiple_of(place_ref[0] * prompt_rows, 16)
    query_term[...] = along(own_normed_ref[...], query_ref[...]).astype(LOW)
    pair_term[...] = along(normed_ref[...], pair_ref[...]).astype(LOW)
    merge_term[...] = along(branch_ref[...], attended_ref[...]).astype(LOW)
    query_back = across(query_ref[...], query_weight_ref[...])
    pair_back = across(pair_ref[...], pair_weight_ref[...])
    own_values = own_ref[prompt_rows:].astype(FULL) * scale_ref[PROMPT_LEN:, :1]
    tail = query_back[prompt_rows:] + pair_back[PROMPT_LEN:]
    group_values = group_ref[...].astype(FULL) * scale_ref[:PROMPT_LEN, :1]
    own_prompt = own_ref[:prompt_rows].astype(FULL) * scale_ref[pl.ds(start, prompt_rows), :1]
    gain_out[...] = (
        jnp.sum(pair_back[:PROMPT_LEN] * group_values, axis=0, keepdims=True)
        + jnp.sum(query_back[:prompt_rows] * own_prompt, axis=0, keepdims=True)
        + jnp.sum(tail * own_values, axis=0, keepdims=True)
    )
    back_out[:prompt_rows] = query_back[:prompt_rows]
    back_out[prompt_rows:] = tail
    pair_back_out[...] = pair_back[:PROMPT_LEN].astype(LOW)


def weights_back(
    place, queries, pairs, branch, attended, normed, own_normed, group_rows, own_inputs, scale, weights
):
    rows, key_count = queries.shape[0], pairs.shape[0]
    wide, tile = HQ * HD, 256
    whole = lambda shape: pl.BlockSpec(shape, lambda j, p: (0, 0))
    tall = lambda count: pl.BlockSpec((count, tile), lambda j, p: (0, j))
    flat = lambda at: pl.BlockSpec((tile, wide), lambda j, p: (j, at))
    return pl.pallas_call(
        weights_back_kernel,
        grid_spec=pltpu.PrefetchScalarGridSpec(
            num_scalar_prefetch=1,
            grid=(D // tile,),
            in_specs=[
                whole((rows, wide)),
                whole((key_count, wide)),
                tall(rows),
                whole((rows, wide)),
                tall(key_count),
                tall(rows),
                tall(PROMPT_LEN),
                tall(rows),
                whole((key_count, 128)),
                flat(0),
                flat(1),
            ],
            out_specs=[flat(0), flat(0), flat(0), tall(rows), tall(PROMPT_LEN), tall(1)],
        ),
        out_shape=[
            jax.ShapeDtypeStruct((D, wide), LOW),
            jax.ShapeDtypeStruct((D, wide), LOW),
            jax.ShapeDtypeStruct((D, wide), LOW),
            jax.ShapeDtypeStruct((rows, D), FULL),
            jax.ShapeDtypeStruct((PROMPT_LEN, D), LOW),
            jax.ShapeDtypeStruct((1, D), FULL),
        ],
        compiler_params=pltpu.CompilerParams(vmem_limit_bytes=VMEM_LIMIT),
        name="weights_back",
    )(
        place,
        queries,
        pairs,
        branch,
        attended,
        normed,
        own_normed,
        group_rows,
        own_inputs,
        scale,
        weights,
        weights,
    )


def forward_back_kernel(
    activated_ref, grad_ref, gate_up_ref, down_ref, out_ref, gate_up_grad_ref
):
    own_hidden = activated_ref.shape[1]
    part = down_ref.shape[0] // 4

    @pl.loop(0, 4)
    def _(at):
        columns = pl.ds(pl.multiple_of(at * part, part), part)
        out_ref[:, columns] = across(activated_ref[...], down_ref[columns]).astype(LOW)

    piece = own_hidden // 2
    for at in range(2):
        columns = slice(at * piece, (at + 1) * piece)
        upper = slice(own_hidden + at * piece, own_hidden + (at + 1) * piece)
        activated_grad = jnp.dot(
            grad_ref[...], down_ref[:, columns], preferred_element_type=FULL
        )
        gate_values, up_values = gate_up_ref[:, columns], gate_up_ref[:, upper]
        gate_sigmoid = jax.nn.sigmoid(gate_values)
        gate_grad, up_grad = gate_backward(
            activated_grad, gate_values, up_values, gate_sigmoid, gate_values * gate_sigmoid
        )
        gate_up_grad_ref[:, columns] = gate_grad
        gate_up_grad_ref[:, upper] = up_grad


def forward_back(rows, activated, grads, gate_up, down_weight):
    count, own_hidden = activated.shape
    block = lambda width: pl.BlockSpec((rows, width), lambda j: (j, 0))
    return pl.pallas_call(
        forward_back_kernel,
        grid=(count // rows,),
        in_specs=[
            block(own_hidden),
            block(D),
            block(2 * own_hidden),
            pl.BlockSpec(down_weight.shape, lambda j: (0, 0)),
        ],
        out_specs=[block(D), block(2 * own_hidden)],
        out_shape=[
            jax.ShapeDtypeStruct((count, D), LOW),
            jax.ShapeDtypeStruct((count, 2 * own_hidden), LOW),
        ],
        compiler_params=pltpu.CompilerParams(vmem_limit_bytes=VMEM_LIMIT),
        name="forward_back",
    )(activated, grads, gate_up, down_weight)


def plane_back_kernel(
    plane,
    rows_ref,
    weight_ref,
    out_ref,
    weight,
    tiles,
    keep,
    give,
    core_in,
    plane_in,
    total,
    load_sem,
    tile_sem,
    core_send,
    core_recv,
    plane_send,
    plane_recv,
    out_sem,
):
    g = lax.axis_index("grp")
    d = lax.axis_index("dp")
    chips = plane // 2
    halves = plane == 8
    order = (3, 1, 2, 0) if halves else tuple(range(chips - 1, -1, -1))
    cut = D // 2
    half_of = (pl.ds(0, cut), pl.ds(cut, D - cut))

    barrier = pltpu.get_barrier_semaphore()
    for offset in range(1, plane):
        pl.semaphore_signal(
            barrier, inc=1, device_id=(g, flip(d, offset)), device_id_type=MESH
        )

    load = pltpu.make_async_copy(weight_ref, weight, load_sem.at[0])
    load.start()

    def tile_copy(turn):
        at = order[turn]
        return pltpu.make_async_copy(
            rows_ref.at[pl.ds(2 * at, 2)], tiles.at[turn % 2], tile_sem.at[turn % 2]
        )

    def core_copy(at):
        return remote(
            give.at[at], core_in.at[at], core_send.at[at], core_recv.at[at], (g, flip(d, 1))
        )

    def plane_copy(at):
        return remote(
            keep.at[at],
            plane_in.at[at],
            plane_send.at[at],
            plane_recv.at[at],
            (g, flip(d, 2 * at)),
        )

    def near_copy(part, relayed):
        there = part + 1
        return remote(
            keep.at[3 if relayed else there, :, half_of[part]],
            plane_in.at[1 if relayed else 0, :, half_of[part]],
            plane_send.at[2 * relayed + part],
            plane_recv.at[2 * relayed + part],
            (g, flip(d, 2 * there)),
        )

    def relay_copy(part):
        there = 2 - part
        return remote(
            keep.at[there, :, half_of[part]],
            plane_in.at[2, :, half_of[part]],
            plane_send.at[4 + part],
            plane_recv.at[4 + part],
            (g, flip(d, 2 * there)),
        )

    tile_copy(0).start()
    tile_copy(1).start()
    pl.semaphore_wait(barrier, plane - 1)
    load.wait()
    part_width = 512

    def product(turn, which, target):
        @pl.loop(0, D // part_width)
        def _(at):
            columns = pl.ds(pl.multiple_of(at * part_width, part_width), part_width)
            target[order[turn], :, columns] = across(
                tiles[turn % 2, which], weight[columns]
            ).astype(LOW)

    def add_into(at, other, first, count):
        step = 256

        @pl.loop(0, count // step)
        def _(k):
            here = pl.ds(pl.multiple_of(first + k * step, step), step)
            keep[at, :, here] = (
                keep[at, :, here].astype(FULL) + other(here).astype(FULL)
            ).astype(LOW)

    def settle(turn):
        at = order[turn]
        core_copy(at).wait_recv()
        add_into(at, lambda here: core_in[at, :, here], 0, D)
        if halves and at == 3:
            near_copy(0, True).start()
            near_copy(1, True).start()
        elif halves and at:
            near_copy(at - 1, False).start()
        elif at:
            plane_copy(at).start()

    for turn in range(chips):
        tile_copy(turn).wait()
        product(turn, 1, give)
        core_copy(order[turn]).start()
        if turn:
            settle(turn - 1)
        product(turn, 0, keep)
        if turn + 2 < chips:
            tile_copy(turn + 2).start()
        if halves and turn == chips - 1:
            for part in range(2):
                near_copy(part, True).wait_recv()
                add_into(
                    2 - part,
                    lambda here: plane_in[1, :, here],
                    part * cut,
                    cut,
                )
                relay_copy(part).start()
    settle(chips - 1)
    if halves:
        for part in range(2):
            near_copy(part, False).wait_recv()
            relay_copy(part).wait_recv()
        arrived = (0, 2)
    else:
        for at in range(1, chips):
            plane_copy(at).wait_recv()
        arrived = tuple(range(1, chips))

    @pl.loop(0, D // 256)
    def _(k):
        here = pl.ds(pl.multiple_of(k * 256, 256), 256)
        value = keep[0, :, here].astype(FULL)
        for at in arrived:
            value = value + plane_in[at, :, here].astype(FULL)
        total[:, here] = value

    out = pltpu.make_async_copy(total, out_ref, out_sem.at[0])
    out.start()
    for at in range(chips):
        core_copy(at).wait_send()
    if halves:
        for part in range(2):
            near_copy(part, False).wait_send()
            near_copy(part, True).wait_send()
            relay_copy(part).wait_send()
    else:
        for at in range(1, chips):
            plane_copy(at).wait_send()
    out.wait()


def plane_back(rows, gate_up_grad, gate_weight):
    plane = lax.axis_size("dp")
    chips = plane // 2
    inner = gate_up_grad.shape[1]
    anywhere = pl.BlockSpec(memory_space=pl.ANY)
    dma = pltpu.SemaphoreType.DMA
    return pl.pallas_call(
        functools.partial(plane_back_kernel, plane),
        out_shape=jax.ShapeDtypeStruct((rows, D), FULL),
        in_specs=[anywhere] * 2,
        out_specs=anywhere,
        scratch_shapes=[
            pltpu.VMEM((D, inner), LOW),
            pltpu.VMEM((2, 2, rows, inner), LOW),
            pltpu.VMEM((chips, rows, D), LOW),
            pltpu.VMEM((chips, rows, D), LOW),
            pltpu.VMEM((chips, rows, D), LOW),
            pltpu.VMEM((3 if plane == 8 else chips, rows, D), LOW),
            pltpu.VMEM((rows, D), FULL),
            dma((1,)),
            dma((2,)),
            dma((chips,)),
            dma((chips,)),
            dma((max(6, chips),)),
            dma((max(6, chips),)),
            dma((1,)),
        ],
        compiler_params=pltpu.CompilerParams(
            collective_id=2, has_side_effects=True, vmem_limit_bytes=VMEM_LIMIT
        ),
        name="plane_back",
    )(gate_up_grad.reshape(plane, rows, inner), gate_weight)


def plane_swap(block, offset):
    size = lax.axis_size("dp")
    return lax.ppermute(block, "dp", [(i, i ^ offset) for i in range(size)])


def plane_gather(block):
    mine = [block] + [plane_swap(block, o) for o in range(2, lax.axis_size("dp"), 2)]
    pairs = [(one, plane_swap(one, 1)) for one in mine]
    return jnp.concatenate([one for pair in pairs for one in pair], axis=0)


def line_scatter(term):
    return lax.psum_scatter(term, "grp", scatter_dimension=0, tiled=True)


def finish_kernel(
    lines,
    plane,
    query_ref,
    pair_ref,
    merge_ref,
    gain_ref,
    gate_ref,
    up_ref,
    down_ref,
    a_master,
    a_first,
    a_second,
    m_master,
    m_first,
    m_second,
    f_master,
    f_first,
    f_second,
    a_grad,
    a_update,
    a_first_new,
    a_second_new,
    m_grad,
    m_update,
    m_first_new,
    m_second_new,
    gain_out,
    f_grad,
    f_update,
    f_first_new,
    f_second_new,
    mine,
    core_in,
    plane_in,
    line_in,
    swap_in,
    state,
    made,
    a_state,
    a_made,
    gain_made,
    mine_sem,
    core_send,
    core_recv,
    plane_send,
    plane_recv,
    line_send,
    line_recv,
    swap_send,
    swap_recv,
    own_sem,
    state_sem,
    made_sem,
    a_sem,
    gain_sem,
):
    g = lax.axis_index("grp")
    d = lax.axis_index("dp")
    chips = plane // 2
    chip, core = lax.div(d, 2), lax.rem(d, 2)
    partner = d + 1 - 2 * core
    rows = a_master.shape[0]
    own_hidden = gate_ref.shape[2]
    width = core_in.shape[3]
    a_width, m_width = a_master.shape[1], m_master.shape[1]
    parts, begin = [], 0
    for ref in (query_ref, pair_ref, merge_ref, gain_ref):
        parts.append((ref, pl.ds(begin, ref.shape[4])))
        begin += ref.shape[4]

    barrier = pltpu.get_barrier_semaphore()
    for step in range(1, plane):
        there = lax.rem(d + step, plane)
        pl.semaphore_signal(barrier, inc=1, device_id=(g, there), device_id_type=MESH)
    for step in range(1, lines):
        there = lax.rem(g + step, lines)
        pl.semaphore_signal(barrier, inc=1, device_id=(there, d), device_id_type=MESH)
    pl.semaphore_wait(barrier, plane + lines - 2)

    def line_at(turn):
        return lax.rem(g + turn + 1, lines)

    def core_copy(turn, part):
        line = line_at(turn)
        ref, columns = parts[part]
        return remote(
            ref.at[line, :, 1 - core],
            core_in.at[line, :, :, columns],
            core_send.at[turn, part],
            core_recv.at[turn, part],
            (g, partner),
        )

    def mine_copy(turn, part):
        line = line_at(turn)
        ref, columns = parts[part]
        return pltpu.make_async_copy(
            ref.at[line, :, core], mine.at[turn % 2, :, :, columns], mine_sem.at[turn, part]
        )

    cut = width // 256 * 128
    columns_of = (pl.ds(0, cut), pl.ds(cut, width - cut))

    def plane_copy(turn, step):
        line = line_at(turn)
        there = lax.rem(chip + step, chips)
        return remote(
            core_in.at[line, there],
            plane_in.at[line, chip],
            plane_send.at[turn, step],
            plane_recv.at[turn, step],
            (g, 2 * there + core),
        )

    def near_copy(turn, part, relayed):
        line = line_at(turn)
        there = flip(chip, part + 1)
        owner = flip(chip, 3) if relayed else there
        return remote(
            core_in.at[line, owner, :, columns_of[part]],
            plane_in.at[line, 1 if relayed else 0, :, columns_of[part]],
            plane_send.at[turn, 2 * relayed + part],
            plane_recv.at[turn, 2 * relayed + part],
            (g, 2 * there + core),
        )

    def relay_copy(turn, part):
        line = line_at(turn)
        there = flip(chip, 2 - part)
        return remote(
            core_in.at[line, there, :, columns_of[part]],
            plane_in.at[line, 2, :, columns_of[part]],
            plane_send.at[turn, 4 + part],
            plane_recv.at[turn, 4 + part],
            (g, 2 * there + core),
        )

    def line_copy(turn):
        line = line_at(turn)
        return remote(
            core_in.at[line, chip],
            line_in.at[g],
            line_send.at[turn],
            line_recv.at[turn],
            (line, d),
        )

    forward_refs = (gate_ref, up_ref, down_ref)

    def swap_copy(step, part):
        there = lax.rem(d + step, plane)
        return remote(
            forward_refs[part].at[there],
            swap_in.at[part, d],
            swap_send.at[step, part],
            swap_recv.at[step, part],
            (g, there),
        )

    own_swap = [
        pltpu.make_async_copy(forward_refs[part].at[d], swap_in.at[part, d], own_sem.at[part])
        for part in range(3)
    ]

    def f_columns(turn):
        block = lax.rem(d + lax.div(turn, 3), plane)
        return pl.ds(
            pl.multiple_of(lax.rem(turn, 3) * FF + block * own_hidden, own_hidden), own_hidden
        )

    def state_copy(turn, which):
        slot = lax.rem(turn, 2)
        return pltpu.make_async_copy(
            (f_master, f_first, f_second)[which].at[:, f_columns(turn)],
            state.at[slot, which],
            state_sem.at[slot, which],
        )

    def made_copy(turn, which):
        slot = lax.rem(turn, 2)
        return pltpu.make_async_copy(
            made.at[slot, which],
            (f_grad, f_update, f_first_new, f_second_new)[which].at[:, f_columns(turn)],
            made_sem.at[slot, which],
        )

    slabs = (pl.ds(0, a_width), pl.ds(a_width, m_width))

    def a_state_copy(which, slab):
        source = ((a_master, a_first, a_second), (m_master, m_first, m_second))[slab][which]
        return pltpu.make_async_copy(
            source, a_state.at[which, :, slabs[slab]], a_sem.at[slab, which]
        )

    def a_made_copy(which, slab):
        target = (
            (a_grad, a_update, a_first_new, a_second_new),
            (m_grad, m_update, m_first_new, m_second_new),
        )[slab][which]
        return pltpu.make_async_copy(
            a_made.at[which, :, slabs[slab]], target, a_sem.at[slab, 3 + which]
        )

    every = range(len(parts))
    for turn in range(lines):
        for part in every:
            core_copy(turn, part).start()
            if turn < 2:
                mine_copy(turn, part).start()
        if turn == 0:
            for step in range(1, plane):
                for part in range(3):
                    swap_copy(step, part).start()
            for one in own_swap:
                one.start()
    for which in range(3):
        state_copy(0, which).start()
        for slab in range(2):
            a_state_copy(which, slab).start()

    tile = 896 if width % 896 == 0 else 128
    halves = plane == 8

    def add_into(line, there, other, columns=None):
        first, count = (0, width) if columns is None else columns
        step = tile if columns is None else 128

        @pl.loop(0, count // step)
        def _(at):
            here = pl.ds(pl.multiple_of(first + at * step, 128), step)
            total = core_in[line, there, :, here].astype(FULL) + other(here).astype(FULL)
            core_in[line, there, :, here] = total.astype(LOW)

    def near_start(turn):
        if halves:
            for relayed in (True, False):
                for part in range(2):
                    near_copy(turn, part, relayed).start()
        else:
            for step in range(1, chips):
                plane_copy(turn, step).start()

    for turn in range(lines):
        line = line_at(turn)
        for part in every:
            core_copy(turn, part).wait_recv()
            mine_copy(turn, part).wait()
        for step in range(1, chips + 1):
            there = lax.rem(chip + step, chips)
            add_into(
                line, there, lambda here, there=there, turn=turn: mine[turn % 2, there, :, here]
            )
        if turn + 2 < lines:
            for part in every:
                mine_copy(turn + 2, part).start()
        if turn < 2:
            near_start(turn)

    def pass_on(turn):
        line = line_at(turn)
        for part, columns in enumerate(((0, cut), (cut, width - cut))):
            near_copy(turn, part, True).wait_recv()
            add_into(
                line,
                flip(chip, 2 - part),
                lambda here, line=line: plane_in[line, 1, :, here],
                columns,
            )
            relay_copy(turn, part).start()

    def forward_turn(turn):
        slot = lax.rem(turn, 2)
        block = lax.rem(d + lax.div(turn, 3), plane)
        part = lax.rem(turn, 3)

        @pl.when(turn + 1 < 3 * plane)
        def _():
            for which in range(3):
                state_copy(turn + 1, which).start()

        @pl.when(turn > 1)
        def _():
            for which in range(4):
                made_copy(turn - 2, which).wait()

        for which in range(3):
            state_copy(turn, which).wait()

        @pl.loop(0, rows // 16)
        def _(at):
            rows_at = pl.ds(pl.multiple_of(at * 16, 16), 16)
            gradient = swap_in[part, block, rows_at].astype(FULL)
            update, first_new, second_new = adam_step(
                state[slot, 0, rows_at],
                state[slot, 1, rows_at],
                state[slot, 2, rows_at],
                gradient,
                WEIGHT_DECAY,
            )
            made[slot, 0, rows_at] = gradient
            made[slot, 1, rows_at] = update
            made[slot, 2, rows_at] = first_new
            made[slot, 3, rows_at] = second_new

        for which in range(4):
            made_copy(turn, which).start()

    def near_done(turn):
        if halves:
            pass_on(turn)
            for part in range(2):
                near_copy(turn, part, False).wait_recv()
        else:
            for step in range(1, chips):
                plane_copy(turn, step).wait_recv()
        if turn + 2 < lines:
            near_start(turn + 2)

    def line_done(turn):
        line = line_at(turn)
        if halves:
            for part in range(2):
                relay_copy(turn, part).wait_recv()
            arrived = (0, 2)
        else:
            arrived = tuple(lax.rem(chip + step, chips) for step in range(1, chips))

        @pl.loop(0, width // tile)
        def _(at):
            columns = pl.ds(pl.multiple_of(at * tile, tile), tile)
            total = core_in[line, chip, :, columns].astype(FULL)
            for block in arrived:
                total = total + plane_in[line, block, :, columns].astype(FULL)
            core_in[line, chip, :, columns] = total.astype(LOW)

        if turn < lines - 1:
            line_copy(turn).start()

    each = 3 * plane // lines

    def forward_some(turn):
        lax.fori_loop(turn * each, (turn + 1) * each, lambda k, c: (forward_turn(k), c)[1], 0)

    near_done(0)
    for turn in range(1, lines):
        if turn == 1:
            for one in own_swap:
                one.wait()
            for step in range(1, plane):
                for part in range(3):
                    swap_copy(step, part).wait_recv()
        near_done(turn)
        line_done(turn - 1)
        forward_some(turn - 1)
    line_done(lines - 1)
    forward_some(lines - 1)
    for which in range(4):
        for turn in (3 * plane - 2, 3 * plane - 1):
            made_copy(turn, which).wait()
    for turn in range(lines - 1):
        line_copy(turn).wait_recv()
    for which in range(3):
        for slab in range(2):
            a_state_copy(which, slab).wait()

    def owned(columns):
        total = core_in[g, chip, :, columns].astype(FULL)
        for step in range(1, lines):
            total = total + line_in[lax.rem(g + step, lines), :, columns].astype(FULL)
        return total

    @pl.loop(0, (a_width + m_width) // 256)
    def _(at):
        columns = pl.ds(pl.multiple_of(at * 256, 256), 256)
        gradient = owned(columns)
        update, first_new, second_new = adam_step(
            a_state[0, :, columns],
            a_state[1, :, columns],
            a_state[2, :, columns],
            gradient,
            WEIGHT_DECAY,
        )
        a_made[0, :, columns] = gradient
        a_made[1, :, columns] = update
        a_made[2, :, columns] = first_new
        a_made[3, :, columns] = second_new

    for which in range(4):
        for slab in range(2):
            a_made_copy(which, slab).start()
    gain_made[...] = owned(pl.ds(a_width + m_width, GAIN_PAD))
    gain_copy = pltpu.make_async_copy(gain_made, gain_out, gain_sem.at[0])
    gain_copy.start()
    for turn in range(lines):
        for part in every:
            core_copy(turn, part).wait_send()
        if halves:
            for part in range(2):
                near_copy(turn, part, False).wait_send()
                near_copy(turn, part, True).wait_send()
                relay_copy(turn, part).wait_send()
        else:
            for step in range(1, chips):
                plane_copy(turn, step).wait_send()
        if turn < lines - 1:
            line_copy(turn).wait_send()
    for step in range(1, plane):
        for part in range(3):
            swap_copy(step, part).wait_send()
    for which in range(4):
        for slab in range(2):
            a_made_copy(which, slab).wait()
    gain_copy.wait()


def finish(terms, forward_parts, attention, merge, forward):
    lines, plane = lax.axis_size("grp"), lax.axis_size("dp")
    chips = plane // 2
    rows, a_width = attention[0].shape
    m_width = merge[0].shape[1]
    own_hidden = forward_parts[0].shape[1]
    width = a_width + m_width + GAIN_PAD
    anywhere = pl.BlockSpec(memory_space=pl.ANY)
    dma = pltpu.SemaphoreType.DMA
    vmem = pltpu.VMEM

    def like(array):
        return jax.ShapeDtypeStruct(array.shape, array.dtype)

    return pl.pallas_call(
        functools.partial(finish_kernel, lines, plane),
        out_shape=(like(attention[0]),) * 4
        + (like(merge[0]),) * 4
        + (jax.ShapeDtypeStruct((rows, GAIN_PAD), FULL),)
        + (like(forward[0]),) * 4,
        in_specs=[anywhere] * 16,
        out_specs=(anywhere,) * 13,
        scratch_shapes=[
            vmem((2, chips, rows, width), LOW),
            vmem((lines, chips, rows, width), LOW),
            vmem((lines, 3 if plane == 8 else chips, rows, width), LOW),
            vmem((lines, rows, width), LOW),
            vmem((3, plane, rows, own_hidden), LOW),
            vmem((2, 3, rows, own_hidden), FULL),
            vmem((2, 4, rows, own_hidden), FULL),
            vmem((3, rows, a_width + m_width), FULL),
            vmem((4, rows, a_width + m_width), FULL),
            vmem((rows, GAIN_PAD), FULL),
            dma((lines, 4)),
            dma((lines, 4)),
            dma((lines, 4)),
            dma((lines, max(6, chips))),
            dma((lines, max(6, chips))),
            dma((lines,)),
            dma((lines,)),
            dma((plane, 3)),
            dma((plane, 3)),
            dma((3,)),
            dma((2, 3)),
            dma((2, 4)),
            dma((2, 7)),
            dma((1,)),
        ],
        compiler_params=pltpu.CompilerParams(
            collective_id=1, has_side_effects=True, vmem_limit_bytes=VMEM_LIMIT
        ),
        name="finish",
    )(
        *(term.reshape(lines, chips, 2, rows, term.shape[1]) for term in terms),
        *(part.reshape(plane, rows, -1) for part in forward_parts),
        *attention,
        *merge,
        *forward,
    )


def body(
    hidden,
    cotangent,
    segment_ids,
    continuation_prompt,
    gain_master,
    gain_first,
    gain_second,
    attention_master,
    attention_first,
    attention_second,
    merge_master,
    merge_first,
    merge_second,
    feedforward_master,
    feedforward_first,
    feedforward_second,
):
    group_index = lax.axis_index("grp")
    dp_size = lax.axis_size("dp")
    row_count = hidden.shape[2]
    prompt_rows = row_count - CONT
    qkv_width = (HQ + 2 * HK) * HD
    own_rows = feedforward_master.shape[0]
    own_hidden = FF // dp_size
    own_inputs = hidden.reshape(row_count, D)

    gain_columns = jnp.pad(gain_master.T, ((0, 0), (0, GAIN_PAD - 2)))
    weight_low = jnp.concatenate(
        [attention_master.astype(LOW), merge_master.astype(LOW), gain_columns.astype(LOW)], axis=1
    )
    weights, group_rows, gate_rows, down_rows = gather_start(
        weight_low, own_inputs, feedforward_master.astype(LOW)
    )
    weights, late_cotangent = lax.optimization_barrier((weights, cotangent))
    weights = weights.reshape(D, -1)
    merge_weight = weights[:, qkv_width : qkv_width + D]
    gain_float = weights[:, qkv_width + D : qkv_width + D + 2].astype(FULL).T
    gate_weight = lax.all_gather(
        gate_rows.reshape(dp_size * own_rows, 2 * own_hidden), "grp", axis=0, tiled=True
    )
    gate_weight, down_rows = lax.optimization_barrier((gate_weight, down_rows))
    down_weight = lax.all_gather(
        down_rows.reshape(dp_size * own_rows, own_hidden), "grp", axis=0, tiled=True
    )
    down_grad = plane_gather(late_cotangent.reshape(row_count, D))

    segment_row = segment_ids[0]
    source_row = continuation_prompt[0]
    prompt_positions, follow_positions = segment_positions(segment_row, source_row)
    cosine, sine_part = angle_table(jnp.concatenate([prompt_positions, follow_positions[0]]))

    place = jnp.reshape(group_index, (1,)).astype(jnp.int32)
    group_rows = group_rows.reshape(PROMPT_LEN, D)
    queries, pairs, key_normed, normed, key_scale = project_heads(
        place, group_rows, own_inputs, gain_float[:1], cosine, sine_part, weights
    )
    inputs = own_inputs.astype(FULL)
    first_scale = norm_scale(inputs)

    row_index = jnp.arange(row_count, dtype=jnp.int32)
    is_prompt = row_index < prompt_rows
    global_row = group_index * prompt_rows + jnp.minimum(row_index, prompt_rows - 1)
    own_segment = lax.dynamic_slice_in_dim(segment_row, group_index * prompt_rows, prompt_rows)
    query_segment = jnp.concatenate([own_segment, jnp.broadcast_to(source_row, (CONT,))])
    key_index = jnp.arange(PROMPT_LEN, dtype=jnp.int32)
    prompt_seen = (segment_row[None, :] == query_segment[:, None]) & (
        (key_index[None, :] <= global_row[:, None]) | ~is_prompt[:, None]
    )
    follow_seen = (~is_prompt)[:, None] & (
        jnp.arange(CONT, dtype=jnp.int32)[None, :] <= (row_index - prompt_rows)[:, None]
    )
    visible = jnp.concatenate([prompt_seen, follow_seen], axis=1)
    seen = visible.astype(FULL)
    attended, row_logsum = attend(queries, pairs, seen)
    middle = inputs + contract(attended, merge_weight, 1, 1)
    second_scale = norm_scale(middle)
    normed_two = (middle * second_scale * gain_float[1]).astype(LOW)
    grad_rows = cotangent.reshape(row_count, D).astype(FULL)

    normed_two, down_grad = lax.optimization_barrier((normed_two, down_grad))
    normed_all = plane_gather(normed_two)
    gate_up = jnp.dot(normed_all, gate_weight, preferred_element_type=FULL)
    gate_values = gate_up[:, :own_hidden]
    up_values = gate_up[:, own_hidden:]
    gate_sigmoid, gate_silu, activated = gate_parts(gate_values, up_values)
    down_term = contract(down_grad, activated, 0, 0).astype(LOW)
    down_term, down_weight = lax.optimization_barrier((down_term, down_weight))
    out_term, gate_up_grad = forward_back(row_count, activated, down_grad, gate_up, down_weight)
    out_chunks = out_term.reshape(dp_size, row_count, D)
    out_swapped = [plane_swap(out_chunks[offset + 1], 1) for offset in range(0, dp_size, 2)]
    down_part = line_scatter(down_term)
    gate_term = contract(normed_all, gate_up_grad[:, :own_hidden], 0, 0).astype(LOW)
    gate_term, out_swapped = lax.optimization_barrier((gate_term, out_swapped))
    out_sums = [
        out_chunks[2 * at].astype(FULL) + one.astype(FULL) for at, one in enumerate(out_swapped)
    ]
    out_low = [one.astype(LOW) for one in out_sums[1:]]
    normed_all, out_low = lax.optimization_barrier((normed_all, out_low))
    out_arrived = [plane_swap(one, 2 * at + 2) for at, one in enumerate(out_low)]
    up_term = contract(normed_all, gate_up_grad[:, own_hidden:], 0, 0).astype(LOW)
    gate_term, down_part = lax.optimization_barrier((gate_term, down_part))
    gate_part = line_scatter(gate_term)
    gate_up_grad, up_term = lax.optimization_barrier((gate_up_grad, up_term))
    normed_two_grad = plane_back(row_count, gate_up_grad, gate_weight)
    normed_two_grad, out_arrived = lax.optimization_barrier((normed_two_grad, out_arrived))
    result = middle + out_sums[0]
    for one in out_arrived:
        result = result + one.astype(FULL)
    block_output = result.astype(LOW).reshape(hidden.shape)
    middle_grad = grad_rows + norm_back(middle, second_scale, gain_float[1], normed_two_grad)
    gain_two_part = jnp.sum(normed_two_grad * middle * second_scale, axis=0)
    branch_grad = middle_grad.astype(LOW)
    attended_grad = contract(branch_grad, merge_weight, 1, 0).astype(LOW)
    attended_grad, gate_part = lax.optimization_barrier((attended_grad, gate_part))
    up_part = line_scatter(up_term)
    query_project, pair_project = attend_back(
        place, queries, pairs, seen, row_logsum, attended_grad, cosine, sine_part
    )
    query_term, pair_term, merge_term, normed_grad, pair_back, gain_one_part = weights_back(
        place,
        query_project,
        pair_project,
        branch_grad,
        attended,
        key_normed,
        normed,
        group_rows,
        own_inputs,
        key_scale,
        weights,
    )
    gain_term = jnp.pad(
        jnp.stack([gain_one_part[0], gain_two_part], axis=1), ((0, 0), (0, GAIN_PAD - 2))
    )
    pair_back, up_part = lax.optimization_barrier((pair_back, up_part))
    pair_sum = line_scatter(pair_back)
    finished = finish(
        (query_term, pair_term, merge_term, gain_term.astype(LOW)),
        (gate_part, up_part, down_part),
        (attention_master, attention_first, attention_second),
        (merge_master, merge_first, merge_second),
        (feedforward_master, feedforward_first, feedforward_second),
    )
    gain_grad = finished[8][:, :2].T
    pair_sum, gain_grad = lax.optimization_barrier((pair_sum, gain_grad))
    pair_sum = pair_sum.astype(FULL)
    normed_grad = normed_grad + jnp.pad(pair_sum, ((0, CONT), (0, 0)))
    input_grad = (middle_grad + norm_back(inputs, first_scale, gain_float[0], normed_grad)).reshape(
        hidden.shape
    )
    gain_new = adam_step(gain_master, gain_first, gain_second, gain_grad, 0.0)
    return (
        block_output,
        input_grad,
        gain_grad,
        *gain_new,
        *finished[:8],
        *finished[9:],
    )


def solution(mesh):
    tokens = P("dp", "grp", None, None)
    gains = P(None, ("grp", "dp"))
    matrix = P(("grp", "dp"), None)
    return jax.shard_map(
        body,
        mesh=mesh,
        in_specs=(tokens, tokens, P("dp", None), P("dp", "grp")) + (gains,) * 3 + (matrix,) * 9,
        out_specs=(tokens, tokens) + (gains,) * 4 + (matrix,) * 12,
        check_vma=False,
    )
```

```python
import functools

import jax
import jax.numpy as jnp
from jax import lax
from jax.experimental import pallas as pl
from jax.experimental.pallas import tpu as pltpu
from jax.sharding import PartitionSpec as P

D = 2048
FF = 8192
HQ = 8
HK = 4
HD = 256
PROMPT_LEN = 1024
PROMPTS = 4
CONT = 64
STEP = 10
GAIN_PAD = 128

EPS_NORM = 1e-06
ROPE_THETA = 1000042.0
MASK_FILL = -1e30
BETA_ONE = 0.9
BETA_TWO = 0.95
ADAM_EPS = 1e-08
LEARN_RATE = 0.02
WEIGHT_DECAY = 0.1
LOW = jnp.bfloat16
FULL = jnp.float32
MESH = pl.DeviceIdType.MESH


def contract(left, right, left_axis, right_axis):
    return lax.dot_general(
        left, right, (((left_axis,), (right_axis,)), ((), ())), preferred_element_type=FULL
    )


def angle_table(positions):
    inverse_rate = ROPE_THETA ** (-(jnp.arange(HD // 2, dtype=FULL) * 2.0) / HD)
    angles = positions.astype(FULL)[..., None] * inverse_rate
    return (jnp.cos(angles), jnp.sin(angles))


def segment_positions(segment_row, source_row):
    labels = jnp.arange(PROMPTS, dtype=jnp.int32)
    member = (segment_row[None, :] == labels[:, None]).astype(jnp.int32)
    lengths = jnp.sum(member, axis=1, dtype=jnp.int32)
    starts = jnp.sum(
        jnp.where(labels[None, :] < labels[:, None], lengths[None, :], 0), axis=1, dtype=jnp.int32
    )
    prompt_index = jnp.arange(segment_row.shape[0], dtype=jnp.int32)
    prompt_positions = prompt_index - jnp.sum(member * starts[:, None], axis=0, dtype=jnp.int32)
    source_length = jnp.sum(
        (source_row[:, None] == labels[None, :]).astype(jnp.int32) * lengths[None, :],
        axis=1,
        dtype=jnp.int32,
    )
    follow_positions = source_length[:, None] + jnp.arange(CONT, dtype=jnp.int32)[None, :]
    return (prompt_positions, follow_positions)


def norm_scale(values):
    return lax.rsqrt(jnp.mean(values * values, axis=-1, keepdims=True) + EPS_NORM)


def norm_back(values, row_scale, gain_row, normed_grad):
    scaled = normed_grad * gain_row
    return row_scale * scaled - values * row_scale**3 * jnp.mean(
        scaled * values, axis=-1, keepdims=True
    )


def adam_step(master, first_moment, second_moment, gradient, decay_rate):
    first_new = BETA_ONE * first_moment + (1.0 - BETA_ONE) * gradient
    second_new = BETA_TWO * second_moment + (1.0 - BETA_TWO) * gradient * gradient
    correct_one = 1.0 - BETA_ONE**STEP
    correct_two = 1.0 - BETA_TWO**STEP
    update = first_new / correct_one / (jnp.sqrt(second_new / correct_two) + ADAM_EPS)
    return (-LEARN_RATE * (update + decay_rate * master), first_new, second_new)


def gate_parts(gate_values, up_values):
    gate_sigmoid = jax.nn.sigmoid(gate_values)
    gate_silu = gate_values * gate_sigmoid
    return (gate_sigmoid, gate_silu, (gate_silu * up_values).astype(LOW))


def gate_backward(activated_grad, gate_values, up_values, gate_sigmoid, gate_silu):
    gate_grad = (
        activated_grad * up_values * gate_sigmoid * (1.0 + gate_values * (1.0 - gate_sigmoid))
    ).astype(LOW)
    up_grad = (activated_grad * gate_silu).astype(LOW)
    return (gate_grad, up_grad)


def flip(index, bits):
    bit = 1
    while bit <= bits:
        if bits & bit:
            index = index + bit - 2 * bit * lax.rem(index // bit, 2)
        bit *= 2
    return index


def remote(source, target, send, recv, there):
    return pltpu.make_async_remote_copy(
        src_ref=source,
        dst_ref=target,
        send_sem=send,
        recv_sem=recv,
        device_id=there,
        device_id_type=MESH,
    )


def gather_kernel(
    lines,
    plane,
    prompt_rows,
    weight_ref,
    hidden_ref,
    forward_ref,
    weights_ref,
    rows_ref,
    gate_ref,
    down_ref,
    local_sem,
    line_send,
    line_recv,
    rows_send,
    rows_recv,
    near_send,
    near_recv,
    half_send,
    half_recv,
    core_send,
    core_recv,
    swap_send,
    swap_recv,
):
    g = lax.axis_index("grp")
    d = lax.axis_index("dp")
    evens = range(0, plane, 2)
    forward_halves = plane == 8
    near = (2, 4) if forward_halves else tuple(evens[1:])
    width = weight_ref.shape[1]
    cut = (width // 256) * 128

    barrier = pltpu.get_barrier_semaphore()
    for offset in range(1, plane):
        pl.semaphore_signal(barrier, inc=1, device_id=(g, flip(d, offset)), device_id_type=MESH)

    for step in range(1, lines):
        there = lax.rem(g + step, lines)
        pl.semaphore_signal(barrier, inc=1, device_id=(there, d), device_id_type=MESH)
    pl.semaphore_wait(barrier, plane + lines - 2)

    copy = remote
    own_rows = hidden_ref.at[pl.ds(0, prompt_rows)]

    def line_weight(way, step):
        block = g - step + 1 if way == 0 else g + step - 1
        source = weight_ref if step == 1 else weights_ref.at[block, d]
        return copy(
            source,
            weights_ref.at[block, d],
            line_send.at[way, step],
            line_recv.at[way, step],
            (g + 1 if way == 0 else g - 1, d),
        )

    def line_rows(way, step):
        block = g - step + 1 if way == 0 else g + step - 1
        source = own_rows if step == 1 else rows_ref.at[block]
        return copy(
            source,
            rows_ref.at[block],
            rows_send.at[way, step],
            rows_recv.at[way, step],
            (g + 1 if way == 0 else g - 1, d),
        )

    def sends(way, step):
        if way == 0:
            return (g < lines - 1) & (g >= step - 1)
        return (g > 0) & (g + step - 1 < lines)

    def receives(way, step):
        return g >= step if way == 0 else g + step < lines

    def near_copy(block, offset, own):
        source = weight_ref if own else weights_ref.at[block, d]
        at = near.index(offset)
        return copy(
            source,
            weights_ref.at[block, d],
            near_send.at[block, at],
            near_recv.at[block, at],
            (g, flip(d, offset)),
        )

    def half_copy(block, part):
        columns = pl.ds(0, cut) if part == 0 else pl.ds(cut, width - cut)
        origin = flip(d, 2) if part == 0 else flip(d, 4)
        there = flip(d, 4) if part == 0 else flip(d, 2)
        piece = weights_ref.at[block, origin, :, columns]
        return copy(
            piece, piece, half_send.at[block, part], half_recv.at[block, part], (g, there)
        )

    def core_copy(block, offset, own=False):
        source = weight_ref if own else weights_ref.at[block, flip(d, offset)]
        return copy(
            source,
            weights_ref.at[block, flip(d, offset)],
            core_send.at[block, offset // 2],
            core_recv.at[block, offset // 2],
            (g, flip(d, 1)),
        )

    own_hidden = down_ref.shape[2]

    def swap_piece(owner, part, source_index):
        source = forward_ref.at[:, pl.ds(part * FF + owner * own_hidden, own_hidden)]
        if part == 2:
            return source, down_ref.at[source_index]
        return source, gate_ref.at[source_index, :, pl.ds(part * own_hidden, own_hidden)]

    def swap_copy(offset, part):
        source, target = swap_piece(flip(d, offset), part, d)
        return copy(
            source,
            target,
            swap_send.at[offset, part],
            swap_recv.at[offset, part],
            (g, flip(d, offset)),
        )

    locals_ = (
        pltpu.make_async_copy(weight_ref, weights_ref.at[g, d], local_sem.at[0]),
        pltpu.make_async_copy(own_rows, rows_ref.at[g], local_sem.at[1]),
        *(
            pltpu.make_async_copy(*swap_piece(d, part, d), local_sem.at[2 + part])
            for part in range(3)
        ),
    )

    def launch(block, own):
        for offset in near:
            near_copy(block, offset, own).start()
        core_copy(block, 0, own).start()

    def relay(block):
        for offset in near:
            near_copy(block, offset, False).wait_recv()
            core_copy(block, offset).start()
        if forward_halves:
            half_copy(block, 0).start()
            half_copy(block, 1).start()

    def finish(block):
        if forward_halves:
            half_copy(block, 0).wait_recv()
            half_copy(block, 1).wait_recv()
            core_copy(block, 6).start()

    def both(step, act):
        for way in (0, 1):
            pl.when(receives(way, step))(
                lambda way=way: act(g - step if way == 0 else g + step)
            )

    def take_rows(step):
        for way in (0, 1):

            @pl.when(receives(way, step))
            def _(way=way):
                line_rows(way, step).wait_recv()

            if step + 1 < lines:
                pl.when(sends(way, step + 1))(
                    lambda way=way: line_rows(way, step + 1).start()
                )

    for way in (0, 1):
        pl.when(sends(way, 1))(lambda way=way: line_weight(way, 1).start())
    launch(g, True)
    for one in locals_:
        one.start()
    for step in range(1, lines):
        for way in (0, 1):

            @pl.when(receives(way, step))
            def _(way=way, step=step):
                line_weight(way, step).wait_recv()

            if step + 1 < lines:
                pl.when(sends(way, step + 1))(
                    lambda way=way, step=step: line_weight(way, step + 1).start()
                )
            else:
                pl.when(sends(way, 1))(lambda way=way: line_rows(way, 1).start())

        both(step, lambda block: launch(block, False))
        if step == 1:
            relay(g)
            for offset in range(1, plane):
                for part in range(3):
                    swap_copy(offset, part).start()
    for step in range(1, lines):
        take_rows(step)
        both(step, relay)
        if step == 1:
            finish(g)
        else:
            both(step - 1, finish)
    both(lines - 1, finish)

    def drain(block):
        for offset in evens:
            core_copy(block, offset).wait()
        for offset in near:
            near_copy(block, offset, False).wait_send()
        if forward_halves:
            half_copy(block, 0).wait_send()
            half_copy(block, 1).wait_send()

    drain(g)
    for step in range(1, lines):
        for way in (0, 1):
            pl.when(receives(way, step))(
                lambda way=way, step=step: drain(g - step if way == 0 else g + step)
            )

            @pl.when(sends(way, step))
            def _(way=way, step=step):
                line_weight(way, step).wait_send()
                line_rows(way, step).wait_send()

    for offset in range(1, plane):
        for part in range(3):
            swap_copy(offset, part).wait()
    for one in locals_:
        one.wait()


def gather_start(weight, hidden, forward):
    lines, plane = lax.axis_size("grp"), lax.axis_size("dp")
    prompt_rows = PROMPT_LEN // lines
    own_rows, width = weight.shape
    anywhere = pl.BlockSpec(memory_space=pl.ANY)
    dma = pltpu.SemaphoreType.DMA
    near_count = 2 if plane == 8 else plane // 2 - 1
    pairs = (
        (2, lines),
        (2, lines),
        (2, lines),
        (2, lines),
        (lines, near_count),
        (lines, near_count),
        (lines, 2),
        (lines, 2),
        (lines, plane // 2),
        (lines, plane // 2),
        (plane, 3),
        (plane, 3),
    )
    own_hidden = FF // plane
    return pl.pallas_call(
        functools.partial(gather_kernel, lines, plane, prompt_rows),
        out_shape=(
            jax.ShapeDtypeStruct((lines, plane, own_rows, width), weight.dtype),
            jax.ShapeDtypeStruct((lines, prompt_rows, D), hidden.dtype),
            jax.ShapeDtypeStruct((plane, own_rows, 2 * own_hidden), forward.dtype),
            jax.ShapeDtypeStruct((plane, own_rows, own_hidden), forward.dtype),
        ),
        in_specs=[anywhere] * 3,
        out_specs=(anywhere,) * 4,
        scratch_shapes=[dma((5,))] + [dma(shape) for shape in pairs],
        compiler_params=pltpu.CompilerParams(collective_id=0, has_side_effects=True),
        name="gather_start",
    )(weight, hidden, forward)


def project_kernel(
    place_ref,
    group_ref,
    own_ref,
    gain_ref,
    cosine_ref,
    sine_ref,
    weight_ref,
    query_ref,
    pair_ref,
    normed_ref,
    own_normed_ref,
    scale_ref,
):
    step = pl.program_id(0)
    own_rows = own_ref.shape[0]
    prompt_rows = own_rows - CONT
    start = pl.multiple_of(place_ref[0] * prompt_rows, 16)
    tile = 32

    def norm_tile(values, at):
        values = values.astype(FULL)
        scale = lax.rsqrt(jnp.mean(values * values, axis=-1, keepdims=True) + EPS_NORM)
        normed_ref[pl.ds(at, tile)] = (values * scale * gain_ref[...]).astype(LOW)
        scale_ref[pl.ds(at, tile)] = jnp.broadcast_to(scale, (tile, 128))

    @pl.when(step == 0)
    def _():
        @pl.loop(0, PROMPT_LEN // tile)
        def _(at):
            first = pl.multiple_of(at * tile, tile)
            norm_tile(group_ref[pl.ds(first, tile)], first)

        for at in range(0, CONT, tile):
            norm_tile(own_ref[prompt_rows + at : prompt_rows + at + tile], PROMPT_LEN + at)
        own_normed_ref[:prompt_rows] = normed_ref[pl.ds(start, prompt_rows)]
        own_normed_ref[prompt_rows:] = normed_ref[PROMPT_LEN:]

    def turn(values, cosine, sine_part):
        front, back = values[:, : HD // 2], values[:, HD // 2 :]
        return front * cosine - back * sine_part, back * cosine + front * sine_part

    def project(rows):
        return jnp.dot(rows, weight_ref[...], preferred_element_type=FULL)

    @pl.when(step < HQ)
    def _():
        for first, count, table in ((0, prompt_rows, start), (prompt_rows, CONT, PROMPT_LEN)):
            values = project(own_normed_ref[first : first + count])
            front, back = turn(
                values, cosine_ref[pl.ds(table, count)], sine_ref[pl.ds(table, count)]
            )
            query_ref[first : first + count, : HD // 2] = front.astype(LOW)
            query_ref[first : first + count, HD // 2 :] = back.astype(LOW)

    key_count = PROMPT_LEN + CONT
    part = key_count // 4

    @pl.when((step >= HQ) & (step < HQ + HK))
    def _():
        @pl.loop(0, 4)
        def _(at):
            rows = pl.ds(pl.multiple_of(at * part, 16), part)
            front, back = turn(project(normed_ref[rows]), cosine_ref[rows], sine_ref[rows])
            pair_ref[rows, : HD // 2] = front.astype(LOW)
            pair_ref[rows, HD // 2 :] = back.astype(LOW)

    @pl.when(step >= HQ + HK)
    def _():
        @pl.loop(0, 4)
        def _(at):
            rows = pl.ds(pl.multiple_of(at * part, 16), part)
            pair_ref[rows] = project(normed_ref[rows]).astype(LOW)


VMEM_LIMIT = 60 * 2**20


def project_heads(place, group_rows, own_inputs, gain_row, cosine, sine_part, weights):
    own_rows = own_inputs.shape[0]
    key_count = PROMPT_LEN + CONT
    whole = lambda shape: pl.BlockSpec(shape, lambda j, p: (0, 0))
    return pl.pallas_call(
        project_kernel,
        grid_spec=pltpu.PrefetchScalarGridSpec(
            num_scalar_prefetch=1,
            grid=(HQ + 2 * HK,),
            in_specs=[
                whole((PROMPT_LEN, D)),
                whole((own_rows, D)),
                whole((1, D)),
                whole((key_count, HD // 2)),
                whole((key_count, HD // 2)),
                pl.BlockSpec((D, HD), lambda j, p: (0, j)),
            ],
            out_specs=[
                pl.BlockSpec((own_rows, HD), lambda j, p: (0, jnp.minimum(j, HQ - 1))),
                pl.BlockSpec((key_count, HD), lambda j, p: (0, jnp.maximum(j - HQ, 0))),
                whole((key_count, D)),
                whole((own_rows, D)),
                whole((key_count, 128)),
            ],
        ),
        out_shape=[
            jax.ShapeDtypeStruct((own_rows, HQ * HD), LOW),
            jax.ShapeDtypeStruct((key_count, 2 * HK * HD), LOW),
            jax.ShapeDtypeStruct((key_count, D), LOW),
            jax.ShapeDtypeStruct((own_rows, D), LOW),
            jax.ShapeDtypeStruct((key_count, 128), FULL),
        ],
        compiler_params=pltpu.CompilerParams(vmem_limit_bytes=VMEM_LIMIT),
        name="project_heads",
    )(place, group_rows, own_inputs, gain_row, cosine, sine_part, weights)


def across(left, right):
    return lax.dot_general(left, right, (((1,), (1,)), ((), ())), preferred_element_type=FULL)


def along(left, right):
    return lax.dot_general(left, right, (((0,), (0,)), ((), ())), preferred_element_type=FULL)


def attend_kernel(query_ref, key_ref, value_ref, seen_ref, attended_ref, logsum_ref):
    group_heads = HQ // HK
    for head in range(group_heads):
        columns = slice(head * HD, (head + 1) * HD)
        scores = across(query_ref[:, columns], key_ref[...]) * HD ** (-0.5)
        scores = jnp.where(seen_ref[...] > 0, scores, MASK_FILL)
        peak = jnp.max(scores, axis=-1, keepdims=True)
        unnormed = jnp.exp(scores - peak)
        total = jnp.sum(unnormed, axis=-1, keepdims=True)
        low = (unnormed / total).astype(LOW)
        attended_ref[:, columns] = jnp.dot(
            low, value_ref[...], preferred_element_type=FULL
        ).astype(LOW)
        logsum_ref[:, head * 128 : (head + 1) * 128] = jnp.broadcast_to(
            peak + jnp.log(total), (query_ref.shape[0], 128)
        )


def attend(queries, pairs, seen):
    rows, key_count = seen.shape
    group_heads = HQ // HK
    return pl.pallas_call(
        attend_kernel,
        grid=(HK,),
        in_specs=[
            pl.BlockSpec((rows, group_heads * HD), lambda j: (0, j)),
            pl.BlockSpec((key_count, HD), lambda j: (0, j)),
            pl.BlockSpec((key_count, HD), lambda j: (0, HK + j)),
            pl.BlockSpec((rows, key_count), lambda j: (0, 0)),
        ],
        out_specs=[
            pl.BlockSpec((rows, group_heads * HD), lambda j: (0, j)),
            pl.BlockSpec((rows, group_heads * 128), lambda j: (0, j)),
        ],
        out_shape=[
            jax.ShapeDtypeStruct((rows, HQ * HD), LOW),
            jax.ShapeDtypeStruct((rows, HQ * 128), FULL),
        ],
        compiler_params=pltpu.CompilerParams(vmem_limit_bytes=VMEM_LIMIT),
        name="attend",
    )(queries, pairs, pairs, seen)


def attend_back_kernel(
    place_ref,
    query_ref,
    key_ref,
    value_ref,
    seen_ref,
    logsum_ref,
    grad_ref,
    cosine_ref,
    sine_ref,
    query_out,
    pair_out,
):
    step = pl.program_id(0)
    group_heads = HQ // HK
    rows = query_ref.shape[0]
    prompt_rows = rows - CONT
    start = pl.multiple_of(place_ref[0] * prompt_rows, 16)
    score_scale = HD ** (-0.5)
    key_grad = value_grad = 0.0

    def turn_back(values, cosine, sine_part):
        front, back = values[:, : HD // 2], values[:, HD // 2 :]
        return jnp.concatenate(
            [front * cosine + back * sine_part, back * cosine - front * sine_part], axis=1
        ).astype(LOW)

    for head in range(group_heads):
        columns = slice(head * HD, (head + 1) * HD)
        scores = across(query_ref[:, columns], key_ref[...]) * score_scale
        scores = jnp.where(seen_ref[...] > 0, scores, MASK_FILL)
        probabilities = jnp.exp(scores - logsum_ref[:, head * 128 : head * 128 + 1])
        grads = grad_ref[:, columns]
        probability_grad = across(grads, value_ref[...])
        delta = jnp.sum(probabilities * probability_grad, axis=-1, keepdims=True)
        score_grad = (probabilities * (probability_grad - delta)).astype(LOW)
        query_grad = jnp.dot(score_grad, key_ref[...], preferred_element_type=FULL) * score_scale
        key_grad = key_grad + along(score_grad, query_ref[:, columns])
        value_grad = value_grad + along(probabilities.astype(LOW), grads)
        query_out[:prompt_rows, columns] = turn_back(
            query_grad[:prompt_rows],
            cosine_ref[pl.ds(start, prompt_rows)],
            sine_ref[pl.ds(start, prompt_rows)],
        )
        query_out[prompt_rows:, columns] = turn_back(
            query_grad[prompt_rows:], cosine_ref[PROMPT_LEN:], sine_ref[PROMPT_LEN:]
        )
    pair_out[:, pl.ds(pl.multiple_of(step * HD, HD), HD)] = turn_back(
        key_grad * score_scale, cosine_ref[...], sine_ref[...]
    )
    pair_out[:, pl.ds(pl.multiple_of((HK + step) * HD, HD), HD)] = value_grad.astype(LOW)


def attend_back(place, queries, pairs, seen, logsum, grads, cosine, sine_part):
    rows, key_count = seen.shape
    group_heads = HQ // HK
    whole = lambda shape: pl.BlockSpec(shape, lambda j, p: (0, 0))
    return pl.pallas_call(
        attend_back_kernel,
        grid_spec=pltpu.PrefetchScalarGridSpec(
            num_scalar_prefetch=1,
            grid=(HK,),
            in_specs=[
                pl.BlockSpec((rows, group_heads * HD), lambda j, p: (0, j)),
                pl.BlockSpec((key_count, HD), lambda j, p: (0, j)),
                pl.BlockSpec((key_count, HD), lambda j, p: (0, HK + j)),
                whole((rows, key_count)),
                pl.BlockSpec((rows, group_heads * 128), lambda j, p: (0, j)),
                pl.BlockSpec((rows, group_heads * HD), lambda j, p: (0, j)),
                whole((key_count, HD // 2)),
                whole((key_count, HD // 2)),
            ],
            out_specs=[
                pl.BlockSpec((rows, group_heads * HD), lambda j, p: (0, j)),
                whole((key_count, 2 * HK * HD)),
            ],
        ),
        out_shape=[
            jax.ShapeDtypeStruct((rows, HQ * HD), LOW),
            jax.ShapeDtypeStruct((key_count, 2 * HK * HD), LOW),
        ],
        compiler_params=pltpu.CompilerParams(vmem_limit_bytes=VMEM_LIMIT),
        name="attend_back",
    )(place, queries, pairs, pairs, seen, logsum, grads, cosine, sine_part)


def weights_back_kernel(
    place_ref,
    query_ref,
    pair_ref,
    branch_ref,
    attended_ref,
    normed_ref,
    own_normed_ref,
    group_ref,
    own_ref,
    scale_ref,
    query_weight_ref,
    pair_weight_ref,
    query_term,
    pair_term,
    merge_term,
    back_out,
    pair_back_out,
    gain_out,
):
    rows = query_ref.shape[0]
    prompt_rows = rows - CONT
    start = pl.multiple_of(place_ref[0] * prompt_rows, 16)
    query_term[...] = along(own_normed_ref[...], query_ref[...]).astype(LOW)
    pair_term[...] = along(normed_ref[...], pair_ref[...]).astype(LOW)
    merge_term[...] = along(branch_ref[...], attended_ref[...]).astype(LOW)
    query_back = across(query_ref[...], query_weight_ref[...])
    pair_back = across(pair_ref[...], pair_weight_ref[...])
    own_values = own_ref[prompt_rows:].astype(FULL) * scale_ref[PROMPT_LEN:, :1]
    tail = query_back[prompt_rows:] + pair_back[PROMPT_LEN:]
    group_values = group_ref[...].astype(FULL) * scale_ref[:PROMPT_LEN, :1]
    own_prompt = own_ref[:prompt_rows].astype(FULL) * scale_ref[pl.ds(start, prompt_rows), :1]
    gain_out[...] = (
        jnp.sum(pair_back[:PROMPT_LEN] * group_values, axis=0, keepdims=True)
        + jnp.sum(query_back[:prompt_rows] * own_prompt, axis=0, keepdims=True)
        + jnp.sum(tail * own_values, axis=0, keepdims=True)
    )
    back_out[:prompt_rows] = query_back[:prompt_rows]
    back_out[prompt_rows:] = tail
    pair_back_out[...] = pair_back[:PROMPT_LEN].astype(LOW)


def weights_back(
    place, queries, pairs, branch, attended, normed, own_normed, group_rows, own_inputs, scale, weights
):
    rows, key_count = queries.shape[0], pairs.shape[0]
    wide, tile = HQ * HD, 256
    whole = lambda shape: pl.BlockSpec(shape, lambda j, p: (0, 0))
    tall = lambda count: pl.BlockSpec((count, tile), lambda j, p: (0, j))
    flat = lambda at: pl.BlockSpec((tile, wide), lambda j, p: (j, at))
    return pl.pallas_call(
        weights_back_kernel,
        grid_spec=pltpu.PrefetchScalarGridSpec(
            num_scalar_prefetch=1,
            grid=(D // tile,),
            in_specs=[
                whole((rows, wide)),
                whole((key_count, wide)),
                tall(rows),
                whole((rows, wide)),
                tall(key_count),
                tall(rows),
                tall(PROMPT_LEN),
                tall(rows),
                whole((key_count, 128)),
                flat(0),
                flat(1),
            ],
            out_specs=[flat(0), flat(0), flat(0), tall(rows), tall(PROMPT_LEN), tall(1)],
        ),
        out_shape=[
            jax.ShapeDtypeStruct((D, wide), LOW),
            jax.ShapeDtypeStruct((D, wide), LOW),
            jax.ShapeDtypeStruct((D, wide), LOW),
            jax.ShapeDtypeStruct((rows, D), FULL),
            jax.ShapeDtypeStruct((PROMPT_LEN, D), LOW),
            jax.ShapeDtypeStruct((1, D), FULL),
        ],
        compiler_params=pltpu.CompilerParams(vmem_limit_bytes=VMEM_LIMIT),
        name="weights_back",
    )(
        place,
        queries,
        pairs,
        branch,
        attended,
        normed,
        own_normed,
        group_rows,
        own_inputs,
        scale,
        weights,
        weights,
    )


def forward_back_kernel(
    activated_ref, grad_ref, gate_up_ref, down_ref, out_ref, gate_up_grad_ref
):
    own_hidden = activated_ref.shape[1]
    part = down_ref.shape[0] // 4

    @pl.loop(0, 4)
    def _(at):
        columns = pl.ds(pl.multiple_of(at * part, part), part)
        out_ref[:, columns] = across(activated_ref[...], down_ref[columns]).astype(LOW)

    piece = own_hidden // 2
    for at in range(2):
        columns = slice(at * piece, (at + 1) * piece)
        upper = slice(own_hidden + at * piece, own_hidden + (at + 1) * piece)
        activated_grad = jnp.dot(
            grad_ref[...], down_ref[:, columns], preferred_element_type=FULL
        )
        gate_values, up_values = gate_up_ref[:, columns], gate_up_ref[:, upper]
        gate_sigmoid = jax.nn.sigmoid(gate_values)
        gate_grad, up_grad = gate_backward(
            activated_grad, gate_values, up_values, gate_sigmoid, gate_values * gate_sigmoid
        )
        gate_up_grad_ref[:, columns] = gate_grad
        gate_up_grad_ref[:, upper] = up_grad


def forward_back(rows, activated, grads, gate_up, down_weight):
    count, own_hidden = activated.shape
    block = lambda width: pl.BlockSpec((rows, width), lambda j: (j, 0))
    return pl.pallas_call(
        forward_back_kernel,
        grid=(count // rows,),
        in_specs=[
            block(own_hidden),
            block(D),
            block(2 * own_hidden),
            pl.BlockSpec(down_weight.shape, lambda j: (0, 0)),
        ],
        out_specs=[block(D), block(2 * own_hidden)],
        out_shape=[
            jax.ShapeDtypeStruct((count, D), LOW),
            jax.ShapeDtypeStruct((count, 2 * own_hidden), LOW),
        ],
        compiler_params=pltpu.CompilerParams(vmem_limit_bytes=VMEM_LIMIT),
        name="forward_back",
    )(activated, grads, gate_up, down_weight)


def plane_back_kernel(
    plane,
    rows_ref,
    weight_ref,
    out_ref,
    weight,
    tiles,
    keep,
    give,
    core_in,
    plane_in,
    total,
    load_sem,
    tile_sem,
    core_send,
    core_recv,
    plane_send,
    plane_recv,
    out_sem,
):
    g = lax.axis_index("grp")
    d = lax.axis_index("dp")
    chips = plane // 2
    halves = plane == 8
    order = (3, 1, 2, 0) if halves else tuple(range(chips - 1, -1, -1))
    cut = D // 2
    half_of = (pl.ds(0, cut), pl.ds(cut, D - cut))

    barrier = pltpu.get_barrier_semaphore()
    for offset in range(1, plane):
        pl.semaphore_signal(
            barrier, inc=1, device_id=(g, flip(d, offset)), device_id_type=MESH
        )

    load = pltpu.make_async_copy(weight_ref, weight, load_sem.at[0])
    load.start()

    def tile_copy(turn):
        at = order[turn]
        return pltpu.make_async_copy(
            rows_ref.at[pl.ds(2 * at, 2)], tiles.at[turn % 2], tile_sem.at[turn % 2]
        )

    def core_copy(at):
        return remote(
            give.at[at], core_in.at[at], core_send.at[at], core_recv.at[at], (g, flip(d, 1))
        )

    def plane_copy(at):
        return remote(
            keep.at[at],
            plane_in.at[at],
            plane_send.at[at],
            plane_recv.at[at],
            (g, flip(d, 2 * at)),
        )

    def near_copy(part, relayed):
        there = part + 1
        return remote(
            keep.at[3 if relayed else there, :, half_of[part]],
            plane_in.at[1 if relayed else 0, :, half_of[part]],
            plane_send.at[2 * relayed + part],
            plane_recv.at[2 * relayed + part],
            (g, flip(d, 2 * there)),
        )

    def relay_copy(part):
        there = 2 - part
        return remote(
            keep.at[there, :, half_of[part]],
            plane_in.at[2, :, half_of[part]],
            plane_send.at[4 + part],
            plane_recv.at[4 + part],
            (g, flip(d, 2 * there)),
        )

    tile_copy(0).start()
    tile_copy(1).start()
    pl.semaphore_wait(barrier, plane - 1)
    load.wait()
    part_width = 512

    def product(turn, which, target):
        @pl.loop(0, D // part_width)
        def _(at):
            columns = pl.ds(pl.multiple_of(at * part_width, part_width), part_width)
            target[order[turn], :, columns] = across(
                tiles[turn % 2, which], weight[columns]
            ).astype(LOW)

    def add_into(at, other, first, count):
        step = 256

        @pl.loop(0, count // step)
        def _(k):
            here = pl.ds(pl.multiple_of(first + k * step, step), step)
            keep[at, :, here] = (
                keep[at, :, here].astype(FULL) + other(here).astype(FULL)
            ).astype(LOW)

    def settle(turn):
        at = order[turn]
        core_copy(at).wait_recv()
        add_into(at, lambda here: core_in[at, :, here], 0, D)
        if halves and at == 3:
            near_copy(0, True).start()
            near_copy(1, True).start()
        elif halves and at:
            near_copy(at - 1, False).start()
        elif at:
            plane_copy(at).start()

    for turn in range(chips):
        tile_copy(turn).wait()
        product(turn, 1, give)
        core_copy(order[turn]).start()
        if turn:
            settle(turn - 1)
        product(turn, 0, keep)
        if turn + 2 < chips:
            tile_copy(turn + 2).start()
        if halves and turn == chips - 1:
            for part in range(2):
                near_copy(part, True).wait_recv()
                add_into(
                    2 - part,
                    lambda here: plane_in[1, :, here],
                    part * cut,
                    cut,
                )
                relay_copy(part).start()
    settle(chips - 1)
    if halves:
        for part in range(2):
            near_copy(part, False).wait_recv()
            relay_copy(part).wait_recv()
        arrived = (0, 2)
    else:
        for at in range(1, chips):
            plane_copy(at).wait_recv()
        arrived = tuple(range(1, chips))

    @pl.loop(0, D // 256)
    def _(k):
        here = pl.ds(pl.multiple_of(k * 256, 256), 256)
        value = keep[0, :, here].astype(FULL)
        for at in arrived:
            value = value + plane_in[at, :, here].astype(FULL)
        total[:, here] = value

    out = pltpu.make_async_copy(total, out_ref, out_sem.at[0])
    out.start()
    for at in range(chips):
        core_copy(at).wait_send()
    if halves:
        for part in range(2):
            near_copy(part, False).wait_send()
            near_copy(part, True).wait_send()
            relay_copy(part).wait_send()
    else:
        for at in range(1, chips):
            plane_copy(at).wait_send()
    out.wait()


def plane_back(rows, gate_up_grad, gate_weight):
    plane = lax.axis_size("dp")
    chips = plane // 2
    inner = gate_up_grad.shape[1]
    anywhere = pl.BlockSpec(memory_space=pl.ANY)
    dma = pltpu.SemaphoreType.DMA
    return pl.pallas_call(
        functools.partial(plane_back_kernel, plane),
        out_shape=jax.ShapeDtypeStruct((rows, D), FULL),
        in_specs=[anywhere] * 2,
        out_specs=anywhere,
        scratch_shapes=[
            pltpu.VMEM((D, inner), LOW),
            pltpu.VMEM((2, 2, rows, inner), LOW),
            pltpu.VMEM((chips, rows, D), LOW),
            pltpu.VMEM((chips, rows, D), LOW),
            pltpu.VMEM((chips, rows, D), LOW),
            pltpu.VMEM((3 if plane == 8 else chips, rows, D), LOW),
            pltpu.VMEM((rows, D), FULL),
            dma((1,)),
            dma((2,)),
            dma((chips,)),
            dma((chips,)),
            dma((max(6, chips),)),
            dma((max(6, chips),)),
            dma((1,)),
        ],
        compiler_params=pltpu.CompilerParams(
            collective_id=2, has_side_effects=True, vmem_limit_bytes=VMEM_LIMIT
        ),
        name="plane_back",
    )(gate_up_grad.reshape(plane, rows, inner), gate_weight)


def plane_swap(block, offset):
    size = lax.axis_size("dp")
    return lax.ppermute(block, "dp", [(i, i ^ offset) for i in range(size)])


def plane_gather(block):
    mine = [block] + [plane_swap(block, o) for o in range(2, lax.axis_size("dp"), 2)]
    pairs = [(one, plane_swap(one, 1)) for one in mine]
    return jnp.concatenate([one for pair in pairs for one in pair], axis=0)


def line_scatter(term):
    return lax.psum_scatter(term, "grp", scatter_dimension=0, tiled=True)


def finish_kernel(
    lines,
    plane,
    query_ref,
    pair_ref,
    merge_ref,
    gain_ref,
    gate_ref,
    up_ref,
    down_ref,
    a_master,
    a_first,
    a_second,
    m_master,
    m_first,
    m_second,
    f_master,
    f_first,
    f_second,
    a_grad,
    a_update,
    a_first_new,
    a_second_new,
    m_grad,
    m_update,
    m_first_new,
    m_second_new,
    gain_out,
    f_grad,
    f_update,
    f_first_new,
    f_second_new,
    mine,
    core_in,
    plane_in,
    line_in,
    swap_in,
    state,
    made,
    a_state,
    a_made,
    gain_made,
    mine_sem,
    core_send,
    core_recv,
    plane_send,
    plane_recv,
    line_send,
    line_recv,
    swap_send,
    swap_recv,
    own_sem,
    state_sem,
    made_sem,
    a_sem,
    gain_sem,
):
    g = lax.axis_index("grp")
    d = lax.axis_index("dp")
    chips = plane // 2
    chip, core = lax.div(d, 2), lax.rem(d, 2)
    partner = d + 1 - 2 * core
    rows = a_master.shape[0]
    own_hidden = gate_ref.shape[2]
    width = core_in.shape[3]
    a_width, m_width = a_master.shape[1], m_master.shape[1]
    parts, begin = [], 0
    for ref in (query_ref, pair_ref, merge_ref, gain_ref):
        parts.append((ref, pl.ds(begin, ref.shape[4])))
        begin += ref.shape[4]

    barrier = pltpu.get_barrier_semaphore()
    for step in range(1, plane):
        there = lax.rem(d + step, plane)
        pl.semaphore_signal(barrier, inc=1, device_id=(g, there), device_id_type=MESH)
    for step in range(1, lines):
        there = lax.rem(g + step, lines)
        pl.semaphore_signal(barrier, inc=1, device_id=(there, d), device_id_type=MESH)
    pl.semaphore_wait(barrier, plane + lines - 2)

    def line_at(turn):
        return lax.rem(g + turn + 1, lines)

    def core_copy(turn, part):
        line = line_at(turn)
        ref, columns = parts[part]
        return remote(
            ref.at[line, :, 1 - core],
            core_in.at[line, :, :, columns],
            core_send.at[turn, part],
            core_recv.at[turn, part],
            (g, partner),
        )

    def mine_copy(turn, part):
        line = line_at(turn)
        ref, columns = parts[part]
        return pltpu.make_async_copy(
            ref.at[line, :, core], mine.at[turn % 2, :, :, columns], mine_sem.at[turn, part]
        )

    cut = width // 256 * 128
    columns_of = (pl.ds(0, cut), pl.ds(cut, width - cut))

    def plane_copy(turn, step):
        line = line_at(turn)
        there = lax.rem(chip + step, chips)
        return remote(
            core_in.at[line, there],
            plane_in.at[line, chip],
            plane_send.at[turn, step],
            plane_recv.at[turn, step],
            (g, 2 * there + core),
        )

    def near_copy(turn, part, relayed):
        line = line_at(turn)
        there = flip(chip, part + 1)
        owner = flip(chip, 3) if relayed else there
        return remote(
            core_in.at[line, owner, :, columns_of[part]],
            plane_in.at[line, 1 if relayed else 0, :, columns_of[part]],
            plane_send.at[turn, 2 * relayed + part],
            plane_recv.at[turn, 2 * relayed + part],
            (g, 2 * there + core),
        )

    def relay_copy(turn, part):
        line = line_at(turn)
        there = flip(chip, 2 - part)
        return remote(
            core_in.at[line, there, :, columns_of[part]],
            plane_in.at[line, 2, :, columns_of[part]],
            plane_send.at[turn, 4 + part],
            plane_recv.at[turn, 4 + part],
            (g, 2 * there + core),
        )

    def line_copy(turn):
        line = line_at(turn)
        return remote(
            core_in.at[line, chip],
            line_in.at[g],
            line_send.at[turn],
            line_recv.at[turn],
            (line, d),
        )

    forward_refs = (gate_ref, up_ref, down_ref)

    def swap_copy(step, part):
        there = lax.rem(d + step, plane)
        return remote(
            forward_refs[part].at[there],
            swap_in.at[part, d],
            swap_send.at[step, part],
            swap_recv.at[step, part],
            (g, there),
        )

    own_swap = [
        pltpu.make_async_copy(forward_refs[part].at[d], swap_in.at[part, d], own_sem.at[part])
        for part in range(3)
    ]

    def f_columns(turn):
        block = lax.rem(d + lax.div(turn, 3), plane)
        return pl.ds(
            pl.multiple_of(lax.rem(turn, 3) * FF + block * own_hidden, own_hidden), own_hidden
        )

    def state_copy(turn, which):
        slot = lax.rem(turn, 2)
        return pltpu.make_async_copy(
            (f_master, f_first, f_second)[which].at[:, f_columns(turn)],
            state.at[slot, which],
            state_sem.at[slot, which],
        )

    def made_copy(turn, which):
        slot = lax.rem(turn, 2)
        return pltpu.make_async_copy(
            made.at[slot, which],
            (f_grad, f_update, f_first_new, f_second_new)[which].at[:, f_columns(turn)],
            made_sem.at[slot, which],
        )

    slabs = (pl.ds(0, a_width), pl.ds(a_width, m_width))

    def a_state_copy(which, slab):
        source = ((a_master, a_first, a_second), (m_master, m_first, m_second))[slab][which]
        return pltpu.make_async_copy(
            source, a_state.at[which, :, slabs[slab]], a_sem.at[slab, which]
        )

    def a_made_copy(which, slab):
        target = (
            (a_grad, a_update, a_first_new, a_second_new),
            (m_grad, m_update, m_first_new, m_second_new),
        )[slab][which]
        return pltpu.make_async_copy(
            a_made.at[which, :, slabs[slab]], target, a_sem.at[slab, 3 + which]
        )

    every = range(len(parts))
    for turn in range(lines):
        for part in every:
            core_copy(turn, part).start()
            if turn < 2:
                mine_copy(turn, part).start()
        if turn == 0:
            for step in range(1, plane):
                for part in range(3):
                    swap_copy(step, part).start()
            for one in own_swap:
                one.start()
    for which in range(3):
        state_copy(0, which).start()
        for slab in range(2):
            a_state_copy(which, slab).start()

    tile = 896 if width % 896 == 0 else 128
    halves = plane == 8

    def add_into(line, there, other, columns=None):
        first, count = (0, width) if columns is None else columns
        step = tile if columns is None else 128

        @pl.loop(0, count // step)
        def _(at):
            here = pl.ds(pl.multiple_of(first + at * step, 128), step)
            total = core_in[line, there, :, here].astype(FULL) + other(here).astype(FULL)
            core_in[line, there, :, here] = total.astype(LOW)

    def near_start(turn):
        if halves:
            for relayed in (True, False):
                for part in range(2):
                    near_copy(turn, part, relayed).start()
        else:
            for step in range(1, chips):
                plane_copy(turn, step).start()

    for turn in range(lines):
        line = line_at(turn)
        for part in every:
            core_copy(turn, part).wait_recv()
            mine_copy(turn, part).wait()
        for step in range(1, chips + 1):
            there = lax.rem(chip + step, chips)
            add_into(
                line, there, lambda here, there=there, turn=turn: mine[turn % 2, there, :, here]
            )
        if turn + 2 < lines:
            for part in every:
                mine_copy(turn + 2, part).start()
        if turn < 2:
            near_start(turn)

    def pass_on(turn):
        line = line_at(turn)
        for part, columns in enumerate(((0, cut), (cut, width - cut))):
            near_copy(turn, part, True).wait_recv()
            add_into(
                line,
                flip(chip, 2 - part),
                lambda here, line=line: plane_in[line, 1, :, here],
                columns,
            )
            relay_copy(turn, part).start()

    def forward_turn(turn):
        slot = lax.rem(turn, 2)
        block = lax.rem(d + lax.div(turn, 3), plane)
        part = lax.rem(turn, 3)

        @pl.when(turn + 1 < 3 * plane)
        def _():
            for which in range(3):
                state_copy(turn + 1, which).start()

        @pl.when(turn > 1)
        def _():
            for which in range(4):
                made_copy(turn - 2, which).wait()

        for which in range(3):
            state_copy(turn, which).wait()

        @pl.loop(0, rows // 16)
        def _(at):
            rows_at = pl.ds(pl.multiple_of(at * 16, 16), 16)
            gradient = swap_in[part, block, rows_at].astype(FULL)
            update, first_new, second_new = adam_step(
                state[slot, 0, rows_at],
                state[slot, 1, rows_at],
                state[slot, 2, rows_at],
                gradient,
                WEIGHT_DECAY,
            )
            made[slot, 0, rows_at] = gradient
            made[slot, 1, rows_at] = update
            made[slot, 2, rows_at] = first_new
            made[slot, 3, rows_at] = second_new

        for which in range(4):
            made_copy(turn, which).start()

    def near_done(turn):
        if halves:
            pass_on(turn)
            for part in range(2):
                near_copy(turn, part, False).wait_recv()
        else:
            for step in range(1, chips):
                plane_copy(turn, step).wait_recv()
        if turn + 2 < lines:
            near_start(turn + 2)

    def line_done(turn):
        line = line_at(turn)
        if halves:
            for part in range(2):
                relay_copy(turn, part).wait_recv()
            arrived = (0, 2)
        else:
            arrived = tuple(lax.rem(chip + step, chips) for step in range(1, chips))

        @pl.loop(0, width // tile)
        def _(at):
            columns = pl.ds(pl.multiple_of(at * tile, tile), tile)
            total = core_in[line, chip, :, columns].astype(FULL)
            for block in arrived:
                total = total + plane_in[line, block, :, columns].astype(FULL)
            core_in[line, chip, :, columns] = total.astype(LOW)

        if turn < lines - 1:
            line_copy(turn).start()

    each = 3 * plane // lines

    def forward_some(turn):
        lax.fori_loop(turn * each, (turn + 1) * each, lambda k, c: (forward_turn(k), c)[1], 0)

    near_done(0)
    for turn in range(1, lines):
        if turn == 1:
            for one in own_swap:
                one.wait()
            for step in range(1, plane):
                for part in range(3):
                    swap_copy(step, part).wait_recv()
        near_done(turn)
        line_done(turn - 1)
        forward_some(turn - 1)
    line_done(lines - 1)
    forward_some(lines - 1)
    for which in range(4):
        for turn in (3 * plane - 2, 3 * plane - 1):
            made_copy(turn, which).wait()
    for turn in range(lines - 1):
        line_copy(turn).wait_recv()
    for which in range(3):
        for slab in range(2):
            a_state_copy(which, slab).wait()

    def owned(columns):
        total = core_in[g, chip, :, columns].astype(FULL)
        for step in range(1, lines):
            total = total + line_in[lax.rem(g + step, lines), :, columns].astype(FULL)
        return total

    @pl.loop(0, (a_width + m_width) // 256)
    def _(at):
        columns = pl.ds(pl.multiple_of(at * 256, 256), 256)
        gradient = owned(columns)
        update, first_new, second_new = adam_step(
            a_state[0, :, columns],
            a_state[1, :, columns],
            a_state[2, :, columns],
            gradient,
            WEIGHT_DECAY,
        )
        a_made[0, :, columns] = gradient
        a_made[1, :, columns] = update
        a_made[2, :, columns] = first_new
        a_made[3, :, columns] = second_new

    for which in range(4):
        for slab in range(2):
            a_made_copy(which, slab).start()
    gain_made[...] = owned(pl.ds(a_width + m_width, GAIN_PAD)).T[:8]
    gain_copy = pltpu.make_async_copy(gain_made, gain_out, gain_sem.at[0])
    gain_copy.start()
    for turn in range(lines):
        for part in every:
            core_copy(turn, part).wait_send()
        if halves:
            for part in range(2):
                near_copy(turn, part, False).wait_send()
                near_copy(turn, part, True).wait_send()
                relay_copy(turn, part).wait_send()
        else:
            for step in range(1, chips):
                plane_copy(turn, step).wait_send()
        if turn < lines - 1:
            line_copy(turn).wait_send()
    for step in range(1, plane):
        for part in range(3):
            swap_copy(step, part).wait_send()
    for which in range(4):
        for slab in range(2):
            a_made_copy(which, slab).wait()
    gain_copy.wait()


def finish(terms, forward_parts, attention, merge, forward):
    lines, plane = lax.axis_size("grp"), lax.axis_size("dp")
    chips = plane // 2
    rows, a_width = attention[0].shape
    m_width = merge[0].shape[1]
    own_hidden = forward_parts[0].shape[1]
    width = a_width + m_width + GAIN_PAD
    anywhere = pl.BlockSpec(memory_space=pl.ANY)
    dma = pltpu.SemaphoreType.DMA
    vmem = pltpu.VMEM

    def like(array):
        return jax.ShapeDtypeStruct(array.shape, array.dtype)

    return pl.pallas_call(
        functools.partial(finish_kernel, lines, plane),
        out_shape=(like(attention[0]),) * 4
        + (like(merge[0]),) * 4
        + (jax.ShapeDtypeStruct((8, rows), FULL),)
        + (like(forward[0]),) * 4,
        in_specs=[anywhere] * 16,
        out_specs=(anywhere,) * 13,
        scratch_shapes=[
            vmem((2, chips, rows, width), LOW),
            vmem((lines, chips, rows, width), LOW),
            vmem((lines, 3 if plane == 8 else chips, rows, width), LOW),
            vmem((lines, rows, width), LOW),
            vmem((3, plane, rows, own_hidden), LOW),
            vmem((2, 3, rows, own_hidden), FULL),
            vmem((2, 4, rows, own_hidden), FULL),
            vmem((3, rows, a_width + m_width), FULL),
            vmem((4, rows, a_width + m_width), FULL),
            vmem((8, rows), FULL),
            dma((lines, 4)),
            dma((lines, 4)),
            dma((lines, 4)),
            dma((lines, max(6, chips))),
            dma((lines, max(6, chips))),
            dma((lines,)),
            dma((lines,)),
            dma((plane, 3)),
            dma((plane, 3)),
            dma((3,)),
            dma((2, 3)),
            dma((2, 4)),
            dma((2, 7)),
            dma((1,)),
        ],
        compiler_params=pltpu.CompilerParams(
            collective_id=1, has_side_effects=True, vmem_limit_bytes=VMEM_LIMIT
        ),
        name="finish",
    )(
        *(term.reshape(lines, chips, 2, rows, term.shape[1]) for term in terms),
        *(part.reshape(plane, rows, -1) for part in forward_parts),
        *attention,
        *merge,
        *forward,
    )


def body(
    hidden,
    cotangent,
    segment_ids,
    continuation_prompt,
    gain_master,
    gain_first,
    gain_second,
    attention_master,
    attention_first,
    attention_second,
    merge_master,
    merge_first,
    merge_second,
    feedforward_master,
    feedforward_first,
    feedforward_second,
):
    group_index = lax.axis_index("grp")
    dp_size = lax.axis_size("dp")
    row_count = hidden.shape[2]
    prompt_rows = row_count - CONT
    qkv_width = (HQ + 2 * HK) * HD
    own_rows = feedforward_master.shape[0]
    own_hidden = FF // dp_size
    own_inputs = hidden.reshape(row_count, D)

    gain_columns = jnp.pad(gain_master.T, ((0, 0), (0, GAIN_PAD - 2)))
    weight_low = jnp.concatenate(
        [attention_master.astype(LOW), merge_master.astype(LOW), gain_columns.astype(LOW)], axis=1
    )
    weights, group_rows, gate_rows, down_rows = gather_start(
        weight_low, own_inputs, feedforward_master.astype(LOW)
    )
    weights, late_cotangent = lax.optimization_barrier((weights, cotangent))
    weights = weights.reshape(D, -1)
    merge_weight = weights[:, qkv_width : qkv_width + D]
    gain_float = weights[:, qkv_width + D : qkv_width + D + 2].astype(FULL).T
    gate_weight = lax.all_gather(
        gate_rows.reshape(dp_size * own_rows, 2 * own_hidden), "grp", axis=0, tiled=True
    )
    gate_weight, down_rows = lax.optimization_barrier((gate_weight, down_rows))
    down_weight = lax.all_gather(
        down_rows.reshape(dp_size * own_rows, own_hidden), "grp", axis=0, tiled=True
    )
    down_grad = plane_gather(late_cotangent.reshape(row_count, D))

    segment_row = segment_ids[0]
    source_row = continuation_prompt[0]
    prompt_positions, follow_positions = segment_positions(segment_row, source_row)
    cosine, sine_part = angle_table(jnp.concatenate([prompt_positions, follow_positions[0]]))

    place = jnp.reshape(group_index, (1,)).astype(jnp.int32)
    group_rows = group_rows.reshape(PROMPT_LEN, D)
    queries, pairs, key_normed, normed, key_scale = project_heads(
        place, group_rows, own_inputs, gain_float[:1], cosine, sine_part, weights
    )
    inputs = own_inputs.astype(FULL)
    first_scale = norm_scale(inputs)

    row_index = jnp.arange(row_count, dtype=jnp.int32)
    is_prompt = row_index < prompt_rows
    global_row = group_index * prompt_rows + jnp.minimum(row_index, prompt_rows - 1)
    own_segment = lax.dynamic_slice_in_dim(segment_row, group_index * prompt_rows, prompt_rows)
    query_segment = jnp.concatenate([own_segment, jnp.broadcast_to(source_row, (CONT,))])
    key_index = jnp.arange(PROMPT_LEN, dtype=jnp.int32)
    prompt_seen = (segment_row[None, :] == query_segment[:, None]) & (
        (key_index[None, :] <= global_row[:, None]) | ~is_prompt[:, None]
    )
    follow_seen = (~is_prompt)[:, None] & (
        jnp.arange(CONT, dtype=jnp.int32)[None, :] <= (row_index - prompt_rows)[:, None]
    )
    visible = jnp.concatenate([prompt_seen, follow_seen], axis=1)
    seen = visible.astype(FULL)
    attended, row_logsum = attend(queries, pairs, seen)
    middle = inputs + contract(attended, merge_weight, 1, 1)
    second_scale = norm_scale(middle)
    normed_two = (middle * second_scale * gain_float[1]).astype(LOW)
    grad_rows = cotangent.reshape(row_count, D).astype(FULL)

    normed_two, down_grad = lax.optimization_barrier((normed_two, down_grad))
    normed_all = plane_gather(normed_two)
    gate_up = jnp.dot(normed_all, gate_weight, preferred_element_type=FULL)
    gate_values = gate_up[:, :own_hidden]
    up_values = gate_up[:, own_hidden:]
    gate_sigmoid, gate_silu, activated = gate_parts(gate_values, up_values)
    down_term = contract(down_grad, activated, 0, 0).astype(LOW)
    down_term, down_weight = lax.optimization_barrier((down_term, down_weight))
    out_term, gate_up_grad = forward_back(row_count, activated, down_grad, gate_up, down_weight)
    down_part = line_scatter(down_term)
    gate_term = contract(normed_all, gate_up_grad[:, :own_hidden], 0, 0).astype(LOW)
    up_term = contract(normed_all, gate_up_grad[:, own_hidden:], 0, 0).astype(LOW)
    gate_up_grad, gate_term, up_term, down_part = lax.optimization_barrier(
        (gate_up_grad, gate_term, up_term, down_part)
    )
    gate_part = line_scatter(gate_term)
    up_part = line_scatter(up_term)
    normed_two_grad = plane_back(row_count, gate_up_grad, gate_weight)
    normed_two_grad, out_term = lax.optimization_barrier((normed_two_grad, out_term))
    out_chunks = out_term.reshape(dp_size, row_count, D)
    out_swapped = [plane_swap(out_chunks[offset + 1], 1) for offset in range(0, dp_size, 2)]
    middle_grad = grad_rows + norm_back(middle, second_scale, gain_float[1], normed_two_grad)
    gain_two_part = jnp.sum(normed_two_grad * middle * second_scale, axis=0)
    branch_grad = middle_grad.astype(LOW)
    attended_grad = contract(branch_grad, merge_weight, 1, 0).astype(LOW)
    attended_grad, out_swapped = lax.optimization_barrier((attended_grad, out_swapped))
    out_sums = [
        out_chunks[2 * at].astype(FULL) + one.astype(FULL) for at, one in enumerate(out_swapped)
    ]
    out_low = [one.astype(LOW) for one in out_sums[1:]]
    attended_grad, out_low = lax.optimization_barrier((attended_grad, out_low))
    out_arrived = [plane_swap(one, 2 * at + 2) for at, one in enumerate(out_low)]
    query_project, pair_project = attend_back(
        place, queries, pairs, seen, row_logsum, attended_grad, cosine, sine_part
    )
    query_term, pair_term, merge_term, normed_grad, pair_back, gain_one_part = weights_back(
        place,
        query_project,
        pair_project,
        branch_grad,
        attended,
        key_normed,
        normed,
        group_rows,
        own_inputs,
        key_scale,
        weights,
    )
    gain_term = jnp.pad(
        jnp.stack([gain_one_part[0], gain_two_part], axis=1), ((0, 0), (0, GAIN_PAD - 2))
    )
    pair_back, up_part, out_arrived = lax.optimization_barrier((pair_back, up_part, out_arrived))
    result = middle + out_sums[0]
    for one in out_arrived:
        result = result + one.astype(FULL)
    block_output = result.astype(LOW).reshape(hidden.shape)
    pair_sum = line_scatter(pair_back)
    finished = finish(
        (query_term, pair_term, merge_term, gain_term.astype(LOW)),
        (gate_part, up_part, down_part),
        (attention_master, attention_first, attention_second),
        (merge_master, merge_first, merge_second),
        (feedforward_master, feedforward_first, feedforward_second),
    )
    gain_grad = finished[8][:2]
    pair_sum, gain_grad = lax.optimization_barrier((pair_sum, gain_grad))
    pair_sum = pair_sum.astype(FULL)
    normed_grad = normed_grad + jnp.pad(pair_sum, ((0, CONT), (0, 0)))
    input_grad = (middle_grad + norm_back(inputs, first_scale, gain_float[0], normed_grad)).reshape(
        hidden.shape
    )
    gain_new = adam_step(gain_master, gain_first, gain_second, gain_grad, 0.0)
    return (
        block_output,
        input_grad,
        gain_grad,
        *gain_new,
        *finished[:8],
        *finished[9:],
    )


def solution(mesh):
    tokens = P("dp", "grp", None, None)
    gains = P(None, ("grp", "dp"))
    matrix = P(("grp", "dp"), None)
    return jax.shard_map(
        body,
        mesh=mesh,
        in_specs=(tokens, tokens, P("dp", None), P("dp", "grp")) + (gains,) * 3 + (matrix,) * 9,
        out_specs=(tokens, tokens) + (gains,) * 4 + (matrix,) * 12,
        check_vma=False,
    )
```

```python
import functools

import jax
import jax.numpy as jnp
from jax import lax
from jax.experimental import pallas as pl
from jax.experimental.pallas import tpu as pltpu
from jax.sharding import PartitionSpec as P

D = 2048
FF = 8192
HQ = 8
HK = 4
HD = 256
PROMPT_LEN = 1024
PROMPTS = 4
CONT = 64
STEP = 10
GAIN_PAD = 128

EPS_NORM = 1e-06
ROPE_THETA = 1000042.0
MASK_FILL = -1e30
BETA_ONE = 0.9
BETA_TWO = 0.95
ADAM_EPS = 1e-08
LEARN_RATE = 0.02
WEIGHT_DECAY = 0.1
LOW = jnp.bfloat16
FULL = jnp.float32
MESH = pl.DeviceIdType.MESH


def contract(left, right, left_axis, right_axis):
    return lax.dot_general(
        left, right, (((left_axis,), (right_axis,)), ((), ())), preferred_element_type=FULL
    )


def angle_table(positions):
    inverse_rate = ROPE_THETA ** (-(jnp.arange(HD // 2, dtype=FULL) * 2.0) / HD)
    angles = positions.astype(FULL)[..., None] * inverse_rate
    return (jnp.cos(angles), jnp.sin(angles))


def segment_positions(segment_row, source_row):
    labels = jnp.arange(PROMPTS, dtype=jnp.int32)
    member = (segment_row[None, :] == labels[:, None]).astype(jnp.int32)
    lengths = jnp.sum(member, axis=1, dtype=jnp.int32)
    starts = jnp.sum(
        jnp.where(labels[None, :] < labels[:, None], lengths[None, :], 0), axis=1, dtype=jnp.int32
    )
    prompt_index = jnp.arange(segment_row.shape[0], dtype=jnp.int32)
    prompt_positions = prompt_index - jnp.sum(member * starts[:, None], axis=0, dtype=jnp.int32)
    source_length = jnp.sum(
        (source_row[:, None] == labels[None, :]).astype(jnp.int32) * lengths[None, :],
        axis=1,
        dtype=jnp.int32,
    )
    follow_positions = source_length[:, None] + jnp.arange(CONT, dtype=jnp.int32)[None, :]
    return (prompt_positions, follow_positions)


def norm_scale(values):
    return lax.rsqrt(jnp.mean(values * values, axis=-1, keepdims=True) + EPS_NORM)


def norm_back(values, row_scale, gain_row, normed_grad):
    scaled = normed_grad * gain_row
    return row_scale * scaled - values * row_scale**3 * jnp.mean(
        scaled * values, axis=-1, keepdims=True
    )


def adam_step(master, first_moment, second_moment, gradient, decay_rate):
    first_new = BETA_ONE * first_moment + (1.0 - BETA_ONE) * gradient
    second_new = BETA_TWO * second_moment + (1.0 - BETA_TWO) * gradient * gradient
    correct_one = 1.0 - BETA_ONE**STEP
    correct_two = 1.0 - BETA_TWO**STEP
    update = first_new / correct_one / (jnp.sqrt(second_new / correct_two) + ADAM_EPS)
    return (-LEARN_RATE * (update + decay_rate * master), first_new, second_new)


def gate_parts(gate_values, up_values):
    gate_sigmoid = jax.nn.sigmoid(gate_values)
    gate_silu = gate_values * gate_sigmoid
    return (gate_sigmoid, gate_silu, (gate_silu * up_values).astype(LOW))


def gate_backward(activated_grad, gate_values, up_values, gate_sigmoid, gate_silu):
    gate_grad = (
        activated_grad * up_values * gate_sigmoid * (1.0 + gate_values * (1.0 - gate_sigmoid))
    ).astype(LOW)
    up_grad = (activated_grad * gate_silu).astype(LOW)
    return (gate_grad, up_grad)


def flip(index, bits):
    bit = 1
    while bit <= bits:
        if bits & bit:
            index = index + bit - 2 * bit * lax.rem(index // bit, 2)
        bit *= 2
    return index


def remote(source, target, send, recv, there):
    return pltpu.make_async_remote_copy(
        src_ref=source,
        dst_ref=target,
        send_sem=send,
        recv_sem=recv,
        device_id=there,
        device_id_type=MESH,
    )


def gather_kernel(
    lines,
    plane,
    prompt_rows,
    weight_ref,
    hidden_ref,
    forward_ref,
    weights_ref,
    rows_ref,
    gate_ref,
    first_ref,
    second_ref,
    local_sem,
    line_send,
    line_recv,
    rows_send,
    rows_recv,
    first_send,
    first_recv,
    near_send,
    near_recv,
    half_send,
    half_recv,
    core_send,
    core_recv,
    swap_send,
    swap_recv,
):
    g = lax.axis_index("grp")
    d = lax.axis_index("dp")
    evens = range(0, plane, 2)
    forward_halves = plane == 8
    near = (2, 4) if forward_halves else tuple(evens[1:])
    width = weight_ref.shape[1]
    cut = (width // 256) * 128

    barrier = pltpu.get_barrier_semaphore()
    for offset in range(1, plane):
        pl.semaphore_signal(barrier, inc=1, device_id=(g, flip(d, offset)), device_id_type=MESH)

    for step in range(1, lines):
        there = lax.rem(g + step, lines)
        pl.semaphore_signal(barrier, inc=1, device_id=(there, d), device_id_type=MESH)
    pl.semaphore_wait(barrier, plane + lines - 2)

    copy = remote
    own_rows = hidden_ref.at[pl.ds(0, prompt_rows)]

    def line_weight(way, step):
        block = g - step + 1 if way == 0 else g + step - 1
        source = weight_ref if step == 1 else weights_ref.at[block, d]
        return copy(
            source,
            weights_ref.at[block, d],
            line_send.at[way, step],
            line_recv.at[way, step],
            (g + 1 if way == 0 else g - 1, d),
        )

    def line_rows(way, step):
        block = g - step + 1 if way == 0 else g + step - 1
        source = own_rows if step == 1 else rows_ref.at[block]
        return copy(
            source,
            rows_ref.at[block],
            rows_send.at[way, step],
            rows_recv.at[way, step],
            (g + 1 if way == 0 else g - 1, d),
        )

    def line_first(way, step):
        block = g - step + 1 if way == 0 else g + step - 1
        return copy(
            first_ref.at[block],
            first_ref.at[block],
            first_send.at[way, step],
            first_recv.at[way, step],
            (g + 1 if way == 0 else g - 1, d),
        )

    def sends(way, step):
        if way == 0:
            return (g < lines - 1) & (g >= step - 1)
        return (g > 0) & (g + step - 1 < lines)

    def receives(way, step):
        return g >= step if way == 0 else g + step < lines

    def near_copy(block, offset, own):
        source = weight_ref if own else weights_ref.at[block, d]
        at = near.index(offset)
        return copy(
            source,
            weights_ref.at[block, d],
            near_send.at[block, at],
            near_recv.at[block, at],
            (g, flip(d, offset)),
        )

    def half_copy(block, part):
        columns = pl.ds(0, cut) if part == 0 else pl.ds(cut, width - cut)
        origin = flip(d, 2) if part == 0 else flip(d, 4)
        there = flip(d, 4) if part == 0 else flip(d, 2)
        piece = weights_ref.at[block, origin, :, columns]
        return copy(
            piece, piece, half_send.at[block, part], half_recv.at[block, part], (g, there)
        )

    def core_copy(block, offset, own=False):
        source = weight_ref if own else weights_ref.at[block, flip(d, offset)]
        return copy(
            source,
            weights_ref.at[block, flip(d, offset)],
            core_send.at[block, offset // 2],
            core_recv.at[block, offset // 2],
            (g, flip(d, 1)),
        )

    half_hidden = second_ref.shape[2]
    own_hidden = 2 * half_hidden

    def swap_piece(owner, part, source_index):
        if part < 2:
            source = forward_ref.at[:, pl.ds(part * FF + owner * own_hidden, own_hidden)]
            return source, gate_ref.at[source_index, :, pl.ds(part * own_hidden, own_hidden)]
        start = 2 * FF + owner * own_hidden + (part - 2) * half_hidden
        source = forward_ref.at[:, pl.ds(start, half_hidden)]
        return source, first_ref.at[g, source_index] if part == 2 else second_ref.at[source_index]

    def swap_copy(offset, part):
        source, target = swap_piece(flip(d, offset), part, d)
        return copy(
            source,
            target,
            swap_send.at[offset, part],
            swap_recv.at[offset, part],
            (g, flip(d, offset)),
        )

    locals_ = (
        pltpu.make_async_copy(weight_ref, weights_ref.at[g, d], local_sem.at[0]),
        pltpu.make_async_copy(own_rows, rows_ref.at[g], local_sem.at[1]),
        *(
            pltpu.make_async_copy(*swap_piece(d, part, d), local_sem.at[2 + part])
            for part in range(4)
        ),
    )

    def launch(block, own):
        for offset in near:
            near_copy(block, offset, own).start()
        core_copy(block, 0, own).start()

    def relay(block):
        for offset in near:
            near_copy(block, offset, False).wait_recv()
            core_copy(block, offset).start()
        if forward_halves:
            half_copy(block, 0).start()
            half_copy(block, 1).start()

    def finish(block):
        if forward_halves:
            half_copy(block, 0).wait_recv()
            half_copy(block, 1).wait_recv()
            core_copy(block, 6).start()

    def both(step, act):
        for way in (0, 1):
            pl.when(receives(way, step))(
                lambda way=way: act(g - step if way == 0 else g + step)
            )

    def take_rows(step):
        for way in (0, 1):

            @pl.when(receives(way, step))
            def _(way=way):
                line_rows(way, step).wait_recv()

            if step + 1 < lines:
                pl.when(sends(way, step + 1))(
                    lambda way=way: line_rows(way, step + 1).start()
                )

    for way in (0, 1):
        pl.when(sends(way, 1))(lambda way=way: line_weight(way, 1).start())
    launch(g, True)
    for one in locals_:
        one.start()
    for step in range(1, lines):
        for way in (0, 1):

            @pl.when(receives(way, step))
            def _(way=way, step=step):
                line_weight(way, step).wait_recv()

            if step + 1 < lines:
                pl.when(sends(way, step + 1))(
                    lambda way=way, step=step: line_weight(way, step + 1).start()
                )
            else:
                pl.when(sends(way, 1))(lambda way=way: line_rows(way, 1).start())

        both(step, lambda block: launch(block, False))
        if step == 1:
            relay(g)
            for offset in range(1, plane):
                for part in (2, 0, 1, 3):
                    swap_copy(offset, part).start()
    for step in range(1, lines):
        take_rows(step)
        if step == lines - 1:
            locals_[4].wait()
            for offset in range(1, plane):
                swap_copy(offset, 2).wait_recv()
            for way in (0, 1):
                pl.when(sends(way, 1))(lambda way=way: line_first(way, 1).start())
        both(step, relay)
        if step == 1:
            finish(g)
        elif step < lines - 1:
            both(step - 1, finish)
    for step in range(1, lines):
        for way in (0, 1):

            @pl.when(receives(way, step))
            def _(way=way, step=step):
                line_first(way, step).wait_recv()

            if step + 1 < lines:
                pl.when(sends(way, step + 1))(
                    lambda way=way, step=step: line_first(way, step + 1).start()
                )
        if step == 1:
            both(lines - 2, finish)
    both(lines - 1, finish)

    def drain(block):
        for offset in evens:
            core_copy(block, offset).wait()
        for offset in near:
            near_copy(block, offset, False).wait_send()
        if forward_halves:
            half_copy(block, 0).wait_send()
            half_copy(block, 1).wait_send()

    drain(g)
    for step in range(1, lines):
        for way in (0, 1):
            pl.when(receives(way, step))(
                lambda way=way, step=step: drain(g - step if way == 0 else g + step)
            )

            @pl.when(sends(way, step))
            def _(way=way, step=step):
                line_weight(way, step).wait_send()
                line_rows(way, step).wait_send()
                line_first(way, step).wait_send()

    for offset in range(1, plane):
        for part in (0, 1, 3):
            swap_copy(offset, part).wait()
        swap_copy(offset, 2).wait_send()
    for at, one in enumerate(locals_):
        if at != 4:
            one.wait()


def gather_start(weight, hidden, forward):
    lines, plane = lax.axis_size("grp"), lax.axis_size("dp")
    prompt_rows = PROMPT_LEN // lines
    own_rows, width = weight.shape
    anywhere = pl.BlockSpec(memory_space=pl.ANY)
    dma = pltpu.SemaphoreType.DMA
    near_count = 2 if plane == 8 else plane // 2 - 1
    pairs = (
        (2, lines),
        (2, lines),
        (2, lines),
        (2, lines),
        (2, lines),
        (2, lines),
        (lines, near_count),
        (lines, near_count),
        (lines, 2),
        (lines, 2),
        (lines, plane // 2),
        (lines, plane // 2),
        (plane, 4),
        (plane, 4),
    )
    own_hidden = FF // plane
    return pl.pallas_call(
        functools.partial(gather_kernel, lines, plane, prompt_rows),
        out_shape=(
            jax.ShapeDtypeStruct((lines, plane, own_rows, width), weight.dtype),
            jax.ShapeDtypeStruct((lines, prompt_rows, D), hidden.dtype),
            jax.ShapeDtypeStruct((plane, own_rows, 2 * own_hidden), forward.dtype),
            jax.ShapeDtypeStruct((lines, plane, own_rows, own_hidden // 2), forward.dtype),
            jax.ShapeDtypeStruct((plane, own_rows, own_hidden // 2), forward.dtype),
        ),
        in_specs=[anywhere] * 3,
        out_specs=(anywhere,) * 5,
        scratch_shapes=[dma((6,))] + [dma(shape) for shape in pairs],
        compiler_params=pltpu.CompilerParams(collective_id=0, has_side_effects=True),
        name="gather_start",
    )(weight, hidden, forward)


def project_kernel(
    place_ref,
    group_ref,
    own_ref,
    gain_ref,
    cosine_ref,
    sine_ref,
    weight_ref,
    query_ref,
    pair_ref,
    normed_ref,
    own_normed_ref,
    scale_ref,
):
    step = pl.program_id(0)
    own_rows = own_ref.shape[0]
    prompt_rows = own_rows - CONT
    start = pl.multiple_of(place_ref[0] * prompt_rows, 16)
    tile = 32

    def norm_tile(values, at):
        values = values.astype(FULL)
        scale = lax.rsqrt(jnp.mean(values * values, axis=-1, keepdims=True) + EPS_NORM)
        normed_ref[pl.ds(at, tile)] = (values * scale * gain_ref[...]).astype(LOW)
        scale_ref[pl.ds(at, tile)] = jnp.broadcast_to(scale, (tile, 128))

    @pl.when(step == 0)
    def _():
        @pl.loop(0, PROMPT_LEN // tile)
        def _(at):
            first = pl.multiple_of(at * tile, tile)
            norm_tile(group_ref[pl.ds(first, tile)], first)

        for at in range(0, CONT, tile):
            norm_tile(own_ref[prompt_rows + at : prompt_rows + at + tile], PROMPT_LEN + at)
        own_normed_ref[:prompt_rows] = normed_ref[pl.ds(start, prompt_rows)]
        own_normed_ref[prompt_rows:] = normed_ref[PROMPT_LEN:]

    def turn(values, cosine, sine_part):
        front, back = values[:, : HD // 2], values[:, HD // 2 :]
        return front * cosine - back * sine_part, back * cosine + front * sine_part

    def project(rows):
        return jnp.dot(rows, weight_ref[...], preferred_element_type=FULL)

    @pl.when(step < HQ)
    def _():
        for first, count, table in ((0, prompt_rows, start), (prompt_rows, CONT, PROMPT_LEN)):
            values = project(own_normed_ref[first : first + count])
            front, back = turn(
                values, cosine_ref[pl.ds(table, count)], sine_ref[pl.ds(table, count)]
            )
            query_ref[first : first + count, : HD // 2] = front.astype(LOW)
            query_ref[first : first + count, HD // 2 :] = back.astype(LOW)

    key_count = PROMPT_LEN + CONT
    part = key_count // 4

    @pl.when((step >= HQ) & (step < HQ + HK))
    def _():
        @pl.loop(0, 4)
        def _(at):
            rows = pl.ds(pl.multiple_of(at * part, 16), part)
            front, back = turn(project(normed_ref[rows]), cosine_ref[rows], sine_ref[rows])
            pair_ref[rows, : HD // 2] = front.astype(LOW)
            pair_ref[rows, HD // 2 :] = back.astype(LOW)

    @pl.when(step >= HQ + HK)
    def _():
        @pl.loop(0, 4)
        def _(at):
            rows = pl.ds(pl.multiple_of(at * part, 16), part)
            pair_ref[rows] = project(normed_ref[rows]).astype(LOW)


VMEM_LIMIT = 60 * 2**20


def project_heads(place, group_rows, own_inputs, gain_row, cosine, sine_part, weights):
    own_rows = own_inputs.shape[0]
    key_count = PROMPT_LEN + CONT
    whole = lambda shape: pl.BlockSpec(shape, lambda j, p: (0, 0))
    return pl.pallas_call(
        project_kernel,
        grid_spec=pltpu.PrefetchScalarGridSpec(
            num_scalar_prefetch=1,
            grid=(HQ + 2 * HK,),
            in_specs=[
                whole((PROMPT_LEN, D)),
                whole((own_rows, D)),
                whole((1, D)),
                whole((key_count, HD // 2)),
                whole((key_count, HD // 2)),
                pl.BlockSpec((D, HD), lambda j, p: (0, j)),
            ],
            out_specs=[
                pl.BlockSpec((own_rows, HD), lambda j, p: (0, jnp.minimum(j, HQ - 1))),
                pl.BlockSpec((key_count, HD), lambda j, p: (0, jnp.maximum(j - HQ, 0))),
                whole((key_count, D)),
                whole((own_rows, D)),
                whole((key_count, 128)),
            ],
        ),
        out_shape=[
            jax.ShapeDtypeStruct((own_rows, HQ * HD), LOW),
            jax.ShapeDtypeStruct((key_count, 2 * HK * HD), LOW),
            jax.ShapeDtypeStruct((key_count, D), LOW),
            jax.ShapeDtypeStruct((own_rows, D), LOW),
            jax.ShapeDtypeStruct((key_count, 128), FULL),
        ],
        compiler_params=pltpu.CompilerParams(vmem_limit_bytes=VMEM_LIMIT),
        name="project_heads",
    )(place, group_rows, own_inputs, gain_row, cosine, sine_part, weights)


def across(left, right):
    return lax.dot_general(left, right, (((1,), (1,)), ((), ())), preferred_element_type=FULL)


def along(left, right):
    return lax.dot_general(left, right, (((0,), (0,)), ((), ())), preferred_element_type=FULL)


def attend_kernel(query_ref, key_ref, value_ref, seen_ref, attended_ref, logsum_ref):
    group_heads = HQ // HK
    for head in range(group_heads):
        columns = slice(head * HD, (head + 1) * HD)
        scores = across(query_ref[:, columns], key_ref[...]) * HD ** (-0.5)
        scores = jnp.where(seen_ref[...] > 0, scores, MASK_FILL)
        peak = jnp.max(scores, axis=-1, keepdims=True)
        unnormed = jnp.exp(scores - peak)
        total = jnp.sum(unnormed, axis=-1, keepdims=True)
        low = (unnormed / total).astype(LOW)
        attended_ref[:, columns] = jnp.dot(
            low, value_ref[...], preferred_element_type=FULL
        ).astype(LOW)
        logsum_ref[:, head * 128 : (head + 1) * 128] = jnp.broadcast_to(
            peak + jnp.log(total), (query_ref.shape[0], 128)
        )


def attend(queries, pairs, seen):
    rows, key_count = seen.shape
    group_heads = HQ // HK
    return pl.pallas_call(
        attend_kernel,
        grid=(HK,),
        in_specs=[
            pl.BlockSpec((rows, group_heads * HD), lambda j: (0, j)),
            pl.BlockSpec((key_count, HD), lambda j: (0, j)),
            pl.BlockSpec((key_count, HD), lambda j: (0, HK + j)),
            pl.BlockSpec((rows, key_count), lambda j: (0, 0)),
        ],
        out_specs=[
            pl.BlockSpec((rows, group_heads * HD), lambda j: (0, j)),
            pl.BlockSpec((rows, group_heads * 128), lambda j: (0, j)),
        ],
        out_shape=[
            jax.ShapeDtypeStruct((rows, HQ * HD), LOW),
            jax.ShapeDtypeStruct((rows, HQ * 128), FULL),
        ],
        compiler_params=pltpu.CompilerParams(vmem_limit_bytes=VMEM_LIMIT),
        name="attend",
    )(queries, pairs, pairs, seen)


def attend_back_kernel(
    place_ref,
    query_ref,
    key_ref,
    value_ref,
    seen_ref,
    logsum_ref,
    grad_ref,
    cosine_ref,
    sine_ref,
    query_out,
    pair_out,
):
    step = pl.program_id(0)
    group_heads = HQ // HK
    rows = query_ref.shape[0]
    prompt_rows = rows - CONT
    start = pl.multiple_of(place_ref[0] * prompt_rows, 16)
    score_scale = HD ** (-0.5)
    key_grad = value_grad = 0.0

    def turn_back(values, cosine, sine_part):
        front, back = values[:, : HD // 2], values[:, HD // 2 :]
        return jnp.concatenate(
            [front * cosine + back * sine_part, back * cosine - front * sine_part], axis=1
        ).astype(LOW)

    for head in range(group_heads):
        columns = slice(head * HD, (head + 1) * HD)
        scores = across(query_ref[:, columns], key_ref[...]) * score_scale
        scores = jnp.where(seen_ref[...] > 0, scores, MASK_FILL)
        probabilities = jnp.exp(scores - logsum_ref[:, head * 128 : head * 128 + 1])
        grads = grad_ref[:, columns]
        probability_grad = across(grads, value_ref[...])
        delta = jnp.sum(probabilities * probability_grad, axis=-1, keepdims=True)
        score_grad = (probabilities * (probability_grad - delta)).astype(LOW)
        query_grad = jnp.dot(score_grad, key_ref[...], preferred_element_type=FULL) * score_scale
        key_grad = key_grad + along(score_grad, query_ref[:, columns])
        value_grad = value_grad + along(probabilities.astype(LOW), grads)
        query_out[:prompt_rows, columns] = turn_back(
            query_grad[:prompt_rows],
            cosine_ref[pl.ds(start, prompt_rows)],
            sine_ref[pl.ds(start, prompt_rows)],
        )
        query_out[prompt_rows:, columns] = turn_back(
            query_grad[prompt_rows:], cosine_ref[PROMPT_LEN:], sine_ref[PROMPT_LEN:]
        )
    pair_out[:, pl.ds(pl.multiple_of(step * HD, HD), HD)] = turn_back(
        key_grad * score_scale, cosine_ref[...], sine_ref[...]
    )
    pair_out[:, pl.ds(pl.multiple_of((HK + step) * HD, HD), HD)] = value_grad.astype(LOW)


def attend_back(place, queries, pairs, seen, logsum, grads, cosine, sine_part):
    rows, key_count = seen.shape
    group_heads = HQ // HK
    whole = lambda shape: pl.BlockSpec(shape, lambda j, p: (0, 0))
    return pl.pallas_call(
        attend_back_kernel,
        grid_spec=pltpu.PrefetchScalarGridSpec(
            num_scalar_prefetch=1,
            grid=(HK,),
            in_specs=[
                pl.BlockSpec((rows, group_heads * HD), lambda j, p: (0, j)),
                pl.BlockSpec((key_count, HD), lambda j, p: (0, j)),
                pl.BlockSpec((key_count, HD), lambda j, p: (0, HK + j)),
                whole((rows, key_count)),
                pl.BlockSpec((rows, group_heads * 128), lambda j, p: (0, j)),
                pl.BlockSpec((rows, group_heads * HD), lambda j, p: (0, j)),
                whole((key_count, HD // 2)),
                whole((key_count, HD // 2)),
            ],
            out_specs=[
                pl.BlockSpec((rows, group_heads * HD), lambda j, p: (0, j)),
                whole((key_count, 2 * HK * HD)),
            ],
        ),
        out_shape=[
            jax.ShapeDtypeStruct((rows, HQ * HD), LOW),
            jax.ShapeDtypeStruct((key_count, 2 * HK * HD), LOW),
        ],
        compiler_params=pltpu.CompilerParams(vmem_limit_bytes=VMEM_LIMIT),
        name="attend_back",
    )(place, queries, pairs, pairs, seen, logsum, grads, cosine, sine_part)


def weights_back_kernel(
    place_ref,
    query_ref,
    pair_ref,
    branch_ref,
    attended_ref,
    normed_ref,
    own_normed_ref,
    group_ref,
    own_ref,
    scale_ref,
    query_weight_ref,
    pair_weight_ref,
    query_term,
    pair_term,
    merge_term,
    back_out,
    pair_back_out,
    gain_out,
):
    rows = query_ref.shape[0]
    prompt_rows = rows - CONT
    start = pl.multiple_of(place_ref[0] * prompt_rows, 16)
    query_term[...] = along(own_normed_ref[...], query_ref[...]).astype(LOW)
    pair_term[...] = along(normed_ref[...], pair_ref[...]).astype(LOW)
    merge_term[...] = along(branch_ref[...], attended_ref[...]).astype(LOW)
    query_back = across(query_ref[...], query_weight_ref[...])
    pair_back = across(pair_ref[...], pair_weight_ref[...])
    own_values = own_ref[prompt_rows:].astype(FULL) * scale_ref[PROMPT_LEN:, :1]
    tail = query_back[prompt_rows:] + pair_back[PROMPT_LEN:]
    group_values = group_ref[...].astype(FULL) * scale_ref[:PROMPT_LEN, :1]
    own_prompt = own_ref[:prompt_rows].astype(FULL) * scale_ref[pl.ds(start, prompt_rows), :1]
    gain_out[...] = (
        jnp.sum(pair_back[:PROMPT_LEN] * group_values, axis=0, keepdims=True)
        + jnp.sum(query_back[:prompt_rows] * own_prompt, axis=0, keepdims=True)
        + jnp.sum(tail * own_values, axis=0, keepdims=True)
    )
    back_out[:prompt_rows] = query_back[:prompt_rows]
    back_out[prompt_rows:] = tail
    pair_back_out[...] = pair_back[:PROMPT_LEN].astype(LOW)


def weights_back(
    place, queries, pairs, branch, attended, normed, own_normed, group_rows, own_inputs, scale, weights
):
    rows, key_count = queries.shape[0], pairs.shape[0]
    wide, tile = HQ * HD, 256
    whole = lambda shape: pl.BlockSpec(shape, lambda j, p: (0, 0))
    tall = lambda count: pl.BlockSpec((count, tile), lambda j, p: (0, j))
    flat = lambda at: pl.BlockSpec((tile, wide), lambda j, p: (j, at))
    return pl.pallas_call(
        weights_back_kernel,
        grid_spec=pltpu.PrefetchScalarGridSpec(
            num_scalar_prefetch=1,
            grid=(D // tile,),
            in_specs=[
                whole((rows, wide)),
                whole((key_count, wide)),
                tall(rows),
                whole((rows, wide)),
                tall(key_count),
                tall(rows),
                tall(PROMPT_LEN),
                tall(rows),
                whole((key_count, 128)),
                flat(0),
                flat(1),
            ],
            out_specs=[flat(0), flat(0), flat(0), tall(rows), tall(PROMPT_LEN), tall(1)],
        ),
        out_shape=[
            jax.ShapeDtypeStruct((D, wide), LOW),
            jax.ShapeDtypeStruct((D, wide), LOW),
            jax.ShapeDtypeStruct((D, wide), LOW),
            jax.ShapeDtypeStruct((rows, D), FULL),
            jax.ShapeDtypeStruct((PROMPT_LEN, D), LOW),
            jax.ShapeDtypeStruct((1, D), FULL),
        ],
        compiler_params=pltpu.CompilerParams(vmem_limit_bytes=VMEM_LIMIT),
        name="weights_back",
    )(
        place,
        queries,
        pairs,
        branch,
        attended,
        normed,
        own_normed,
        group_rows,
        own_inputs,
        scale,
        weights,
        weights,
    )


def forward_back_kernel(
    activated_ref, grad_ref, gate_up_ref, first_ref, second_ref, out_ref, gate_up_grad_ref
):
    own_hidden = activated_ref.shape[1]
    part = first_ref.shape[0] // 4
    piece = own_hidden // 2

    @pl.loop(0, 4)
    def _(at):
        columns = pl.ds(pl.multiple_of(at * part, part), part)
        out_ref[:, columns] = (
            across(activated_ref[:, :piece], first_ref[columns])
            + across(activated_ref[:, piece:], second_ref[columns])
        ).astype(LOW)

    for at, down_ref in enumerate((first_ref, second_ref)):
        columns = slice(at * piece, (at + 1) * piece)
        upper = slice(own_hidden + at * piece, own_hidden + (at + 1) * piece)
        activated_grad = jnp.dot(grad_ref[...], down_ref[...], preferred_element_type=FULL)
        gate_values, up_values = gate_up_ref[:, columns], gate_up_ref[:, upper]
        gate_sigmoid = jax.nn.sigmoid(gate_values)
        gate_grad, up_grad = gate_backward(
            activated_grad, gate_values, up_values, gate_sigmoid, gate_values * gate_sigmoid
        )
        gate_up_grad_ref[:, columns] = gate_grad
        gate_up_grad_ref[:, upper] = up_grad


def forward_back(rows, activated, grads, gate_up, first_down, second_down):
    count, own_hidden = activated.shape
    block = lambda width: pl.BlockSpec((rows, width), lambda j: (j, 0))
    return pl.pallas_call(
        forward_back_kernel,
        grid=(count // rows,),
        in_specs=[
            block(own_hidden),
            block(D),
            block(2 * own_hidden),
            pl.BlockSpec(first_down.shape, lambda j: (0, 0)),
            pl.BlockSpec(second_down.shape, lambda j: (0, 0)),
        ],
        out_specs=[block(D), block(2 * own_hidden)],
        out_shape=[
            jax.ShapeDtypeStruct((count, D), LOW),
            jax.ShapeDtypeStruct((count, 2 * own_hidden), LOW),
        ],
        compiler_params=pltpu.CompilerParams(vmem_limit_bytes=VMEM_LIMIT),
        name="forward_back",
    )(activated, grads, gate_up, first_down, second_down)


def plane_back_kernel(
    plane,
    rows_ref,
    weight_ref,
    down_ref,
    out_ref,
    swapped_ref,
    weight,
    tiles,
    keep,
    give,
    core_in,
    plane_in,
    total,
    load_sem,
    tile_sem,
    core_send,
    core_recv,
    plane_send,
    plane_recv,
    out_sem,
    swap_send,
    swap_recv,
):
    g = lax.axis_index("grp")
    d = lax.axis_index("dp")
    chips = plane // 2
    halves = plane == 8
    order = (3, 1, 2, 0) if halves else tuple(range(chips - 1, -1, -1))
    cut = D // 2
    half_of = (pl.ds(0, cut), pl.ds(cut, D - cut))

    barrier = pltpu.get_barrier_semaphore()
    for offset in range(1, plane):
        pl.semaphore_signal(
            barrier, inc=1, device_id=(g, flip(d, offset)), device_id_type=MESH
        )

    load = pltpu.make_async_copy(weight_ref, weight, load_sem.at[0])
    load.start()

    def tile_copy(turn):
        at = order[turn]
        return pltpu.make_async_copy(
            rows_ref.at[pl.ds(2 * at, 2)], tiles.at[turn % 2], tile_sem.at[turn % 2]
        )

    def core_copy(at):
        return remote(
            give.at[at], core_in.at[at], core_send.at[at], core_recv.at[at], (g, flip(d, 1))
        )

    def plane_copy(at):
        return remote(
            keep.at[at],
            plane_in.at[at],
            plane_send.at[at],
            plane_recv.at[at],
            (g, flip(d, 2 * at)),
        )

    def near_copy(part, relayed):
        there = part + 1
        return remote(
            keep.at[3 if relayed else there, :, half_of[part]],
            plane_in.at[1 if relayed else 0, :, half_of[part]],
            plane_send.at[2 * relayed + part],
            plane_recv.at[2 * relayed + part],
            (g, flip(d, 2 * there)),
        )

    def relay_copy(part):
        there = 2 - part
        return remote(
            keep.at[there, :, half_of[part]],
            plane_in.at[2, :, half_of[part]],
            plane_send.at[4 + part],
            plane_recv.at[4 + part],
            (g, flip(d, 2 * there)),
        )

    def swap_copy(offset):
        there = flip(d, offset)
        return remote(
            down_ref.at[there],
            swapped_ref.at[d],
            swap_send.at[offset],
            swap_recv.at[offset],
            (g, there),
        )

    own_swap = pltpu.make_async_copy(down_ref.at[d], swapped_ref.at[d], out_sem.at[1])
    tile_copy(0).start()
    tile_copy(1).start()
    pl.semaphore_wait(barrier, plane - 1)
    for offset in range(1, plane):
        swap_copy(offset).start()
    own_swap.start()
    load.wait()
    part_width = 512

    def product(turn, which, target):
        @pl.loop(0, D // part_width)
        def _(at):
            columns = pl.ds(pl.multiple_of(at * part_width, part_width), part_width)
            target[order[turn], :, columns] = across(
                tiles[turn % 2, which], weight[columns]
            ).astype(LOW)

    def add_into(at, other, first, count):
        step = 256

        @pl.loop(0, count // step)
        def _(k):
            here = pl.ds(pl.multiple_of(first + k * step, step), step)
            keep[at, :, here] = (
                keep[at, :, here].astype(FULL) + other(here).astype(FULL)
            ).astype(LOW)

    def settle(turn):
        at = order[turn]
        core_copy(at).wait_recv()
        add_into(at, lambda here: core_in[at, :, here], 0, D)
        if halves and at == 3:
            near_copy(0, True).start()
            near_copy(1, True).start()
        elif halves and at:
            near_copy(at - 1, False).start()
        elif at:
            plane_copy(at).start()

    for turn in range(chips):
        tile_copy(turn).wait()
        product(turn, 1, give)
        core_copy(order[turn]).start()
        if turn:
            settle(turn - 1)
        product(turn, 0, keep)
        if turn + 2 < chips:
            tile_copy(turn + 2).start()
        if halves and turn == chips - 1:
            for part in range(2):
                near_copy(part, True).wait_recv()
                add_into(
                    2 - part,
                    lambda here: plane_in[1, :, here],
                    part * cut,
                    cut,
                )
                relay_copy(part).start()
    settle(chips - 1)
    if halves:
        for part in range(2):
            near_copy(part, False).wait_recv()
            relay_copy(part).wait_recv()
        arrived = (0, 2)
    else:
        for at in range(1, chips):
            plane_copy(at).wait_recv()
        arrived = tuple(range(1, chips))

    @pl.loop(0, D // 256)
    def _(k):
        here = pl.ds(pl.multiple_of(k * 256, 256), 256)
        value = keep[0, :, here].astype(FULL)
        for at in arrived:
            value = value + plane_in[at, :, here].astype(FULL)
        total[:, here] = value

    out = pltpu.make_async_copy(total, out_ref, out_sem.at[0])
    out.start()
    for at in range(chips):
        core_copy(at).wait_send()
    if halves:
        for part in range(2):
            near_copy(part, False).wait_send()
            near_copy(part, True).wait_send()
            relay_copy(part).wait_send()
    else:
        for at in range(1, chips):
            plane_copy(at).wait_send()
    for offset in range(1, plane):
        swap_copy(offset).wait()
    own_swap.wait()
    out.wait()


def plane_back(rows, gate_up_grad, gate_weight, down_part):
    plane = lax.axis_size("dp")
    chips = plane // 2
    inner = gate_up_grad.shape[1]
    anywhere = pl.BlockSpec(memory_space=pl.ANY)
    dma = pltpu.SemaphoreType.DMA
    return pl.pallas_call(
        functools.partial(plane_back_kernel, plane),
        out_shape=(
            jax.ShapeDtypeStruct((rows, D), FULL),
            jax.ShapeDtypeStruct(down_part.shape, LOW),
        ),
        in_specs=[anywhere] * 3,
        out_specs=(anywhere,) * 2,
        scratch_shapes=[
            pltpu.VMEM((D, inner), LOW),
            pltpu.VMEM((2, 2, rows, inner), LOW),
            pltpu.VMEM((chips, rows, D), LOW),
            pltpu.VMEM((chips, rows, D), LOW),
            pltpu.VMEM((chips, rows, D), LOW),
            pltpu.VMEM((3 if plane == 8 else chips, rows, D), LOW),
            pltpu.VMEM((rows, D), FULL),
            dma((1,)),
            dma((2,)),
            dma((chips,)),
            dma((chips,)),
            dma((max(6, chips),)),
            dma((max(6, chips),)),
            dma((2,)),
            dma((plane,)),
            dma((plane,)),
        ],
        compiler_params=pltpu.CompilerParams(
            collective_id=2, has_side_effects=True, vmem_limit_bytes=VMEM_LIMIT
        ),
        name="plane_back",
    )(gate_up_grad.reshape(plane, rows, inner), gate_weight, down_part)


def plane_swap(block, offset):
    size = lax.axis_size("dp")
    return lax.ppermute(block, "dp", [(i, i ^ offset) for i in range(size)])


def plane_gather(block):
    mine = [block] + [plane_swap(block, o) for o in range(2, lax.axis_size("dp"), 2)]
    pairs = [(one, plane_swap(one, 1)) for one in mine]
    return jnp.concatenate([one for pair in pairs for one in pair], axis=0)


def line_scatter(term):
    return lax.psum_scatter(term, "grp", scatter_dimension=0, tiled=True)


def finish_kernel(
    lines,
    plane,
    query_ref,
    pair_ref,
    merge_ref,
    gain_ref,
    gate_ref,
    up_ref,
    down_ref,
    a_master,
    a_first,
    a_second,
    m_master,
    m_first,
    m_second,
    f_master,
    f_first,
    f_second,
    a_grad,
    a_update,
    a_first_new,
    a_second_new,
    m_grad,
    m_update,
    m_first_new,
    m_second_new,
    gain_out,
    f_grad,
    f_update,
    f_first_new,
    f_second_new,
    mine,
    core_in,
    plane_in,
    line_in,
    swap_in,
    state,
    made,
    a_state,
    a_made,
    gain_made,
    mine_sem,
    core_send,
    core_recv,
    plane_send,
    plane_recv,
    line_send,
    line_recv,
    swap_send,
    swap_recv,
    own_sem,
    state_sem,
    made_sem,
    a_sem,
    gain_sem,
):
    g = lax.axis_index("grp")
    d = lax.axis_index("dp")
    chips = plane // 2
    chip, core = lax.div(d, 2), lax.rem(d, 2)
    partner = d + 1 - 2 * core
    rows = a_master.shape[0]
    own_hidden = gate_ref.shape[2]
    width = core_in.shape[3]
    a_width, m_width = a_master.shape[1], m_master.shape[1]
    parts, begin = [], 0
    for ref in (query_ref, pair_ref, merge_ref, gain_ref):
        parts.append((ref, pl.ds(begin, ref.shape[4])))
        begin += ref.shape[4]

    barrier = pltpu.get_barrier_semaphore()
    for step in range(1, plane):
        there = lax.rem(d + step, plane)
        pl.semaphore_signal(barrier, inc=1, device_id=(g, there), device_id_type=MESH)
    for step in range(1, lines):
        there = lax.rem(g + step, lines)
        pl.semaphore_signal(barrier, inc=1, device_id=(there, d), device_id_type=MESH)
    pl.semaphore_wait(barrier, plane + lines - 2)

    def line_at(turn):
        return lax.rem(g + turn + 1, lines)

    def core_copy(turn, part):
        line = line_at(turn)
        ref, columns = parts[part]
        return remote(
            ref.at[line, :, 1 - core],
            core_in.at[line, :, :, columns],
            core_send.at[turn, part],
            core_recv.at[turn, part],
            (g, partner),
        )

    def mine_copy(turn, part):
        line = line_at(turn)
        ref, columns = parts[part]
        return pltpu.make_async_copy(
            ref.at[line, :, core], mine.at[turn % 2, :, :, columns], mine_sem.at[turn, part]
        )

    cut = width // 256 * 128
    columns_of = (pl.ds(0, cut), pl.ds(cut, width - cut))

    def plane_copy(turn, step):
        line = line_at(turn)
        there = lax.rem(chip + step, chips)
        return remote(
            core_in.at[line, there],
            plane_in.at[line, chip],
            plane_send.at[turn, step],
            plane_recv.at[turn, step],
            (g, 2 * there + core),
        )

    def near_copy(turn, part, relayed):
        line = line_at(turn)
        there = flip(chip, part + 1)
        owner = flip(chip, 3) if relayed else there
        return remote(
            core_in.at[line, owner, :, columns_of[part]],
            plane_in.at[line, 1 if relayed else 0, :, columns_of[part]],
            plane_send.at[turn, 2 * relayed + part],
            plane_recv.at[turn, 2 * relayed + part],
            (g, 2 * there + core),
        )

    def relay_copy(turn, part):
        line = line_at(turn)
        there = flip(chip, 2 - part)
        return remote(
            core_in.at[line, there, :, columns_of[part]],
            plane_in.at[line, 2, :, columns_of[part]],
            plane_send.at[turn, 4 + part],
            plane_recv.at[turn, 4 + part],
            (g, 2 * there + core),
        )

    def line_copy(turn):
        line = line_at(turn)
        return remote(
            core_in.at[line, chip],
            line_in.at[g],
            line_send.at[turn],
            line_recv.at[turn],
            (line, d),
        )

    forward_refs = (gate_ref, up_ref, down_ref)

    def swap_copy(step, part):
        there = lax.rem(d + step, plane)
        return remote(
            forward_refs[part].at[there],
            swap_in.at[part, d],
            swap_send.at[step, part],
            swap_recv.at[step, part],
            (g, there),
        )

    own_swap = [
        pltpu.make_async_copy(forward_refs[part].at[d], swap_in.at[part, d], own_sem.at[part])
        for part in range(2)
    ] + [pltpu.make_async_copy(down_ref, swap_in.at[2], own_sem.at[2])]

    def f_columns(turn):
        block = lax.rem(d + lax.div(turn, 3), plane)
        return pl.ds(
            pl.multiple_of(lax.rem(turn, 3) * FF + block * own_hidden, own_hidden), own_hidden
        )

    def state_copy(turn, which):
        slot = lax.rem(turn, 2)
        return pltpu.make_async_copy(
            (f_master, f_first, f_second)[which].at[:, f_columns(turn)],
            state.at[slot, which],
            state_sem.at[slot, which],
        )

    def made_copy(turn, which):
        slot = lax.rem(turn, 2)
        return pltpu.make_async_copy(
            made.at[slot, which],
            (f_grad, f_update, f_first_new, f_second_new)[which].at[:, f_columns(turn)],
            made_sem.at[slot, which],
        )

    slabs = (pl.ds(0, a_width), pl.ds(a_width, m_width))

    def a_state_copy(which, slab):
        source = ((a_master, a_first, a_second), (m_master, m_first, m_second))[slab][which]
        return pltpu.make_async_copy(
            source, a_state.at[which, :, slabs[slab]], a_sem.at[slab, which]
        )

    def a_made_copy(which, slab):
        target = (
            (a_grad, a_update, a_first_new, a_second_new),
            (m_grad, m_update, m_first_new, m_second_new),
        )[slab][which]
        return pltpu.make_async_copy(
            a_made.at[which, :, slabs[slab]], target, a_sem.at[slab, 3 + which]
        )

    every = range(len(parts))
    for turn in range(lines):
        for part in every:
            core_copy(turn, part).start()
            if turn < 2:
                mine_copy(turn, part).start()
        if turn == 0:
            for step in range(1, plane):
                for part in range(2):
                    swap_copy(step, part).start()
            for one in own_swap:
                one.start()
    for which in range(3):
        state_copy(0, which).start()
        for slab in range(2):
            a_state_copy(which, slab).start()

    tile = 896 if width % 896 == 0 else 128
    halves = plane == 8

    def add_into(line, there, other, columns=None):
        first, count = (0, width) if columns is None else columns
        step = tile if columns is None else 128

        @pl.loop(0, count // step)
        def _(at):
            here = pl.ds(pl.multiple_of(first + at * step, 128), step)
            total = core_in[line, there, :, here].astype(FULL) + other(here).astype(FULL)
            core_in[line, there, :, here] = total.astype(LOW)

    def near_start(turn):
        if halves:
            for relayed in (True, False):
                for part in range(2):
                    near_copy(turn, part, relayed).start()
        else:
            for step in range(1, chips):
                plane_copy(turn, step).start()

    for turn in range(lines):
        line = line_at(turn)
        for part in every:
            core_copy(turn, part).wait_recv()
            mine_copy(turn, part).wait()
        for step in range(1, chips + 1):
            there = lax.rem(chip + step, chips)
            add_into(
                line, there, lambda here, there=there, turn=turn: mine[turn % 2, there, :, here]
            )
        if turn + 2 < lines:
            for part in every:
                mine_copy(turn + 2, part).start()
        if turn < 2:
            near_start(turn)

    def pass_on(turn):
        line = line_at(turn)
        for part, columns in enumerate(((0, cut), (cut, width - cut))):
            near_copy(turn, part, True).wait_recv()
            add_into(
                line,
                flip(chip, 2 - part),
                lambda here, line=line: plane_in[line, 1, :, here],
                columns,
            )
            relay_copy(turn, part).start()

    def forward_turn(turn):
        slot = lax.rem(turn, 2)
        block = lax.rem(d + lax.div(turn, 3), plane)
        part = lax.rem(turn, 3)

        @pl.when(turn + 1 < 3 * plane)
        def _():
            for which in range(3):
                state_copy(turn + 1, which).start()

        @pl.when(turn > 1)
        def _():
            for which in range(4):
                made_copy(turn - 2, which).wait()

        for which in range(3):
            state_copy(turn, which).wait()

        @pl.loop(0, rows // 16)
        def _(at):
            rows_at = pl.ds(pl.multiple_of(at * 16, 16), 16)
            gradient = swap_in[part, block, rows_at].astype(FULL)
            update, first_new, second_new = adam_step(
                state[slot, 0, rows_at],
                state[slot, 1, rows_at],
                state[slot, 2, rows_at],
                gradient,
                WEIGHT_DECAY,
            )
            made[slot, 0, rows_at] = gradient
            made[slot, 1, rows_at] = update
            made[slot, 2, rows_at] = first_new
            made[slot, 3, rows_at] = second_new

        for which in range(4):
            made_copy(turn, which).start()

    def near_done(turn):
        if halves:
            pass_on(turn)
            for part in range(2):
                near_copy(turn, part, False).wait_recv()
        else:
            for step in range(1, chips):
                plane_copy(turn, step).wait_recv()
        if turn + 2 < lines:
            near_start(turn + 2)

    def line_done(turn):
        line = line_at(turn)
        if halves:
            for part in range(2):
                relay_copy(turn, part).wait_recv()
            arrived = (0, 2)
        else:
            arrived = tuple(lax.rem(chip + step, chips) for step in range(1, chips))

        @pl.loop(0, width // tile)
        def _(at):
            columns = pl.ds(pl.multiple_of(at * tile, tile), tile)
            total = core_in[line, chip, :, columns].astype(FULL)
            for block in arrived:
                total = total + plane_in[line, block, :, columns].astype(FULL)
            core_in[line, chip, :, columns] = total.astype(LOW)

        if turn < lines - 1:
            line_copy(turn).start()

    each = 3 * plane // lines

    def forward_some(turn):
        lax.fori_loop(turn * each, (turn + 1) * each, lambda k, c: (forward_turn(k), c)[1], 0)

    near_done(0)
    for turn in range(1, lines):
        if turn == 1:
            for one in own_swap:
                one.wait()
            for step in range(1, plane):
                for part in range(2):
                    swap_copy(step, part).wait_recv()
        near_done(turn)
        line_done(turn - 1)
        forward_some(turn - 1)
    line_done(lines - 1)
    forward_some(lines - 1)
    for which in range(4):
        for turn in (3 * plane - 2, 3 * plane - 1):
            made_copy(turn, which).wait()
    for turn in range(lines - 1):
        line_copy(turn).wait_recv()
    for which in range(3):
        for slab in range(2):
            a_state_copy(which, slab).wait()

    def owned(columns):
        total = core_in[g, chip, :, columns].astype(FULL)
        for step in range(1, lines):
            total = total + line_in[lax.rem(g + step, lines), :, columns].astype(FULL)
        return total

    @pl.loop(0, (a_width + m_width) // 256)
    def _(at):
        columns = pl.ds(pl.multiple_of(at * 256, 256), 256)
        gradient = owned(columns)
        update, first_new, second_new = adam_step(
            a_state[0, :, columns],
            a_state[1, :, columns],
            a_state[2, :, columns],
            gradient,
            WEIGHT_DECAY,
        )
        a_made[0, :, columns] = gradient
        a_made[1, :, columns] = update
        a_made[2, :, columns] = first_new
        a_made[3, :, columns] = second_new

    for which in range(4):
        for slab in range(2):
            a_made_copy(which, slab).start()
    gain_made[...] = owned(pl.ds(a_width + m_width, GAIN_PAD)).T[:8]
    gain_copy = pltpu.make_async_copy(gain_made, gain_out, gain_sem.at[0])
    gain_copy.start()
    for turn in range(lines):
        for part in every:
            core_copy(turn, part).wait_send()
        if halves:
            for part in range(2):
                near_copy(turn, part, False).wait_send()
                near_copy(turn, part, True).wait_send()
                relay_copy(turn, part).wait_send()
        else:
            for step in range(1, chips):
                plane_copy(turn, step).wait_send()
        if turn < lines - 1:
            line_copy(turn).wait_send()
    for step in range(1, plane):
        for part in range(2):
            swap_copy(step, part).wait_send()
    for which in range(4):
        for slab in range(2):
            a_made_copy(which, slab).wait()
    gain_copy.wait()


def finish(terms, forward_parts, attention, merge, forward):
    lines, plane = lax.axis_size("grp"), lax.axis_size("dp")
    chips = plane // 2
    rows, a_width = attention[0].shape
    m_width = merge[0].shape[1]
    own_hidden = forward_parts[0].shape[-1]
    width = a_width + m_width + GAIN_PAD
    anywhere = pl.BlockSpec(memory_space=pl.ANY)
    dma = pltpu.SemaphoreType.DMA
    vmem = pltpu.VMEM

    def like(array):
        return jax.ShapeDtypeStruct(array.shape, array.dtype)

    return pl.pallas_call(
        functools.partial(finish_kernel, lines, plane),
        out_shape=(like(attention[0]),) * 4
        + (like(merge[0]),) * 4
        + (jax.ShapeDtypeStruct((8, rows), FULL),)
        + (like(forward[0]),) * 4,
        in_specs=[anywhere] * 16,
        out_specs=(anywhere,) * 13,
        scratch_shapes=[
            vmem((2, chips, rows, width), LOW),
            vmem((lines, chips, rows, width), LOW),
            vmem((lines, 3 if plane == 8 else chips, rows, width), LOW),
            vmem((lines, rows, width), LOW),
            vmem((3, plane, rows, own_hidden), LOW),
            vmem((2, 3, rows, own_hidden), FULL),
            vmem((2, 4, rows, own_hidden), FULL),
            vmem((3, rows, a_width + m_width), FULL),
            vmem((4, rows, a_width + m_width), FULL),
            vmem((8, rows), FULL),
            dma((lines, 4)),
            dma((lines, 4)),
            dma((lines, 4)),
            dma((lines, max(6, chips))),
            dma((lines, max(6, chips))),
            dma((lines,)),
            dma((lines,)),
            dma((plane, 2)),
            dma((plane, 2)),
            dma((3,)),
            dma((2, 3)),
            dma((2, 4)),
            dma((2, 7)),
            dma((1,)),
        ],
        compiler_params=pltpu.CompilerParams(
            collective_id=1, has_side_effects=True, vmem_limit_bytes=VMEM_LIMIT
        ),
        name="finish",
    )(
        *(term.reshape(lines, chips, 2, rows, term.shape[1]) for term in terms),
        *(part.reshape(plane, rows, own_hidden) for part in forward_parts),
        *attention,
        *merge,
        *forward,
    )


def body(
    hidden,
    cotangent,
    segment_ids,
    continuation_prompt,
    gain_master,
    gain_first,
    gain_second,
    attention_master,
    attention_first,
    attention_second,
    merge_master,
    merge_first,
    merge_second,
    feedforward_master,
    feedforward_first,
    feedforward_second,
):
    group_index = lax.axis_index("grp")
    dp_size = lax.axis_size("dp")
    row_count = hidden.shape[2]
    prompt_rows = row_count - CONT
    qkv_width = (HQ + 2 * HK) * HD
    own_rows = feedforward_master.shape[0]
    own_hidden = FF // dp_size
    own_inputs = hidden.reshape(row_count, D)

    gain_columns = jnp.pad(gain_master.T, ((0, 0), (0, GAIN_PAD - 2)))
    weight_low = jnp.concatenate(
        [attention_master.astype(LOW), merge_master.astype(LOW), gain_columns.astype(LOW)], axis=1
    )
    weights, group_rows, gate_rows, first_rows, second_rows = gather_start(
        weight_low, own_inputs, feedforward_master.astype(LOW)
    )
    weights, late_cotangent = lax.optimization_barrier((weights, cotangent))
    weights = weights.reshape(D, -1)
    merge_weight = weights[:, qkv_width : qkv_width + D]
    gain_float = weights[:, qkv_width + D : qkv_width + D + 2].astype(FULL).T
    gate_weight = lax.all_gather(
        gate_rows.reshape(dp_size * own_rows, 2 * own_hidden), "grp", axis=0, tiled=True
    )
    gate_weight, second_rows = lax.optimization_barrier((gate_weight, second_rows))
    first_down = first_rows.reshape(D, own_hidden // 2)
    second_down = lax.all_gather(
        second_rows.reshape(dp_size * own_rows, own_hidden // 2), "grp", axis=0, tiled=True
    )
    down_grad = plane_gather(late_cotangent.reshape(row_count, D))

    segment_row = segment_ids[0]
    source_row = continuation_prompt[0]
    prompt_positions, follow_positions = segment_positions(segment_row, source_row)
    cosine, sine_part = angle_table(jnp.concatenate([prompt_positions, follow_positions[0]]))

    place = jnp.reshape(group_index, (1,)).astype(jnp.int32)
    group_rows = group_rows.reshape(PROMPT_LEN, D)
    queries, pairs, key_normed, normed, key_scale = project_heads(
        place, group_rows, own_inputs, gain_float[:1], cosine, sine_part, weights
    )
    inputs = own_inputs.astype(FULL)
    first_scale = norm_scale(inputs)

    row_index = jnp.arange(row_count, dtype=jnp.int32)
    is_prompt = row_index < prompt_rows
    global_row = group_index * prompt_rows + jnp.minimum(row_index, prompt_rows - 1)
    own_segment = lax.dynamic_slice_in_dim(segment_row, group_index * prompt_rows, prompt_rows)
    query_segment = jnp.concatenate([own_segment, jnp.broadcast_to(source_row, (CONT,))])
    key_index = jnp.arange(PROMPT_LEN, dtype=jnp.int32)
    prompt_seen = (segment_row[None, :] == query_segment[:, None]) & (
        (key_index[None, :] <= global_row[:, None]) | ~is_prompt[:, None]
    )
    follow_seen = (~is_prompt)[:, None] & (
        jnp.arange(CONT, dtype=jnp.int32)[None, :] <= (row_index - prompt_rows)[:, None]
    )
    visible = jnp.concatenate([prompt_seen, follow_seen], axis=1)
    seen = visible.astype(FULL)
    attended, row_logsum = attend(queries, pairs, seen)
    middle = inputs + contract(attended, merge_weight, 1, 1)
    second_scale = norm_scale(middle)
    normed_two = (middle * second_scale * gain_float[1]).astype(LOW)
    grad_rows = cotangent.reshape(row_count, D).astype(FULL)

    normed_two, down_grad = lax.optimization_barrier((normed_two, down_grad))
    normed_all = plane_gather(normed_two)
    gate_up = jnp.dot(normed_all, gate_weight, preferred_element_type=FULL)
    gate_values = gate_up[:, :own_hidden]
    up_values = gate_up[:, own_hidden:]
    gate_sigmoid, gate_silu, activated = gate_parts(gate_values, up_values)
    down_term = contract(down_grad, activated, 0, 0).astype(LOW)
    down_term, second_down = lax.optimization_barrier((down_term, second_down))
    out_term, gate_up_grad = forward_back(
        row_count, activated, down_grad, gate_up, first_down, second_down
    )
    down_part = line_scatter(down_term)
    gate_term = contract(normed_all, gate_up_grad[:, :own_hidden], 0, 0).astype(LOW)
    up_term = contract(normed_all, gate_up_grad[:, own_hidden:], 0, 0).astype(LOW)
    gate_up_grad, gate_term, up_term, down_part = lax.optimization_barrier(
        (gate_up_grad, gate_term, up_term, down_part)
    )
    gate_part = line_scatter(gate_term)
    up_part = line_scatter(up_term)
    normed_two_grad, down_swapped = plane_back(
        row_count, gate_up_grad, gate_weight, down_part.reshape(dp_size, own_rows, own_hidden)
    )
    normed_two_grad, out_term = lax.optimization_barrier((normed_two_grad, out_term))
    out_chunks = out_term.reshape(dp_size, row_count, D)
    out_swapped = [plane_swap(out_chunks[offset + 1], 1) for offset in range(0, dp_size, 2)]
    middle_grad = grad_rows + norm_back(middle, second_scale, gain_float[1], normed_two_grad)
    gain_two_part = jnp.sum(normed_two_grad * middle * second_scale, axis=0)
    branch_grad = middle_grad.astype(LOW)
    attended_grad = contract(branch_grad, merge_weight, 1, 0).astype(LOW)
    attended_grad, out_swapped = lax.optimization_barrier((attended_grad, out_swapped))
    out_sums = [
        out_chunks[2 * at].astype(FULL) + one.astype(FULL) for at, one in enumerate(out_swapped)
    ]
    out_low = [one.astype(LOW) for one in out_sums[1:]]
    attended_grad, out_low = lax.optimization_barrier((attended_grad, out_low))
    out_arrived = [plane_swap(one, 2 * at + 2) for at, one in enumerate(out_low)]
    query_project, pair_project = attend_back(
        place, queries, pairs, seen, row_logsum, attended_grad, cosine, sine_part
    )
    query_term, pair_term, merge_term, normed_grad, pair_back, gain_one_part = weights_back(
        place,
        query_project,
        pair_project,
        branch_grad,
        attended,
        key_normed,
        normed,
        group_rows,
        own_inputs,
        key_scale,
        weights,
    )
    gain_term = jnp.pad(
        jnp.stack([gain_one_part[0], gain_two_part], axis=1), ((0, 0), (0, GAIN_PAD - 2))
    )
    pair_back, up_part, out_arrived = lax.optimization_barrier((pair_back, up_part, out_arrived))
    result = middle + out_sums[0]
    for one in out_arrived:
        result = result + one.astype(FULL)
    block_output, query_term = lax.optimization_barrier((result.astype(LOW), query_term))
    block_output = block_output.reshape(hidden.shape)
    pair_sum = line_scatter(pair_back)
    finished = finish(
        (query_term, pair_term, merge_term, gain_term.astype(LOW)),
        (gate_part, up_part, down_swapped),
        (attention_master, attention_first, attention_second),
        (merge_master, merge_first, merge_second),
        (feedforward_master, feedforward_first, feedforward_second),
    )
    gain_grad = finished[8][:2]
    pair_sum, gain_grad = lax.optimization_barrier((pair_sum, gain_grad))
    pair_sum = pair_sum.astype(FULL)
    normed_grad = normed_grad + jnp.pad(pair_sum, ((0, CONT), (0, 0)))
    input_grad = (middle_grad + norm_back(inputs, first_scale, gain_float[0], normed_grad)).reshape(
        hidden.shape
    )
    gain_new = adam_step(gain_master, gain_first, gain_second, gain_grad, 0.0)
    return (
        block_output,
        input_grad,
        gain_grad,
        *gain_new,
        *finished[:8],
        *finished[9:],
    )


def solution(mesh):
    tokens = P("dp", "grp", None, None)
    gains = P(None, ("grp", "dp"))
    matrix = P(("grp", "dp"), None)
    return jax.shard_map(
        body,
        mesh=mesh,
        in_specs=(tokens, tokens, P("dp", None), P("dp", "grp")) + (gains,) * 3 + (matrix,) * 9,
        out_specs=(tokens, tokens) + (gains,) * 4 + (matrix,) * 12,
        check_vma=False,
    )
```

```python
import functools

import jax
import jax.numpy as jnp
from jax import lax
from jax.experimental import pallas as pl
from jax.experimental.pallas import tpu as pltpu
from jax.sharding import PartitionSpec as P

D = 2048
FF = 8192
HQ = 8
HK = 4
HD = 256
PROMPT_LEN = 1024
PROMPTS = 4
CONT = 64
STEP = 10
GAIN_PAD = 128

EPS_NORM = 1e-06
ROPE_THETA = 1000042.0
MASK_FILL = -1e30
BETA_ONE = 0.9
BETA_TWO = 0.95
ADAM_EPS = 1e-08
LEARN_RATE = 0.02
WEIGHT_DECAY = 0.1
LOW = jnp.bfloat16
FULL = jnp.float32
MESH = pl.DeviceIdType.MESH


def contract(left, right, left_axis, right_axis):
    return lax.dot_general(
        left, right, (((left_axis,), (right_axis,)), ((), ())), preferred_element_type=FULL
    )


def angle_table(positions):
    inverse_rate = ROPE_THETA ** (-(jnp.arange(HD // 2, dtype=FULL) * 2.0) / HD)
    angles = positions.astype(FULL)[..., None] * inverse_rate
    return (jnp.cos(angles), jnp.sin(angles))


def segment_positions(segment_row, source_row):
    labels = jnp.arange(PROMPTS, dtype=jnp.int32)
    member = (segment_row[None, :] == labels[:, None]).astype(jnp.int32)
    lengths = jnp.sum(member, axis=1, dtype=jnp.int32)
    starts = jnp.sum(
        jnp.where(labels[None, :] < labels[:, None], lengths[None, :], 0), axis=1, dtype=jnp.int32
    )
    prompt_index = jnp.arange(segment_row.shape[0], dtype=jnp.int32)
    prompt_positions = prompt_index - jnp.sum(member * starts[:, None], axis=0, dtype=jnp.int32)
    source_length = jnp.sum(
        (source_row[:, None] == labels[None, :]).astype(jnp.int32) * lengths[None, :],
        axis=1,
        dtype=jnp.int32,
    )
    follow_positions = source_length[:, None] + jnp.arange(CONT, dtype=jnp.int32)[None, :]
    return (prompt_positions, follow_positions)


def norm_scale(values):
    return lax.rsqrt(jnp.mean(values * values, axis=-1, keepdims=True) + EPS_NORM)


def norm_back(values, row_scale, gain_row, normed_grad):
    scaled = normed_grad * gain_row
    return row_scale * scaled - values * row_scale**3 * jnp.mean(
        scaled * values, axis=-1, keepdims=True
    )


def adam_step(master, first_moment, second_moment, gradient, decay_rate):
    first_new = BETA_ONE * first_moment + (1.0 - BETA_ONE) * gradient
    second_new = BETA_TWO * second_moment + (1.0 - BETA_TWO) * gradient * gradient
    correct_one = 1.0 - BETA_ONE**STEP
    correct_two = 1.0 - BETA_TWO**STEP
    update = first_new / correct_one / (jnp.sqrt(second_new / correct_two) + ADAM_EPS)
    return (-LEARN_RATE * (update + decay_rate * master), first_new, second_new)


def gate_parts(gate_values, up_values):
    gate_sigmoid = jax.nn.sigmoid(gate_values)
    gate_silu = gate_values * gate_sigmoid
    return (gate_sigmoid, gate_silu, (gate_silu * up_values).astype(LOW))


def gate_backward(activated_grad, gate_values, up_values, gate_sigmoid, gate_silu):
    gate_grad = (
        activated_grad * up_values * gate_sigmoid * (1.0 + gate_values * (1.0 - gate_sigmoid))
    ).astype(LOW)
    up_grad = (activated_grad * gate_silu).astype(LOW)
    return (gate_grad, up_grad)


def flip(index, bits):
    bit = 1
    while bit <= bits:
        if bits & bit:
            index = index + bit - 2 * bit * lax.rem(index // bit, 2)
        bit *= 2
    return index


def remote(source, target, send, recv, there):
    return pltpu.make_async_remote_copy(
        src_ref=source,
        dst_ref=target,
        send_sem=send,
        recv_sem=recv,
        device_id=there,
        device_id_type=MESH,
    )


def gather_kernel(
    lines,
    plane,
    prompt_rows,
    weight_ref,
    hidden_ref,
    forward_ref,
    weights_ref,
    rows_ref,
    gate_ref,
    first_ref,
    second_ref,
    local_sem,
    line_send,
    line_recv,
    rows_send,
    rows_recv,
    first_send,
    first_recv,
    near_send,
    near_recv,
    half_send,
    half_recv,
    core_send,
    core_recv,
    swap_send,
    swap_recv,
):
    g = lax.axis_index("grp")
    d = lax.axis_index("dp")
    evens = range(0, plane, 2)
    forward_halves = plane == 8
    near = (2, 4) if forward_halves else tuple(evens[1:])
    width = weight_ref.shape[1]
    cut = (width // 256) * 128

    barrier = pltpu.get_barrier_semaphore()
    for offset in range(1, plane):
        pl.semaphore_signal(barrier, inc=1, device_id=(g, flip(d, offset)), device_id_type=MESH)

    for step in range(1, lines):
        there = lax.rem(g + step, lines)
        pl.semaphore_signal(barrier, inc=1, device_id=(there, d), device_id_type=MESH)
    pl.semaphore_wait(barrier, plane + lines - 2)

    copy = remote
    own_rows = hidden_ref.at[pl.ds(0, prompt_rows)]

    def line_weight(way, step):
        block = g - step + 1 if way == 0 else g + step - 1
        source = weight_ref if step == 1 else weights_ref.at[block, d]
        return copy(
            source,
            weights_ref.at[block, d],
            line_send.at[way, step],
            line_recv.at[way, step],
            (g + 1 if way == 0 else g - 1, d),
        )

    def line_rows(way, step):
        block = g - step + 1 if way == 0 else g + step - 1
        source = own_rows if step == 1 else rows_ref.at[block]
        return copy(
            source,
            rows_ref.at[block],
            rows_send.at[way, step],
            rows_recv.at[way, step],
            (g + 1 if way == 0 else g - 1, d),
        )

    def line_first(way, step):
        block = g - step + 1 if way == 0 else g + step - 1
        return copy(
            first_ref.at[block],
            first_ref.at[block],
            first_send.at[way, step],
            first_recv.at[way, step],
            (g + 1 if way == 0 else g - 1, d),
        )

    def sends(way, step):
        if way == 0:
            return (g < lines - 1) & (g >= step - 1)
        return (g > 0) & (g + step - 1 < lines)

    def receives(way, step):
        return g >= step if way == 0 else g + step < lines

    def near_copy(block, offset, own):
        source = weight_ref if own else weights_ref.at[block, d]
        at = near.index(offset)
        return copy(
            source,
            weights_ref.at[block, d],
            near_send.at[block, at],
            near_recv.at[block, at],
            (g, flip(d, offset)),
        )

    def half_copy(block, part):
        columns = pl.ds(0, cut) if part == 0 else pl.ds(cut, width - cut)
        origin = flip(d, 2) if part == 0 else flip(d, 4)
        there = flip(d, 4) if part == 0 else flip(d, 2)
        piece = weights_ref.at[block, origin, :, columns]
        return copy(
            piece, piece, half_send.at[block, part], half_recv.at[block, part], (g, there)
        )

    def core_copy(block, offset, own=False):
        source = weight_ref if own else weights_ref.at[block, flip(d, offset)]
        return copy(
            source,
            weights_ref.at[block, flip(d, offset)],
            core_send.at[block, offset // 2],
            core_recv.at[block, offset // 2],
            (g, flip(d, 1)),
        )

    half_hidden = second_ref.shape[2]
    own_hidden = 2 * half_hidden

    def swap_piece(owner, part, source_index):
        if part < 2:
            source = forward_ref.at[:, pl.ds(part * FF + owner * own_hidden, own_hidden)]
            return source, gate_ref.at[source_index, :, pl.ds(part * own_hidden, own_hidden)]
        start = 2 * FF + owner * own_hidden + (part - 2) * half_hidden
        source = forward_ref.at[:, pl.ds(start, half_hidden)]
        return source, first_ref.at[g, source_index] if part == 2 else second_ref.at[source_index]

    def swap_copy(offset, part):
        source, target = swap_piece(flip(d, offset), part, d)
        return copy(
            source,
            target,
            swap_send.at[offset, part],
            swap_recv.at[offset, part],
            (g, flip(d, offset)),
        )

    locals_ = (
        pltpu.make_async_copy(weight_ref, weights_ref.at[g, d], local_sem.at[0]),
        pltpu.make_async_copy(own_rows, rows_ref.at[g], local_sem.at[1]),
        *(
            pltpu.make_async_copy(*swap_piece(d, part, d), local_sem.at[2 + part])
            for part in range(4)
        ),
    )

    def launch(block, own):
        for offset in near:
            near_copy(block, offset, own).start()
        core_copy(block, 0, own).start()

    def relay(block):
        for offset in near:
            near_copy(block, offset, False).wait_recv()
            core_copy(block, offset).start()
        if forward_halves:
            half_copy(block, 0).start()
            half_copy(block, 1).start()

    def finish(block):
        if forward_halves:
            half_copy(block, 0).wait_recv()
            half_copy(block, 1).wait_recv()
            core_copy(block, 6).start()

    def both(step, act):
        for way in (0, 1):
            pl.when(receives(way, step))(
                lambda way=way: act(g - step if way == 0 else g + step)
            )

    def take_rows(step):
        for way in (0, 1):

            @pl.when(receives(way, step))
            def _(way=way):
                line_rows(way, step).wait_recv()

            if step + 1 < lines:
                pl.when(sends(way, step + 1))(
                    lambda way=way: line_rows(way, step + 1).start()
                )

    for way in (0, 1):
        pl.when(sends(way, 1))(lambda way=way: line_weight(way, 1).start())
    launch(g, True)
    for one in locals_:
        one.start()
    for step in range(1, lines):
        for way in (0, 1):

            @pl.when(receives(way, step))
            def _(way=way, step=step):
                line_weight(way, step).wait_recv()

            if step + 1 < lines:
                pl.when(sends(way, step + 1))(
                    lambda way=way, step=step: line_weight(way, step + 1).start()
                )
            else:
                pl.when(sends(way, 1))(lambda way=way: line_rows(way, 1).start())

        both(step, lambda block: launch(block, False))
        if step == 1:
            relay(g)
            for offset in range(1, plane):
                for part in (2, 0, 1, 3):
                    swap_copy(offset, part).start()
    for step in range(1, lines):
        take_rows(step)
        if step == lines - 1:
            locals_[4].wait()
            for offset in range(1, plane):
                swap_copy(offset, 2).wait_recv()
            for way in (0, 1):
                pl.when(sends(way, 1))(lambda way=way: line_first(way, 1).start())
        both(step, relay)
        if step == 1:
            finish(g)
        elif step < lines - 1:
            both(step - 1, finish)
    for step in range(1, lines):
        for way in (0, 1):

            @pl.when(receives(way, step))
            def _(way=way, step=step):
                line_first(way, step).wait_recv()

            if step + 1 < lines:
                pl.when(sends(way, step + 1))(
                    lambda way=way, step=step: line_first(way, step + 1).start()
                )
        if step == 1:
            both(lines - 2, finish)
    both(lines - 1, finish)

    def drain(block):
        for offset in evens:
            core_copy(block, offset).wait()
        for offset in near:
            near_copy(block, offset, False).wait_send()
        if forward_halves:
            half_copy(block, 0).wait_send()
            half_copy(block, 1).wait_send()

    drain(g)
    for step in range(1, lines):
        for way in (0, 1):
            pl.when(receives(way, step))(
                lambda way=way, step=step: drain(g - step if way == 0 else g + step)
            )

            @pl.when(sends(way, step))
            def _(way=way, step=step):
                line_weight(way, step).wait_send()
                line_rows(way, step).wait_send()
                line_first(way, step).wait_send()

    for offset in range(1, plane):
        for part in (0, 1, 3):
            swap_copy(offset, part).wait()
        swap_copy(offset, 2).wait_send()
    for at, one in enumerate(locals_):
        if at != 4:
            one.wait()


def gather_start(weight, hidden, forward):
    lines, plane = lax.axis_size("grp"), lax.axis_size("dp")
    prompt_rows = PROMPT_LEN // lines
    own_rows, width = weight.shape
    anywhere = pl.BlockSpec(memory_space=pl.ANY)
    dma = pltpu.SemaphoreType.DMA
    near_count = 2 if plane == 8 else plane // 2 - 1
    pairs = (
        (2, lines),
        (2, lines),
        (2, lines),
        (2, lines),
        (2, lines),
        (2, lines),
        (lines, near_count),
        (lines, near_count),
        (lines, 2),
        (lines, 2),
        (lines, plane // 2),
        (lines, plane // 2),
        (plane, 4),
        (plane, 4),
    )
    own_hidden = FF // plane
    return pl.pallas_call(
        functools.partial(gather_kernel, lines, plane, prompt_rows),
        out_shape=(
            jax.ShapeDtypeStruct((lines, plane, own_rows, width), weight.dtype),
            jax.ShapeDtypeStruct((lines, prompt_rows, D), hidden.dtype),
            jax.ShapeDtypeStruct((plane, own_rows, 2 * own_hidden), forward.dtype),
            jax.ShapeDtypeStruct((lines, plane, own_rows, own_hidden // 2), forward.dtype),
            jax.ShapeDtypeStruct((plane, own_rows, own_hidden // 2), forward.dtype),
        ),
        in_specs=[anywhere] * 3,
        out_specs=(anywhere,) * 5,
        scratch_shapes=[dma((6,))] + [dma(shape) for shape in pairs],
        compiler_params=pltpu.CompilerParams(collective_id=0, has_side_effects=True),
        name="gather_start",
    )(weight, hidden, forward)


def project_kernel(
    place_ref,
    group_ref,
    own_ref,
    gain_ref,
    cosine_ref,
    sine_ref,
    weight_ref,
    query_ref,
    pair_ref,
    normed_ref,
    own_normed_ref,
    scale_ref,
):
    step = pl.program_id(0)
    own_rows = own_ref.shape[0]
    prompt_rows = own_rows - CONT
    start = pl.multiple_of(place_ref[0] * prompt_rows, 16)
    tile = 32

    def norm_tile(values, at):
        values = values.astype(FULL)
        scale = lax.rsqrt(jnp.mean(values * values, axis=-1, keepdims=True) + EPS_NORM)
        normed_ref[pl.ds(at, tile)] = (values * scale * gain_ref[...]).astype(LOW)
        scale_ref[pl.ds(at, tile)] = jnp.broadcast_to(scale, (tile, 128))

    @pl.when(step == 0)
    def _():
        @pl.loop(0, PROMPT_LEN // tile)
        def _(at):
            first = pl.multiple_of(at * tile, tile)
            norm_tile(group_ref[pl.ds(first, tile)], first)

        for at in range(0, CONT, tile):
            norm_tile(own_ref[prompt_rows + at : prompt_rows + at + tile], PROMPT_LEN + at)
        own_normed_ref[:prompt_rows] = normed_ref[pl.ds(start, prompt_rows)]
        own_normed_ref[prompt_rows:] = normed_ref[PROMPT_LEN:]

    def turn(values, cosine, sine_part):
        front, back = values[:, : HD // 2], values[:, HD // 2 :]
        return front * cosine - back * sine_part, back * cosine + front * sine_part

    def project(rows):
        return jnp.dot(rows, weight_ref[...], preferred_element_type=FULL)

    @pl.when(step < HQ)
    def _():
        for first, count, table in ((0, prompt_rows, start), (prompt_rows, CONT, PROMPT_LEN)):
            values = project(own_normed_ref[first : first + count])
            front, back = turn(
                values, cosine_ref[pl.ds(table, count)], sine_ref[pl.ds(table, count)]
            )
            query_ref[first : first + count, : HD // 2] = front.astype(LOW)
            query_ref[first : first + count, HD // 2 :] = back.astype(LOW)

    key_count = PROMPT_LEN + CONT
    part = key_count // 4

    @pl.when((step >= HQ) & (step < HQ + HK))
    def _():
        @pl.loop(0, 4)
        def _(at):
            rows = pl.ds(pl.multiple_of(at * part, 16), part)
            front, back = turn(project(normed_ref[rows]), cosine_ref[rows], sine_ref[rows])
            pair_ref[rows, : HD // 2] = front.astype(LOW)
            pair_ref[rows, HD // 2 :] = back.astype(LOW)

    @pl.when(step >= HQ + HK)
    def _():
        @pl.loop(0, 4)
        def _(at):
            rows = pl.ds(pl.multiple_of(at * part, 16), part)
            pair_ref[rows] = project(normed_ref[rows]).astype(LOW)


VMEM_LIMIT = 60 * 2**20


def project_heads(place, group_rows, own_inputs, gain_row, cosine, sine_part, weights):
    own_rows = own_inputs.shape[0]
    key_count = PROMPT_LEN + CONT
    whole = lambda shape: pl.BlockSpec(shape, lambda j, p: (0, 0))
    return pl.pallas_call(
        project_kernel,
        grid_spec=pltpu.PrefetchScalarGridSpec(
            num_scalar_prefetch=1,
            grid=(HQ + 2 * HK,),
            in_specs=[
                whole((PROMPT_LEN, D)),
                whole((own_rows, D)),
                whole((1, D)),
                whole((key_count, HD // 2)),
                whole((key_count, HD // 2)),
                pl.BlockSpec((D, HD), lambda j, p: (0, j)),
            ],
            out_specs=[
                pl.BlockSpec((own_rows, HD), lambda j, p: (0, jnp.minimum(j, HQ - 1))),
                pl.BlockSpec((key_count, HD), lambda j, p: (0, jnp.maximum(j - HQ, 0))),
                whole((key_count, D)),
                whole((own_rows, D)),
                whole((key_count, 128)),
            ],
        ),
        out_shape=[
            jax.ShapeDtypeStruct((own_rows, HQ * HD), LOW),
            jax.ShapeDtypeStruct((key_count, 2 * HK * HD), LOW),
            jax.ShapeDtypeStruct((key_count, D), LOW),
            jax.ShapeDtypeStruct((own_rows, D), LOW),
            jax.ShapeDtypeStruct((key_count, 128), FULL),
        ],
        compiler_params=pltpu.CompilerParams(vmem_limit_bytes=VMEM_LIMIT),
        name="project_heads",
    )(place, group_rows, own_inputs, gain_row, cosine, sine_part, weights)


def across(left, right):
    return lax.dot_general(left, right, (((1,), (1,)), ((), ())), preferred_element_type=FULL)


def along(left, right):
    return lax.dot_general(left, right, (((0,), (0,)), ((), ())), preferred_element_type=FULL)


def attend_kernel(query_ref, key_ref, value_ref, seen_ref, attended_ref, logsum_ref):
    group_heads = HQ // HK
    for head in range(group_heads):
        columns = slice(head * HD, (head + 1) * HD)
        scores = across(query_ref[:, columns], key_ref[...]) * HD ** (-0.5)
        scores = jnp.where(seen_ref[...] > 0, scores, MASK_FILL)
        peak = jnp.max(scores, axis=-1, keepdims=True)
        unnormed = jnp.exp(scores - peak)
        total = jnp.sum(unnormed, axis=-1, keepdims=True)
        low = (unnormed / total).astype(LOW)
        attended_ref[:, columns] = jnp.dot(
            low, value_ref[...], preferred_element_type=FULL
        ).astype(LOW)
        logsum_ref[:, head * 128 : (head + 1) * 128] = jnp.broadcast_to(
            peak + jnp.log(total), (query_ref.shape[0], 128)
        )


def attend(queries, pairs, seen):
    rows, key_count = seen.shape
    group_heads = HQ // HK
    return pl.pallas_call(
        attend_kernel,
        grid=(HK,),
        in_specs=[
            pl.BlockSpec((rows, group_heads * HD), lambda j: (0, j)),
            pl.BlockSpec((key_count, HD), lambda j: (0, j)),
            pl.BlockSpec((key_count, HD), lambda j: (0, HK + j)),
            pl.BlockSpec((rows, key_count), lambda j: (0, 0)),
        ],
        out_specs=[
            pl.BlockSpec((rows, group_heads * HD), lambda j: (0, j)),
            pl.BlockSpec((rows, group_heads * 128), lambda j: (0, j)),
        ],
        out_shape=[
            jax.ShapeDtypeStruct((rows, HQ * HD), LOW),
            jax.ShapeDtypeStruct((rows, HQ * 128), FULL),
        ],
        compiler_params=pltpu.CompilerParams(vmem_limit_bytes=VMEM_LIMIT),
        name="attend",
    )(queries, pairs, pairs, seen)


def attend_back_kernel(
    place_ref,
    query_ref,
    key_ref,
    value_ref,
    seen_ref,
    logsum_ref,
    grad_ref,
    cosine_ref,
    sine_ref,
    query_out,
    pair_out,
):
    step = pl.program_id(0)
    group_heads = HQ // HK
    rows = query_ref.shape[0]
    prompt_rows = rows - CONT
    start = pl.multiple_of(place_ref[0] * prompt_rows, 16)
    score_scale = HD ** (-0.5)
    key_grad = value_grad = 0.0

    def turn_back(values, cosine, sine_part):
        front, back = values[:, : HD // 2], values[:, HD // 2 :]
        return jnp.concatenate(
            [front * cosine + back * sine_part, back * cosine - front * sine_part], axis=1
        ).astype(LOW)

    for head in range(group_heads):
        columns = slice(head * HD, (head + 1) * HD)
        scores = across(query_ref[:, columns], key_ref[...]) * score_scale
        scores = jnp.where(seen_ref[...] > 0, scores, MASK_FILL)
        probabilities = jnp.exp(scores - logsum_ref[:, head * 128 : head * 128 + 1])
        grads = grad_ref[:, columns]
        probability_grad = across(grads, value_ref[...])
        delta = jnp.sum(probabilities * probability_grad, axis=-1, keepdims=True)
        score_grad = (probabilities * (probability_grad - delta)).astype(LOW)
        query_grad = jnp.dot(score_grad, key_ref[...], preferred_element_type=FULL) * score_scale
        key_grad = key_grad + along(score_grad, query_ref[:, columns])
        value_grad = value_grad + along(probabilities.astype(LOW), grads)
        query_out[:prompt_rows, columns] = turn_back(
            query_grad[:prompt_rows],
            cosine_ref[pl.ds(start, prompt_rows)],
            sine_ref[pl.ds(start, prompt_rows)],
        )
        query_out[prompt_rows:, columns] = turn_back(
            query_grad[prompt_rows:], cosine_ref[PROMPT_LEN:], sine_ref[PROMPT_LEN:]
        )
    pair_out[:, pl.ds(pl.multiple_of(step * HD, HD), HD)] = turn_back(
        key_grad * score_scale, cosine_ref[...], sine_ref[...]
    )
    pair_out[:, pl.ds(pl.multiple_of((HK + step) * HD, HD), HD)] = value_grad.astype(LOW)


def attend_back(place, queries, pairs, seen, logsum, grads, cosine, sine_part):
    rows, key_count = seen.shape
    group_heads = HQ // HK
    whole = lambda shape: pl.BlockSpec(shape, lambda j, p: (0, 0))
    return pl.pallas_call(
        attend_back_kernel,
        grid_spec=pltpu.PrefetchScalarGridSpec(
            num_scalar_prefetch=1,
            grid=(HK,),
            in_specs=[
                pl.BlockSpec((rows, group_heads * HD), lambda j, p: (0, j)),
                pl.BlockSpec((key_count, HD), lambda j, p: (0, j)),
                pl.BlockSpec((key_count, HD), lambda j, p: (0, HK + j)),
                whole((rows, key_count)),
                pl.BlockSpec((rows, group_heads * 128), lambda j, p: (0, j)),
                pl.BlockSpec((rows, group_heads * HD), lambda j, p: (0, j)),
                whole((key_count, HD // 2)),
                whole((key_count, HD // 2)),
            ],
            out_specs=[
                pl.BlockSpec((rows, group_heads * HD), lambda j, p: (0, j)),
                whole((key_count, 2 * HK * HD)),
            ],
        ),
        out_shape=[
            jax.ShapeDtypeStruct((rows, HQ * HD), LOW),
            jax.ShapeDtypeStruct((key_count, 2 * HK * HD), LOW),
        ],
        compiler_params=pltpu.CompilerParams(vmem_limit_bytes=VMEM_LIMIT),
        name="attend_back",
    )(place, queries, pairs, pairs, seen, logsum, grads, cosine, sine_part)


def weights_back_kernel(
    place_ref,
    query_ref,
    pair_ref,
    branch_ref,
    attended_ref,
    normed_ref,
    own_normed_ref,
    group_ref,
    own_ref,
    scale_ref,
    query_weight_ref,
    pair_weight_ref,
    query_term,
    pair_term,
    merge_term,
    back_out,
    pair_back_out,
    gain_out,
):
    rows = query_ref.shape[0]
    prompt_rows = rows - CONT
    start = pl.multiple_of(place_ref[0] * prompt_rows, 16)
    query_term[...] = along(own_normed_ref[...], query_ref[...]).astype(LOW)
    pair_term[...] = along(normed_ref[...], pair_ref[...]).astype(LOW)
    merge_term[...] = along(branch_ref[...], attended_ref[...]).astype(LOW)
    query_back = across(query_ref[...], query_weight_ref[...])
    pair_back = across(pair_ref[...], pair_weight_ref[...])
    own_values = own_ref[prompt_rows:].astype(FULL) * scale_ref[PROMPT_LEN:, :1]
    tail = query_back[prompt_rows:] + pair_back[PROMPT_LEN:]
    group_values = group_ref[...].astype(FULL) * scale_ref[:PROMPT_LEN, :1]
    own_prompt = own_ref[:prompt_rows].astype(FULL) * scale_ref[pl.ds(start, prompt_rows), :1]
    gain_out[...] = (
        jnp.sum(pair_back[:PROMPT_LEN] * group_values, axis=0, keepdims=True)
        + jnp.sum(query_back[:prompt_rows] * own_prompt, axis=0, keepdims=True)
        + jnp.sum(tail * own_values, axis=0, keepdims=True)
    )
    back_out[:prompt_rows] = query_back[:prompt_rows]
    back_out[prompt_rows:] = tail
    pair_back_out[...] = pair_back[:PROMPT_LEN].astype(LOW)


def weights_back(
    place, queries, pairs, branch, attended, normed, own_normed, group_rows, own_inputs, scale, weights
):
    rows, key_count = queries.shape[0], pairs.shape[0]
    wide, tile = HQ * HD, 256
    whole = lambda shape: pl.BlockSpec(shape, lambda j, p: (0, 0))
    tall = lambda count: pl.BlockSpec((count, tile), lambda j, p: (0, j))
    flat = lambda at: pl.BlockSpec((tile, wide), lambda j, p: (j, at))
    return pl.pallas_call(
        weights_back_kernel,
        grid_spec=pltpu.PrefetchScalarGridSpec(
            num_scalar_prefetch=1,
            grid=(D // tile,),
            in_specs=[
                whole((rows, wide)),
                whole((key_count, wide)),
                tall(rows),
                whole((rows, wide)),
                tall(key_count),
                tall(rows),
                tall(PROMPT_LEN),
                tall(rows),
                whole((key_count, 128)),
                flat(0),
                flat(1),
            ],
            out_specs=[flat(0), flat(0), flat(0), tall(rows), tall(PROMPT_LEN), tall(1)],
        ),
        out_shape=[
            jax.ShapeDtypeStruct((D, wide), LOW),
            jax.ShapeDtypeStruct((D, wide), LOW),
            jax.ShapeDtypeStruct((D, wide), LOW),
            jax.ShapeDtypeStruct((rows, D), FULL),
            jax.ShapeDtypeStruct((PROMPT_LEN, D), LOW),
            jax.ShapeDtypeStruct((1, D), FULL),
        ],
        compiler_params=pltpu.CompilerParams(vmem_limit_bytes=VMEM_LIMIT),
        name="weights_back",
    )(
        place,
        queries,
        pairs,
        branch,
        attended,
        normed,
        own_normed,
        group_rows,
        own_inputs,
        scale,
        weights,
        weights,
    )


def forward_back_kernel(
    activated_ref, grad_ref, gate_up_ref, first_ref, second_ref, out_ref, gate_up_grad_ref
):
    own_hidden = activated_ref.shape[1]
    part = first_ref.shape[0] // 4
    piece = own_hidden // 2

    @pl.loop(0, 4)
    def _(at):
        columns = pl.ds(pl.multiple_of(at * part, part), part)
        out_ref[:, columns] = (
            across(activated_ref[:, :piece], first_ref[columns])
            + across(activated_ref[:, piece:], second_ref[columns])
        ).astype(LOW)

    for at, down_ref in enumerate((first_ref, second_ref)):
        columns = slice(at * piece, (at + 1) * piece)
        upper = slice(own_hidden + at * piece, own_hidden + (at + 1) * piece)
        activated_grad = jnp.dot(grad_ref[...], down_ref[...], preferred_element_type=FULL)
        gate_values, up_values = gate_up_ref[:, columns], gate_up_ref[:, upper]
        gate_sigmoid = jax.nn.sigmoid(gate_values)
        gate_grad, up_grad = gate_backward(
            activated_grad, gate_values, up_values, gate_sigmoid, gate_values * gate_sigmoid
        )
        gate_up_grad_ref[:, columns] = gate_grad
        gate_up_grad_ref[:, upper] = up_grad


def forward_back(rows, activated, grads, gate_up, first_down, second_down):
    count, own_hidden = activated.shape
    block = lambda width: pl.BlockSpec((rows, width), lambda j: (j, 0))
    return pl.pallas_call(
        forward_back_kernel,
        grid=(count // rows,),
        in_specs=[
            block(own_hidden),
            block(D),
            block(2 * own_hidden),
            pl.BlockSpec(first_down.shape, lambda j: (0, 0)),
            pl.BlockSpec(second_down.shape, lambda j: (0, 0)),
        ],
        out_specs=[block(D), block(2 * own_hidden)],
        out_shape=[
            jax.ShapeDtypeStruct((count, D), LOW),
            jax.ShapeDtypeStruct((count, 2 * own_hidden), LOW),
        ],
        compiler_params=pltpu.CompilerParams(vmem_limit_bytes=VMEM_LIMIT),
        name="forward_back",
    )(activated, grads, gate_up, first_down, second_down)


def plane_back_kernel(
    plane,
    rows_ref,
    weight_ref,
    down_ref,
    out_ref,
    swapped_ref,
    weight,
    tiles,
    keep,
    give,
    core_in,
    plane_in,
    total,
    load_sem,
    tile_sem,
    core_send,
    core_recv,
    plane_send,
    plane_recv,
    out_sem,
    swap_send,
    swap_recv,
):
    g = lax.axis_index("grp")
    d = lax.axis_index("dp")
    chips = plane // 2
    own_hidden = down_ref.shape[2]
    halves = plane == 8
    order = (3, 1, 2, 0) if halves else tuple(range(chips - 1, -1, -1))
    cut = D // 2
    half_of = (pl.ds(0, cut), pl.ds(cut, D - cut))

    barrier = pltpu.get_barrier_semaphore()
    for offset in range(1, plane):
        pl.semaphore_signal(
            barrier, inc=1, device_id=(g, flip(d, offset)), device_id_type=MESH
        )

    load = pltpu.make_async_copy(weight_ref, weight, load_sem.at[0])
    load.start()

    def tile_copy(turn):
        at = order[turn]
        return pltpu.make_async_copy(
            rows_ref.at[pl.ds(2 * at, 2)], tiles.at[turn % 2], tile_sem.at[turn % 2]
        )

    def core_copy(at):
        return remote(
            give.at[at], core_in.at[at], core_send.at[at], core_recv.at[at], (g, flip(d, 1))
        )

    def plane_copy(at):
        return remote(
            keep.at[at],
            plane_in.at[at],
            plane_send.at[at],
            plane_recv.at[at],
            (g, flip(d, 2 * at)),
        )

    def near_copy(part, relayed):
        there = part + 1
        return remote(
            keep.at[3 if relayed else there, :, half_of[part]],
            plane_in.at[1 if relayed else 0, :, half_of[part]],
            plane_send.at[2 * relayed + part],
            plane_recv.at[2 * relayed + part],
            (g, flip(d, 2 * there)),
        )

    def relay_copy(part):
        there = 2 - part
        return remote(
            keep.at[there, :, half_of[part]],
            plane_in.at[2, :, half_of[part]],
            plane_send.at[4 + part],
            plane_recv.at[4 + part],
            (g, flip(d, 2 * there)),
        )

    def swap_copy(offset):
        there = flip(d, offset)
        return remote(
            down_ref.at[there],
            swapped_ref.at[:, pl.ds(d * own_hidden, own_hidden)],
            swap_send.at[offset],
            swap_recv.at[offset],
            (g, there),
        )

    own_swap = pltpu.make_async_copy(
        down_ref.at[d], swapped_ref.at[:, pl.ds(d * own_hidden, own_hidden)], out_sem.at[1]
    )
    tile_copy(0).start()
    tile_copy(1).start()
    pl.semaphore_wait(barrier, plane - 1)
    for offset in range(1, plane):
        swap_copy(offset).start()
    own_swap.start()
    load.wait()
    part_width = 512

    def product(turn, which, target):
        @pl.loop(0, D // part_width)
        def _(at):
            columns = pl.ds(pl.multiple_of(at * part_width, part_width), part_width)
            target[order[turn], :, columns] = across(
                tiles[turn % 2, which], weight[columns]
            ).astype(LOW)

    def add_into(at, other, first, count):
        step = 256

        @pl.loop(0, count // step)
        def _(k):
            here = pl.ds(pl.multiple_of(first + k * step, step), step)
            keep[at, :, here] = (
                keep[at, :, here].astype(FULL) + other(here).astype(FULL)
            ).astype(LOW)

    def settle(turn):
        at = order[turn]
        core_copy(at).wait_recv()
        add_into(at, lambda here: core_in[at, :, here], 0, D)
        if halves and at == 3:
            near_copy(0, True).start()
            near_copy(1, True).start()
        elif halves and at:
            near_copy(at - 1, False).start()
        elif at:
            plane_copy(at).start()

    for turn in range(chips):
        tile_copy(turn).wait()
        product(turn, 1, give)
        core_copy(order[turn]).start()
        if turn:
            settle(turn - 1)
        product(turn, 0, keep)
        if turn + 2 < chips:
            tile_copy(turn + 2).start()
        if halves and turn == chips - 1:
            for part in range(2):
                near_copy(part, True).wait_recv()
                add_into(
                    2 - part,
                    lambda here: plane_in[1, :, here],
                    part * cut,
                    cut,
                )
                relay_copy(part).start()
    settle(chips - 1)
    if halves:
        for part in range(2):
            near_copy(part, False).wait_recv()
            relay_copy(part).wait_recv()
        arrived = (0, 2)
    else:
        for at in range(1, chips):
            plane_copy(at).wait_recv()
        arrived = tuple(range(1, chips))

    @pl.loop(0, D // 256)
    def _(k):
        here = pl.ds(pl.multiple_of(k * 256, 256), 256)
        value = keep[0, :, here].astype(FULL)
        for at in arrived:
            value = value + plane_in[at, :, here].astype(FULL)
        total[:, here] = value

    out = pltpu.make_async_copy(total, out_ref, out_sem.at[0])
    out.start()
    for at in range(chips):
        core_copy(at).wait_send()
    if halves:
        for part in range(2):
            near_copy(part, False).wait_send()
            near_copy(part, True).wait_send()
            relay_copy(part).wait_send()
    else:
        for at in range(1, chips):
            plane_copy(at).wait_send()
    for offset in range(1, plane):
        swap_copy(offset).wait()
    own_swap.wait()
    out.wait()


def plane_back(rows, gate_up_grad, gate_weight, down_part):
    plane = lax.axis_size("dp")
    chips = plane // 2
    inner = gate_up_grad.shape[1]
    anywhere = pl.BlockSpec(memory_space=pl.ANY)
    dma = pltpu.SemaphoreType.DMA
    return pl.pallas_call(
        functools.partial(plane_back_kernel, plane),
        out_shape=(
            jax.ShapeDtypeStruct((rows, D), FULL),
            jax.ShapeDtypeStruct((down_part.shape[1], FF), LOW),
        ),
        in_specs=[anywhere] * 3,
        out_specs=(anywhere,) * 2,
        scratch_shapes=[
            pltpu.VMEM((D, inner), LOW),
            pltpu.VMEM((2, 2, rows, inner), LOW),
            pltpu.VMEM((chips, rows, D), LOW),
            pltpu.VMEM((chips, rows, D), LOW),
            pltpu.VMEM((chips, rows, D), LOW),
            pltpu.VMEM((3 if plane == 8 else chips, rows, D), LOW),
            pltpu.VMEM((rows, D), FULL),
            dma((1,)),
            dma((2,)),
            dma((chips,)),
            dma((chips,)),
            dma((max(6, chips),)),
            dma((max(6, chips),)),
            dma((2,)),
            dma((plane,)),
            dma((plane,)),
        ],
        compiler_params=pltpu.CompilerParams(
            collective_id=2, has_side_effects=True, vmem_limit_bytes=VMEM_LIMIT
        ),
        name="plane_back",
    )(gate_up_grad.reshape(plane, rows, inner), gate_weight, down_part)


def plane_swap(block, offset):
    size = lax.axis_size("dp")
    return lax.ppermute(block, "dp", [(i, i ^ offset) for i in range(size)])


def plane_gather(block):
    mine = [block] + [plane_swap(block, o) for o in range(2, lax.axis_size("dp"), 2)]
    pairs = [(one, plane_swap(one, 1)) for one in mine]
    return jnp.concatenate([one for pair in pairs for one in pair], axis=0)


def line_scatter(term):
    return lax.psum_scatter(term, "grp", scatter_dimension=0, tiled=True)


def finish_kernel(
    lines,
    plane,
    query_ref,
    pair_ref,
    merge_ref,
    gain_ref,
    gate_ref,
    up_ref,
    down_ref,
    a_out,
    m_out,
    gain_out,
    f_out,
    mine,
    core_in,
    plane_in,
    line_in,
    owned,
    gain_made,
    mine_sem,
    core_send,
    core_recv,
    plane_send,
    plane_recv,
    line_send,
    line_recv,
    swap_send,
    swap_recv,
    own_sem,
    out_sem,
):
    g = lax.axis_index("grp")
    d = lax.axis_index("dp")
    chips = plane // 2
    chip, core = lax.div(d, 2), lax.rem(d, 2)
    partner = d + 1 - 2 * core
    own_hidden = gate_ref.shape[2]
    width = core_in.shape[3]
    a_width, m_width = a_out.shape[1], m_out.shape[1]
    parts, begin = [], 0
    for ref in (query_ref, pair_ref, merge_ref, gain_ref):
        parts.append((ref, pl.ds(begin, ref.shape[4])))
        begin += ref.shape[4]

    barrier = pltpu.get_barrier_semaphore()
    for step in range(1, plane):
        there = lax.rem(d + step, plane)
        pl.semaphore_signal(barrier, inc=1, device_id=(g, there), device_id_type=MESH)
    for step in range(1, lines):
        there = lax.rem(g + step, lines)
        pl.semaphore_signal(barrier, inc=1, device_id=(there, d), device_id_type=MESH)
    pl.semaphore_wait(barrier, plane + lines - 2)

    def line_at(turn):
        return lax.rem(g + turn + 1, lines)

    def core_copy(turn, part):
        line = line_at(turn)
        ref, columns = parts[part]
        return remote(
            ref.at[line, :, 1 - core],
            core_in.at[line, :, :, columns],
            core_send.at[turn, part],
            core_recv.at[turn, part],
            (g, partner),
        )

    def mine_copy(turn, part):
        line = line_at(turn)
        ref, columns = parts[part]
        return pltpu.make_async_copy(
            ref.at[line, :, core], mine.at[turn % 2, :, :, columns], mine_sem.at[turn, part]
        )

    cut = width // 256 * 128
    columns_of = (pl.ds(0, cut), pl.ds(cut, width - cut))

    def plane_copy(turn, step):
        line = line_at(turn)
        there = lax.rem(chip + step, chips)
        return remote(
            core_in.at[line, there],
            plane_in.at[line, chip],
            plane_send.at[turn, step],
            plane_recv.at[turn, step],
            (g, 2 * there + core),
        )

    def near_copy(turn, part, relayed):
        line = line_at(turn)
        there = flip(chip, part + 1)
        owner = flip(chip, 3) if relayed else there
        return remote(
            core_in.at[line, owner, :, columns_of[part]],
            plane_in.at[line, 1 if relayed else 0, :, columns_of[part]],
            plane_send.at[turn, 2 * relayed + part],
            plane_recv.at[turn, 2 * relayed + part],
            (g, 2 * there + core),
        )

    def relay_copy(turn, part):
        line = line_at(turn)
        there = flip(chip, 2 - part)
        return remote(
            core_in.at[line, there, :, columns_of[part]],
            plane_in.at[line, 2, :, columns_of[part]],
            plane_send.at[turn, 4 + part],
            plane_recv.at[turn, 4 + part],
            (g, 2 * there + core),
        )

    def line_copy(turn):
        line = line_at(turn)
        return remote(
            core_in.at[line, chip],
            line_in.at[g],
            line_send.at[turn],
            line_recv.at[turn],
            (line, d),
        )

    forward_refs = (gate_ref, up_ref)

    def swap_place(part):
        return f_out.at[:, pl.ds(part * FF + d * own_hidden, own_hidden)]

    def swap_copy(step, part):
        there = lax.rem(d + step, plane)
        return remote(
            forward_refs[part].at[there],
            swap_place(part),
            swap_send.at[step, part],
            swap_recv.at[step, part],
            (g, there),
        )

    own_swap = [
        pltpu.make_async_copy(forward_refs[part].at[d], swap_place(part), own_sem.at[part])
        for part in range(2)
    ] + [pltpu.make_async_copy(down_ref, f_out.at[:, pl.ds(2 * FF, FF)], own_sem.at[2])]

    every = range(len(parts))
    for turn in range(lines):
        for part in every:
            core_copy(turn, part).start()
            if turn < 2:
                mine_copy(turn, part).start()
        if turn == 0:
            for step in range(1, plane):
                for part in range(2):
                    swap_copy(step, part).start()
            for one in own_swap:
                one.start()
    tile = 896 if width % 896 == 0 else 128
    halves = plane == 8

    def add_into(line, there, other, columns=None):
        first, count = (0, width) if columns is None else columns
        step = tile if columns is None else 128

        @pl.loop(0, count // step)
        def _(at):
            here = pl.ds(pl.multiple_of(first + at * step, 128), step)
            total = core_in[line, there, :, here].astype(FULL) + other(here).astype(FULL)
            core_in[line, there, :, here] = total.astype(LOW)

    def near_start(turn):
        if halves:
            for relayed in (True, False):
                for part in range(2):
                    near_copy(turn, part, relayed).start()
        else:
            for step in range(1, chips):
                plane_copy(turn, step).start()

    for turn in range(lines):
        line = line_at(turn)
        for part in every:
            core_copy(turn, part).wait_recv()
            mine_copy(turn, part).wait()
        for step in range(1, chips + 1):
            there = lax.rem(chip + step, chips)
            add_into(
                line, there, lambda here, there=there, turn=turn: mine[turn % 2, there, :, here]
            )
        if turn + 2 < lines:
            for part in every:
                mine_copy(turn + 2, part).start()
        if turn < 2:
            near_start(turn)

    def pass_on(turn):
        line = line_at(turn)
        for part, columns in enumerate(((0, cut), (cut, width - cut))):
            near_copy(turn, part, True).wait_recv()
            add_into(
                line,
                flip(chip, 2 - part),
                lambda here, line=line: plane_in[line, 1, :, here],
                columns,
            )
            relay_copy(turn, part).start()

    def near_done(turn):
        if halves:
            pass_on(turn)
            for part in range(2):
                near_copy(turn, part, False).wait_recv()
        else:
            for step in range(1, chips):
                plane_copy(turn, step).wait_recv()
        if turn + 2 < lines:
            near_start(turn + 2)

    def line_done(turn):
        line = line_at(turn)
        if halves:
            for part in range(2):
                relay_copy(turn, part).wait_recv()
            arrived = (0, 2)
        else:
            arrived = tuple(lax.rem(chip + step, chips) for step in range(1, chips))

        @pl.loop(0, width // tile)
        def _(at):
            columns = pl.ds(pl.multiple_of(at * tile, tile), tile)
            total = core_in[line, chip, :, columns].astype(FULL)
            for block in arrived:
                total = total + plane_in[line, block, :, columns].astype(FULL)
            core_in[line, chip, :, columns] = total.astype(LOW)

        if turn < lines - 1:
            line_copy(turn).start()

    near_done(0)
    for turn in range(1, lines):
        near_done(turn)
        line_done(turn - 1)
    line_done(lines - 1)
    for turn in range(lines - 1):
        line_copy(turn).wait_recv()

    def total_of(columns):
        total = core_in[g, chip, :, columns].astype(FULL)
        for step in range(1, lines):
            total = total + line_in[lax.rem(g + step, lines), :, columns].astype(FULL)
        return total

    @pl.loop(0, (a_width + m_width) // 256)
    def _(at):
        columns = pl.ds(pl.multiple_of(at * 256, 256), 256)
        owned[:, columns] = total_of(columns)

    gain_made[...] = total_of(pl.ds(a_width + m_width, GAIN_PAD)).T[:8]
    outs = (
        pltpu.make_async_copy(owned.at[:, pl.ds(0, a_width)], a_out, out_sem.at[0]),
        pltpu.make_async_copy(owned.at[:, pl.ds(a_width, m_width)], m_out, out_sem.at[1]),
        pltpu.make_async_copy(gain_made, gain_out, out_sem.at[2]),
    )
    for one in outs:
        one.start()
    for turn in range(lines):
        for part in every:
            core_copy(turn, part).wait_send()
        if halves:
            for part in range(2):
                near_copy(turn, part, False).wait_send()
                near_copy(turn, part, True).wait_send()
                relay_copy(turn, part).wait_send()
        else:
            for step in range(1, chips):
                plane_copy(turn, step).wait_send()
        if turn < lines - 1:
            line_copy(turn).wait_send()
    for step in range(1, plane):
        for part in range(2):
            swap_copy(step, part).wait()
    for one in own_swap:
        one.wait()
    for one in outs:
        one.wait()


def finish(terms, gate_part, up_part, down_swapped):
    lines, plane = lax.axis_size("grp"), lax.axis_size("dp")
    chips = plane // 2
    rows = D // (lines * plane)
    m_width = terms[2].shape[1]
    a_width = terms[0].shape[1] + terms[1].shape[1]
    width = a_width + m_width + GAIN_PAD
    anywhere = pl.BlockSpec(memory_space=pl.ANY)
    dma = pltpu.SemaphoreType.DMA
    vmem = pltpu.VMEM
    return pl.pallas_call(
        functools.partial(finish_kernel, lines, plane),
        out_shape=(
            jax.ShapeDtypeStruct((rows, a_width), FULL),
            jax.ShapeDtypeStruct((rows, m_width), FULL),
            jax.ShapeDtypeStruct((8, rows), FULL),
            jax.ShapeDtypeStruct((rows, 3 * FF), LOW),
        ),
        in_specs=[anywhere] * 7,
        out_specs=(anywhere,) * 4,
        scratch_shapes=[
            vmem((2, chips, rows, width), LOW),
            vmem((lines, chips, rows, width), LOW),
            vmem((lines, 3 if plane == 8 else chips, rows, width), LOW),
            vmem((lines, rows, width), LOW),
            vmem((rows, a_width + m_width), FULL),
            vmem((8, rows), FULL),
            dma((lines, 4)),
            dma((lines, 4)),
            dma((lines, 4)),
            dma((lines, max(6, chips))),
            dma((lines, max(6, chips))),
            dma((lines,)),
            dma((lines,)),
            dma((plane, 2)),
            dma((plane, 2)),
            dma((3,)),
            dma((3,)),
        ],
        compiler_params=pltpu.CompilerParams(
            collective_id=1, has_side_effects=True, vmem_limit_bytes=VMEM_LIMIT
        ),
        name="finish",
    )(
        *(term.reshape(lines, chips, 2, rows, term.shape[1]) for term in terms),
        gate_part.reshape(plane, rows, -1),
        up_part.reshape(plane, rows, -1),
        down_swapped,
    )


def body(
    hidden,
    cotangent,
    segment_ids,
    continuation_prompt,
    gain_master,
    gain_first,
    gain_second,
    attention_master,
    attention_first,
    attention_second,
    merge_master,
    merge_first,
    merge_second,
    feedforward_master,
    feedforward_first,
    feedforward_second,
):
    group_index = lax.axis_index("grp")
    dp_size = lax.axis_size("dp")
    row_count = hidden.shape[2]
    prompt_rows = row_count - CONT
    qkv_width = (HQ + 2 * HK) * HD
    own_rows = feedforward_master.shape[0]
    own_hidden = FF // dp_size
    own_inputs = hidden.reshape(row_count, D)

    gain_columns = jnp.pad(gain_master.T, ((0, 0), (0, GAIN_PAD - 2)))
    weight_low = jnp.concatenate(
        [attention_master.astype(LOW), merge_master.astype(LOW), gain_columns.astype(LOW)], axis=1
    )
    weights, group_rows, gate_rows, first_rows, second_rows = gather_start(
        weight_low, own_inputs, feedforward_master.astype(LOW)
    )
    weights, late_cotangent = lax.optimization_barrier((weights, cotangent))
    weights = weights.reshape(D, -1)
    merge_weight = weights[:, qkv_width : qkv_width + D]
    gain_float = weights[:, qkv_width + D : qkv_width + D + 2].astype(FULL).T
    gate_weight = lax.all_gather(
        gate_rows.reshape(dp_size * own_rows, 2 * own_hidden), "grp", axis=0, tiled=True
    )
    gate_weight, second_rows = lax.optimization_barrier((gate_weight, second_rows))
    first_down = first_rows.reshape(D, own_hidden // 2)
    second_down = lax.all_gather(
        second_rows.reshape(dp_size * own_rows, own_hidden // 2), "grp", axis=0, tiled=True
    )
    down_grad = plane_gather(late_cotangent.reshape(row_count, D))

    segment_row = segment_ids[0]
    source_row = continuation_prompt[0]
    prompt_positions, follow_positions = segment_positions(segment_row, source_row)
    cosine, sine_part = angle_table(jnp.concatenate([prompt_positions, follow_positions[0]]))

    place = jnp.reshape(group_index, (1,)).astype(jnp.int32)
    group_rows = group_rows.reshape(PROMPT_LEN, D)
    queries, pairs, key_normed, normed, key_scale = project_heads(
        place, group_rows, own_inputs, gain_float[:1], cosine, sine_part, weights
    )
    inputs = own_inputs.astype(FULL)
    first_scale = norm_scale(inputs)

    row_index = jnp.arange(row_count, dtype=jnp.int32)
    is_prompt = row_index < prompt_rows
    global_row = group_index * prompt_rows + jnp.minimum(row_index, prompt_rows - 1)
    own_segment = lax.dynamic_slice_in_dim(segment_row, group_index * prompt_rows, prompt_rows)
    query_segment = jnp.concatenate([own_segment, jnp.broadcast_to(source_row, (CONT,))])
    key_index = jnp.arange(PROMPT_LEN, dtype=jnp.int32)
    prompt_seen = (segment_row[None, :] == query_segment[:, None]) & (
        (key_index[None, :] <= global_row[:, None]) | ~is_prompt[:, None]
    )
    follow_seen = (~is_prompt)[:, None] & (
        jnp.arange(CONT, dtype=jnp.int32)[None, :] <= (row_index - prompt_rows)[:, None]
    )
    visible = jnp.concatenate([prompt_seen, follow_seen], axis=1)
    seen = visible.astype(FULL)
    attended, row_logsum = attend(queries, pairs, seen)
    middle = inputs + contract(attended, merge_weight, 1, 1)
    second_scale = norm_scale(middle)
    normed_two = (middle * second_scale * gain_float[1]).astype(LOW)
    grad_rows = cotangent.reshape(row_count, D).astype(FULL)

    normed_two, down_grad = lax.optimization_barrier((normed_two, down_grad))
    normed_all = plane_gather(normed_two)
    gate_up = jnp.dot(normed_all, gate_weight, preferred_element_type=FULL)
    gate_values = gate_up[:, :own_hidden]
    up_values = gate_up[:, own_hidden:]
    gate_sigmoid, gate_silu, activated = gate_parts(gate_values, up_values)
    down_term = contract(down_grad, activated, 0, 0).astype(LOW)
    down_term, second_down = lax.optimization_barrier((down_term, second_down))
    out_term, gate_up_grad = forward_back(
        row_count, activated, down_grad, gate_up, first_down, second_down
    )
    down_part = line_scatter(down_term)
    gate_term = contract(normed_all, gate_up_grad[:, :own_hidden], 0, 0).astype(LOW)
    up_term = contract(normed_all, gate_up_grad[:, own_hidden:], 0, 0).astype(LOW)
    gate_up_grad, gate_term, up_term, down_part = lax.optimization_barrier(
        (gate_up_grad, gate_term, up_term, down_part)
    )
    gate_part = line_scatter(gate_term)
    up_part = line_scatter(up_term)
    normed_two_grad, down_swapped = plane_back(
        row_count, gate_up_grad, gate_weight, down_part.reshape(dp_size, own_rows, own_hidden)
    )
    normed_two_grad, out_term = lax.optimization_barrier((normed_two_grad, out_term))
    out_chunks = out_term.reshape(dp_size, row_count, D)
    out_swapped = [plane_swap(out_chunks[offset + 1], 1) for offset in range(0, dp_size, 2)]
    middle_grad = grad_rows + norm_back(middle, second_scale, gain_float[1], normed_two_grad)
    gain_two_part = jnp.sum(normed_two_grad * middle * second_scale, axis=0)
    branch_grad = middle_grad.astype(LOW)
    attended_grad = contract(branch_grad, merge_weight, 1, 0).astype(LOW)
    attended_grad, out_swapped = lax.optimization_barrier((attended_grad, out_swapped))
    out_sums = [
        out_chunks[2 * at].astype(FULL) + one.astype(FULL) for at, one in enumerate(out_swapped)
    ]
    out_low = [one.astype(LOW) for one in out_sums[1:]]
    attended_grad, out_low = lax.optimization_barrier((attended_grad, out_low))
    out_arrived = [plane_swap(one, 2 * at + 2) for at, one in enumerate(out_low)]
    query_project, pair_project = attend_back(
        place, queries, pairs, seen, row_logsum, attended_grad, cosine, sine_part
    )
    query_term, pair_term, merge_term, normed_grad, pair_back, gain_one_part = weights_back(
        place,
        query_project,
        pair_project,
        branch_grad,
        attended,
        key_normed,
        normed,
        group_rows,
        own_inputs,
        key_scale,
        weights,
    )
    gain_term = jnp.pad(
        jnp.stack([gain_one_part[0], gain_two_part], axis=1), ((0, 0), (0, GAIN_PAD - 2))
    )
    pair_back, up_part, out_arrived = lax.optimization_barrier((pair_back, up_part, out_arrived))
    result = middle + out_sums[0]
    for one in out_arrived:
        result = result + one.astype(FULL)
    block_output, query_term = lax.optimization_barrier((result.astype(LOW), query_term))
    block_output = block_output.reshape(hidden.shape)
    pair_sum = line_scatter(pair_back)
    attention_grad, merge_grad, gain_sums, forward_low = finish(
        (query_term, pair_term, merge_term, gain_term.astype(LOW)),
        gate_part,
        up_part,
        down_swapped,
    )
    gain_grad = gain_sums[:2]
    pair_sum, gain_grad = lax.optimization_barrier((pair_sum, gain_grad))
    pair_sum = pair_sum.astype(FULL)
    normed_grad = normed_grad + jnp.pad(pair_sum, ((0, CONT), (0, 0)))
    input_grad = (middle_grad + norm_back(inputs, first_scale, gain_float[0], normed_grad)).reshape(
        hidden.shape
    )
    feedforward_grad = forward_low.astype(FULL)
    gain_new = adam_step(gain_master, gain_first, gain_second, gain_grad, 0.0)
    attention_new = adam_step(
        attention_master, attention_first, attention_second, attention_grad, WEIGHT_DECAY
    )
    merge_new = adam_step(merge_master, merge_first, merge_second, merge_grad, WEIGHT_DECAY)
    feedforward_new = adam_step(
        feedforward_master, feedforward_first, feedforward_second, feedforward_grad, WEIGHT_DECAY
    )
    return (
        block_output,
        input_grad,
        gain_grad,
        *gain_new,
        attention_grad,
        *attention_new,
        merge_grad,
        *merge_new,
        feedforward_grad,
        *feedforward_new,
    )


def solution(mesh):
    tokens = P("dp", "grp", None, None)
    gains = P(None, ("grp", "dp"))
    matrix = P(("grp", "dp"), None)
    return jax.shard_map(
        body,
        mesh=mesh,
        in_specs=(tokens, tokens, P("dp", None), P("dp", "grp")) + (gains,) * 3 + (matrix,) * 9,
        out_specs=(tokens, tokens) + (gains,) * 4 + (matrix,) * 12,
        check_vma=False,
    )
```

```python
import functools

import jax
import jax.numpy as jnp
from jax import lax
from jax.experimental import pallas as pl
from jax.experimental.pallas import tpu as pltpu
from jax.sharding import PartitionSpec as P

D = 2048
FF = 8192
HQ = 8
HK = 4
HD = 256
PROMPT_LEN = 1024
PROMPTS = 4
CONT = 64
STEP = 10
GAIN_PAD = 128

EPS_NORM = 1e-06
ROPE_THETA = 1000042.0
MASK_FILL = -1e30
BETA_ONE = 0.9
BETA_TWO = 0.95
ADAM_EPS = 1e-08
LEARN_RATE = 0.02
WEIGHT_DECAY = 0.1
LOW = jnp.bfloat16
FULL = jnp.float32
MESH = pl.DeviceIdType.MESH


def contract(left, right, left_axis, right_axis):
    return lax.dot_general(
        left, right, (((left_axis,), (right_axis,)), ((), ())), preferred_element_type=FULL
    )


def angle_table(positions):
    inverse_rate = ROPE_THETA ** (-(jnp.arange(HD // 2, dtype=FULL) * 2.0) / HD)
    angles = positions.astype(FULL)[..., None] * inverse_rate
    return (jnp.cos(angles), jnp.sin(angles))


def segment_positions(segment_row, source_row):
    labels = jnp.arange(PROMPTS, dtype=jnp.int32)
    member = (segment_row[None, :] == labels[:, None]).astype(jnp.int32)
    lengths = jnp.sum(member, axis=1, dtype=jnp.int32)
    starts = jnp.sum(
        jnp.where(labels[None, :] < labels[:, None], lengths[None, :], 0), axis=1, dtype=jnp.int32
    )
    prompt_index = jnp.arange(segment_row.shape[0], dtype=jnp.int32)
    prompt_positions = prompt_index - jnp.sum(member * starts[:, None], axis=0, dtype=jnp.int32)
    source_length = jnp.sum(
        (source_row[:, None] == labels[None, :]).astype(jnp.int32) * lengths[None, :],
        axis=1,
        dtype=jnp.int32,
    )
    follow_positions = source_length[:, None] + jnp.arange(CONT, dtype=jnp.int32)[None, :]
    return (prompt_positions, follow_positions)


def norm_scale(values):
    return lax.rsqrt(jnp.mean(values * values, axis=-1, keepdims=True) + EPS_NORM)


def norm_back(values, row_scale, gain_row, normed_grad):
    scaled = normed_grad * gain_row
    return row_scale * scaled - values * row_scale**3 * jnp.mean(
        scaled * values, axis=-1, keepdims=True
    )


def adam_step(master, first_moment, second_moment, gradient, decay_rate):
    first_new = BETA_ONE * first_moment + (1.0 - BETA_ONE) * gradient
    second_new = BETA_TWO * second_moment + (1.0 - BETA_TWO) * gradient * gradient
    correct_one = 1.0 - BETA_ONE**STEP
    correct_two = 1.0 - BETA_TWO**STEP
    update = first_new / correct_one / (jnp.sqrt(second_new / correct_two) + ADAM_EPS)
    return (-LEARN_RATE * (update + decay_rate * master), first_new, second_new)


def gate_parts(gate_values, up_values):
    gate_sigmoid = jax.nn.sigmoid(gate_values)
    gate_silu = gate_values * gate_sigmoid
    return (gate_sigmoid, gate_silu, (gate_silu * up_values).astype(LOW))


def gate_backward(activated_grad, gate_values, up_values, gate_sigmoid, gate_silu):
    gate_grad = (
        activated_grad * up_values * gate_sigmoid * (1.0 + gate_values * (1.0 - gate_sigmoid))
    ).astype(LOW)
    up_grad = (activated_grad * gate_silu).astype(LOW)
    return (gate_grad, up_grad)


def flip(index, bits):
    bit = 1
    while bit <= bits:
        if bits & bit:
            index = index + bit - 2 * bit * lax.rem(index // bit, 2)
        bit *= 2
    return index


def remote(source, target, send, recv, there):
    return pltpu.make_async_remote_copy(
        src_ref=source,
        dst_ref=target,
        send_sem=send,
        recv_sem=recv,
        device_id=there,
        device_id_type=MESH,
    )


def gather_kernel(
    lines,
    plane,
    prompt_rows,
    weight_ref,
    hidden_ref,
    forward_ref,
    weights_ref,
    rows_ref,
    gate_ref,
    first_ref,
    second_ref,
    local_sem,
    line_send,
    line_recv,
    rows_send,
    rows_recv,
    first_send,
    first_recv,
    near_send,
    near_recv,
    half_send,
    half_recv,
    core_send,
    core_recv,
    swap_send,
    swap_recv,
):
    g = lax.axis_index("grp")
    d = lax.axis_index("dp")
    evens = range(0, plane, 2)
    forward_halves = plane == 8
    near = (2, 4) if forward_halves else tuple(evens[1:])
    width = weight_ref.shape[1]
    cut = (width // 256) * 128

    barrier = pltpu.get_barrier_semaphore()
    for offset in range(1, plane):
        pl.semaphore_signal(barrier, inc=1, device_id=(g, flip(d, offset)), device_id_type=MESH)

    for step in range(1, lines):
        there = lax.rem(g + step, lines)
        pl.semaphore_signal(barrier, inc=1, device_id=(there, d), device_id_type=MESH)
    pl.semaphore_wait(barrier, plane + lines - 2)

    copy = remote
    own_rows = hidden_ref.at[pl.ds(0, prompt_rows)]

    def line_weight(way, step):
        block = g - step + 1 if way == 0 else g + step - 1
        source = weight_ref if step == 1 else weights_ref.at[block, d]
        return copy(
            source,
            weights_ref.at[block, d],
            line_send.at[way, step],
            line_recv.at[way, step],
            (g + 1 if way == 0 else g - 1, d),
        )

    def line_rows(way, step):
        block = g - step + 1 if way == 0 else g + step - 1
        source = own_rows if step == 1 else rows_ref.at[block]
        return copy(
            source,
            rows_ref.at[block],
            rows_send.at[way, step],
            rows_recv.at[way, step],
            (g + 1 if way == 0 else g - 1, d),
        )

    def line_first(way, step):
        block = g - step + 1 if way == 0 else g + step - 1
        return copy(
            first_ref.at[block],
            first_ref.at[block],
            first_send.at[way, step],
            first_recv.at[way, step],
            (g + 1 if way == 0 else g - 1, d),
        )

    def sends(way, step):
        if way == 0:
            return (g < lines - 1) & (g >= step - 1)
        return (g > 0) & (g + step - 1 < lines)

    def receives(way, step):
        return g >= step if way == 0 else g + step < lines

    def near_copy(block, offset, own):
        source = weight_ref if own else weights_ref.at[block, d]
        at = near.index(offset)
        return copy(
            source,
            weights_ref.at[block, d],
            near_send.at[block, at],
            near_recv.at[block, at],
            (g, flip(d, offset)),
        )

    def half_copy(block, part):
        columns = pl.ds(0, cut) if part == 0 else pl.ds(cut, width - cut)
        origin = flip(d, 2) if part == 0 else flip(d, 4)
        there = flip(d, 4) if part == 0 else flip(d, 2)
        piece = weights_ref.at[block, origin, :, columns]
        return copy(
            piece, piece, half_send.at[block, part], half_recv.at[block, part], (g, there)
        )

    def core_copy(block, offset, own=False):
        source = weight_ref if own else weights_ref.at[block, flip(d, offset)]
        return copy(
            source,
            weights_ref.at[block, flip(d, offset)],
            core_send.at[block, offset // 2],
            core_recv.at[block, offset // 2],
            (g, flip(d, 1)),
        )

    half_hidden = second_ref.shape[2]
    own_hidden = 2 * half_hidden

    def swap_piece(owner, part, source_index):
        if part < 2:
            source = forward_ref.at[:, pl.ds(part * FF + owner * own_hidden, own_hidden)]
            return source, gate_ref.at[source_index, :, pl.ds(part * own_hidden, own_hidden)]
        start = 2 * FF + owner * own_hidden + (part - 2) * half_hidden
        source = forward_ref.at[:, pl.ds(start, half_hidden)]
        return source, first_ref.at[g, source_index] if part == 2 else second_ref.at[source_index]

    def swap_copy(offset, part):
        source, target = swap_piece(flip(d, offset), part, d)
        return copy(
            source,
            target,
            swap_send.at[offset, part],
            swap_recv.at[offset, part],
            (g, flip(d, offset)),
        )

    locals_ = (
        pltpu.make_async_copy(weight_ref, weights_ref.at[g, d], local_sem.at[0]),
        pltpu.make_async_copy(own_rows, rows_ref.at[g], local_sem.at[1]),
        *(
            pltpu.make_async_copy(*swap_piece(d, part, d), local_sem.at[2 + part])
            for part in range(4)
        ),
    )

    def launch(block, own):
        for offset in near:
            near_copy(block, offset, own).start()
        core_copy(block, 0, own).start()

    def relay(block):
        for offset in near:
            near_copy(block, offset, False).wait_recv()
            core_copy(block, offset).start()
        if forward_halves:
            half_copy(block, 0).start()
            half_copy(block, 1).start()

    def finish(block):
        if forward_halves:
            half_copy(block, 0).wait_recv()
            half_copy(block, 1).wait_recv()
            core_copy(block, 6).start()

    def both(step, act):
        for way in (0, 1):
            pl.when(receives(way, step))(
                lambda way=way: act(g - step if way == 0 else g + step)
            )

    def take_rows(step):
        for way in (0, 1):

            @pl.when(receives(way, step))
            def _(way=way):
                line_rows(way, step).wait_recv()

            if step + 1 < lines:
                pl.when(sends(way, step + 1))(
                    lambda way=way: line_rows(way, step + 1).start()
                )

    for way in (0, 1):
        pl.when(sends(way, 1))(lambda way=way: line_weight(way, 1).start())
    launch(g, True)
    for one in locals_:
        one.start()
    for step in range(1, lines):
        for way in (0, 1):

            @pl.when(receives(way, step))
            def _(way=way, step=step):
                line_weight(way, step).wait_recv()

            if step + 1 < lines:
                pl.when(sends(way, step + 1))(
                    lambda way=way, step=step: line_weight(way, step + 1).start()
                )
            else:
                pl.when(sends(way, 1))(lambda way=way: line_rows(way, 1).start())

        both(step, lambda block: launch(block, False))
        if step == 1:
            relay(g)
            for offset in range(1, plane):
                swap_copy(offset, 2).start()
    for step in range(1, lines):
        take_rows(step)
        if step == lines - 1:
            locals_[4].wait()
            for offset in range(1, plane):
                swap_copy(offset, 2).wait_recv()
            for way in (0, 1):
                pl.when(sends(way, 1))(lambda way=way: line_first(way, 1).start())
        both(step, relay)
        if step == 1:
            finish(g)
        elif step < lines - 1:
            both(step - 1, finish)
        if step == 1:
            for offset in range(1, plane):
                for part in (0, 1, 3):
                    swap_copy(offset, part).start()
    for step in range(1, lines):
        for way in (0, 1):

            @pl.when(receives(way, step))
            def _(way=way, step=step):
                line_first(way, step).wait_recv()

            if step + 1 < lines:
                pl.when(sends(way, step + 1))(
                    lambda way=way, step=step: line_first(way, step + 1).start()
                )
        if step == 1:
            both(lines - 2, finish)
    both(lines - 1, finish)

    def drain(block):
        for offset in evens:
            core_copy(block, offset).wait()
        for offset in near:
            near_copy(block, offset, False).wait_send()
        if forward_halves:
            half_copy(block, 0).wait_send()
            half_copy(block, 1).wait_send()

    drain(g)
    for step in range(1, lines):
        for way in (0, 1):
            pl.when(receives(way, step))(
                lambda way=way, step=step: drain(g - step if way == 0 else g + step)
            )

            @pl.when(sends(way, step))
            def _(way=way, step=step):
                line_weight(way, step).wait_send()
                line_rows(way, step).wait_send()
                line_first(way, step).wait_send()

    for offset in range(1, plane):
        for part in (0, 1, 3):
            swap_copy(offset, part).wait()
        swap_copy(offset, 2).wait_send()
    for at, one in enumerate(locals_):
        if at != 4:
            one.wait()


def gather_start(weight, hidden, forward):
    lines, plane = lax.axis_size("grp"), lax.axis_size("dp")
    prompt_rows = PROMPT_LEN // lines
    own_rows, width = weight.shape
    anywhere = pl.BlockSpec(memory_space=pl.ANY)
    dma = pltpu.SemaphoreType.DMA
    near_count = 2 if plane == 8 else plane // 2 - 1
    pairs = (
        (2, lines),
        (2, lines),
        (2, lines),
        (2, lines),
        (2, lines),
        (2, lines),
        (lines, near_count),
        (lines, near_count),
        (lines, 2),
        (lines, 2),
        (lines, plane // 2),
        (lines, plane // 2),
        (plane, 4),
        (plane, 4),
    )
    own_hidden = FF // plane
    return pl.pallas_call(
        functools.partial(gather_kernel, lines, plane, prompt_rows),
        out_shape=(
            jax.ShapeDtypeStruct((lines, plane, own_rows, width), weight.dtype),
            jax.ShapeDtypeStruct((lines, prompt_rows, D), hidden.dtype),
            jax.ShapeDtypeStruct((plane, own_rows, 2 * own_hidden), forward.dtype),
            jax.ShapeDtypeStruct((lines, plane, own_rows, own_hidden // 2), forward.dtype),
            jax.ShapeDtypeStruct((plane, own_rows, own_hidden // 2), forward.dtype),
        ),
        in_specs=[anywhere] * 3,
        out_specs=(anywhere,) * 5,
        scratch_shapes=[dma((6,))] + [dma(shape) for shape in pairs],
        compiler_params=pltpu.CompilerParams(collective_id=0, has_side_effects=True),
        name="gather_start",
    )(weight, hidden, forward)


def project_kernel(
    place_ref,
    group_ref,
    own_ref,
    gain_ref,
    cosine_ref,
    sine_ref,
    weight_ref,
    query_ref,
    pair_ref,
    normed_ref,
    own_normed_ref,
    scale_ref,
):
    step = pl.program_id(0)
    own_rows = own_ref.shape[0]
    prompt_rows = own_rows - CONT
    start = pl.multiple_of(place_ref[0] * prompt_rows, 16)
    tile = 32

    def norm_tile(values, at):
        values = values.astype(FULL)
        scale = lax.rsqrt(jnp.mean(values * values, axis=-1, keepdims=True) + EPS_NORM)
        normed_ref[pl.ds(at, tile)] = (values * scale * gain_ref[...]).astype(LOW)
        scale_ref[pl.ds(at, tile)] = jnp.broadcast_to(scale, (tile, 128))

    @pl.when(step == 0)
    def _():
        @pl.loop(0, PROMPT_LEN // tile)
        def _(at):
            first = pl.multiple_of(at * tile, tile)
            norm_tile(group_ref[pl.ds(first, tile)], first)

        for at in range(0, CONT, tile):
            norm_tile(own_ref[prompt_rows + at : prompt_rows + at + tile], PROMPT_LEN + at)
        own_normed_ref[:prompt_rows] = normed_ref[pl.ds(start, prompt_rows)]
        own_normed_ref[prompt_rows:] = normed_ref[PROMPT_LEN:]

    def turn(values, cosine, sine_part):
        front, back = values[:, : HD // 2], values[:, HD // 2 :]
        return front * cosine - back * sine_part, back * cosine + front * sine_part

    def project(rows):
        return jnp.dot(rows, weight_ref[...], preferred_element_type=FULL)

    @pl.when(step < HQ)
    def _():
        for first, count, table in ((0, prompt_rows, start), (prompt_rows, CONT, PROMPT_LEN)):
            values = project(own_normed_ref[first : first + count])
            front, back = turn(
                values, cosine_ref[pl.ds(table, count)], sine_ref[pl.ds(table, count)]
            )
            query_ref[first : first + count, : HD // 2] = front.astype(LOW)
            query_ref[first : first + count, HD // 2 :] = back.astype(LOW)

    key_count = PROMPT_LEN + CONT
    part = key_count // 4

    @pl.when((step >= HQ) & (step < HQ + HK))
    def _():
        @pl.loop(0, 4)
        def _(at):
            rows = pl.ds(pl.multiple_of(at * part, 16), part)
            front, back = turn(project(normed_ref[rows]), cosine_ref[rows], sine_ref[rows])
            pair_ref[rows, : HD // 2] = front.astype(LOW)
            pair_ref[rows, HD // 2 :] = back.astype(LOW)

    @pl.when(step >= HQ + HK)
    def _():
        @pl.loop(0, 4)
        def _(at):
            rows = pl.ds(pl.multiple_of(at * part, 16), part)
            pair_ref[rows] = project(normed_ref[rows]).astype(LOW)


VMEM_LIMIT = 60 * 2**20


def project_heads(place, group_rows, own_inputs, gain_row, cosine, sine_part, weights):
    own_rows = own_inputs.shape[0]
    key_count = PROMPT_LEN + CONT
    whole = lambda shape: pl.BlockSpec(shape, lambda j, p: (0, 0))
    return pl.pallas_call(
        project_kernel,
        grid_spec=pltpu.PrefetchScalarGridSpec(
            num_scalar_prefetch=1,
            grid=(HQ + 2 * HK,),
            in_specs=[
                whole((PROMPT_LEN, D)),
                whole((own_rows, D)),
                whole((1, D)),
                whole((key_count, HD // 2)),
                whole((key_count, HD // 2)),
                pl.BlockSpec((D, HD), lambda j, p: (0, j)),
            ],
            out_specs=[
                pl.BlockSpec((own_rows, HD), lambda j, p: (0, jnp.minimum(j, HQ - 1))),
                pl.BlockSpec((key_count, HD), lambda j, p: (0, jnp.maximum(j - HQ, 0))),
                whole((key_count, D)),
                whole((own_rows, D)),
                whole((key_count, 128)),
            ],
        ),
        out_shape=[
            jax.ShapeDtypeStruct((own_rows, HQ * HD), LOW),
            jax.ShapeDtypeStruct((key_count, 2 * HK * HD), LOW),
            jax.ShapeDtypeStruct((key_count, D), LOW),
            jax.ShapeDtypeStruct((own_rows, D), LOW),
            jax.ShapeDtypeStruct((key_count, 128), FULL),
        ],
        compiler_params=pltpu.CompilerParams(vmem_limit_bytes=VMEM_LIMIT),
        name="project_heads",
    )(place, group_rows, own_inputs, gain_row, cosine, sine_part, weights)


def across(left, right):
    return lax.dot_general(left, right, (((1,), (1,)), ((), ())), preferred_element_type=FULL)


def along(left, right):
    return lax.dot_general(left, right, (((0,), (0,)), ((), ())), preferred_element_type=FULL)


def attend_kernel(query_ref, key_ref, value_ref, seen_ref, attended_ref, logsum_ref):
    group_heads = HQ // HK
    for head in range(group_heads):
        columns = slice(head * HD, (head + 1) * HD)
        scores = across(query_ref[:, columns], key_ref[...]) * HD ** (-0.5)
        scores = jnp.where(seen_ref[...] > 0, scores, MASK_FILL)
        peak = jnp.max(scores, axis=-1, keepdims=True)
        unnormed = jnp.exp(scores - peak)
        total = jnp.sum(unnormed, axis=-1, keepdims=True)
        low = (unnormed / total).astype(LOW)
        attended_ref[:, columns] = jnp.dot(
            low, value_ref[...], preferred_element_type=FULL
        ).astype(LOW)
        logsum_ref[:, head * 128 : (head + 1) * 128] = jnp.broadcast_to(
            peak + jnp.log(total), (query_ref.shape[0], 128)
        )


def attend(queries, pairs, seen):
    rows, key_count = seen.shape
    group_heads = HQ // HK
    return pl.pallas_call(
        attend_kernel,
        grid=(HK,),
        in_specs=[
            pl.BlockSpec((rows, group_heads * HD), lambda j: (0, j)),
            pl.BlockSpec((key_count, HD), lambda j: (0, j)),
            pl.BlockSpec((key_count, HD), lambda j: (0, HK + j)),
            pl.BlockSpec((rows, key_count), lambda j: (0, 0)),
        ],
        out_specs=[
            pl.BlockSpec((rows, group_heads * HD), lambda j: (0, j)),
            pl.BlockSpec((rows, group_heads * 128), lambda j: (0, j)),
        ],
        out_shape=[
            jax.ShapeDtypeStruct((rows, HQ * HD), LOW),
            jax.ShapeDtypeStruct((rows, HQ * 128), FULL),
        ],
        compiler_params=pltpu.CompilerParams(vmem_limit_bytes=VMEM_LIMIT),
        name="attend",
    )(queries, pairs, pairs, seen)


def attend_back_kernel(
    place_ref,
    query_ref,
    key_ref,
    value_ref,
    seen_ref,
    logsum_ref,
    grad_ref,
    cosine_ref,
    sine_ref,
    query_out,
    pair_out,
):
    step = pl.program_id(0)
    group_heads = HQ // HK
    rows = query_ref.shape[0]
    prompt_rows = rows - CONT
    start = pl.multiple_of(place_ref[0] * prompt_rows, 16)
    score_scale = HD ** (-0.5)
    key_grad = value_grad = 0.0

    def turn_back(values, cosine, sine_part):
        front, back = values[:, : HD // 2], values[:, HD // 2 :]
        return jnp.concatenate(
            [front * cosine + back * sine_part, back * cosine - front * sine_part], axis=1
        ).astype(LOW)

    for head in range(group_heads):
        columns = slice(head * HD, (head + 1) * HD)
        scores = across(query_ref[:, columns], key_ref[...]) * score_scale
        scores = jnp.where(seen_ref[...] > 0, scores, MASK_FILL)
        probabilities = jnp.exp(scores - logsum_ref[:, head * 128 : head * 128 + 1])
        grads = grad_ref[:, columns]
        probability_grad = across(grads, value_ref[...])
        delta = jnp.sum(probabilities * probability_grad, axis=-1, keepdims=True)
        score_grad = (probabilities * (probability_grad - delta)).astype(LOW)
        query_grad = jnp.dot(score_grad, key_ref[...], preferred_element_type=FULL) * score_scale
        key_grad = key_grad + along(score_grad, query_ref[:, columns])
        value_grad = value_grad + along(probabilities.astype(LOW), grads)
        query_out[:prompt_rows, columns] = turn_back(
            query_grad[:prompt_rows],
            cosine_ref[pl.ds(start, prompt_rows)],
            sine_ref[pl.ds(start, prompt_rows)],
        )
        query_out[prompt_rows:, columns] = turn_back(
            query_grad[prompt_rows:], cosine_ref[PROMPT_LEN:], sine_ref[PROMPT_LEN:]
        )
    pair_out[:, pl.ds(pl.multiple_of(step * HD, HD), HD)] = turn_back(
        key_grad * score_scale, cosine_ref[...], sine_ref[...]
    )
    pair_out[:, pl.ds(pl.multiple_of((HK + step) * HD, HD), HD)] = value_grad.astype(LOW)


def attend_back(place, queries, pairs, seen, logsum, grads, cosine, sine_part):
    rows, key_count = seen.shape
    group_heads = HQ // HK
    whole = lambda shape: pl.BlockSpec(shape, lambda j, p: (0, 0))
    return pl.pallas_call(
        attend_back_kernel,
        grid_spec=pltpu.PrefetchScalarGridSpec(
            num_scalar_prefetch=1,
            grid=(HK,),
            in_specs=[
                pl.BlockSpec((rows, group_heads * HD), lambda j, p: (0, j)),
                pl.BlockSpec((key_count, HD), lambda j, p: (0, j)),
                pl.BlockSpec((key_count, HD), lambda j, p: (0, HK + j)),
                whole((rows, key_count)),
                pl.BlockSpec((rows, group_heads * 128), lambda j, p: (0, j)),
                pl.BlockSpec((rows, group_heads * HD), lambda j, p: (0, j)),
                whole((key_count, HD // 2)),
                whole((key_count, HD // 2)),
            ],
            out_specs=[
                pl.BlockSpec((rows, group_heads * HD), lambda j, p: (0, j)),
                whole((key_count, 2 * HK * HD)),
            ],
        ),
        out_shape=[
            jax.ShapeDtypeStruct((rows, HQ * HD), LOW),
            jax.ShapeDtypeStruct((key_count, 2 * HK * HD), LOW),
        ],
        compiler_params=pltpu.CompilerParams(vmem_limit_bytes=VMEM_LIMIT),
        name="attend_back",
    )(place, queries, pairs, pairs, seen, logsum, grads, cosine, sine_part)


def weights_back_kernel(
    place_ref,
    query_ref,
    pair_ref,
    branch_ref,
    attended_ref,
    normed_ref,
    own_normed_ref,
    group_ref,
    own_ref,
    scale_ref,
    query_weight_ref,
    pair_weight_ref,
    query_term,
    pair_term,
    merge_term,
    back_out,
    pair_back_out,
    gain_out,
):
    rows = query_ref.shape[0]
    prompt_rows = rows - CONT
    start = pl.multiple_of(place_ref[0] * prompt_rows, 16)
    query_term[...] = along(own_normed_ref[...], query_ref[...]).astype(LOW)
    pair_term[...] = along(normed_ref[...], pair_ref[...]).astype(LOW)
    merge_term[...] = along(branch_ref[...], attended_ref[...]).astype(LOW)
    query_back = across(query_ref[...], query_weight_ref[...])
    pair_back = across(pair_ref[...], pair_weight_ref[...])
    own_values = own_ref[prompt_rows:].astype(FULL) * scale_ref[PROMPT_LEN:, :1]
    tail = query_back[prompt_rows:] + pair_back[PROMPT_LEN:]
    group_values = group_ref[...].astype(FULL) * scale_ref[:PROMPT_LEN, :1]
    own_prompt = own_ref[:prompt_rows].astype(FULL) * scale_ref[pl.ds(start, prompt_rows), :1]
    gain_out[...] = (
        jnp.sum(pair_back[:PROMPT_LEN] * group_values, axis=0, keepdims=True)
        + jnp.sum(query_back[:prompt_rows] * own_prompt, axis=0, keepdims=True)
        + jnp.sum(tail * own_values, axis=0, keepdims=True)
    )
    back_out[:prompt_rows] = query_back[:prompt_rows]
    back_out[prompt_rows:] = tail
    pair_back_out[...] = pair_back[:PROMPT_LEN].astype(LOW)


def weights_back(
    place, queries, pairs, branch, attended, normed, own_normed, group_rows, own_inputs, scale, weights
):
    rows, key_count = queries.shape[0], pairs.shape[0]
    wide, tile = HQ * HD, 256
    whole = lambda shape: pl.BlockSpec(shape, lambda j, p: (0, 0))
    tall = lambda count: pl.BlockSpec((count, tile), lambda j, p: (0, j))
    flat = lambda at: pl.BlockSpec((tile, wide), lambda j, p: (j, at))
    return pl.pallas_call(
        weights_back_kernel,
        grid_spec=pltpu.PrefetchScalarGridSpec(
            num_scalar_prefetch=1,
            grid=(D // tile,),
            in_specs=[
                whole((rows, wide)),
                whole((key_count, wide)),
                tall(rows),
                whole((rows, wide)),
                tall(key_count),
                tall(rows),
                tall(PROMPT_LEN),
                tall(rows),
                whole((key_count, 128)),
                flat(0),
                flat(1),
            ],
            out_specs=[flat(0), flat(0), flat(0), tall(rows), tall(PROMPT_LEN), tall(1)],
        ),
        out_shape=[
            jax.ShapeDtypeStruct((D, wide), LOW),
            jax.ShapeDtypeStruct((D, wide), LOW),
            jax.ShapeDtypeStruct((D, wide), LOW),
            jax.ShapeDtypeStruct((rows, D), FULL),
            jax.ShapeDtypeStruct((PROMPT_LEN, D), LOW),
            jax.ShapeDtypeStruct((1, D), FULL),
        ],
        compiler_params=pltpu.CompilerParams(vmem_limit_bytes=VMEM_LIMIT),
        name="weights_back",
    )(
        place,
        queries,
        pairs,
        branch,
        attended,
        normed,
        own_normed,
        group_rows,
        own_inputs,
        scale,
        weights,
        weights,
    )


def forward_back_kernel(
    activated_ref, grad_ref, gate_up_ref, first_ref, second_ref, out_ref, gate_up_grad_ref
):
    own_hidden = activated_ref.shape[1]
    part = first_ref.shape[0] // 4
    piece = own_hidden // 2

    @pl.loop(0, 4)
    def _(at):
        columns = pl.ds(pl.multiple_of(at * part, part), part)
        out_ref[:, columns] = (
            across(activated_ref[:, :piece], first_ref[columns])
            + across(activated_ref[:, piece:], second_ref[columns])
        ).astype(LOW)

    for at, down_ref in enumerate((first_ref, second_ref)):
        columns = slice(at * piece, (at + 1) * piece)
        upper = slice(own_hidden + at * piece, own_hidden + (at + 1) * piece)
        activated_grad = jnp.dot(grad_ref[...], down_ref[...], preferred_element_type=FULL)
        gate_values, up_values = gate_up_ref[:, columns], gate_up_ref[:, upper]
        gate_sigmoid = jax.nn.sigmoid(gate_values)
        gate_grad, up_grad = gate_backward(
            activated_grad, gate_values, up_values, gate_sigmoid, gate_values * gate_sigmoid
        )
        gate_up_grad_ref[:, columns] = gate_grad
        gate_up_grad_ref[:, upper] = up_grad


def forward_back(rows, activated, grads, gate_up, first_down, second_down):
    count, own_hidden = activated.shape
    block = lambda width: pl.BlockSpec((rows, width), lambda j: (j, 0))
    return pl.pallas_call(
        forward_back_kernel,
        grid=(count // rows,),
        in_specs=[
            block(own_hidden),
            block(D),
            block(2 * own_hidden),
            pl.BlockSpec(first_down.shape, lambda j: (0, 0)),
            pl.BlockSpec(second_down.shape, lambda j: (0, 0)),
        ],
        out_specs=[block(D), block(2 * own_hidden)],
        out_shape=[
            jax.ShapeDtypeStruct((count, D), LOW),
            jax.ShapeDtypeStruct((count, 2 * own_hidden), LOW),
        ],
        compiler_params=pltpu.CompilerParams(vmem_limit_bytes=VMEM_LIMIT),
        name="forward_back",
    )(activated, grads, gate_up, first_down, second_down)


def plane_back_kernel(
    plane,
    rows_ref,
    weight_ref,
    down_ref,
    out_ref,
    swapped_ref,
    weight,
    tiles,
    keep,
    give,
    core_in,
    plane_in,
    total,
    load_sem,
    tile_sem,
    core_send,
    core_recv,
    plane_send,
    plane_recv,
    out_sem,
    swap_send,
    swap_recv,
):
    g = lax.axis_index("grp")
    d = lax.axis_index("dp")
    chips = plane // 2
    own_hidden = down_ref.shape[2]
    halves = plane == 8
    order = (3, 1, 2, 0) if halves else tuple(range(chips - 1, -1, -1))
    cut = D // 2
    half_of = (pl.ds(0, cut), pl.ds(cut, D - cut))

    barrier = pltpu.get_barrier_semaphore()
    for offset in range(1, plane):
        pl.semaphore_signal(
            barrier, inc=1, device_id=(g, flip(d, offset)), device_id_type=MESH
        )

    load = pltpu.make_async_copy(weight_ref, weight, load_sem.at[0])
    load.start()

    def tile_copy(turn):
        at = order[turn]
        return pltpu.make_async_copy(
            rows_ref.at[pl.ds(2 * at, 2)], tiles.at[turn % 2], tile_sem.at[turn % 2]
        )

    def core_copy(at):
        return remote(
            give.at[at], core_in.at[at], core_send.at[at], core_recv.at[at], (g, flip(d, 1))
        )

    def plane_copy(at):
        return remote(
            keep.at[at],
            plane_in.at[at],
            plane_send.at[at],
            plane_recv.at[at],
            (g, flip(d, 2 * at)),
        )

    def near_copy(part, relayed):
        there = part + 1
        return remote(
            keep.at[3 if relayed else there, :, half_of[part]],
            plane_in.at[1 if relayed else 0, :, half_of[part]],
            plane_send.at[2 * relayed + part],
            plane_recv.at[2 * relayed + part],
            (g, flip(d, 2 * there)),
        )

    def relay_copy(part):
        there = 2 - part
        return remote(
            keep.at[there, :, half_of[part]],
            plane_in.at[2, :, half_of[part]],
            plane_send.at[4 + part],
            plane_recv.at[4 + part],
            (g, flip(d, 2 * there)),
        )

    def swap_copy(offset):
        there = flip(d, offset)
        return remote(
            down_ref.at[there],
            swapped_ref.at[:, pl.ds(d * own_hidden, own_hidden)],
            swap_send.at[offset],
            swap_recv.at[offset],
            (g, there),
        )

    own_swap = pltpu.make_async_copy(
        down_ref.at[d], swapped_ref.at[:, pl.ds(d * own_hidden, own_hidden)], out_sem.at[1]
    )
    tile_copy(0).start()
    tile_copy(1).start()
    pl.semaphore_wait(barrier, plane - 1)
    for offset in range(1, plane):
        swap_copy(offset).start()
    own_swap.start()
    load.wait()
    part_width = 512

    def product(turn, which, target):
        @pl.loop(0, D // part_width)
        def _(at):
            columns = pl.ds(pl.multiple_of(at * part_width, part_width), part_width)
            target[order[turn], :, columns] = across(
                tiles[turn % 2, which], weight[columns]
            ).astype(LOW)

    def add_into(at, other, first, count):
        step = 256

        @pl.loop(0, count // step)
        def _(k):
            here = pl.ds(pl.multiple_of(first + k * step, step), step)
            keep[at, :, here] = (
                keep[at, :, here].astype(FULL) + other(here).astype(FULL)
            ).astype(LOW)

    def settle(turn):
        at = order[turn]
        core_copy(at).wait_recv()
        add_into(at, lambda here: core_in[at, :, here], 0, D)
        if halves and at == 3:
            near_copy(0, True).start()
            near_copy(1, True).start()
        elif halves and at:
            near_copy(at - 1, False).start()
        elif at:
            plane_copy(at).start()

    for turn in range(chips):
        tile_copy(turn).wait()
        product(turn, 1, give)
        core_copy(order[turn]).start()
        if turn:
            settle(turn - 1)
        product(turn, 0, keep)
        if turn + 2 < chips:
            tile_copy(turn + 2).start()
        if halves and turn == chips - 1:
            for part in range(2):
                near_copy(part, True).wait_recv()
                add_into(
                    2 - part,
                    lambda here: plane_in[1, :, here],
                    part * cut,
                    cut,
                )
                relay_copy(part).start()
    settle(chips - 1)
    if halves:
        for part in range(2):
            near_copy(part, False).wait_recv()
            relay_copy(part).wait_recv()
        arrived = (0, 2)
    else:
        for at in range(1, chips):
            plane_copy(at).wait_recv()
        arrived = tuple(range(1, chips))

    @pl.loop(0, D // 256)
    def _(k):
        here = pl.ds(pl.multiple_of(k * 256, 256), 256)
        value = keep[0, :, here].astype(FULL)
        for at in arrived:
            value = value + plane_in[at, :, here].astype(FULL)
        total[:, here] = value

    out = pltpu.make_async_copy(total, out_ref, out_sem.at[0])
    out.start()
    for at in range(chips):
        core_copy(at).wait_send()
    if halves:
        for part in range(2):
            near_copy(part, False).wait_send()
            near_copy(part, True).wait_send()
            relay_copy(part).wait_send()
    else:
        for at in range(1, chips):
            plane_copy(at).wait_send()
    for offset in range(1, plane):
        swap_copy(offset).wait()
    own_swap.wait()
    out.wait()


def plane_back(rows, gate_up_grad, gate_weight, down_part):
    plane = lax.axis_size("dp")
    chips = plane // 2
    inner = gate_up_grad.shape[1]
    anywhere = pl.BlockSpec(memory_space=pl.ANY)
    dma = pltpu.SemaphoreType.DMA
    return pl.pallas_call(
        functools.partial(plane_back_kernel, plane),
        out_shape=(
            jax.ShapeDtypeStruct((rows, D), FULL),
            jax.ShapeDtypeStruct((down_part.shape[1], FF), LOW),
        ),
        in_specs=[anywhere] * 3,
        out_specs=(anywhere,) * 2,
        scratch_shapes=[
            pltpu.VMEM((D, inner), LOW),
            pltpu.VMEM((2, 2, rows, inner), LOW),
            pltpu.VMEM((chips, rows, D), LOW),
            pltpu.VMEM((chips, rows, D), LOW),
            pltpu.VMEM((chips, rows, D), LOW),
            pltpu.VMEM((3 if plane == 8 else chips, rows, D), LOW),
            pltpu.VMEM((rows, D), FULL),
            dma((1,)),
            dma((2,)),
            dma((chips,)),
            dma((chips,)),
            dma((max(6, chips),)),
            dma((max(6, chips),)),
            dma((2,)),
            dma((plane,)),
            dma((plane,)),
        ],
        compiler_params=pltpu.CompilerParams(
            collective_id=2, has_side_effects=True, vmem_limit_bytes=VMEM_LIMIT
        ),
        name="plane_back",
    )(gate_up_grad.reshape(plane, rows, inner), gate_weight, down_part)


def plane_swap(block, offset):
    size = lax.axis_size("dp")
    return lax.ppermute(block, "dp", [(i, i ^ offset) for i in range(size)])


def plane_gather(block):
    mine = [block] + [plane_swap(block, o) for o in range(2, lax.axis_size("dp"), 2)]
    pairs = [(one, plane_swap(one, 1)) for one in mine]
    return jnp.concatenate([one for pair in pairs for one in pair], axis=0)


def line_scatter(term):
    return lax.psum_scatter(term, "grp", scatter_dimension=0, tiled=True)


def finish_kernel(
    lines,
    plane,
    query_ref,
    pair_ref,
    merge_ref,
    gain_ref,
    gate_ref,
    up_ref,
    down_ref,
    a_out,
    m_out,
    gain_out,
    f_out,
    mine,
    core_in,
    plane_in,
    line_in,
    owned,
    gain_made,
    mine_sem,
    core_send,
    core_recv,
    plane_send,
    plane_recv,
    line_send,
    line_recv,
    swap_send,
    swap_recv,
    own_sem,
    out_sem,
):
    g = lax.axis_index("grp")
    d = lax.axis_index("dp")
    chips = plane // 2
    chip, core = lax.div(d, 2), lax.rem(d, 2)
    partner = d + 1 - 2 * core
    own_hidden = gate_ref.shape[2]
    width = core_in.shape[3]
    a_width, m_width = a_out.shape[1], m_out.shape[1]
    parts, begin = [], 0
    for ref in (query_ref, pair_ref, merge_ref, gain_ref):
        parts.append((ref, pl.ds(begin, ref.shape[4])))
        begin += ref.shape[4]

    barrier = pltpu.get_barrier_semaphore()
    for step in range(1, plane):
        there = lax.rem(d + step, plane)
        pl.semaphore_signal(barrier, inc=1, device_id=(g, there), device_id_type=MESH)
    for step in range(1, lines):
        there = lax.rem(g + step, lines)
        pl.semaphore_signal(barrier, inc=1, device_id=(there, d), device_id_type=MESH)
    pl.semaphore_wait(barrier, plane + lines - 2)

    def line_at(turn):
        return lax.rem(g + turn + 1, lines)

    def core_copy(turn, part):
        line = line_at(turn)
        ref, columns = parts[part]
        return remote(
            ref.at[line, :, 1 - core],
            core_in.at[line, :, :, columns],
            core_send.at[turn, part],
            core_recv.at[turn, part],
            (g, partner),
        )

    def mine_copy(turn, part):
        line = line_at(turn)
        ref, columns = parts[part]
        return pltpu.make_async_copy(
            ref.at[line, :, core], mine.at[turn % 2, :, :, columns], mine_sem.at[turn, part]
        )

    cut = width // 256 * 128
    columns_of = (pl.ds(0, cut), pl.ds(cut, width - cut))

    def plane_copy(turn, step):
        line = line_at(turn)
        there = lax.rem(chip + step, chips)
        return remote(
            core_in.at[line, there],
            plane_in.at[line, chip],
            plane_send.at[turn, step],
            plane_recv.at[turn, step],
            (g, 2 * there + core),
        )

    def near_copy(turn, part, relayed):
        line = line_at(turn)
        there = flip(chip, part + 1)
        owner = flip(chip, 3) if relayed else there
        return remote(
            core_in.at[line, owner, :, columns_of[part]],
            plane_in.at[line, 1 if relayed else 0, :, columns_of[part]],
            plane_send.at[turn, 2 * relayed + part],
            plane_recv.at[turn, 2 * relayed + part],
            (g, 2 * there + core),
        )

    def relay_copy(turn, part):
        line = line_at(turn)
        there = flip(chip, 2 - part)
        return remote(
            core_in.at[line, there, :, columns_of[part]],
            plane_in.at[line, 2, :, columns_of[part]],
            plane_send.at[turn, 4 + part],
            plane_recv.at[turn, 4 + part],
            (g, 2 * there + core),
        )

    def line_copy(turn):
        line = line_at(turn)
        return remote(
            core_in.at[line, chip],
            line_in.at[g],
            line_send.at[turn],
            line_recv.at[turn],
            (line, d),
        )

    forward_refs = (gate_ref, up_ref)

    def swap_place(part):
        return f_out.at[:, pl.ds(part * FF + d * own_hidden, own_hidden)]

    def swap_copy(step, part):
        there = lax.rem(d + step, plane)
        return remote(
            forward_refs[part].at[there],
            swap_place(part),
            swap_send.at[step, part],
            swap_recv.at[step, part],
            (g, there),
        )

    own_swap = [
        pltpu.make_async_copy(forward_refs[part].at[d], swap_place(part), own_sem.at[part])
        for part in range(2)
    ] + [pltpu.make_async_copy(down_ref, f_out.at[:, pl.ds(2 * FF, FF)], own_sem.at[2])]

    every = range(len(parts))
    for turn in range(lines):
        for part in every:
            core_copy(turn, part).start()
            if turn < 2:
                mine_copy(turn, part).start()
    tile = 896 if width % 896 == 0 else 128
    halves = plane == 8

    def add_into(line, there, other, columns=None):
        first, count = (0, width) if columns is None else columns
        step = tile if columns is None else 128

        @pl.loop(0, count // step)
        def _(at):
            here = pl.ds(pl.multiple_of(first + at * step, 128), step)
            total = core_in[line, there, :, here].astype(FULL) + other(here).astype(FULL)
            core_in[line, there, :, here] = total.astype(LOW)

    def near_start(turn):
        if halves:
            for relayed in (True, False):
                for part in range(2):
                    near_copy(turn, part, relayed).start()
        else:
            for step in range(1, chips):
                plane_copy(turn, step).start()

    for turn in range(lines):
        line = line_at(turn)
        for part in every:
            core_copy(turn, part).wait_recv()
            mine_copy(turn, part).wait()
        for step in range(1, chips + 1):
            there = lax.rem(chip + step, chips)
            add_into(
                line, there, lambda here, there=there, turn=turn: mine[turn % 2, there, :, here]
            )
        if turn + 2 < lines:
            for part in every:
                mine_copy(turn + 2, part).start()
        if turn < 2:
            near_start(turn)

    def pass_on(turn):
        line = line_at(turn)
        for part, columns in enumerate(((0, cut), (cut, width - cut))):
            near_copy(turn, part, True).wait_recv()
            add_into(
                line,
                flip(chip, 2 - part),
                lambda here, line=line: plane_in[line, 1, :, here],
                columns,
            )
            relay_copy(turn, part).start()

    def near_done(turn):
        if halves:
            pass_on(turn)
            for part in range(2):
                near_copy(turn, part, False).wait_recv()
        else:
            for step in range(1, chips):
                plane_copy(turn, step).wait_recv()
        if turn + 2 < lines:
            near_start(turn + 2)

    def line_done(turn):
        line = line_at(turn)
        if halves:
            for part in range(2):
                relay_copy(turn, part).wait_recv()
            arrived = (0, 2)
        else:
            arrived = tuple(lax.rem(chip + step, chips) for step in range(1, chips))

        @pl.loop(0, width // tile)
        def _(at):
            columns = pl.ds(pl.multiple_of(at * tile, tile), tile)
            total = core_in[line, chip, :, columns].astype(FULL)
            for block in arrived:
                total = total + plane_in[line, block, :, columns].astype(FULL)
            core_in[line, chip, :, columns] = total.astype(LOW)

        if turn < lines - 1:
            line_copy(turn).start()

    near_done(0)
    for turn in range(1, lines):
        near_done(turn)
        line_done(turn - 1)
        if turn == lines - 2:
            for step in range(1, plane):
                for part in range(2):
                    swap_copy(step, part).start()
            for one in own_swap:
                one.start()
    line_done(lines - 1)
    for turn in range(lines - 1):
        line_copy(turn).wait_recv()

    def total_of(columns):
        total = core_in[g, chip, :, columns].astype(FULL)
        for step in range(1, lines):
            total = total + line_in[lax.rem(g + step, lines), :, columns].astype(FULL)
        return total

    @pl.loop(0, (a_width + m_width) // 256)
    def _(at):
        columns = pl.ds(pl.multiple_of(at * 256, 256), 256)
        owned[:, columns] = total_of(columns)

    gain_made[...] = total_of(pl.ds(a_width + m_width, GAIN_PAD)).T[:8]
    outs = (
        pltpu.make_async_copy(owned.at[:, pl.ds(0, a_width)], a_out, out_sem.at[0]),
        pltpu.make_async_copy(owned.at[:, pl.ds(a_width, m_width)], m_out, out_sem.at[1]),
        pltpu.make_async_copy(gain_made, gain_out, out_sem.at[2]),
    )
    for one in outs:
        one.start()
    for turn in range(lines):
        for part in every:
            core_copy(turn, part).wait_send()
        if halves:
            for part in range(2):
                near_copy(turn, part, False).wait_send()
                near_copy(turn, part, True).wait_send()
                relay_copy(turn, part).wait_send()
        else:
            for step in range(1, chips):
                plane_copy(turn, step).wait_send()
        if turn < lines - 1:
            line_copy(turn).wait_send()
    for step in range(1, plane):
        for part in range(2):
            swap_copy(step, part).wait()
    for one in own_swap:
        one.wait()
    for one in outs:
        one.wait()


def finish(terms, gate_part, up_part, down_swapped):
    lines, plane = lax.axis_size("grp"), lax.axis_size("dp")
    chips = plane // 2
    rows = D // (lines * plane)
    m_width = terms[2].shape[1]
    a_width = terms[0].shape[1] + terms[1].shape[1]
    width = a_width + m_width + GAIN_PAD
    anywhere = pl.BlockSpec(memory_space=pl.ANY)
    dma = pltpu.SemaphoreType.DMA
    vmem = pltpu.VMEM
    return pl.pallas_call(
        functools.partial(finish_kernel, lines, plane),
        out_shape=(
            jax.ShapeDtypeStruct((rows, a_width), FULL),
            jax.ShapeDtypeStruct((rows, m_width), FULL),
            jax.ShapeDtypeStruct((8, rows), FULL),
            jax.ShapeDtypeStruct((rows, 3 * FF), LOW),
        ),
        in_specs=[anywhere] * 7,
        out_specs=(anywhere,) * 4,
        scratch_shapes=[
            vmem((2, chips, rows, width), LOW),
            vmem((lines, chips, rows, width), LOW),
            vmem((lines, 3 if plane == 8 else chips, rows, width), LOW),
            vmem((lines, rows, width), LOW),
            vmem((rows, a_width + m_width), FULL),
            vmem((8, rows), FULL),
            dma((lines, 4)),
            dma((lines, 4)),
            dma((lines, 4)),
            dma((lines, max(6, chips))),
            dma((lines, max(6, chips))),
            dma((lines,)),
            dma((lines,)),
            dma((plane, 2)),
            dma((plane, 2)),
            dma((3,)),
            dma((3,)),
        ],
        compiler_params=pltpu.CompilerParams(
            collective_id=1, has_side_effects=True, vmem_limit_bytes=VMEM_LIMIT
        ),
        name="finish",
    )(
        *(term.reshape(lines, chips, 2, rows, term.shape[1]) for term in terms),
        gate_part.reshape(plane, rows, -1),
        up_part.reshape(plane, rows, -1),
        down_swapped,
    )


def body(
    hidden,
    cotangent,
    segment_ids,
    continuation_prompt,
    gain_master,
    gain_first,
    gain_second,
    attention_master,
    attention_first,
    attention_second,
    merge_master,
    merge_first,
    merge_second,
    feedforward_master,
    feedforward_first,
    feedforward_second,
):
    group_index = lax.axis_index("grp")
    dp_size = lax.axis_size("dp")
    row_count = hidden.shape[2]
    prompt_rows = row_count - CONT
    qkv_width = (HQ + 2 * HK) * HD
    own_rows = feedforward_master.shape[0]
    own_hidden = FF // dp_size
    own_inputs = hidden.reshape(row_count, D)

    gain_columns = jnp.pad(gain_master.T, ((0, 0), (0, GAIN_PAD - 2)))
    weight_low = jnp.concatenate(
        [attention_master.astype(LOW), merge_master.astype(LOW), gain_columns.astype(LOW)], axis=1
    )
    weights, group_rows, gate_rows, first_rows, second_rows = gather_start(
        weight_low, own_inputs, feedforward_master.astype(LOW)
    )
    weights, late_cotangent = lax.optimization_barrier((weights, cotangent))
    weights = weights.reshape(D, -1)
    merge_weight = weights[:, qkv_width : qkv_width + D]
    gain_float = weights[:, qkv_width + D : qkv_width + D + 2].astype(FULL).T
    gate_weight = lax.all_gather(
        gate_rows.reshape(dp_size * own_rows, 2 * own_hidden), "grp", axis=0, tiled=True
    )
    gate_weight, second_rows = lax.optimization_barrier((gate_weight, second_rows))
    first_down = first_rows.reshape(D, own_hidden // 2)
    second_down = lax.all_gather(
        second_rows.reshape(dp_size * own_rows, own_hidden // 2), "grp", axis=0, tiled=True
    )
    down_grad = plane_gather(late_cotangent.reshape(row_count, D))

    segment_row = segment_ids[0]
    source_row = continuation_prompt[0]
    prompt_positions, follow_positions = segment_positions(segment_row, source_row)
    cosine, sine_part = angle_table(jnp.concatenate([prompt_positions, follow_positions[0]]))

    place = jnp.reshape(group_index, (1,)).astype(jnp.int32)
    group_rows = group_rows.reshape(PROMPT_LEN, D)
    queries, pairs, key_normed, normed, key_scale = project_heads(
        place, group_rows, own_inputs, gain_float[:1], cosine, sine_part, weights
    )
    inputs = own_inputs.astype(FULL)
    first_scale = norm_scale(inputs)

    row_index = jnp.arange(row_count, dtype=jnp.int32)
    is_prompt = row_index < prompt_rows
    global_row = group_index * prompt_rows + jnp.minimum(row_index, prompt_rows - 1)
    own_segment = lax.dynamic_slice_in_dim(segment_row, group_index * prompt_rows, prompt_rows)
    query_segment = jnp.concatenate([own_segment, jnp.broadcast_to(source_row, (CONT,))])
    key_index = jnp.arange(PROMPT_LEN, dtype=jnp.int32)
    prompt_seen = (segment_row[None, :] == query_segment[:, None]) & (
        (key_index[None, :] <= global_row[:, None]) | ~is_prompt[:, None]
    )
    follow_seen = (~is_prompt)[:, None] & (
        jnp.arange(CONT, dtype=jnp.int32)[None, :] <= (row_index - prompt_rows)[:, None]
    )
    visible = jnp.concatenate([prompt_seen, follow_seen], axis=1)
    seen = visible.astype(FULL)
    attended, row_logsum = attend(queries, pairs, seen)
    middle = inputs + contract(attended, merge_weight, 1, 1)
    second_scale = norm_scale(middle)
    normed_two = (middle * second_scale * gain_float[1]).astype(LOW)
    grad_rows = cotangent.reshape(row_count, D).astype(FULL)

    normed_two, down_grad = lax.optimization_barrier((normed_two, down_grad))
    normed_all = plane_gather(normed_two)
    gate_up = jnp.dot(normed_all, gate_weight, preferred_element_type=FULL)
    gate_values = gate_up[:, :own_hidden]
    up_values = gate_up[:, own_hidden:]
    gate_sigmoid, gate_silu, activated = gate_parts(gate_values, up_values)
    down_term = contract(down_grad, activated, 0, 0).astype(LOW)
    down_term, second_down = lax.optimization_barrier((down_term, second_down))
    out_term, gate_up_grad = forward_back(
        row_count, activated, down_grad, gate_up, first_down, second_down
    )
    down_part = line_scatter(down_term)
    gate_term = contract(normed_all, gate_up_grad[:, :own_hidden], 0, 0).astype(LOW)
    up_term = contract(normed_all, gate_up_grad[:, own_hidden:], 0, 0).astype(LOW)
    gate_up_grad, gate_term, up_term, down_part = lax.optimization_barrier(
        (gate_up_grad, gate_term, up_term, down_part)
    )
    gate_part = line_scatter(gate_term)
    up_part = line_scatter(up_term)
    normed_two_grad, down_swapped = plane_back(
        row_count, gate_up_grad, gate_weight, down_part.reshape(dp_size, own_rows, own_hidden)
    )
    normed_two_grad, out_term = lax.optimization_barrier((normed_two_grad, out_term))
    out_chunks = out_term.reshape(dp_size, row_count, D)
    out_swapped = [plane_swap(out_chunks[offset + 1], 1) for offset in range(0, dp_size, 2)]
    middle_grad = grad_rows + norm_back(middle, second_scale, gain_float[1], normed_two_grad)
    gain_two_part = jnp.sum(normed_two_grad * middle * second_scale, axis=0)
    branch_grad = middle_grad.astype(LOW)
    attended_grad = contract(branch_grad, merge_weight, 1, 0).astype(LOW)
    attended_grad, out_swapped = lax.optimization_barrier((attended_grad, out_swapped))
    out_sums = [
        out_chunks[2 * at].astype(FULL) + one.astype(FULL) for at, one in enumerate(out_swapped)
    ]
    out_low = [one.astype(LOW) for one in out_sums[1:]]
    attended_grad, out_low = lax.optimization_barrier((attended_grad, out_low))
    out_arrived = [plane_swap(one, 2 * at + 2) for at, one in enumerate(out_low)]
    query_project, pair_project = attend_back(
        place, queries, pairs, seen, row_logsum, attended_grad, cosine, sine_part
    )
    query_term, pair_term, merge_term, normed_grad, pair_back, gain_one_part = weights_back(
        place,
        query_project,
        pair_project,
        branch_grad,
        attended,
        key_normed,
        normed,
        group_rows,
        own_inputs,
        key_scale,
        weights,
    )
    gain_term = jnp.pad(
        jnp.stack([gain_one_part[0], gain_two_part], axis=1), ((0, 0), (0, GAIN_PAD - 2))
    )
    pair_back, up_part, out_arrived = lax.optimization_barrier((pair_back, up_part, out_arrived))
    result = middle + out_sums[0]
    for one in out_arrived:
        result = result + one.astype(FULL)
    block_output, query_term = lax.optimization_barrier((result.astype(LOW), query_term))
    block_output = block_output.reshape(hidden.shape)
    pair_sum = line_scatter(pair_back)
    attention_grad, merge_grad, gain_sums, forward_low = finish(
        (query_term, pair_term, merge_term, gain_term.astype(LOW)),
        gate_part,
        up_part,
        down_swapped,
    )
    gain_grad = gain_sums[:2]
    pair_sum, gain_grad = lax.optimization_barrier((pair_sum, gain_grad))
    pair_sum = pair_sum.astype(FULL)
    normed_grad = normed_grad + jnp.pad(pair_sum, ((0, CONT), (0, 0)))
    input_grad = (middle_grad + norm_back(inputs, first_scale, gain_float[0], normed_grad)).reshape(
        hidden.shape
    )
    feedforward_grad = forward_low.astype(FULL)
    gain_new = adam_step(gain_master, gain_first, gain_second, gain_grad, 0.0)
    attention_new = adam_step(
        attention_master, attention_first, attention_second, attention_grad, WEIGHT_DECAY
    )
    merge_new = adam_step(merge_master, merge_first, merge_second, merge_grad, WEIGHT_DECAY)
    feedforward_new = adam_step(
        feedforward_master, feedforward_first, feedforward_second, feedforward_grad, WEIGHT_DECAY
    )
    return (
        block_output,
        input_grad,
        gain_grad,
        *gain_new,
        attention_grad,
        *attention_new,
        merge_grad,
        *merge_new,
        feedforward_grad,
        *feedforward_new,
    )


def solution(mesh):
    tokens = P("dp", "grp", None, None)
    gains = P(None, ("grp", "dp"))
    matrix = P(("grp", "dp"), None)
    return jax.shard_map(
        body,
        mesh=mesh,
        in_specs=(tokens, tokens, P("dp", None), P("dp", "grp")) + (gains,) * 3 + (matrix,) * 9,
        out_specs=(tokens, tokens) + (gains,) * 4 + (matrix,) * 12,
        check_vma=False,
    )
```

```python
import functools

import jax
import jax.numpy as jnp
from jax import lax
from jax.experimental import pallas as pl
from jax.experimental.pallas import tpu as pltpu
from jax.sharding import PartitionSpec as P

D = 2048
FF = 8192
HQ = 8
HK = 4
HD = 256
PROMPT_LEN = 1024
PROMPTS = 4
CONT = 64
STEP = 10
GAIN_PAD = 128

EPS_NORM = 1e-06
ROPE_THETA = 1000042.0
MASK_FILL = -1e30
BETA_ONE = 0.9
BETA_TWO = 0.95
ADAM_EPS = 1e-08
LEARN_RATE = 0.02
WEIGHT_DECAY = 0.1
LOW = jnp.bfloat16
FULL = jnp.float32
MESH = pl.DeviceIdType.MESH


def contract(left, right, left_axis, right_axis):
    return lax.dot_general(
        left, right, (((left_axis,), (right_axis,)), ((), ())), preferred_element_type=FULL
    )


def angle_table(positions):
    inverse_rate = ROPE_THETA ** (-(jnp.arange(HD // 2, dtype=FULL) * 2.0) / HD)
    angles = positions.astype(FULL)[..., None] * inverse_rate
    return (jnp.cos(angles), jnp.sin(angles))


def segment_positions(segment_row, source_row):
    labels = jnp.arange(PROMPTS, dtype=jnp.int32)
    member = (segment_row[None, :] == labels[:, None]).astype(jnp.int32)
    lengths = jnp.sum(member, axis=1, dtype=jnp.int32)
    starts = jnp.sum(
        jnp.where(labels[None, :] < labels[:, None], lengths[None, :], 0), axis=1, dtype=jnp.int32
    )
    prompt_index = jnp.arange(segment_row.shape[0], dtype=jnp.int32)
    prompt_positions = prompt_index - jnp.sum(member * starts[:, None], axis=0, dtype=jnp.int32)
    source_length = jnp.sum(
        (source_row[:, None] == labels[None, :]).astype(jnp.int32) * lengths[None, :],
        axis=1,
        dtype=jnp.int32,
    )
    follow_positions = source_length[:, None] + jnp.arange(CONT, dtype=jnp.int32)[None, :]
    return (prompt_positions, follow_positions)


def norm_scale(values):
    return lax.rsqrt(jnp.mean(values * values, axis=-1, keepdims=True) + EPS_NORM)


def norm_back(values, row_scale, gain_row, normed_grad):
    scaled = normed_grad * gain_row
    return row_scale * scaled - values * row_scale**3 * jnp.mean(
        scaled * values, axis=-1, keepdims=True
    )


def adam_step(master, first_moment, second_moment, gradient, decay_rate):
    first_new = BETA_ONE * first_moment + (1.0 - BETA_ONE) * gradient
    second_new = BETA_TWO * second_moment + (1.0 - BETA_TWO) * gradient * gradient
    correct_one = 1.0 - BETA_ONE**STEP
    correct_two = 1.0 - BETA_TWO**STEP
    update = first_new / correct_one / (jnp.sqrt(second_new / correct_two) + ADAM_EPS)
    return (-LEARN_RATE * (update + decay_rate * master), first_new, second_new)


def gate_parts(gate_values, up_values):
    gate_sigmoid = jax.nn.sigmoid(gate_values)
    gate_silu = gate_values * gate_sigmoid
    return (gate_sigmoid, gate_silu, (gate_silu * up_values).astype(LOW))


def gate_backward(activated_grad, gate_values, up_values, gate_sigmoid, gate_silu):
    gate_grad = (
        activated_grad * up_values * gate_sigmoid * (1.0 + gate_values * (1.0 - gate_sigmoid))
    ).astype(LOW)
    up_grad = (activated_grad * gate_silu).astype(LOW)
    return (gate_grad, up_grad)


def flip(index, bits):
    bit = 1
    while bit <= bits:
        if bits & bit:
            index = index + bit - 2 * bit * lax.rem(index // bit, 2)
        bit *= 2
    return index


def remote(source, target, send, recv, there):
    return pltpu.make_async_remote_copy(
        src_ref=source,
        dst_ref=target,
        send_sem=send,
        recv_sem=recv,
        device_id=there,
        device_id_type=MESH,
    )


def gather_kernel(
    lines,
    plane,
    prompt_rows,
    weight_ref,
    hidden_ref,
    forward_ref,
    weights_ref,
    rows_ref,
    gate_ref,
    first_ref,
    second_ref,
    local_sem,
    line_send,
    line_recv,
    rows_send,
    rows_recv,
    first_send,
    first_recv,
    near_send,
    near_recv,
    half_send,
    half_recv,
    core_send,
    core_recv,
    swap_send,
    swap_recv,
):
    g = lax.axis_index("grp")
    d = lax.axis_index("dp")
    evens = range(0, plane, 2)
    forward_halves = plane == 8
    near = (2, 4) if forward_halves else tuple(evens[1:])
    width = weight_ref.shape[1]
    cut = (width // 256) * 128

    barrier = pltpu.get_barrier_semaphore()
    for offset in range(1, plane):
        pl.semaphore_signal(barrier, inc=1, device_id=(g, flip(d, offset)), device_id_type=MESH)

    for step in range(1, lines):
        there = lax.rem(g + step, lines)
        pl.semaphore_signal(barrier, inc=1, device_id=(there, d), device_id_type=MESH)
    pl.semaphore_wait(barrier, plane + lines - 2)

    copy = remote
    own_rows = hidden_ref.at[pl.ds(0, prompt_rows)]

    def line_weight(way, step):
        block = g - step + 1 if way == 0 else g + step - 1
        source = weight_ref if step == 1 else weights_ref.at[block, d]
        return copy(
            source,
            weights_ref.at[block, d],
            line_send.at[way, step],
            line_recv.at[way, step],
            (g + 1 if way == 0 else g - 1, d),
        )

    def line_rows(way, step):
        block = g - step + 1 if way == 0 else g + step - 1
        source = own_rows if step == 1 else rows_ref.at[block]
        return copy(
            source,
            rows_ref.at[block],
            rows_send.at[way, step],
            rows_recv.at[way, step],
            (g + 1 if way == 0 else g - 1, d),
        )

    def line_first(way, step):
        block = g - step + 1 if way == 0 else g + step - 1
        return copy(
            first_ref.at[block],
            first_ref.at[block],
            first_send.at[way, step],
            first_recv.at[way, step],
            (g + 1 if way == 0 else g - 1, d),
        )

    def sends(way, step):
        if way == 0:
            return (g < lines - 1) & (g >= step - 1)
        return (g > 0) & (g + step - 1 < lines)

    def receives(way, step):
        return g >= step if way == 0 else g + step < lines

    def near_copy(block, offset, own):
        source = weight_ref if own else weights_ref.at[block, d]
        at = near.index(offset)
        return copy(
            source,
            weights_ref.at[block, d],
            near_send.at[block, at],
            near_recv.at[block, at],
            (g, flip(d, offset)),
        )

    def half_copy(block, part):
        columns = pl.ds(0, cut) if part == 0 else pl.ds(cut, width - cut)
        origin = flip(d, 2) if part == 0 else flip(d, 4)
        there = flip(d, 4) if part == 0 else flip(d, 2)
        piece = weights_ref.at[block, origin, :, columns]
        return copy(
            piece, piece, half_send.at[block, part], half_recv.at[block, part], (g, there)
        )

    def core_copy(block, offset, own=False):
        source = weight_ref if own else weights_ref.at[block, flip(d, offset)]
        return copy(
            source,
            weights_ref.at[block, flip(d, offset)],
            core_send.at[block, offset // 2],
            core_recv.at[block, offset // 2],
            (g, flip(d, 1)),
        )

    half_hidden = second_ref.shape[2]
    own_hidden = 2 * half_hidden

    def swap_piece(owner, part, source_index):
        if part < 2:
            source = forward_ref.at[:, pl.ds(part * FF + owner * own_hidden, own_hidden)]
            return source, gate_ref.at[source_index, :, pl.ds(part * own_hidden, own_hidden)]
        start = 2 * FF + owner * own_hidden + (part - 2) * half_hidden
        source = forward_ref.at[:, pl.ds(start, half_hidden)]
        return source, first_ref.at[g, source_index] if part == 2 else second_ref.at[source_index]

    def swap_copy(offset, part):
        source, target = swap_piece(flip(d, offset), part, d)
        return copy(
            source,
            target,
            swap_send.at[offset, part],
            swap_recv.at[offset, part],
            (g, flip(d, offset)),
        )

    locals_ = (
        pltpu.make_async_copy(weight_ref, weights_ref.at[g, d], local_sem.at[0]),
        pltpu.make_async_copy(own_rows, rows_ref.at[g], local_sem.at[1]),
        *(
            pltpu.make_async_copy(*swap_piece(d, part, d), local_sem.at[2 + part])
            for part in range(4)
        ),
    )

    def launch(block, own):
        for offset in near:
            near_copy(block, offset, own).start()
        core_copy(block, 0, own).start()

    def relay(block):
        for offset in near:
            near_copy(block, offset, False).wait_recv()
            core_copy(block, offset).start()
        if forward_halves:
            half_copy(block, 0).start()
            half_copy(block, 1).start()

    def finish(block):
        if forward_halves:
            half_copy(block, 0).wait_recv()
            half_copy(block, 1).wait_recv()
            core_copy(block, 6).start()

    def both(step, act):
        for way in (0, 1):
            pl.when(receives(way, step))(
                lambda way=way: act(g - step if way == 0 else g + step)
            )

    def take_rows(step):
        for way in (0, 1):

            @pl.when(receives(way, step))
            def _(way=way):
                line_rows(way, step).wait_recv()

            if step + 1 < lines:
                pl.when(sends(way, step + 1))(
                    lambda way=way: line_rows(way, step + 1).start()
                )

    for way in (0, 1):
        pl.when(sends(way, 1))(lambda way=way: line_weight(way, 1).start())
    launch(g, True)
    for one in locals_:
        one.start()
    for step in range(1, lines):
        for way in (0, 1):

            @pl.when(receives(way, step))
            def _(way=way, step=step):
                line_weight(way, step).wait_recv()

            if step + 1 < lines:
                pl.when(sends(way, step + 1))(
                    lambda way=way, step=step: line_weight(way, step + 1).start()
                )
            else:
                pl.when(sends(way, 1))(lambda way=way: line_rows(way, 1).start())

        both(step, lambda block: launch(block, False))
        if step == 1:
            relay(g)
            for offset in range(1, plane):
                swap_copy(offset, 2).start()
    for step in range(1, lines):
        take_rows(step)
        if step == lines - 1:
            locals_[4].wait()
            for offset in range(1, plane):
                swap_copy(offset, 2).wait_recv()
            for way in (0, 1):
                pl.when(sends(way, 1))(lambda way=way: line_first(way, 1).start())
        both(step, relay)
        if step == 1:
            finish(g)
        elif step < lines - 1:
            both(step - 1, finish)
        if step == 1:
            for offset in range(1, plane):
                for part in (0, 1, 3):
                    swap_copy(offset, part).start()
    for step in range(1, lines):
        for way in (0, 1):

            @pl.when(receives(way, step))
            def _(way=way, step=step):
                line_first(way, step).wait_recv()

            if step + 1 < lines:
                pl.when(sends(way, step + 1))(
                    lambda way=way, step=step: line_first(way, step + 1).start()
                )
        if step == 1:
            both(lines - 2, finish)
    both(lines - 1, finish)

    def drain(block):
        for offset in evens:
            core_copy(block, offset).wait()
        for offset in near:
            near_copy(block, offset, False).wait_send()
        if forward_halves:
            half_copy(block, 0).wait_send()
            half_copy(block, 1).wait_send()

    drain(g)
    for step in range(1, lines):
        for way in (0, 1):
            pl.when(receives(way, step))(
                lambda way=way, step=step: drain(g - step if way == 0 else g + step)
            )

            @pl.when(sends(way, step))
            def _(way=way, step=step):
                line_weight(way, step).wait_send()
                line_rows(way, step).wait_send()
                line_first(way, step).wait_send()

    for offset in range(1, plane):
        for part in (0, 1, 3):
            swap_copy(offset, part).wait()
        swap_copy(offset, 2).wait_send()
    for at, one in enumerate(locals_):
        if at != 4:
            one.wait()


def gather_start(weight, hidden, forward):
    lines, plane = lax.axis_size("grp"), lax.axis_size("dp")
    prompt_rows = PROMPT_LEN // lines
    own_rows, width = weight.shape
    anywhere = pl.BlockSpec(memory_space=pl.ANY)
    dma = pltpu.SemaphoreType.DMA
    near_count = 2 if plane == 8 else plane // 2 - 1
    pairs = (
        (2, lines),
        (2, lines),
        (2, lines),
        (2, lines),
        (2, lines),
        (2, lines),
        (lines, near_count),
        (lines, near_count),
        (lines, 2),
        (lines, 2),
        (lines, plane // 2),
        (lines, plane // 2),
        (plane, 4),
        (plane, 4),
    )
    own_hidden = FF // plane
    return pl.pallas_call(
        functools.partial(gather_kernel, lines, plane, prompt_rows),
        out_shape=(
            jax.ShapeDtypeStruct((lines, plane, own_rows, width), weight.dtype),
            jax.ShapeDtypeStruct((lines, prompt_rows, D), hidden.dtype),
            jax.ShapeDtypeStruct((plane, own_rows, 2 * own_hidden), forward.dtype),
            jax.ShapeDtypeStruct((lines, plane, own_rows, own_hidden // 2), forward.dtype),
            jax.ShapeDtypeStruct((plane, own_rows, own_hidden // 2), forward.dtype),
        ),
        in_specs=[anywhere] * 3,
        out_specs=(anywhere,) * 5,
        scratch_shapes=[dma((6,))] + [dma(shape) for shape in pairs],
        compiler_params=pltpu.CompilerParams(collective_id=0, has_side_effects=True),
        name="gather_start",
    )(weight, hidden, forward)


def project_kernel(
    place_ref,
    group_ref,
    own_ref,
    gain_ref,
    cosine_ref,
    sine_ref,
    weight_ref,
    query_ref,
    pair_ref,
    normed_ref,
    own_normed_ref,
    scale_ref,
):
    step = pl.program_id(0)
    own_rows = own_ref.shape[0]
    prompt_rows = own_rows - CONT
    start = pl.multiple_of(place_ref[0] * prompt_rows, 16)
    tile = 32

    def norm_tile(values, at):
        values = values.astype(FULL)
        scale = lax.rsqrt(jnp.mean(values * values, axis=-1, keepdims=True) + EPS_NORM)
        normed_ref[pl.ds(at, tile)] = (values * scale * gain_ref[...]).astype(LOW)
        scale_ref[pl.ds(at, tile)] = jnp.broadcast_to(scale, (tile, 128))

    @pl.when(step == 0)
    def _():
        @pl.loop(0, PROMPT_LEN // tile)
        def _(at):
            first = pl.multiple_of(at * tile, tile)
            norm_tile(group_ref[pl.ds(first, tile)], first)

        for at in range(0, CONT, tile):
            norm_tile(own_ref[prompt_rows + at : prompt_rows + at + tile], PROMPT_LEN + at)
        own_normed_ref[:prompt_rows] = normed_ref[pl.ds(start, prompt_rows)]
        own_normed_ref[prompt_rows:] = normed_ref[PROMPT_LEN:]

    def turn(values, cosine, sine_part):
        front, back = values[:, : HD // 2], values[:, HD // 2 :]
        return front * cosine - back * sine_part, back * cosine + front * sine_part

    def project(rows):
        return jnp.dot(rows, weight_ref[...], preferred_element_type=FULL)

    @pl.when(step < HQ)
    def _():
        for first, count, table in ((0, prompt_rows, start), (prompt_rows, CONT, PROMPT_LEN)):
            values = project(own_normed_ref[first : first + count])
            front, back = turn(
                values, cosine_ref[pl.ds(table, count)], sine_ref[pl.ds(table, count)]
            )
            query_ref[first : first + count, : HD // 2] = front.astype(LOW)
            query_ref[first : first + count, HD // 2 :] = back.astype(LOW)

    key_count = PROMPT_LEN + CONT
    part = key_count // 4

    @pl.when((step >= HQ) & (step < HQ + HK))
    def _():
        @pl.loop(0, 4)
        def _(at):
            rows = pl.ds(pl.multiple_of(at * part, 16), part)
            front, back = turn(project(normed_ref[rows]), cosine_ref[rows], sine_ref[rows])
            pair_ref[rows, : HD // 2] = front.astype(LOW)
            pair_ref[rows, HD // 2 :] = back.astype(LOW)

    @pl.when(step >= HQ + HK)
    def _():
        @pl.loop(0, 4)
        def _(at):
            rows = pl.ds(pl.multiple_of(at * part, 16), part)
            pair_ref[rows] = project(normed_ref[rows]).astype(LOW)


VMEM_LIMIT = 60 * 2**20


def project_heads(place, group_rows, own_inputs, gain_row, cosine, sine_part, weights):
    own_rows = own_inputs.shape[0]
    key_count = PROMPT_LEN + CONT
    whole = lambda shape: pl.BlockSpec(shape, lambda j, p: (0, 0))
    return pl.pallas_call(
        project_kernel,
        grid_spec=pltpu.PrefetchScalarGridSpec(
            num_scalar_prefetch=1,
            grid=(HQ + 2 * HK,),
            in_specs=[
                whole((PROMPT_LEN, D)),
                whole((own_rows, D)),
                whole((1, D)),
                whole((key_count, HD // 2)),
                whole((key_count, HD // 2)),
                pl.BlockSpec((D, HD), lambda j, p: (0, j)),
            ],
            out_specs=[
                pl.BlockSpec((own_rows, HD), lambda j, p: (0, jnp.minimum(j, HQ - 1))),
                pl.BlockSpec((key_count, HD), lambda j, p: (0, jnp.maximum(j - HQ, 0))),
                whole((key_count, D)),
                whole((own_rows, D)),
                whole((key_count, 128)),
            ],
        ),
        out_shape=[
            jax.ShapeDtypeStruct((own_rows, HQ * HD), LOW),
            jax.ShapeDtypeStruct((key_count, 2 * HK * HD), LOW),
            jax.ShapeDtypeStruct((key_count, D), LOW),
            jax.ShapeDtypeStruct((own_rows, D), LOW),
            jax.ShapeDtypeStruct((key_count, 128), FULL),
        ],
        compiler_params=pltpu.CompilerParams(vmem_limit_bytes=VMEM_LIMIT),
        name="project_heads",
    )(place, group_rows, own_inputs, gain_row, cosine, sine_part, weights)


def across(left, right):
    return lax.dot_general(left, right, (((1,), (1,)), ((), ())), preferred_element_type=FULL)


def along(left, right):
    return lax.dot_general(left, right, (((0,), (0,)), ((), ())), preferred_element_type=FULL)


def attend_kernel(query_ref, key_ref, value_ref, seen_ref, attended_ref, logsum_ref):
    group_heads = HQ // HK
    for head in range(group_heads):
        columns = slice(head * HD, (head + 1) * HD)
        scores = across(query_ref[:, columns], key_ref[...]) * HD ** (-0.5)
        scores = jnp.where(seen_ref[...] > 0, scores, MASK_FILL)
        peak = jnp.max(scores, axis=-1, keepdims=True)
        unnormed = jnp.exp(scores - peak)
        total = jnp.sum(unnormed, axis=-1, keepdims=True)
        low = (unnormed / total).astype(LOW)
        attended_ref[:, columns] = jnp.dot(
            low, value_ref[...], preferred_element_type=FULL
        ).astype(LOW)
        logsum_ref[:, head * 128 : (head + 1) * 128] = jnp.broadcast_to(
            peak + jnp.log(total), (query_ref.shape[0], 128)
        )


def attend(queries, pairs, seen):
    rows, key_count = seen.shape
    group_heads = HQ // HK
    return pl.pallas_call(
        attend_kernel,
        grid=(HK,),
        in_specs=[
            pl.BlockSpec((rows, group_heads * HD), lambda j: (0, j)),
            pl.BlockSpec((key_count, HD), lambda j: (0, j)),
            pl.BlockSpec((key_count, HD), lambda j: (0, HK + j)),
            pl.BlockSpec((rows, key_count), lambda j: (0, 0)),
        ],
        out_specs=[
            pl.BlockSpec((rows, group_heads * HD), lambda j: (0, j)),
            pl.BlockSpec((rows, group_heads * 128), lambda j: (0, j)),
        ],
        out_shape=[
            jax.ShapeDtypeStruct((rows, HQ * HD), LOW),
            jax.ShapeDtypeStruct((rows, HQ * 128), FULL),
        ],
        compiler_params=pltpu.CompilerParams(vmem_limit_bytes=VMEM_LIMIT),
        name="attend",
    )(queries, pairs, pairs, seen)


def attend_back_kernel(
    place_ref,
    query_ref,
    key_ref,
    value_ref,
    seen_ref,
    logsum_ref,
    grad_ref,
    cosine_ref,
    sine_ref,
    query_out,
    pair_out,
):
    step = pl.program_id(0)
    group_heads = HQ // HK
    rows = query_ref.shape[0]
    prompt_rows = rows - CONT
    start = pl.multiple_of(place_ref[0] * prompt_rows, 16)
    score_scale = HD ** (-0.5)
    key_grad = value_grad = 0.0

    def turn_back(values, cosine, sine_part):
        front, back = values[:, : HD // 2], values[:, HD // 2 :]
        return jnp.concatenate(
            [front * cosine + back * sine_part, back * cosine - front * sine_part], axis=1
        ).astype(LOW)

    for head in range(group_heads):
        columns = slice(head * HD, (head + 1) * HD)
        scores = across(query_ref[:, columns], key_ref[...]) * score_scale
        scores = jnp.where(seen_ref[...] > 0, scores, MASK_FILL)
        probabilities = jnp.exp(scores - logsum_ref[:, head * 128 : head * 128 + 1])
        grads = grad_ref[:, columns]
        probability_grad = across(grads, value_ref[...])
        delta = jnp.sum(probabilities * probability_grad, axis=-1, keepdims=True)
        score_grad = (probabilities * (probability_grad - delta)).astype(LOW)
        query_grad = jnp.dot(score_grad, key_ref[...], preferred_element_type=FULL) * score_scale
        key_grad = key_grad + along(score_grad, query_ref[:, columns])
        value_grad = value_grad + along(probabilities.astype(LOW), grads)
        query_out[:prompt_rows, columns] = turn_back(
            query_grad[:prompt_rows],
            cosine_ref[pl.ds(start, prompt_rows)],
            sine_ref[pl.ds(start, prompt_rows)],
        )
        query_out[prompt_rows:, columns] = turn_back(
            query_grad[prompt_rows:], cosine_ref[PROMPT_LEN:], sine_ref[PROMPT_LEN:]
        )
    pair_out[:, pl.ds(pl.multiple_of(step * HD, HD), HD)] = turn_back(
        key_grad * score_scale, cosine_ref[...], sine_ref[...]
    )
    pair_out[:, pl.ds(pl.multiple_of((HK + step) * HD, HD), HD)] = value_grad.astype(LOW)


def attend_back(place, queries, pairs, seen, logsum, grads, cosine, sine_part):
    rows, key_count = seen.shape
    group_heads = HQ // HK
    whole = lambda shape: pl.BlockSpec(shape, lambda j, p: (0, 0))
    return pl.pallas_call(
        attend_back_kernel,
        grid_spec=pltpu.PrefetchScalarGridSpec(
            num_scalar_prefetch=1,
            grid=(HK,),
            in_specs=[
                pl.BlockSpec((rows, group_heads * HD), lambda j, p: (0, j)),
                pl.BlockSpec((key_count, HD), lambda j, p: (0, j)),
                pl.BlockSpec((key_count, HD), lambda j, p: (0, HK + j)),
                whole((rows, key_count)),
                pl.BlockSpec((rows, group_heads * 128), lambda j, p: (0, j)),
                pl.BlockSpec((rows, group_heads * HD), lambda j, p: (0, j)),
                whole((key_count, HD // 2)),
                whole((key_count, HD // 2)),
            ],
            out_specs=[
                pl.BlockSpec((rows, group_heads * HD), lambda j, p: (0, j)),
                whole((key_count, 2 * HK * HD)),
            ],
        ),
        out_shape=[
            jax.ShapeDtypeStruct((rows, HQ * HD), LOW),
            jax.ShapeDtypeStruct((key_count, 2 * HK * HD), LOW),
        ],
        compiler_params=pltpu.CompilerParams(vmem_limit_bytes=VMEM_LIMIT),
        name="attend_back",
    )(place, queries, pairs, pairs, seen, logsum, grads, cosine, sine_part)


def weights_back_kernel(
    place_ref,
    query_ref,
    pair_ref,
    branch_ref,
    attended_ref,
    normed_ref,
    own_normed_ref,
    group_ref,
    own_ref,
    scale_ref,
    query_weight_ref,
    pair_weight_ref,
    query_term,
    pair_term,
    merge_term,
    back_out,
    pair_back_out,
    gain_out,
):
    rows = query_ref.shape[0]
    prompt_rows = rows - CONT
    start = pl.multiple_of(place_ref[0] * prompt_rows, 16)
    query_term[...] = along(own_normed_ref[...], query_ref[...]).astype(LOW)
    pair_term[...] = along(normed_ref[...], pair_ref[...]).astype(LOW)
    merge_term[...] = along(branch_ref[...], attended_ref[...]).astype(LOW)
    query_back = across(query_ref[...], query_weight_ref[...])
    pair_back = across(pair_ref[...], pair_weight_ref[...])
    own_values = own_ref[prompt_rows:].astype(FULL) * scale_ref[PROMPT_LEN:, :1]
    tail = query_back[prompt_rows:] + pair_back[PROMPT_LEN:]
    group_values = group_ref[...].astype(FULL) * scale_ref[:PROMPT_LEN, :1]
    own_prompt = own_ref[:prompt_rows].astype(FULL) * scale_ref[pl.ds(start, prompt_rows), :1]
    gain_out[...] = (
        jnp.sum(pair_back[:PROMPT_LEN] * group_values, axis=0, keepdims=True)
        + jnp.sum(query_back[:prompt_rows] * own_prompt, axis=0, keepdims=True)
        + jnp.sum(tail * own_values, axis=0, keepdims=True)
    )
    back_out[:prompt_rows] = query_back[:prompt_rows]
    back_out[prompt_rows:] = tail
    pair_back_out[...] = pair_back[:PROMPT_LEN].astype(LOW)


def weights_back(
    place, queries, pairs, branch, attended, normed, own_normed, group_rows, own_inputs, scale, weights
):
    rows, key_count = queries.shape[0], pairs.shape[0]
    wide, tile = HQ * HD, 256
    whole = lambda shape: pl.BlockSpec(shape, lambda j, p: (0, 0))
    tall = lambda count: pl.BlockSpec((count, tile), lambda j, p: (0, j))
    flat = lambda at: pl.BlockSpec((tile, wide), lambda j, p: (j, at))
    return pl.pallas_call(
        weights_back_kernel,
        grid_spec=pltpu.PrefetchScalarGridSpec(
            num_scalar_prefetch=1,
            grid=(D // tile,),
            in_specs=[
                whole((rows, wide)),
                whole((key_count, wide)),
                tall(rows),
                whole((rows, wide)),
                tall(key_count),
                tall(rows),
                tall(PROMPT_LEN),
                tall(rows),
                whole((key_count, 128)),
                flat(0),
                flat(1),
            ],
            out_specs=[flat(0), flat(0), flat(0), tall(rows), tall(PROMPT_LEN), tall(1)],
        ),
        out_shape=[
            jax.ShapeDtypeStruct((D, wide), LOW),
            jax.ShapeDtypeStruct((D, wide), LOW),
            jax.ShapeDtypeStruct((D, wide), LOW),
            jax.ShapeDtypeStruct((rows, D), FULL),
            jax.ShapeDtypeStruct((PROMPT_LEN, D), LOW),
            jax.ShapeDtypeStruct((1, D), FULL),
        ],
        compiler_params=pltpu.CompilerParams(vmem_limit_bytes=VMEM_LIMIT),
        name="weights_back",
    )(
        place,
        queries,
        pairs,
        branch,
        attended,
        normed,
        own_normed,
        group_rows,
        own_inputs,
        scale,
        weights,
        weights,
    )


def forward_back_kernel(
    activated_ref, grad_ref, gate_up_ref, first_ref, second_ref, out_ref, gate_up_grad_ref
):
    own_hidden = activated_ref.shape[1]
    part = first_ref.shape[0] // 4
    piece = own_hidden // 2

    @pl.loop(0, 4)
    def _(at):
        columns = pl.ds(pl.multiple_of(at * part, part), part)
        out_ref[:, columns] = (
            across(activated_ref[:, :piece], first_ref[columns])
            + across(activated_ref[:, piece:], second_ref[columns])
        ).astype(LOW)

    for at, down_ref in enumerate((first_ref, second_ref)):
        columns = slice(at * piece, (at + 1) * piece)
        upper = slice(own_hidden + at * piece, own_hidden + (at + 1) * piece)
        activated_grad = jnp.dot(grad_ref[...], down_ref[...], preferred_element_type=FULL)
        gate_values, up_values = gate_up_ref[:, columns], gate_up_ref[:, upper]
        gate_sigmoid = jax.nn.sigmoid(gate_values)
        gate_grad, up_grad = gate_backward(
            activated_grad, gate_values, up_values, gate_sigmoid, gate_values * gate_sigmoid
        )
        gate_up_grad_ref[:, columns] = gate_grad
        gate_up_grad_ref[:, upper] = up_grad


def forward_back(rows, activated, grads, gate_up, first_down, second_down):
    count, own_hidden = activated.shape
    block = lambda width: pl.BlockSpec((rows, width), lambda j: (j, 0))
    return pl.pallas_call(
        forward_back_kernel,
        grid=(count // rows,),
        in_specs=[
            block(own_hidden),
            block(D),
            block(2 * own_hidden),
            pl.BlockSpec(first_down.shape, lambda j: (0, 0)),
            pl.BlockSpec(second_down.shape, lambda j: (0, 0)),
        ],
        out_specs=[block(D), block(2 * own_hidden)],
        out_shape=[
            jax.ShapeDtypeStruct((count, D), LOW),
            jax.ShapeDtypeStruct((count, 2 * own_hidden), LOW),
        ],
        compiler_params=pltpu.CompilerParams(vmem_limit_bytes=VMEM_LIMIT),
        name="forward_back",
    )(activated, grads, gate_up, first_down, second_down)


def plane_back_kernel(
    plane,
    rows_ref,
    weight_ref,
    down_ref,
    out_ref,
    swapped_ref,
    weight,
    tiles,
    keep,
    give,
    core_in,
    plane_in,
    total,
    load_sem,
    tile_sem,
    core_send,
    core_recv,
    plane_send,
    plane_recv,
    out_sem,
    swap_send,
    swap_recv,
):
    g = lax.axis_index("grp")
    d = lax.axis_index("dp")
    chips = plane // 2
    own_hidden = down_ref.shape[2]
    halves = plane == 8
    order = (3, 1, 2, 0) if halves else tuple(range(chips - 1, -1, -1))
    cut = D // 2
    half_of = (pl.ds(0, cut), pl.ds(cut, D - cut))

    barrier = pltpu.get_barrier_semaphore()
    for offset in range(1, plane):
        pl.semaphore_signal(
            barrier, inc=1, device_id=(g, flip(d, offset)), device_id_type=MESH
        )

    load = pltpu.make_async_copy(weight_ref, weight, load_sem.at[0])
    load.start()

    def tile_copy(turn):
        at = order[turn]
        return pltpu.make_async_copy(
            rows_ref.at[pl.ds(2 * at, 2)], tiles.at[turn % 2], tile_sem.at[turn % 2]
        )

    def core_copy(at):
        return remote(
            give.at[at], core_in.at[at], core_send.at[at], core_recv.at[at], (g, flip(d, 1))
        )

    def plane_copy(at):
        return remote(
            keep.at[at],
            plane_in.at[at],
            plane_send.at[at],
            plane_recv.at[at],
            (g, flip(d, 2 * at)),
        )

    def near_copy(part, relayed):
        there = part + 1
        return remote(
            keep.at[3 if relayed else there, :, half_of[part]],
            plane_in.at[1 if relayed else 0, :, half_of[part]],
            plane_send.at[2 * relayed + part],
            plane_recv.at[2 * relayed + part],
            (g, flip(d, 2 * there)),
        )

    def relay_copy(part):
        there = 2 - part
        return remote(
            keep.at[there, :, half_of[part]],
            plane_in.at[2, :, half_of[part]],
            plane_send.at[4 + part],
            plane_recv.at[4 + part],
            (g, flip(d, 2 * there)),
        )

    def swap_copy(offset):
        there = flip(d, offset)
        return remote(
            down_ref.at[there],
            swapped_ref.at[:, pl.ds(d * own_hidden, own_hidden)],
            swap_send.at[offset],
            swap_recv.at[offset],
            (g, there),
        )

    own_swap = pltpu.make_async_copy(
        down_ref.at[d], swapped_ref.at[:, pl.ds(d * own_hidden, own_hidden)], out_sem.at[1]
    )
    tile_copy(0).start()
    tile_copy(1).start()
    pl.semaphore_wait(barrier, plane - 1)
    for offset in range(1, plane):
        swap_copy(offset).start()
    own_swap.start()
    load.wait()
    part_width = 512

    def product(turn, which, target):
        @pl.loop(0, D // part_width)
        def _(at):
            columns = pl.ds(pl.multiple_of(at * part_width, part_width), part_width)
            target[order[turn], :, columns] = across(
                tiles[turn % 2, which], weight[columns]
            ).astype(LOW)

    def add_into(at, other, first, count):
        step = 256

        @pl.loop(0, count // step)
        def _(k):
            here = pl.ds(pl.multiple_of(first + k * step, step), step)
            keep[at, :, here] = (
                keep[at, :, here].astype(FULL) + other(here).astype(FULL)
            ).astype(LOW)

    def settle(turn):
        at = order[turn]
        core_copy(at).wait_recv()
        add_into(at, lambda here: core_in[at, :, here], 0, D)
        if halves and at == 3:
            near_copy(0, True).start()
            near_copy(1, True).start()
        elif halves and at:
            near_copy(at - 1, False).start()
        elif at:
            plane_copy(at).start()

    for turn in range(chips):
        tile_copy(turn).wait()
        product(turn, 1, give)
        core_copy(order[turn]).start()
        if turn:
            settle(turn - 1)
        product(turn, 0, keep)
        if turn + 2 < chips:
            tile_copy(turn + 2).start()
        if halves and turn == chips - 1:
            for part in range(2):
                near_copy(part, True).wait_recv()
                add_into(
                    2 - part,
                    lambda here: plane_in[1, :, here],
                    part * cut,
                    cut,
                )
                relay_copy(part).start()
    settle(chips - 1)
    if halves:
        for part in range(2):
            near_copy(part, False).wait_recv()
            relay_copy(part).wait_recv()
        arrived = (0, 2)
    else:
        for at in range(1, chips):
            plane_copy(at).wait_recv()
        arrived = tuple(range(1, chips))

    @pl.loop(0, D // 256)
    def _(k):
        here = pl.ds(pl.multiple_of(k * 256, 256), 256)
        value = keep[0, :, here].astype(FULL)
        for at in arrived:
            value = value + plane_in[at, :, here].astype(FULL)
        total[:, here] = value

    out = pltpu.make_async_copy(total, out_ref, out_sem.at[0])
    out.start()
    for at in range(chips):
        core_copy(at).wait_send()
    if halves:
        for part in range(2):
            near_copy(part, False).wait_send()
            near_copy(part, True).wait_send()
            relay_copy(part).wait_send()
    else:
        for at in range(1, chips):
            plane_copy(at).wait_send()
    for offset in range(1, plane):
        swap_copy(offset).wait()
    own_swap.wait()
    out.wait()


def plane_back(rows, gate_up_grad, gate_weight, down_part):
    plane = lax.axis_size("dp")
    chips = plane // 2
    inner = gate_up_grad.shape[1]
    anywhere = pl.BlockSpec(memory_space=pl.ANY)
    dma = pltpu.SemaphoreType.DMA
    return pl.pallas_call(
        functools.partial(plane_back_kernel, plane),
        out_shape=(
            jax.ShapeDtypeStruct((rows, D), FULL),
            jax.ShapeDtypeStruct((down_part.shape[1], FF), LOW),
        ),
        in_specs=[anywhere] * 3,
        out_specs=(anywhere,) * 2,
        scratch_shapes=[
            pltpu.VMEM((D, inner), LOW),
            pltpu.VMEM((2, 2, rows, inner), LOW),
            pltpu.VMEM((chips, rows, D), LOW),
            pltpu.VMEM((chips, rows, D), LOW),
            pltpu.VMEM((chips, rows, D), LOW),
            pltpu.VMEM((3 if plane == 8 else chips, rows, D), LOW),
            pltpu.VMEM((rows, D), FULL),
            dma((1,)),
            dma((2,)),
            dma((chips,)),
            dma((chips,)),
            dma((max(6, chips),)),
            dma((max(6, chips),)),
            dma((2,)),
            dma((plane,)),
            dma((plane,)),
        ],
        compiler_params=pltpu.CompilerParams(
            collective_id=2, has_side_effects=True, vmem_limit_bytes=VMEM_LIMIT
        ),
        name="plane_back",
    )(gate_up_grad.reshape(plane, rows, inner), gate_weight, down_part)


def plane_swap(block, offset):
    size = lax.axis_size("dp")
    return lax.ppermute(block, "dp", [(i, i ^ offset) for i in range(size)])


def plane_gather(block):
    mine = [block] + [plane_swap(block, o) for o in range(2, lax.axis_size("dp"), 2)]
    pairs = [(one, plane_swap(one, 1)) for one in mine]
    return jnp.concatenate([one for pair in pairs for one in pair], axis=0)


def line_scatter(term):
    return lax.psum_scatter(term, "grp", scatter_dimension=0, tiled=True)


def finish_kernel(
    lines,
    plane,
    query_ref,
    pair_ref,
    merge_ref,
    gain_ref,
    gate_ref,
    down_ref,
    a_out,
    m_out,
    gain_out,
    f_out,
    mine,
    core_in,
    plane_in,
    line_in,
    owned,
    gain_made,
    mine_sem,
    core_send,
    core_recv,
    plane_send,
    plane_recv,
    line_send,
    line_recv,
    swap_send,
    swap_recv,
    own_sem,
    out_sem,
):
    g = lax.axis_index("grp")
    d = lax.axis_index("dp")
    chips = plane // 2
    chip, core = lax.div(d, 2), lax.rem(d, 2)
    partner = d + 1 - 2 * core
    own_hidden = gate_ref.shape[2] // 2
    width = core_in.shape[3]
    a_width, m_width = a_out.shape[1], m_out.shape[1]
    parts, begin = [], 0
    for ref in (query_ref, pair_ref, merge_ref, gain_ref):
        parts.append((ref, pl.ds(begin, ref.shape[4])))
        begin += ref.shape[4]

    barrier = pltpu.get_barrier_semaphore()
    for step in range(1, plane):
        there = lax.rem(d + step, plane)
        pl.semaphore_signal(barrier, inc=1, device_id=(g, there), device_id_type=MESH)
    for step in range(1, lines):
        there = lax.rem(g + step, lines)
        pl.semaphore_signal(barrier, inc=1, device_id=(there, d), device_id_type=MESH)
    pl.semaphore_wait(barrier, plane + lines - 2)

    def line_at(turn):
        return lax.rem(g + turn + 1, lines)

    def core_copy(turn, part):
        line = line_at(turn)
        ref, columns = parts[part]
        return remote(
            ref.at[line, :, 1 - core],
            core_in.at[line, :, :, columns],
            core_send.at[turn, part],
            core_recv.at[turn, part],
            (g, partner),
        )

    def mine_copy(turn, part):
        line = line_at(turn)
        ref, columns = parts[part]
        return pltpu.make_async_copy(
            ref.at[line, :, core], mine.at[turn % 2, :, :, columns], mine_sem.at[turn, part]
        )

    cut = width // 256 * 128
    columns_of = (pl.ds(0, cut), pl.ds(cut, width - cut))

    def plane_copy(turn, step):
        line = line_at(turn)
        there = lax.rem(chip + step, chips)
        return remote(
            core_in.at[line, there],
            plane_in.at[line, chip],
            plane_send.at[turn, step],
            plane_recv.at[turn, step],
            (g, 2 * there + core),
        )

    def near_copy(turn, part, relayed):
        line = line_at(turn)
        there = flip(chip, part + 1)
        owner = flip(chip, 3) if relayed else there
        return remote(
            core_in.at[line, owner, :, columns_of[part]],
            plane_in.at[line, 1 if relayed else 0, :, columns_of[part]],
            plane_send.at[turn, 2 * relayed + part],
            plane_recv.at[turn, 2 * relayed + part],
            (g, 2 * there + core),
        )

    def relay_copy(turn, part):
        line = line_at(turn)
        there = flip(chip, 2 - part)
        return remote(
            core_in.at[line, there, :, columns_of[part]],
            plane_in.at[line, 2, :, columns_of[part]],
            plane_send.at[turn, 4 + part],
            plane_recv.at[turn, 4 + part],
            (g, 2 * there + core),
        )

    def line_copy(turn):
        line = line_at(turn)
        return remote(
            core_in.at[line, chip],
            line_in.at[g],
            line_send.at[turn],
            line_recv.at[turn],
            (line, d),
        )

    def swap_source(owner, part):
        return gate_ref.at[owner, :, pl.ds(part * own_hidden, own_hidden)]

    def swap_place(part):
        return f_out.at[:, pl.ds(part * FF + d * own_hidden, own_hidden)]

    def swap_copy(step, part):
        there = lax.rem(d + step, plane)
        return remote(
            swap_source(there, part),
            swap_place(part),
            swap_send.at[step, part],
            swap_recv.at[step, part],
            (g, there),
        )

    own_swap = [
        pltpu.make_async_copy(swap_source(d, part), swap_place(part), own_sem.at[part])
        for part in range(2)
    ] + [pltpu.make_async_copy(down_ref, f_out.at[:, pl.ds(2 * FF, FF)], own_sem.at[2])]

    every = range(len(parts))
    for turn in range(lines):
        for part in every:
            core_copy(turn, part).start()
            if turn < 2:
                mine_copy(turn, part).start()
    tile = 896 if width % 896 == 0 else 128
    halves = plane == 8

    def add_into(line, there, other, columns=None):
        first, count = (0, width) if columns is None else columns
        step = tile if columns is None else 128

        @pl.loop(0, count // step)
        def _(at):
            here = pl.ds(pl.multiple_of(first + at * step, 128), step)
            total = core_in[line, there, :, here].astype(FULL) + other(here).astype(FULL)
            core_in[line, there, :, here] = total.astype(LOW)

    def near_start(turn):
        if halves:
            for relayed in (True, False):
                for part in range(2):
                    near_copy(turn, part, relayed).start()
        else:
            for step in range(1, chips):
                plane_copy(turn, step).start()

    for turn in range(lines):
        line = line_at(turn)
        for part in every:
            core_copy(turn, part).wait_recv()
            mine_copy(turn, part).wait()
        for step in range(1, chips + 1):
            there = lax.rem(chip + step, chips)
            add_into(
                line, there, lambda here, there=there, turn=turn: mine[turn % 2, there, :, here]
            )
        if turn + 2 < lines:
            for part in every:
                mine_copy(turn + 2, part).start()
        if turn < 2:
            near_start(turn)

    def pass_on(turn):
        line = line_at(turn)
        for part, columns in enumerate(((0, cut), (cut, width - cut))):
            near_copy(turn, part, True).wait_recv()
            add_into(
                line,
                flip(chip, 2 - part),
                lambda here, line=line: plane_in[line, 1, :, here],
                columns,
            )
            relay_copy(turn, part).start()

    def near_done(turn):
        if halves:
            pass_on(turn)
            for part in range(2):
                near_copy(turn, part, False).wait_recv()
        else:
            for step in range(1, chips):
                plane_copy(turn, step).wait_recv()
        if turn + 2 < lines:
            near_start(turn + 2)

    def line_done(turn):
        line = line_at(turn)
        if halves:
            for part in range(2):
                relay_copy(turn, part).wait_recv()
            arrived = (0, 2)
        else:
            arrived = tuple(lax.rem(chip + step, chips) for step in range(1, chips))

        @pl.loop(0, width // tile)
        def _(at):
            columns = pl.ds(pl.multiple_of(at * tile, tile), tile)
            total = core_in[line, chip, :, columns].astype(FULL)
            for block in arrived:
                total = total + plane_in[line, block, :, columns].astype(FULL)
            core_in[line, chip, :, columns] = total.astype(LOW)

        if turn < lines - 1:
            line_copy(turn).start()

    near_done(0)
    for turn in range(1, lines):
        near_done(turn)
        line_done(turn - 1)
        if turn == lines - 2:
            for step in range(1, plane):
                for part in range(2):
                    swap_copy(step, part).start()
            for one in own_swap:
                one.start()
    line_done(lines - 1)
    for turn in range(lines - 1):
        line_copy(turn).wait_recv()

    def total_of(columns):
        total = core_in[g, chip, :, columns].astype(FULL)
        for step in range(1, lines):
            total = total + line_in[lax.rem(g + step, lines), :, columns].astype(FULL)
        return total

    @pl.loop(0, (a_width + m_width) // 256)
    def _(at):
        columns = pl.ds(pl.multiple_of(at * 256, 256), 256)
        owned[:, columns] = total_of(columns)

    gain_made[...] = total_of(pl.ds(a_width + m_width, GAIN_PAD)).T[:8]
    outs = (
        pltpu.make_async_copy(owned.at[:, pl.ds(0, a_width)], a_out, out_sem.at[0]),
        pltpu.make_async_copy(owned.at[:, pl.ds(a_width, m_width)], m_out, out_sem.at[1]),
        pltpu.make_async_copy(gain_made, gain_out, out_sem.at[2]),
    )
    for one in outs:
        one.start()
    for turn in range(lines):
        for part in every:
            core_copy(turn, part).wait_send()
        if halves:
            for part in range(2):
                near_copy(turn, part, False).wait_send()
                near_copy(turn, part, True).wait_send()
                relay_copy(turn, part).wait_send()
        else:
            for step in range(1, chips):
                plane_copy(turn, step).wait_send()
        if turn < lines - 1:
            line_copy(turn).wait_send()
    for step in range(1, plane):
        for part in range(2):
            swap_copy(step, part).wait()
    for one in own_swap:
        one.wait()
    for one in outs:
        one.wait()


def finish(terms, gate_part, down_swapped):
    lines, plane = lax.axis_size("grp"), lax.axis_size("dp")
    chips = plane // 2
    rows = D // (lines * plane)
    m_width = terms[2].shape[1]
    a_width = terms[0].shape[1] + terms[1].shape[1]
    width = a_width + m_width + GAIN_PAD
    anywhere = pl.BlockSpec(memory_space=pl.ANY)
    dma = pltpu.SemaphoreType.DMA
    vmem = pltpu.VMEM
    return pl.pallas_call(
        functools.partial(finish_kernel, lines, plane),
        out_shape=(
            jax.ShapeDtypeStruct((rows, a_width), FULL),
            jax.ShapeDtypeStruct((rows, m_width), FULL),
            jax.ShapeDtypeStruct((8, rows), FULL),
            jax.ShapeDtypeStruct((rows, 3 * FF), LOW),
        ),
        in_specs=[anywhere] * 6,
        out_specs=(anywhere,) * 4,
        scratch_shapes=[
            vmem((2, chips, rows, width), LOW),
            vmem((lines, chips, rows, width), LOW),
            vmem((lines, 3 if plane == 8 else chips, rows, width), LOW),
            vmem((lines, rows, width), LOW),
            vmem((rows, a_width + m_width), FULL),
            vmem((8, rows), FULL),
            dma((lines, 4)),
            dma((lines, 4)),
            dma((lines, 4)),
            dma((lines, max(6, chips))),
            dma((lines, max(6, chips))),
            dma((lines,)),
            dma((lines,)),
            dma((plane, 2)),
            dma((plane, 2)),
            dma((3,)),
            dma((3,)),
        ],
        compiler_params=pltpu.CompilerParams(
            collective_id=1, has_side_effects=True, vmem_limit_bytes=VMEM_LIMIT
        ),
        name="finish",
    )(
        *(term.reshape(lines, chips, 2, rows, term.shape[1]) for term in terms),
        gate_part.reshape(plane, rows, -1),
        down_swapped,
    )


def body(
    hidden,
    cotangent,
    segment_ids,
    continuation_prompt,
    gain_master,
    gain_first,
    gain_second,
    attention_master,
    attention_first,
    attention_second,
    merge_master,
    merge_first,
    merge_second,
    feedforward_master,
    feedforward_first,
    feedforward_second,
):
    group_index = lax.axis_index("grp")
    dp_size = lax.axis_size("dp")
    row_count = hidden.shape[2]
    prompt_rows = row_count - CONT
    qkv_width = (HQ + 2 * HK) * HD
    own_rows = feedforward_master.shape[0]
    own_hidden = FF // dp_size
    own_inputs = hidden.reshape(row_count, D)

    gain_columns = jnp.pad(gain_master.T, ((0, 0), (0, GAIN_PAD - 2)))
    weight_low = jnp.concatenate(
        [attention_master.astype(LOW), merge_master.astype(LOW), gain_columns.astype(LOW)], axis=1
    )
    weights, group_rows, gate_rows, first_rows, second_rows = gather_start(
        weight_low, own_inputs, feedforward_master.astype(LOW)
    )
    weights, late_cotangent = lax.optimization_barrier((weights, cotangent))
    weights = weights.reshape(D, -1)
    merge_weight = weights[:, qkv_width : qkv_width + D]
    gain_float = weights[:, qkv_width + D : qkv_width + D + 2].astype(FULL).T
    gate_weight = lax.all_gather(
        gate_rows.reshape(dp_size * own_rows, 2 * own_hidden), "grp", axis=0, tiled=True
    )
    gate_weight, second_rows = lax.optimization_barrier((gate_weight, second_rows))
    first_down = first_rows.reshape(D, own_hidden // 2)
    second_down = lax.all_gather(
        second_rows.reshape(dp_size * own_rows, own_hidden // 2), "grp", axis=0, tiled=True
    )
    down_grad = plane_gather(late_cotangent.reshape(row_count, D))

    segment_row = segment_ids[0]
    source_row = continuation_prompt[0]
    prompt_positions, follow_positions = segment_positions(segment_row, source_row)
    cosine, sine_part = angle_table(jnp.concatenate([prompt_positions, follow_positions[0]]))

    place = jnp.reshape(group_index, (1,)).astype(jnp.int32)
    group_rows = group_rows.reshape(PROMPT_LEN, D)
    queries, pairs, key_normed, normed, key_scale = project_heads(
        place, group_rows, own_inputs, gain_float[:1], cosine, sine_part, weights
    )
    inputs = own_inputs.astype(FULL)
    first_scale = norm_scale(inputs)

    row_index = jnp.arange(row_count, dtype=jnp.int32)
    is_prompt = row_index < prompt_rows
    global_row = group_index * prompt_rows + jnp.minimum(row_index, prompt_rows - 1)
    own_segment = lax.dynamic_slice_in_dim(segment_row, group_index * prompt_rows, prompt_rows)
    query_segment = jnp.concatenate([own_segment, jnp.broadcast_to(source_row, (CONT,))])
    key_index = jnp.arange(PROMPT_LEN, dtype=jnp.int32)
    prompt_seen = (segment_row[None, :] == query_segment[:, None]) & (
        (key_index[None, :] <= global_row[:, None]) | ~is_prompt[:, None]
    )
    follow_seen = (~is_prompt)[:, None] & (
        jnp.arange(CONT, dtype=jnp.int32)[None, :] <= (row_index - prompt_rows)[:, None]
    )
    visible = jnp.concatenate([prompt_seen, follow_seen], axis=1)
    seen = visible.astype(FULL)
    attended, row_logsum = attend(queries, pairs, seen)
    middle = inputs + contract(attended, merge_weight, 1, 1)
    second_scale = norm_scale(middle)
    normed_two = (middle * second_scale * gain_float[1]).astype(LOW)
    grad_rows = cotangent.reshape(row_count, D).astype(FULL)

    normed_two, down_grad = lax.optimization_barrier((normed_two, down_grad))
    normed_all = plane_gather(normed_two)
    gate_up = jnp.dot(normed_all, gate_weight, preferred_element_type=FULL)
    gate_values = gate_up[:, :own_hidden]
    up_values = gate_up[:, own_hidden:]
    gate_sigmoid, gate_silu, activated = gate_parts(gate_values, up_values)
    down_term = contract(down_grad, activated, 0, 0).astype(LOW)
    down_term, second_down = lax.optimization_barrier((down_term, second_down))
    out_term, gate_up_grad = forward_back(
        row_count, activated, down_grad, gate_up, first_down, second_down
    )
    down_part = line_scatter(down_term)
    gate_term = contract(normed_all, gate_up_grad, 0, 0).astype(LOW)
    gate_up_grad, gate_term, down_part = lax.optimization_barrier(
        (gate_up_grad, gate_term, down_part)
    )
    gate_part = line_scatter(gate_term)
    normed_two_grad, down_swapped = plane_back(
        row_count, gate_up_grad, gate_weight, down_part.reshape(dp_size, own_rows, own_hidden)
    )
    normed_two_grad, out_term = lax.optimization_barrier((normed_two_grad, out_term))
    out_chunks = out_term.reshape(dp_size, row_count, D)
    out_swapped = [plane_swap(out_chunks[offset + 1], 1) for offset in range(0, dp_size, 2)]
    middle_grad = grad_rows + norm_back(middle, second_scale, gain_float[1], normed_two_grad)
    gain_two_part = jnp.sum(normed_two_grad * middle * second_scale, axis=0)
    branch_grad = middle_grad.astype(LOW)
    attended_grad = contract(branch_grad, merge_weight, 1, 0).astype(LOW)
    attended_grad, out_swapped = lax.optimization_barrier((attended_grad, out_swapped))
    out_sums = [
        out_chunks[2 * at].astype(FULL) + one.astype(FULL) for at, one in enumerate(out_swapped)
    ]
    out_low = [one.astype(LOW) for one in out_sums[1:]]
    attended_grad, out_low = lax.optimization_barrier((attended_grad, out_low))
    out_arrived = [plane_swap(one, 2 * at + 2) for at, one in enumerate(out_low)]
    query_project, pair_project = attend_back(
        place, queries, pairs, seen, row_logsum, attended_grad, cosine, sine_part
    )
    query_term, pair_term, merge_term, normed_grad, pair_back, gain_one_part = weights_back(
        place,
        query_project,
        pair_project,
        branch_grad,
        attended,
        key_normed,
        normed,
        group_rows,
        own_inputs,
        key_scale,
        weights,
    )
    gain_term = jnp.pad(
        jnp.stack([gain_one_part[0], gain_two_part], axis=1), ((0, 0), (0, GAIN_PAD - 2))
    )
    pair_back, gate_part, out_arrived = lax.optimization_barrier(
        (pair_back, gate_part, out_arrived)
    )
    result = middle + out_sums[0]
    for one in out_arrived:
        result = result + one.astype(FULL)
    block_output, query_term = lax.optimization_barrier((result.astype(LOW), query_term))
    block_output = block_output.reshape(hidden.shape)
    pair_sum = line_scatter(pair_back)
    attention_grad, merge_grad, gain_sums, forward_low = finish(
        (query_term, pair_term, merge_term, gain_term.astype(LOW)),
        gate_part,
        down_swapped,
    )
    gain_grad = gain_sums[:2]
    pair_sum, gain_grad = lax.optimization_barrier((pair_sum, gain_grad))
    pair_sum = pair_sum.astype(FULL)
    normed_grad = normed_grad + jnp.pad(pair_sum, ((0, CONT), (0, 0)))
    input_grad = (middle_grad + norm_back(inputs, first_scale, gain_float[0], normed_grad)).reshape(
        hidden.shape
    )
    feedforward_grad = forward_low.astype(FULL)
    gain_new = adam_step(gain_master, gain_first, gain_second, gain_grad, 0.0)
    attention_new = adam_step(
        attention_master, attention_first, attention_second, attention_grad, WEIGHT_DECAY
    )
    merge_new = adam_step(merge_master, merge_first, merge_second, merge_grad, WEIGHT_DECAY)
    feedforward_new = adam_step(
        feedforward_master, feedforward_first, feedforward_second, feedforward_grad, WEIGHT_DECAY
    )
    return (
        block_output,
        input_grad,
        gain_grad,
        *gain_new,
        attention_grad,
        *attention_new,
        merge_grad,
        *merge_new,
        feedforward_grad,
        *feedforward_new,
    )


def solution(mesh):
    tokens = P("dp", "grp", None, None)
    gains = P(None, ("grp", "dp"))
    matrix = P(("grp", "dp"), None)
    return jax.shard_map(
        body,
        mesh=mesh,
        in_specs=(tokens, tokens, P("dp", None), P("dp", "grp")) + (gains,) * 3 + (matrix,) * 9,
        out_specs=(tokens, tokens) + (gains,) * 4 + (matrix,) * 12,
        check_vma=False,
    )
```

```python
import functools

import jax
import jax.numpy as jnp
from jax import lax
from jax.experimental import pallas as pl
from jax.experimental.pallas import tpu as pltpu
from jax.sharding import PartitionSpec as P

D = 2048
FF = 8192
HQ = 8
HK = 4
HD = 256
PROMPT_LEN = 1024
PROMPTS = 4
CONT = 64
STEP = 10
GAIN_PAD = 128

EPS_NORM = 1e-06
ROPE_THETA = 1000042.0
MASK_FILL = -1e30
BETA_ONE = 0.9
BETA_TWO = 0.95
ADAM_EPS = 1e-08
LEARN_RATE = 0.02
WEIGHT_DECAY = 0.1
LOW = jnp.bfloat16
FULL = jnp.float32
MESH = pl.DeviceIdType.MESH


def contract(left, right, left_axis, right_axis):
    return lax.dot_general(
        left, right, (((left_axis,), (right_axis,)), ((), ())), preferred_element_type=FULL
    )


def angle_table(positions):
    inverse_rate = ROPE_THETA ** (-(jnp.arange(HD // 2, dtype=FULL) * 2.0) / HD)
    angles = positions.astype(FULL)[..., None] * inverse_rate
    return (jnp.cos(angles), jnp.sin(angles))


def segment_positions(segment_row, source_row):
    labels = jnp.arange(PROMPTS, dtype=jnp.int32)
    member = (segment_row[None, :] == labels[:, None]).astype(jnp.int32)
    lengths = jnp.sum(member, axis=1, dtype=jnp.int32)
    starts = jnp.sum(
        jnp.where(labels[None, :] < labels[:, None], lengths[None, :], 0), axis=1, dtype=jnp.int32
    )
    prompt_index = jnp.arange(segment_row.shape[0], dtype=jnp.int32)
    prompt_positions = prompt_index - jnp.sum(member * starts[:, None], axis=0, dtype=jnp.int32)
    source_length = jnp.sum(
        (source_row[:, None] == labels[None, :]).astype(jnp.int32) * lengths[None, :],
        axis=1,
        dtype=jnp.int32,
    )
    follow_positions = source_length[:, None] + jnp.arange(CONT, dtype=jnp.int32)[None, :]
    return (prompt_positions, follow_positions)


def norm_scale(values):
    return lax.rsqrt(jnp.mean(values * values, axis=-1, keepdims=True) + EPS_NORM)


def norm_back(values, row_scale, gain_row, normed_grad):
    scaled = normed_grad * gain_row
    return row_scale * scaled - values * row_scale**3 * jnp.mean(
        scaled * values, axis=-1, keepdims=True
    )


def adam_step(master, first_moment, second_moment, gradient, decay_rate):
    first_new = BETA_ONE * first_moment + (1.0 - BETA_ONE) * gradient
    second_new = BETA_TWO * second_moment + (1.0 - BETA_TWO) * gradient * gradient
    correct_one = 1.0 - BETA_ONE**STEP
    correct_two = 1.0 - BETA_TWO**STEP
    update = first_new / correct_one / (jnp.sqrt(second_new / correct_two) + ADAM_EPS)
    return (-LEARN_RATE * (update + decay_rate * master), first_new, second_new)


def gate_parts(gate_values, up_values):
    gate_sigmoid = jax.nn.sigmoid(gate_values)
    gate_silu = gate_values * gate_sigmoid
    return (gate_sigmoid, gate_silu, (gate_silu * up_values).astype(LOW))


def gate_backward(activated_grad, gate_values, up_values, gate_sigmoid, gate_silu):
    gate_grad = (
        activated_grad * up_values * gate_sigmoid * (1.0 + gate_values * (1.0 - gate_sigmoid))
    ).astype(LOW)
    up_grad = (activated_grad * gate_silu).astype(LOW)
    return (gate_grad, up_grad)


def flip(index, bits):
    bit = 1
    while bit <= bits:
        if bits & bit:
            index = index + bit - 2 * bit * lax.rem(index // bit, 2)
        bit *= 2
    return index


def remote(source, target, send, recv, there):
    return pltpu.make_async_remote_copy(
        src_ref=source,
        dst_ref=target,
        send_sem=send,
        recv_sem=recv,
        device_id=there,
        device_id_type=MESH,
    )


def gather_kernel(
    lines,
    plane,
    prompt_rows,
    weight_ref,
    hidden_ref,
    forward_ref,
    weights_ref,
    rows_ref,
    gate_ref,
    first_ref,
    second_ref,
    local_sem,
    line_send,
    line_recv,
    rows_send,
    rows_recv,
    first_send,
    first_recv,
    near_send,
    near_recv,
    half_send,
    half_recv,
    core_send,
    core_recv,
    swap_send,
    swap_recv,
):
    g = lax.axis_index("grp")
    d = lax.axis_index("dp")
    evens = range(0, plane, 2)
    forward_halves = plane == 8
    near = (2, 4) if forward_halves else tuple(evens[1:])
    width = weight_ref.shape[1]
    cut = (width // 256) * 128

    barrier = pltpu.get_barrier_semaphore()
    for offset in range(1, plane):
        pl.semaphore_signal(barrier, inc=1, device_id=(g, flip(d, offset)), device_id_type=MESH)

    for step in range(1, lines):
        there = lax.rem(g + step, lines)
        pl.semaphore_signal(barrier, inc=1, device_id=(there, d), device_id_type=MESH)
    pl.semaphore_wait(barrier, plane + lines - 2)

    copy = remote
    own_rows = hidden_ref.at[pl.ds(0, prompt_rows)]

    def line_weight(way, step):
        block = g - step + 1 if way == 0 else g + step - 1
        source = weight_ref if step == 1 else weights_ref.at[block, d]
        return copy(
            source,
            weights_ref.at[block, d],
            line_send.at[way, step],
            line_recv.at[way, step],
            (g + 1 if way == 0 else g - 1, d),
        )

    def line_rows(way, step):
        block = g - step + 1 if way == 0 else g + step - 1
        source = own_rows if step == 1 else rows_ref.at[block]
        return copy(
            source,
            rows_ref.at[block],
            rows_send.at[way, step],
            rows_recv.at[way, step],
            (g + 1 if way == 0 else g - 1, d),
        )

    def line_first(way, step):
        block = g - step + 1 if way == 0 else g + step - 1
        return copy(
            first_ref.at[block],
            first_ref.at[block],
            first_send.at[way, step],
            first_recv.at[way, step],
            (g + 1 if way == 0 else g - 1, d),
        )

    def sends(way, step):
        if way == 0:
            return (g < lines - 1) & (g >= step - 1)
        return (g > 0) & (g + step - 1 < lines)

    def receives(way, step):
        return g >= step if way == 0 else g + step < lines

    def near_copy(block, offset, own):
        source = weight_ref if own else weights_ref.at[block, d]
        at = near.index(offset)
        return copy(
            source,
            weights_ref.at[block, d],
            near_send.at[block, at],
            near_recv.at[block, at],
            (g, flip(d, offset)),
        )

    def half_copy(block, part):
        columns = pl.ds(0, cut) if part == 0 else pl.ds(cut, width - cut)
        origin = flip(d, 2) if part == 0 else flip(d, 4)
        there = flip(d, 4) if part == 0 else flip(d, 2)
        piece = weights_ref.at[block, origin, :, columns]
        return copy(
            piece, piece, half_send.at[block, part], half_recv.at[block, part], (g, there)
        )

    def core_copy(block, offset, own=False):
        source = weight_ref if own else weights_ref.at[block, flip(d, offset)]
        return copy(
            source,
            weights_ref.at[block, flip(d, offset)],
            core_send.at[block, offset // 2],
            core_recv.at[block, offset // 2],
            (g, flip(d, 1)),
        )

    half_hidden = second_ref.shape[2]
    own_hidden = 2 * half_hidden

    def swap_piece(owner, part, source_index):
        if part < 2:
            source = forward_ref.at[:, pl.ds(part * FF + owner * own_hidden, own_hidden)]
            return source, gate_ref.at[source_index, :, pl.ds(part * own_hidden, own_hidden)]
        start = 2 * FF + owner * own_hidden + (part - 2) * half_hidden
        source = forward_ref.at[:, pl.ds(start, half_hidden)]
        return source, first_ref.at[g, source_index] if part == 2 else second_ref.at[source_index]

    def swap_copy(offset, part):
        source, target = swap_piece(flip(d, offset), part, d)
        return copy(
            source,
            target,
            swap_send.at[offset, part],
            swap_recv.at[offset, part],
            (g, flip(d, offset)),
        )

    locals_ = (
        pltpu.make_async_copy(weight_ref, weights_ref.at[g, d], local_sem.at[0]),
        pltpu.make_async_copy(own_rows, rows_ref.at[g], local_sem.at[1]),
        *(
            pltpu.make_async_copy(*swap_piece(d, part, d), local_sem.at[2 + part])
            for part in range(4)
        ),
    )

    def launch(block, own):
        for offset in near:
            near_copy(block, offset, own).start()
        core_copy(block, 0, own).start()

    def relay(block):
        for offset in near:
            near_copy(block, offset, False).wait_recv()
            core_copy(block, offset).start()
        if forward_halves:
            half_copy(block, 0).start()
            half_copy(block, 1).start()

    def finish(block):
        if forward_halves:
            half_copy(block, 0).wait_recv()
            half_copy(block, 1).wait_recv()
            core_copy(block, 6).start()

    def both(step, act):
        for way in (0, 1):
            pl.when(receives(way, step))(
                lambda way=way: act(g - step if way == 0 else g + step)
            )

    def take_rows(step):
        for way in (0, 1):

            @pl.when(receives(way, step))
            def _(way=way):
                line_rows(way, step).wait_recv()

            if step + 1 < lines:
                pl.when(sends(way, step + 1))(
                    lambda way=way: line_rows(way, step + 1).start()
                )

    for way in (0, 1):
        pl.when(sends(way, 1))(lambda way=way: line_weight(way, 1).start())
    launch(g, True)
    for one in locals_:
        one.start()
    for step in range(1, lines):
        for way in (0, 1):

            @pl.when(receives(way, step))
            def _(way=way, step=step):
                line_weight(way, step).wait_recv()

            if step + 1 < lines:
                pl.when(sends(way, step + 1))(
                    lambda way=way, step=step: line_weight(way, step + 1).start()
                )

        both(step, lambda block: launch(block, False))
        if step == 1:
            for way in (0, 1):
                pl.when(sends(way, 1))(lambda way=way: line_rows(way, 1).start())
        if step == 1:
            relay(g)
            for offset in range(1, plane):
                swap_copy(offset, 2).start()
    for step in range(1, lines):
        take_rows(step)
        if step == lines - 2:
            locals_[4].wait()
            for offset in range(1, plane):
                swap_copy(offset, 2).wait_recv()
            for way in (0, 1):
                pl.when(sends(way, 1))(lambda way=way: line_first(way, 1).start())
        both(step, relay)
        if step == 1:
            finish(g)
        elif step < lines - 1:
            both(step - 1, finish)
        if step == 1:
            for offset in range(1, plane):
                for part in (0, 1, 3):
                    swap_copy(offset, part).start()
    for step in range(1, lines):
        for way in (0, 1):

            @pl.when(receives(way, step))
            def _(way=way, step=step):
                line_first(way, step).wait_recv()

            if step + 1 < lines:
                pl.when(sends(way, step + 1))(
                    lambda way=way, step=step: line_first(way, step + 1).start()
                )
        if step == 1:
            both(lines - 2, finish)
    both(lines - 1, finish)

    def drain(block):
        for offset in evens:
            core_copy(block, offset).wait()
        for offset in near:
            near_copy(block, offset, False).wait_send()
        if forward_halves:
            half_copy(block, 0).wait_send()
            half_copy(block, 1).wait_send()

    drain(g)
    for step in range(1, lines):
        for way in (0, 1):
            pl.when(receives(way, step))(
                lambda way=way, step=step: drain(g - step if way == 0 else g + step)
            )

            @pl.when(sends(way, step))
            def _(way=way, step=step):
                line_weight(way, step).wait_send()
                line_rows(way, step).wait_send()
                line_first(way, step).wait_send()

    for offset in range(1, plane):
        for part in (0, 1, 3):
            swap_copy(offset, part).wait()
        swap_copy(offset, 2).wait_send()
    for at, one in enumerate(locals_):
        if at != 4:
            one.wait()


def gather_start(weight, hidden, forward):
    lines, plane = lax.axis_size("grp"), lax.axis_size("dp")
    prompt_rows = PROMPT_LEN // lines
    own_rows, width = weight.shape
    anywhere = pl.BlockSpec(memory_space=pl.ANY)
    dma = pltpu.SemaphoreType.DMA
    near_count = 2 if plane == 8 else plane // 2 - 1
    pairs = (
        (2, lines),
        (2, lines),
        (2, lines),
        (2, lines),
        (2, lines),
        (2, lines),
        (lines, near_count),
        (lines, near_count),
        (lines, 2),
        (lines, 2),
        (lines, plane // 2),
        (lines, plane // 2),
        (plane, 4),
        (plane, 4),
    )
    own_hidden = FF // plane
    return pl.pallas_call(
        functools.partial(gather_kernel, lines, plane, prompt_rows),
        out_shape=(
            jax.ShapeDtypeStruct((lines, plane, own_rows, width), weight.dtype),
            jax.ShapeDtypeStruct((lines, prompt_rows, D), hidden.dtype),
            jax.ShapeDtypeStruct((plane, own_rows, 2 * own_hidden), forward.dtype),
            jax.ShapeDtypeStruct((lines, plane, own_rows, own_hidden // 2), forward.dtype),
            jax.ShapeDtypeStruct((plane, own_rows, own_hidden // 2), forward.dtype),
        ),
        in_specs=[anywhere] * 3,
        out_specs=(anywhere,) * 5,
        scratch_shapes=[dma((6,))] + [dma(shape) for shape in pairs],
        compiler_params=pltpu.CompilerParams(collective_id=0, has_side_effects=True),
        name="gather_start",
    )(weight, hidden, forward)


def project_kernel(
    place_ref,
    group_ref,
    own_ref,
    gain_ref,
    cosine_ref,
    sine_ref,
    weight_ref,
    query_ref,
    pair_ref,
    normed_ref,
    own_normed_ref,
    scale_ref,
):
    step = pl.program_id(0)
    own_rows = own_ref.shape[0]
    prompt_rows = own_rows - CONT
    start = pl.multiple_of(place_ref[0] * prompt_rows, 16)
    tile = 32

    def norm_tile(values, at):
        values = values.astype(FULL)
        scale = lax.rsqrt(jnp.mean(values * values, axis=-1, keepdims=True) + EPS_NORM)
        normed_ref[pl.ds(at, tile)] = (values * scale * gain_ref[...]).astype(LOW)
        scale_ref[pl.ds(at, tile)] = jnp.broadcast_to(scale, (tile, 128))

    @pl.when(step == 0)
    def _():
        @pl.loop(0, PROMPT_LEN // tile)
        def _(at):
            first = pl.multiple_of(at * tile, tile)
            norm_tile(group_ref[pl.ds(first, tile)], first)

        for at in range(0, CONT, tile):
            norm_tile(own_ref[prompt_rows + at : prompt_rows + at + tile], PROMPT_LEN + at)
        own_normed_ref[:prompt_rows] = normed_ref[pl.ds(start, prompt_rows)]
        own_normed_ref[prompt_rows:] = normed_ref[PROMPT_LEN:]

    def turn(values, cosine, sine_part):
        front, back = values[:, : HD // 2], values[:, HD // 2 :]
        return front * cosine - back * sine_part, back * cosine + front * sine_part

    def project(rows):
        return jnp.dot(rows, weight_ref[...], preferred_element_type=FULL)

    @pl.when(step < HQ)
    def _():
        for first, count, table in ((0, prompt_rows, start), (prompt_rows, CONT, PROMPT_LEN)):
            values = project(own_normed_ref[first : first + count])
            front, back = turn(
                values, cosine_ref[pl.ds(table, count)], sine_ref[pl.ds(table, count)]
            )
            query_ref[first : first + count, : HD // 2] = front.astype(LOW)
            query_ref[first : first + count, HD // 2 :] = back.astype(LOW)

    key_count = PROMPT_LEN + CONT
    part = key_count // 4

    @pl.when((step >= HQ) & (step < HQ + HK))
    def _():
        @pl.loop(0, 4)
        def _(at):
            rows = pl.ds(pl.multiple_of(at * part, 16), part)
            front, back = turn(project(normed_ref[rows]), cosine_ref[rows], sine_ref[rows])
            pair_ref[rows, : HD // 2] = front.astype(LOW)
            pair_ref[rows, HD // 2 :] = back.astype(LOW)

    @pl.when(step >= HQ + HK)
    def _():
        @pl.loop(0, 4)
        def _(at):
            rows = pl.ds(pl.multiple_of(at * part, 16), part)
            pair_ref[rows] = project(normed_ref[rows]).astype(LOW)


VMEM_LIMIT = 60 * 2**20


def project_heads(place, group_rows, own_inputs, gain_row, cosine, sine_part, weights):
    own_rows = own_inputs.shape[0]
    key_count = PROMPT_LEN + CONT
    whole = lambda shape: pl.BlockSpec(shape, lambda j, p: (0, 0))
    return pl.pallas_call(
        project_kernel,
        grid_spec=pltpu.PrefetchScalarGridSpec(
            num_scalar_prefetch=1,
            grid=(HQ + 2 * HK,),
            in_specs=[
                whole((PROMPT_LEN, D)),
                whole((own_rows, D)),
                whole((1, D)),
                whole((key_count, HD // 2)),
                whole((key_count, HD // 2)),
                pl.BlockSpec((D, HD), lambda j, p: (0, j)),
            ],
            out_specs=[
                pl.BlockSpec((own_rows, HD), lambda j, p: (0, jnp.minimum(j, HQ - 1))),
                pl.BlockSpec((key_count, HD), lambda j, p: (0, jnp.maximum(j - HQ, 0))),
                whole((key_count, D)),
                whole((own_rows, D)),
                whole((key_count, 128)),
            ],
        ),
        out_shape=[
            jax.ShapeDtypeStruct((own_rows, HQ * HD), LOW),
            jax.ShapeDtypeStruct((key_count, 2 * HK * HD), LOW),
            jax.ShapeDtypeStruct((key_count, D), LOW),
            jax.ShapeDtypeStruct((own_rows, D), LOW),
            jax.ShapeDtypeStruct((key_count, 128), FULL),
        ],
        compiler_params=pltpu.CompilerParams(vmem_limit_bytes=VMEM_LIMIT),
        name="project_heads",
    )(place, group_rows, own_inputs, gain_row, cosine, sine_part, weights)


def across(left, right):
    return lax.dot_general(left, right, (((1,), (1,)), ((), ())), preferred_element_type=FULL)


def along(left, right):
    return lax.dot_general(left, right, (((0,), (0,)), ((), ())), preferred_element_type=FULL)


def attend_kernel(query_ref, key_ref, value_ref, seen_ref, attended_ref, logsum_ref):
    group_heads = HQ // HK
    for head in range(group_heads):
        columns = slice(head * HD, (head + 1) * HD)
        scores = across(query_ref[:, columns], key_ref[...]) * HD ** (-0.5)
        scores = jnp.where(seen_ref[...] > 0, scores, MASK_FILL)
        peak = jnp.max(scores, axis=-1, keepdims=True)
        unnormed = jnp.exp(scores - peak)
        total = jnp.sum(unnormed, axis=-1, keepdims=True)
        low = (unnormed / total).astype(LOW)
        attended_ref[:, columns] = jnp.dot(
            low, value_ref[...], preferred_element_type=FULL
        ).astype(LOW)
        logsum_ref[:, head * 128 : (head + 1) * 128] = jnp.broadcast_to(
            peak + jnp.log(total), (query_ref.shape[0], 128)
        )


def attend(queries, pairs, seen):
    rows, key_count = seen.shape
    group_heads = HQ // HK
    return pl.pallas_call(
        attend_kernel,
        grid=(HK,),
        in_specs=[
            pl.BlockSpec((rows, group_heads * HD), lambda j: (0, j)),
            pl.BlockSpec((key_count, HD), lambda j: (0, j)),
            pl.BlockSpec((key_count, HD), lambda j: (0, HK + j)),
            pl.BlockSpec((rows, key_count), lambda j: (0, 0)),
        ],
        out_specs=[
            pl.BlockSpec((rows, group_heads * HD), lambda j: (0, j)),
            pl.BlockSpec((rows, group_heads * 128), lambda j: (0, j)),
        ],
        out_shape=[
            jax.ShapeDtypeStruct((rows, HQ * HD), LOW),
            jax.ShapeDtypeStruct((rows, HQ * 128), FULL),
        ],
        compiler_params=pltpu.CompilerParams(vmem_limit_bytes=VMEM_LIMIT),
        name="attend",
    )(queries, pairs, pairs, seen)


def attend_back_kernel(
    place_ref,
    query_ref,
    key_ref,
    value_ref,
    seen_ref,
    logsum_ref,
    grad_ref,
    cosine_ref,
    sine_ref,
    query_out,
    pair_out,
):
    step = pl.program_id(0)
    group_heads = HQ // HK
    rows = query_ref.shape[0]
    prompt_rows = rows - CONT
    start = pl.multiple_of(place_ref[0] * prompt_rows, 16)
    score_scale = HD ** (-0.5)
    key_grad = value_grad = 0.0

    def turn_back(values, cosine, sine_part):
        front, back = values[:, : HD // 2], values[:, HD // 2 :]
        return jnp.concatenate(
            [front * cosine + back * sine_part, back * cosine - front * sine_part], axis=1
        ).astype(LOW)

    for head in range(group_heads):
        columns = slice(head * HD, (head + 1) * HD)
        scores = across(query_ref[:, columns], key_ref[...]) * score_scale
        scores = jnp.where(seen_ref[...] > 0, scores, MASK_FILL)
        probabilities = jnp.exp(scores - logsum_ref[:, head * 128 : head * 128 + 1])
        grads = grad_ref[:, columns]
        probability_grad = across(grads, value_ref[...])
        delta = jnp.sum(probabilities * probability_grad, axis=-1, keepdims=True)
        score_grad = (probabilities * (probability_grad - delta)).astype(LOW)
        query_grad = jnp.dot(score_grad, key_ref[...], preferred_element_type=FULL) * score_scale
        key_grad = key_grad + along(score_grad, query_ref[:, columns])
        value_grad = value_grad + along(probabilities.astype(LOW), grads)
        query_out[:prompt_rows, columns] = turn_back(
            query_grad[:prompt_rows],
            cosine_ref[pl.ds(start, prompt_rows)],
            sine_ref[pl.ds(start, prompt_rows)],
        )
        query_out[prompt_rows:, columns] = turn_back(
            query_grad[prompt_rows:], cosine_ref[PROMPT_LEN:], sine_ref[PROMPT_LEN:]
        )
    pair_out[:, pl.ds(pl.multiple_of(step * HD, HD), HD)] = turn_back(
        key_grad * score_scale, cosine_ref[...], sine_ref[...]
    )
    pair_out[:, pl.ds(pl.multiple_of((HK + step) * HD, HD), HD)] = value_grad.astype(LOW)


def attend_back(place, queries, pairs, seen, logsum, grads, cosine, sine_part):
    rows, key_count = seen.shape
    group_heads = HQ // HK
    whole = lambda shape: pl.BlockSpec(shape, lambda j, p: (0, 0))
    return pl.pallas_call(
        attend_back_kernel,
        grid_spec=pltpu.PrefetchScalarGridSpec(
            num_scalar_prefetch=1,
            grid=(HK,),
            in_specs=[
                pl.BlockSpec((rows, group_heads * HD), lambda j, p: (0, j)),
                pl.BlockSpec((key_count, HD), lambda j, p: (0, j)),
                pl.BlockSpec((key_count, HD), lambda j, p: (0, HK + j)),
                whole((rows, key_count)),
                pl.BlockSpec((rows, group_heads * 128), lambda j, p: (0, j)),
                pl.BlockSpec((rows, group_heads * HD), lambda j, p: (0, j)),
                whole((key_count, HD // 2)),
                whole((key_count, HD // 2)),
            ],
            out_specs=[
                pl.BlockSpec((rows, group_heads * HD), lambda j, p: (0, j)),
                whole((key_count, 2 * HK * HD)),
            ],
        ),
        out_shape=[
            jax.ShapeDtypeStruct((rows, HQ * HD), LOW),
            jax.ShapeDtypeStruct((key_count, 2 * HK * HD), LOW),
        ],
        compiler_params=pltpu.CompilerParams(vmem_limit_bytes=VMEM_LIMIT),
        name="attend_back",
    )(place, queries, pairs, pairs, seen, logsum, grads, cosine, sine_part)


def weights_back_kernel(
    place_ref,
    query_ref,
    pair_ref,
    branch_ref,
    attended_ref,
    normed_ref,
    own_normed_ref,
    group_ref,
    own_ref,
    scale_ref,
    query_weight_ref,
    pair_weight_ref,
    query_term,
    pair_term,
    merge_term,
    back_out,
    pair_back_out,
    gain_out,
):
    rows = query_ref.shape[0]
    prompt_rows = rows - CONT
    start = pl.multiple_of(place_ref[0] * prompt_rows, 16)
    query_term[...] = along(own_normed_ref[...], query_ref[...]).astype(LOW)
    pair_term[...] = along(normed_ref[...], pair_ref[...]).astype(LOW)
    merge_term[...] = along(branch_ref[...], attended_ref[...]).astype(LOW)
    query_back = across(query_ref[...], query_weight_ref[...])
    pair_back = across(pair_ref[...], pair_weight_ref[...])
    own_values = own_ref[prompt_rows:].astype(FULL) * scale_ref[PROMPT_LEN:, :1]
    tail = query_back[prompt_rows:] + pair_back[PROMPT_LEN:]
    group_values = group_ref[...].astype(FULL) * scale_ref[:PROMPT_LEN, :1]
    own_prompt = own_ref[:prompt_rows].astype(FULL) * scale_ref[pl.ds(start, prompt_rows), :1]
    gain_out[...] = (
        jnp.sum(pair_back[:PROMPT_LEN] * group_values, axis=0, keepdims=True)
        + jnp.sum(query_back[:prompt_rows] * own_prompt, axis=0, keepdims=True)
        + jnp.sum(tail * own_values, axis=0, keepdims=True)
    )
    back_out[:prompt_rows] = query_back[:prompt_rows]
    back_out[prompt_rows:] = tail
    pair_back_out[...] = pair_back[:PROMPT_LEN].astype(LOW)


def weights_back(
    place, queries, pairs, branch, attended, normed, own_normed, group_rows, own_inputs, scale, weights
):
    rows, key_count = queries.shape[0], pairs.shape[0]
    wide, tile = HQ * HD, 256
    whole = lambda shape: pl.BlockSpec(shape, lambda j, p: (0, 0))
    tall = lambda count: pl.BlockSpec((count, tile), lambda j, p: (0, j))
    flat = lambda at: pl.BlockSpec((tile, wide), lambda j, p: (j, at))
    return pl.pallas_call(
        weights_back_kernel,
        grid_spec=pltpu.PrefetchScalarGridSpec(
            num_scalar_prefetch=1,
            grid=(D // tile,),
            in_specs=[
                whole((rows, wide)),
                whole((key_count, wide)),
                tall(rows),
                whole((rows, wide)),
                tall(key_count),
                tall(rows),
                tall(PROMPT_LEN),
                tall(rows),
                whole((key_count, 128)),
                flat(0),
                flat(1),
            ],
            out_specs=[flat(0), flat(0), flat(0), tall(rows), tall(PROMPT_LEN), tall(1)],
        ),
        out_shape=[
            jax.ShapeDtypeStruct((D, wide), LOW),
            jax.ShapeDtypeStruct((D, wide), LOW),
            jax.ShapeDtypeStruct((D, wide), LOW),
            jax.ShapeDtypeStruct((rows, D), FULL),
            jax.ShapeDtypeStruct((PROMPT_LEN, D), LOW),
            jax.ShapeDtypeStruct((1, D), FULL),
        ],
        compiler_params=pltpu.CompilerParams(vmem_limit_bytes=VMEM_LIMIT),
        name="weights_back",
    )(
        place,
        queries,
        pairs,
        branch,
        attended,
        normed,
        own_normed,
        group_rows,
        own_inputs,
        scale,
        weights,
        weights,
    )


def forward_back_kernel(
    activated_ref, grad_ref, gate_up_ref, first_ref, second_ref, out_ref, gate_up_grad_ref
):
    own_hidden = activated_ref.shape[1]
    part = first_ref.shape[0] // 4
    piece = own_hidden // 2

    @pl.loop(0, 4)
    def _(at):
        columns = pl.ds(pl.multiple_of(at * part, part), part)
        out_ref[:, columns] = (
            across(activated_ref[:, :piece], first_ref[columns])
            + across(activated_ref[:, piece:], second_ref[columns])
        ).astype(LOW)

    for at, down_ref in enumerate((first_ref, second_ref)):
        columns = slice(at * piece, (at + 1) * piece)
        upper = slice(own_hidden + at * piece, own_hidden + (at + 1) * piece)
        activated_grad = jnp.dot(grad_ref[...], down_ref[...], preferred_element_type=FULL)
        gate_values, up_values = gate_up_ref[:, columns], gate_up_ref[:, upper]
        gate_sigmoid = jax.nn.sigmoid(gate_values)
        gate_grad, up_grad = gate_backward(
            activated_grad, gate_values, up_values, gate_sigmoid, gate_values * gate_sigmoid
        )
        gate_up_grad_ref[:, columns] = gate_grad
        gate_up_grad_ref[:, upper] = up_grad


def forward_back(rows, activated, grads, gate_up, first_down, second_down):
    count, own_hidden = activated.shape
    block = lambda width: pl.BlockSpec((rows, width), lambda j: (j, 0))
    return pl.pallas_call(
        forward_back_kernel,
        grid=(count // rows,),
        in_specs=[
            block(own_hidden),
            block(D),
            block(2 * own_hidden),
            pl.BlockSpec(first_down.shape, lambda j: (0, 0)),
            pl.BlockSpec(second_down.shape, lambda j: (0, 0)),
        ],
        out_specs=[block(D), block(2 * own_hidden)],
        out_shape=[
            jax.ShapeDtypeStruct((count, D), LOW),
            jax.ShapeDtypeStruct((count, 2 * own_hidden), LOW),
        ],
        compiler_params=pltpu.CompilerParams(vmem_limit_bytes=VMEM_LIMIT),
        name="forward_back",
    )(activated, grads, gate_up, first_down, second_down)


def plane_back_kernel(
    plane,
    rows_ref,
    weight_ref,
    down_ref,
    out_ref,
    swapped_ref,
    weight,
    tiles,
    keep,
    give,
    core_in,
    plane_in,
    total,
    load_sem,
    tile_sem,
    core_send,
    core_recv,
    plane_send,
    plane_recv,
    out_sem,
    swap_send,
    swap_recv,
):
    g = lax.axis_index("grp")
    d = lax.axis_index("dp")
    chips = plane // 2
    own_hidden = down_ref.shape[2]
    halves = plane == 8
    order = (3, 1, 2, 0) if halves else tuple(range(chips - 1, -1, -1))
    cut = D // 2
    half_of = (pl.ds(0, cut), pl.ds(cut, D - cut))

    barrier = pltpu.get_barrier_semaphore()
    for offset in range(1, plane):
        pl.semaphore_signal(
            barrier, inc=1, device_id=(g, flip(d, offset)), device_id_type=MESH
        )

    load = pltpu.make_async_copy(weight_ref, weight, load_sem.at[0])
    load.start()

    def tile_copy(turn):
        at = order[turn]
        return pltpu.make_async_copy(
            rows_ref.at[pl.ds(2 * at, 2)], tiles.at[turn % 2], tile_sem.at[turn % 2]
        )

    def core_copy(at):
        return remote(
            give.at[at], core_in.at[at], core_send.at[at], core_recv.at[at], (g, flip(d, 1))
        )

    def plane_copy(at):
        return remote(
            keep.at[at],
            plane_in.at[at],
            plane_send.at[at],
            plane_recv.at[at],
            (g, flip(d, 2 * at)),
        )

    def near_copy(part, relayed):
        there = part + 1
        return remote(
            keep.at[3 if relayed else there, :, half_of[part]],
            plane_in.at[1 if relayed else 0, :, half_of[part]],
            plane_send.at[2 * relayed + part],
            plane_recv.at[2 * relayed + part],
            (g, flip(d, 2 * there)),
        )

    def relay_copy(part):
        there = 2 - part
        return remote(
            keep.at[there, :, half_of[part]],
            plane_in.at[2, :, half_of[part]],
            plane_send.at[4 + part],
            plane_recv.at[4 + part],
            (g, flip(d, 2 * there)),
        )

    def swap_copy(offset):
        there = flip(d, offset)
        return remote(
            down_ref.at[there],
            swapped_ref.at[:, pl.ds(d * own_hidden, own_hidden)],
            swap_send.at[offset],
            swap_recv.at[offset],
            (g, there),
        )

    own_swap = pltpu.make_async_copy(
        down_ref.at[d], swapped_ref.at[:, pl.ds(d * own_hidden, own_hidden)], out_sem.at[1]
    )
    tile_copy(0).start()
    tile_copy(1).start()
    pl.semaphore_wait(barrier, plane - 1)
    for offset in range(1, plane):
        swap_copy(offset).start()
    own_swap.start()
    load.wait()
    part_width = 512

    def product(turn, which, target):
        @pl.loop(0, D // part_width)
        def _(at):
            columns = pl.ds(pl.multiple_of(at * part_width, part_width), part_width)
            target[order[turn], :, columns] = across(
                tiles[turn % 2, which], weight[columns]
            ).astype(LOW)

    def add_into(at, other, first, count):
        step = 256

        @pl.loop(0, count // step)
        def _(k):
            here = pl.ds(pl.multiple_of(first + k * step, step), step)
            keep[at, :, here] = (
                keep[at, :, here].astype(FULL) + other(here).astype(FULL)
            ).astype(LOW)

    def settle(turn):
        at = order[turn]
        core_copy(at).wait_recv()
        add_into(at, lambda here: core_in[at, :, here], 0, D)
        if halves and at == 3:
            near_copy(0, True).start()
            near_copy(1, True).start()
        elif halves and at:
            near_copy(at - 1, False).start()
        elif at:
            plane_copy(at).start()

    for turn in range(chips):
        tile_copy(turn).wait()
        product(turn, 1, give)
        core_copy(order[turn]).start()
        if turn:
            settle(turn - 1)
        product(turn, 0, keep)
        if turn + 2 < chips:
            tile_copy(turn + 2).start()
        if halves and turn == chips - 1:
            for part in range(2):
                near_copy(part, True).wait_recv()
                add_into(
                    2 - part,
                    lambda here: plane_in[1, :, here],
                    part * cut,
                    cut,
                )
                relay_copy(part).start()
    settle(chips - 1)
    if halves:
        for part in range(2):
            near_copy(part, False).wait_recv()
            relay_copy(part).wait_recv()
        arrived = (0, 2)
    else:
        for at in range(1, chips):
            plane_copy(at).wait_recv()
        arrived = tuple(range(1, chips))

    @pl.loop(0, D // 256)
    def _(k):
        here = pl.ds(pl.multiple_of(k * 256, 256), 256)
        value = keep[0, :, here].astype(FULL)
        for at in arrived:
            value = value + plane_in[at, :, here].astype(FULL)
        total[:, here] = value

    out = pltpu.make_async_copy(total, out_ref, out_sem.at[0])
    out.start()
    for at in range(chips):
        core_copy(at).wait_send()
    if halves:
        for part in range(2):
            near_copy(part, False).wait_send()
            near_copy(part, True).wait_send()
            relay_copy(part).wait_send()
    else:
        for at in range(1, chips):
            plane_copy(at).wait_send()
    for offset in range(1, plane):
        swap_copy(offset).wait()
    own_swap.wait()
    out.wait()


def plane_back(rows, gate_up_grad, gate_weight, down_part):
    plane = lax.axis_size("dp")
    chips = plane // 2
    inner = gate_up_grad.shape[1]
    anywhere = pl.BlockSpec(memory_space=pl.ANY)
    dma = pltpu.SemaphoreType.DMA
    return pl.pallas_call(
        functools.partial(plane_back_kernel, plane),
        out_shape=(
            jax.ShapeDtypeStruct((rows, D), FULL),
            jax.ShapeDtypeStruct((down_part.shape[1], FF), LOW),
        ),
        in_specs=[anywhere] * 3,
        out_specs=(anywhere,) * 2,
        scratch_shapes=[
            pltpu.VMEM((D, inner), LOW),
            pltpu.VMEM((2, 2, rows, inner), LOW),
            pltpu.VMEM((chips, rows, D), LOW),
            pltpu.VMEM((chips, rows, D), LOW),
            pltpu.VMEM((chips, rows, D), LOW),
            pltpu.VMEM((3 if plane == 8 else chips, rows, D), LOW),
            pltpu.VMEM((rows, D), FULL),
            dma((1,)),
            dma((2,)),
            dma((chips,)),
            dma((chips,)),
            dma((max(6, chips),)),
            dma((max(6, chips),)),
            dma((2,)),
            dma((plane,)),
            dma((plane,)),
        ],
        compiler_params=pltpu.CompilerParams(
            collective_id=2, has_side_effects=True, vmem_limit_bytes=VMEM_LIMIT
        ),
        name="plane_back",
    )(gate_up_grad.reshape(plane, rows, inner), gate_weight, down_part)


def plane_swap(block, offset):
    size = lax.axis_size("dp")
    return lax.ppermute(block, "dp", [(i, i ^ offset) for i in range(size)])


def plane_gather(block):
    mine = [block] + [plane_swap(block, o) for o in range(2, lax.axis_size("dp"), 2)]
    pairs = [(one, plane_swap(one, 1)) for one in mine]
    return jnp.concatenate([one for pair in pairs for one in pair], axis=0)


def line_scatter(term):
    return lax.psum_scatter(term, "grp", scatter_dimension=0, tiled=True)


def finish_kernel(
    lines,
    plane,
    query_ref,
    pair_ref,
    merge_ref,
    gain_ref,
    gate_ref,
    down_ref,
    a_out,
    m_out,
    gain_out,
    f_out,
    mine,
    core_in,
    plane_in,
    line_in,
    owned,
    gain_made,
    mine_sem,
    core_send,
    core_recv,
    plane_send,
    plane_recv,
    line_send,
    line_recv,
    swap_send,
    swap_recv,
    own_sem,
    out_sem,
):
    g = lax.axis_index("grp")
    d = lax.axis_index("dp")
    chips = plane // 2
    chip, core = lax.div(d, 2), lax.rem(d, 2)
    partner = d + 1 - 2 * core
    own_hidden = gate_ref.shape[2] // 2
    width = core_in.shape[3]
    a_width, m_width = a_out.shape[1], m_out.shape[1]
    parts, begin = [], 0
    for ref in (query_ref, pair_ref, merge_ref, gain_ref):
        parts.append((ref, pl.ds(begin, ref.shape[4])))
        begin += ref.shape[4]

    barrier = pltpu.get_barrier_semaphore()
    for step in range(1, plane):
        there = lax.rem(d + step, plane)
        pl.semaphore_signal(barrier, inc=1, device_id=(g, there), device_id_type=MESH)
    for step in range(1, lines):
        there = lax.rem(g + step, lines)
        pl.semaphore_signal(barrier, inc=1, device_id=(there, d), device_id_type=MESH)
    pl.semaphore_wait(barrier, plane + lines - 2)

    def line_at(turn):
        return lax.rem(g + turn + 1, lines)

    def core_copy(turn, part):
        line = line_at(turn)
        ref, columns = parts[part]
        return remote(
            ref.at[line, :, 1 - core],
            core_in.at[line, :, :, columns],
            core_send.at[turn, part],
            core_recv.at[turn, part],
            (g, partner),
        )

    def mine_copy(turn, part):
        line = line_at(turn)
        ref, columns = parts[part]
        return pltpu.make_async_copy(
            ref.at[line, :, core], mine.at[turn % 2, :, :, columns], mine_sem.at[turn, part]
        )

    cut = width // 256 * 128
    columns_of = (pl.ds(0, cut), pl.ds(cut, width - cut))

    def plane_copy(turn, step):
        line = line_at(turn)
        there = lax.rem(chip + step, chips)
        return remote(
            core_in.at[line, there],
            plane_in.at[line, chip],
            plane_send.at[turn, step],
            plane_recv.at[turn, step],
            (g, 2 * there + core),
        )

    def near_copy(turn, part, relayed):
        line = line_at(turn)
        there = flip(chip, part + 1)
        owner = flip(chip, 3) if relayed else there
        return remote(
            core_in.at[line, owner, :, columns_of[part]],
            plane_in.at[line, 1 if relayed else 0, :, columns_of[part]],
            plane_send.at[turn, 2 * relayed + part],
            plane_recv.at[turn, 2 * relayed + part],
            (g, 2 * there + core),
        )

    def relay_copy(turn, part):
        line = line_at(turn)
        there = flip(chip, 2 - part)
        return remote(
            core_in.at[line, there, :, columns_of[part]],
            plane_in.at[line, 2, :, columns_of[part]],
            plane_send.at[turn, 4 + part],
            plane_recv.at[turn, 4 + part],
            (g, 2 * there + core),
        )

    def line_copy(turn):
        line = line_at(turn)
        return remote(
            core_in.at[line, chip],
            line_in.at[g],
            line_send.at[turn],
            line_recv.at[turn],
            (line, d),
        )

    def swap_source(owner, part):
        return gate_ref.at[owner, :, pl.ds(part * own_hidden, own_hidden)]

    def swap_place(part):
        return f_out.at[:, pl.ds(part * FF + d * own_hidden, own_hidden)]

    def swap_copy(step, part):
        there = lax.rem(d + step, plane)
        return remote(
            swap_source(there, part),
            swap_place(part),
            swap_send.at[step, part],
            swap_recv.at[step, part],
            (g, there),
        )

    own_swap = [
        pltpu.make_async_copy(swap_source(d, part), swap_place(part), own_sem.at[part])
        for part in range(2)
    ] + [pltpu.make_async_copy(down_ref, f_out.at[:, pl.ds(2 * FF, FF)], own_sem.at[2])]

    every = range(len(parts))
    for turn in range(lines):
        for part in every:
            core_copy(turn, part).start()
            if turn < 2:
                mine_copy(turn, part).start()
    tile = 896 if width % 896 == 0 else 128
    halves = plane == 8

    def add_into(line, there, other, columns=None):
        first, count = (0, width) if columns is None else columns
        step = tile if columns is None else 128

        @pl.loop(0, count // step)
        def _(at):
            here = pl.ds(pl.multiple_of(first + at * step, 128), step)
            total = core_in[line, there, :, here].astype(FULL) + other(here).astype(FULL)
            core_in[line, there, :, here] = total.astype(LOW)

    def near_start(turn):
        if halves:
            for relayed in (True, False):
                for part in range(2):
                    near_copy(turn, part, relayed).start()
        else:
            for step in range(1, chips):
                plane_copy(turn, step).start()

    for turn in range(lines):
        line = line_at(turn)
        for part in every:
            core_copy(turn, part).wait_recv()
            mine_copy(turn, part).wait()
        for step in range(1, chips + 1):
            there = lax.rem(chip + step, chips)
            add_into(
                line, there, lambda here, there=there, turn=turn: mine[turn % 2, there, :, here]
            )
        if turn + 2 < lines:
            for part in every:
                mine_copy(turn + 2, part).start()
        if turn < 2:
            near_start(turn)

    def pass_on(turn):
        line = line_at(turn)
        for part, columns in enumerate(((0, cut), (cut, width - cut))):
            near_copy(turn, part, True).wait_recv()
            add_into(
                line,
                flip(chip, 2 - part),
                lambda here, line=line: plane_in[line, 1, :, here],
                columns,
            )
            relay_copy(turn, part).start()

    def near_done(turn):
        if halves:
            pass_on(turn)
            for part in range(2):
                near_copy(turn, part, False).wait_recv()
        else:
            for step in range(1, chips):
                plane_copy(turn, step).wait_recv()
        if turn + 2 < lines:
            near_start(turn + 2)

    def line_done(turn):
        line = line_at(turn)
        if halves:
            for part in range(2):
                relay_copy(turn, part).wait_recv()
            arrived = (0, 2)
        else:
            arrived = tuple(lax.rem(chip + step, chips) for step in range(1, chips))

        @pl.loop(0, width // tile)
        def _(at):
            columns = pl.ds(pl.multiple_of(at * tile, tile), tile)
            total = core_in[line, chip, :, columns].astype(FULL)
            for block in arrived:
                total = total + plane_in[line, block, :, columns].astype(FULL)
            core_in[line, chip, :, columns] = total.astype(LOW)

        if turn < lines - 1:
            line_copy(turn).start()

    near_done(0)
    for turn in range(1, lines):
        near_done(turn)
        line_done(turn - 1)
        if turn == lines - 2:
            for step in range(1, plane):
                for part in range(2):
                    swap_copy(step, part).start()
            for one in own_swap:
                one.start()
    line_done(lines - 1)
    for turn in range(lines - 1):
        line_copy(turn).wait_recv()

    def total_of(columns):
        total = core_in[g, chip, :, columns].astype(FULL)
        for step in range(1, lines):
            total = total + line_in[lax.rem(g + step, lines), :, columns].astype(FULL)
        return total

    @pl.loop(0, (a_width + m_width) // 256)
    def _(at):
        columns = pl.ds(pl.multiple_of(at * 256, 256), 256)
        owned[:, columns] = total_of(columns)

    gain_made[...] = total_of(pl.ds(a_width + m_width, GAIN_PAD)).T[:8]
    outs = (
        pltpu.make_async_copy(owned.at[:, pl.ds(0, a_width)], a_out, out_sem.at[0]),
        pltpu.make_async_copy(owned.at[:, pl.ds(a_width, m_width)], m_out, out_sem.at[1]),
        pltpu.make_async_copy(gain_made, gain_out, out_sem.at[2]),
    )
    for one in outs:
        one.start()
    for turn in range(lines):
        for part in every:
            core_copy(turn, part).wait_send()
        if halves:
            for part in range(2):
                near_copy(turn, part, False).wait_send()
                near_copy(turn, part, True).wait_send()
                relay_copy(turn, part).wait_send()
        else:
            for step in range(1, chips):
                plane_copy(turn, step).wait_send()
        if turn < lines - 1:
            line_copy(turn).wait_send()
    for step in range(1, plane):
        for part in range(2):
            swap_copy(step, part).wait()
    for one in own_swap:
        one.wait()
    for one in outs:
        one.wait()


def finish(terms, gate_part, down_swapped):
    lines, plane = lax.axis_size("grp"), lax.axis_size("dp")
    chips = plane // 2
    rows = D // (lines * plane)
    m_width = terms[2].shape[1]
    a_width = terms[0].shape[1] + terms[1].shape[1]
    width = a_width + m_width + GAIN_PAD
    anywhere = pl.BlockSpec(memory_space=pl.ANY)
    dma = pltpu.SemaphoreType.DMA
    vmem = pltpu.VMEM
    return pl.pallas_call(
        functools.partial(finish_kernel, lines, plane),
        out_shape=(
            jax.ShapeDtypeStruct((rows, a_width), FULL),
            jax.ShapeDtypeStruct((rows, m_width), FULL),
            jax.ShapeDtypeStruct((8, rows), FULL),
            jax.ShapeDtypeStruct((rows, 3 * FF), LOW),
        ),
        in_specs=[anywhere] * 6,
        out_specs=(anywhere,) * 4,
        scratch_shapes=[
            vmem((2, chips, rows, width), LOW),
            vmem((lines, chips, rows, width), LOW),
            vmem((lines, 3 if plane == 8 else chips, rows, width), LOW),
            vmem((lines, rows, width), LOW),
            vmem((rows, a_width + m_width), FULL),
            vmem((8, rows), FULL),
            dma((lines, 4)),
            dma((lines, 4)),
            dma((lines, 4)),
            dma((lines, max(6, chips))),
            dma((lines, max(6, chips))),
            dma((lines,)),
            dma((lines,)),
            dma((plane, 2)),
            dma((plane, 2)),
            dma((3,)),
            dma((3,)),
        ],
        compiler_params=pltpu.CompilerParams(
            collective_id=1, has_side_effects=True, vmem_limit_bytes=VMEM_LIMIT
        ),
        name="finish",
    )(
        *(term.reshape(lines, chips, 2, rows, term.shape[1]) for term in terms),
        gate_part.reshape(plane, rows, -1),
        down_swapped,
    )


def body(
    hidden,
    cotangent,
    segment_ids,
    continuation_prompt,
    gain_master,
    gain_first,
    gain_second,
    attention_master,
    attention_first,
    attention_second,
    merge_master,
    merge_first,
    merge_second,
    feedforward_master,
    feedforward_first,
    feedforward_second,
):
    group_index = lax.axis_index("grp")
    dp_size = lax.axis_size("dp")
    row_count = hidden.shape[2]
    prompt_rows = row_count - CONT
    qkv_width = (HQ + 2 * HK) * HD
    own_rows = feedforward_master.shape[0]
    own_hidden = FF // dp_size
    own_inputs = hidden.reshape(row_count, D)

    gain_columns = jnp.pad(gain_master.T, ((0, 0), (0, GAIN_PAD - 2)))
    weight_low = jnp.concatenate(
        [attention_master.astype(LOW), merge_master.astype(LOW), gain_columns.astype(LOW)], axis=1
    )
    weights, group_rows, gate_rows, first_rows, second_rows = gather_start(
        weight_low, own_inputs, feedforward_master.astype(LOW)
    )
    weights, late_cotangent = lax.optimization_barrier((weights, cotangent))
    weights = weights.reshape(D, -1)
    merge_weight = weights[:, qkv_width : qkv_width + D]
    gain_float = weights[:, qkv_width + D : qkv_width + D + 2].astype(FULL).T
    gate_weight = lax.all_gather(
        gate_rows.reshape(dp_size * own_rows, 2 * own_hidden), "grp", axis=0, tiled=True
    )
    gate_weight, second_rows = lax.optimization_barrier((gate_weight, second_rows))
    first_down = first_rows.reshape(D, own_hidden // 2)
    second_down = lax.all_gather(
        second_rows.reshape(dp_size * own_rows, own_hidden // 2), "grp", axis=0, tiled=True
    )
    down_grad = plane_gather(late_cotangent.reshape(row_count, D))

    segment_row = segment_ids[0]
    source_row = continuation_prompt[0]
    prompt_positions, follow_positions = segment_positions(segment_row, source_row)
    cosine, sine_part = angle_table(jnp.concatenate([prompt_positions, follow_positions[0]]))

    place = jnp.reshape(group_index, (1,)).astype(jnp.int32)
    group_rows = group_rows.reshape(PROMPT_LEN, D)
    queries, pairs, key_normed, normed, key_scale = project_heads(
        place, group_rows, own_inputs, gain_float[:1], cosine, sine_part, weights
    )
    inputs = own_inputs.astype(FULL)
    first_scale = norm_scale(inputs)

    row_index = jnp.arange(row_count, dtype=jnp.int32)
    is_prompt = row_index < prompt_rows
    global_row = group_index * prompt_rows + jnp.minimum(row_index, prompt_rows - 1)
    own_segment = lax.dynamic_slice_in_dim(segment_row, group_index * prompt_rows, prompt_rows)
    query_segment = jnp.concatenate([own_segment, jnp.broadcast_to(source_row, (CONT,))])
    key_index = jnp.arange(PROMPT_LEN, dtype=jnp.int32)
    prompt_seen = (segment_row[None, :] == query_segment[:, None]) & (
        (key_index[None, :] <= global_row[:, None]) | ~is_prompt[:, None]
    )
    follow_seen = (~is_prompt)[:, None] & (
        jnp.arange(CONT, dtype=jnp.int32)[None, :] <= (row_index - prompt_rows)[:, None]
    )
    visible = jnp.concatenate([prompt_seen, follow_seen], axis=1)
    seen = visible.astype(FULL)
    attended, row_logsum = attend(queries, pairs, seen)
    middle = inputs + contract(attended, merge_weight, 1, 1)
    second_scale = norm_scale(middle)
    normed_two = (middle * second_scale * gain_float[1]).astype(LOW)
    grad_rows = cotangent.reshape(row_count, D).astype(FULL)

    normed_two, down_grad = lax.optimization_barrier((normed_two, down_grad))
    normed_all = plane_gather(normed_two)
    gate_up = jnp.dot(normed_all, gate_weight, preferred_element_type=FULL)
    gate_values = gate_up[:, :own_hidden]
    up_values = gate_up[:, own_hidden:]
    gate_sigmoid, gate_silu, activated = gate_parts(gate_values, up_values)
    down_term = contract(down_grad, activated, 0, 0).astype(LOW)
    down_term, second_down = lax.optimization_barrier((down_term, second_down))
    out_term, gate_up_grad = forward_back(
        row_count, activated, down_grad, gate_up, first_down, second_down
    )
    down_part = line_scatter(down_term)
    gate_term = contract(normed_all, gate_up_grad, 0, 0).astype(LOW)
    gate_up_grad, gate_term, down_part = lax.optimization_barrier(
        (gate_up_grad, gate_term, down_part)
    )
    gate_part = line_scatter(gate_term)
    normed_two_grad, down_swapped = plane_back(
        row_count, gate_up_grad, gate_weight, down_part.reshape(dp_size, own_rows, own_hidden)
    )
    normed_two_grad, out_term = lax.optimization_barrier((normed_two_grad, out_term))
    out_chunks = out_term.reshape(dp_size, row_count, D)
    out_swapped = [plane_swap(out_chunks[offset + 1], 1) for offset in range(0, dp_size, 2)]
    middle_grad = grad_rows + norm_back(middle, second_scale, gain_float[1], normed_two_grad)
    gain_two_part = jnp.sum(normed_two_grad * middle * second_scale, axis=0)
    branch_grad = middle_grad.astype(LOW)
    attended_grad = contract(branch_grad, merge_weight, 1, 0).astype(LOW)
    attended_grad, out_swapped = lax.optimization_barrier((attended_grad, out_swapped))
    out_sums = [
        out_chunks[2 * at].astype(FULL) + one.astype(FULL) for at, one in enumerate(out_swapped)
    ]
    out_low = [one.astype(LOW) for one in out_sums[1:]]
    attended_grad, out_low = lax.optimization_barrier((attended_grad, out_low))
    out_arrived = [plane_swap(one, 2 * at + 2) for at, one in enumerate(out_low)]
    query_project, pair_project = attend_back(
        place, queries, pairs, seen, row_logsum, attended_grad, cosine, sine_part
    )
    query_term, pair_term, merge_term, normed_grad, pair_back, gain_one_part = weights_back(
        place,
        query_project,
        pair_project,
        branch_grad,
        attended,
        key_normed,
        normed,
        group_rows,
        own_inputs,
        key_scale,
        weights,
    )
    gain_term = jnp.pad(
        jnp.stack([gain_one_part[0], gain_two_part], axis=1), ((0, 0), (0, GAIN_PAD - 2))
    )
    pair_back, gate_part, out_arrived = lax.optimization_barrier(
        (pair_back, gate_part, out_arrived)
    )
    result = middle + out_sums[0]
    for one in out_arrived:
        result = result + one.astype(FULL)
    block_output, query_term = lax.optimization_barrier((result.astype(LOW), query_term))
    block_output = block_output.reshape(hidden.shape)
    pair_sum = line_scatter(pair_back)
    attention_grad, merge_grad, gain_sums, forward_low = finish(
        (query_term, pair_term, merge_term, gain_term.astype(LOW)),
        gate_part,
        down_swapped,
    )
    gain_grad = gain_sums[:2]
    pair_sum, gain_grad = lax.optimization_barrier((pair_sum, gain_grad))
    pair_sum = pair_sum.astype(FULL)
    normed_grad = normed_grad + jnp.pad(pair_sum, ((0, CONT), (0, 0)))
    input_grad = (middle_grad + norm_back(inputs, first_scale, gain_float[0], normed_grad)).reshape(
        hidden.shape
    )
    feedforward_grad = forward_low.astype(FULL)
    gain_new = adam_step(gain_master, gain_first, gain_second, gain_grad, 0.0)
    attention_new = adam_step(
        attention_master, attention_first, attention_second, attention_grad, WEIGHT_DECAY
    )
    merge_new = adam_step(merge_master, merge_first, merge_second, merge_grad, WEIGHT_DECAY)
    feedforward_new = adam_step(
        feedforward_master, feedforward_first, feedforward_second, feedforward_grad, WEIGHT_DECAY
    )
    return (
        block_output,
        input_grad,
        gain_grad,
        *gain_new,
        attention_grad,
        *attention_new,
        merge_grad,
        *merge_new,
        feedforward_grad,
        *feedforward_new,
    )


def solution(mesh):
    tokens = P("dp", "grp", None, None)
    gains = P(None, ("grp", "dp"))
    matrix = P(("grp", "dp"), None)
    return jax.shard_map(
        body,
        mesh=mesh,
        in_specs=(tokens, tokens, P("dp", None), P("dp", "grp")) + (gains,) * 3 + (matrix,) * 9,
        out_specs=(tokens, tokens) + (gains,) * 4 + (matrix,) * 12,
        check_vma=False,
    )
```

```python
import functools

import jax
import jax.numpy as jnp
from jax import lax
from jax.experimental import pallas as pl
from jax.experimental.pallas import tpu as pltpu
from jax.sharding import PartitionSpec as P

D = 2048
FF = 8192
HQ = 8
HK = 4
HD = 256
PROMPT_LEN = 1024
PROMPTS = 4
CONT = 64
STEP = 10
GAIN_PAD = 128

EPS_NORM = 1e-06
ROPE_THETA = 1000042.0
MASK_FILL = -1e30
BETA_ONE = 0.9
BETA_TWO = 0.95
ADAM_EPS = 1e-08
LEARN_RATE = 0.02
WEIGHT_DECAY = 0.1
LOW = jnp.bfloat16
FULL = jnp.float32
MESH = pl.DeviceIdType.MESH


def contract(left, right, left_axis, right_axis):
    return lax.dot_general(
        left, right, (((left_axis,), (right_axis,)), ((), ())), preferred_element_type=FULL
    )


def angle_table(positions):
    inverse_rate = ROPE_THETA ** (-(jnp.arange(HD // 2, dtype=FULL) * 2.0) / HD)
    angles = positions.astype(FULL)[..., None] * inverse_rate
    return (jnp.cos(angles), jnp.sin(angles))


def segment_positions(segment_row, source_row):
    labels = jnp.arange(PROMPTS, dtype=jnp.int32)
    member = (segment_row[None, :] == labels[:, None]).astype(jnp.int32)
    lengths = jnp.sum(member, axis=1, dtype=jnp.int32)
    starts = jnp.sum(
        jnp.where(labels[None, :] < labels[:, None], lengths[None, :], 0), axis=1, dtype=jnp.int32
    )
    prompt_index = jnp.arange(segment_row.shape[0], dtype=jnp.int32)
    prompt_positions = prompt_index - jnp.sum(member * starts[:, None], axis=0, dtype=jnp.int32)
    source_length = jnp.sum(
        (source_row[:, None] == labels[None, :]).astype(jnp.int32) * lengths[None, :],
        axis=1,
        dtype=jnp.int32,
    )
    follow_positions = source_length[:, None] + jnp.arange(CONT, dtype=jnp.int32)[None, :]
    return (prompt_positions, follow_positions)


def norm_scale(values):
    return lax.rsqrt(jnp.mean(values * values, axis=-1, keepdims=True) + EPS_NORM)


def norm_back(values, row_scale, gain_row, normed_grad):
    scaled = normed_grad * gain_row
    return row_scale * scaled - values * row_scale**3 * jnp.mean(
        scaled * values, axis=-1, keepdims=True
    )


def adam_step(master, first_moment, second_moment, gradient, decay_rate):
    first_new = BETA_ONE * first_moment + (1.0 - BETA_ONE) * gradient
    second_new = BETA_TWO * second_moment + (1.0 - BETA_TWO) * gradient * gradient
    correct_one = 1.0 - BETA_ONE**STEP
    correct_two = 1.0 - BETA_TWO**STEP
    update = first_new / correct_one / (jnp.sqrt(second_new / correct_two) + ADAM_EPS)
    return (-LEARN_RATE * (update + decay_rate * master), first_new, second_new)


def gate_parts(gate_values, up_values):
    gate_sigmoid = jax.nn.sigmoid(gate_values)
    gate_silu = gate_values * gate_sigmoid
    return (gate_sigmoid, gate_silu, (gate_silu * up_values).astype(LOW))


def gate_backward(activated_grad, gate_values, up_values, gate_sigmoid, gate_silu):
    gate_grad = (
        activated_grad * up_values * gate_sigmoid * (1.0 + gate_values * (1.0 - gate_sigmoid))
    ).astype(LOW)
    up_grad = (activated_grad * gate_silu).astype(LOW)
    return (gate_grad, up_grad)


def flip(index, bits):
    bit = 1
    while bit <= bits:
        if bits & bit:
            index = index + bit - 2 * bit * lax.rem(index // bit, 2)
        bit *= 2
    return index


def remote(source, target, send, recv, there):
    return pltpu.make_async_remote_copy(
        src_ref=source,
        dst_ref=target,
        send_sem=send,
        recv_sem=recv,
        device_id=there,
        device_id_type=MESH,
    )


def gather_kernel(
    lines,
    plane,
    prompt_rows,
    weight_ref,
    hidden_ref,
    forward_ref,
    weights_ref,
    rows_ref,
    gate_ref,
    first_ref,
    second_ref,
    local_sem,
    line_send,
    line_recv,
    rows_send,
    rows_recv,
    first_send,
    first_recv,
    near_send,
    near_recv,
    half_send,
    half_recv,
    core_send,
    core_recv,
    swap_send,
    swap_recv,
):
    g = lax.axis_index("grp")
    d = lax.axis_index("dp")
    evens = range(0, plane, 2)
    forward_halves = plane == 8
    near = (2, 4) if forward_halves else tuple(evens[1:])
    width = weight_ref.shape[1]
    cut = (width // 256) * 128

    barrier = pltpu.get_barrier_semaphore()
    for offset in range(1, plane):
        pl.semaphore_signal(barrier, inc=1, device_id=(g, flip(d, offset)), device_id_type=MESH)

    for step in range(1, lines):
        there = lax.rem(g + step, lines)
        pl.semaphore_signal(barrier, inc=1, device_id=(there, d), device_id_type=MESH)
    pl.semaphore_wait(barrier, plane + lines - 2)

    copy = remote
    own_rows = hidden_ref.at[pl.ds(0, prompt_rows)]

    def line_weight(way, step):
        block = g - step + 1 if way == 0 else g + step - 1
        source = weight_ref if step == 1 else weights_ref.at[block, d]
        return copy(
            source,
            weights_ref.at[block, d],
            line_send.at[way, step],
            line_recv.at[way, step],
            (g + 1 if way == 0 else g - 1, d),
        )

    def line_rows(way, step):
        block = g - step + 1 if way == 0 else g + step - 1
        source = own_rows if step == 1 else rows_ref.at[block]
        return copy(
            source,
            rows_ref.at[block],
            rows_send.at[way, step],
            rows_recv.at[way, step],
            (g + 1 if way == 0 else g - 1, d),
        )

    def line_first(way, step):
        block = g - step + 1 if way == 0 else g + step - 1
        return copy(
            first_ref.at[block],
            first_ref.at[block],
            first_send.at[way, step],
            first_recv.at[way, step],
            (g + 1 if way == 0 else g - 1, d),
        )

    def sends(way, step):
        if way == 0:
            return (g < lines - 1) & (g >= step - 1)
        return (g > 0) & (g + step - 1 < lines)

    def receives(way, step):
        return g >= step if way == 0 else g + step < lines

    def near_copy(block, offset, own):
        source = weight_ref if own else weights_ref.at[block, d]
        at = near.index(offset)
        return copy(
            source,
            weights_ref.at[block, d],
            near_send.at[block, at],
            near_recv.at[block, at],
            (g, flip(d, offset)),
        )

    def half_copy(block, part):
        columns = pl.ds(0, cut) if part == 0 else pl.ds(cut, width - cut)
        origin = flip(d, 2) if part == 0 else flip(d, 4)
        there = flip(d, 4) if part == 0 else flip(d, 2)
        piece = weights_ref.at[block, origin, :, columns]
        return copy(
            piece, piece, half_send.at[block, part], half_recv.at[block, part], (g, there)
        )

    def core_copy(block, offset, own=False):
        source = weight_ref if own else weights_ref.at[block, flip(d, offset)]
        return copy(
            source,
            weights_ref.at[block, flip(d, offset)],
            core_send.at[block, offset // 2],
            core_recv.at[block, offset // 2],
            (g, flip(d, 1)),
        )

    half_hidden = second_ref.shape[2]
    own_hidden = 2 * half_hidden

    def swap_piece(owner, part, source_index):
        if part < 2:
            source = forward_ref.at[:, pl.ds(part * FF + owner * own_hidden, own_hidden)]
            return source, gate_ref.at[source_index, :, pl.ds(part * own_hidden, own_hidden)]
        start = 2 * FF + owner * own_hidden + (part - 2) * half_hidden
        source = forward_ref.at[:, pl.ds(start, half_hidden)]
        return source, first_ref.at[g, source_index] if part == 2 else second_ref.at[source_index]

    def swap_copy(offset, part):
        source, target = swap_piece(flip(d, offset), part, d)
        return copy(
            source,
            target,
            swap_send.at[offset, part],
            swap_recv.at[offset, part],
            (g, flip(d, offset)),
        )

    locals_ = (
        pltpu.make_async_copy(weight_ref, weights_ref.at[g, d], local_sem.at[0]),
        pltpu.make_async_copy(own_rows, rows_ref.at[g], local_sem.at[1]),
        *(
            pltpu.make_async_copy(*swap_piece(d, part, d), local_sem.at[2 + part])
            for part in range(4)
        ),
    )

    def launch(block, own):
        for offset in near:
            near_copy(block, offset, own).start()
        core_copy(block, 0, own).start()

    def relay(block):
        for offset in near:
            near_copy(block, offset, False).wait_recv()
            core_copy(block, offset).start()
        if forward_halves:
            half_copy(block, 0).start()
            half_copy(block, 1).start()

    def finish(block):
        if forward_halves:
            half_copy(block, 0).wait_recv()
            half_copy(block, 1).wait_recv()
            core_copy(block, 6).start()

    def both(step, act):
        for way in (0, 1):
            pl.when(receives(way, step))(
                lambda way=way: act(g - step if way == 0 else g + step)
            )

    def take_rows(step):
        for way in (0, 1):

            @pl.when(receives(way, step))
            def _(way=way):
                line_rows(way, step).wait_recv()

            if step + 1 < lines:
                pl.when(sends(way, step + 1))(
                    lambda way=way: line_rows(way, step + 1).start()
                )

    for way in (0, 1):
        pl.when(sends(way, 1))(lambda way=way: line_weight(way, 1).start())
    launch(g, True)
    for one in locals_:
        one.start()
    for step in range(1, lines):
        for way in (0, 1):

            @pl.when(receives(way, step))
            def _(way=way, step=step):
                line_weight(way, step).wait_recv()

            if step + 1 < lines:
                pl.when(sends(way, step + 1))(
                    lambda way=way, step=step: line_weight(way, step + 1).start()
                )

        both(step, lambda block: launch(block, False))
        if step == 1:
            for way in (0, 1):
                pl.when(sends(way, 1))(lambda way=way: line_rows(way, 1).start())
        if step == 1:
            relay(g)
            for offset in range(1, plane):
                swap_copy(offset, 2).start()
    for step in range(1, lines):
        take_rows(step)
        if step == lines - 2:
            locals_[4].wait()
            for offset in range(1, plane):
                swap_copy(offset, 2).wait_recv()
            for way in (0, 1):
                pl.when(sends(way, 1))(lambda way=way: line_first(way, 1).start())
        both(step, relay)
        if step == 1:
            finish(g)
        elif step < lines - 1:
            both(step - 1, finish)
        if step == 1:
            for offset in range(1, plane):
                for part in (0, 1, 3):
                    swap_copy(offset, part).start()
    for step in range(1, lines):
        for way in (0, 1):

            @pl.when(receives(way, step))
            def _(way=way, step=step):
                line_first(way, step).wait_recv()

            if step + 1 < lines:
                pl.when(sends(way, step + 1))(
                    lambda way=way, step=step: line_first(way, step + 1).start()
                )
        if step == 1:
            both(lines - 2, finish)
    both(lines - 1, finish)

    def drain(block):
        for offset in evens:
            core_copy(block, offset).wait()
        for offset in near:
            near_copy(block, offset, False).wait_send()
        if forward_halves:
            half_copy(block, 0).wait_send()
            half_copy(block, 1).wait_send()

    drain(g)
    for step in range(1, lines):
        for way in (0, 1):
            pl.when(receives(way, step))(
                lambda way=way, step=step: drain(g - step if way == 0 else g + step)
            )

            @pl.when(sends(way, step))
            def _(way=way, step=step):
                line_weight(way, step).wait_send()
                line_rows(way, step).wait_send()
                line_first(way, step).wait_send()

    for offset in range(1, plane):
        for part in (0, 1, 3):
            swap_copy(offset, part).wait()
        swap_copy(offset, 2).wait_send()
    for at, one in enumerate(locals_):
        if at != 4:
            one.wait()


def gather_start(weight, hidden, forward):
    lines, plane = lax.axis_size("grp"), lax.axis_size("dp")
    prompt_rows = PROMPT_LEN // lines
    own_rows, width = weight.shape
    anywhere = pl.BlockSpec(memory_space=pl.ANY)
    dma = pltpu.SemaphoreType.DMA
    near_count = 2 if plane == 8 else plane // 2 - 1
    pairs = (
        (2, lines),
        (2, lines),
        (2, lines),
        (2, lines),
        (2, lines),
        (2, lines),
        (lines, near_count),
        (lines, near_count),
        (lines, 2),
        (lines, 2),
        (lines, plane // 2),
        (lines, plane // 2),
        (plane, 4),
        (plane, 4),
    )
    own_hidden = FF // plane
    return pl.pallas_call(
        functools.partial(gather_kernel, lines, plane, prompt_rows),
        out_shape=(
            jax.ShapeDtypeStruct((lines, plane, own_rows, width), weight.dtype),
            jax.ShapeDtypeStruct((lines, prompt_rows, D), hidden.dtype),
            jax.ShapeDtypeStruct((plane, own_rows, 2 * own_hidden), forward.dtype),
            jax.ShapeDtypeStruct((lines, plane, own_rows, own_hidden // 2), forward.dtype),
            jax.ShapeDtypeStruct((plane, own_rows, own_hidden // 2), forward.dtype),
        ),
        in_specs=[anywhere] * 3,
        out_specs=(anywhere,) * 5,
        scratch_shapes=[dma((6,))] + [dma(shape) for shape in pairs],
        compiler_params=pltpu.CompilerParams(collective_id=0, has_side_effects=True),
        name="gather_start",
    )(weight, hidden, forward)


def project_kernel(
    place_ref,
    group_ref,
    own_ref,
    gain_ref,
    cosine_ref,
    sine_ref,
    weight_ref,
    query_ref,
    pair_ref,
    normed_ref,
    own_normed_ref,
    scale_ref,
):
    step = pl.program_id(0)
    own_rows = own_ref.shape[0]
    prompt_rows = own_rows - CONT
    start = pl.multiple_of(place_ref[0] * prompt_rows, 16)
    tile = 32

    def norm_tile(values, at):
        values = values.astype(FULL)
        scale = lax.rsqrt(jnp.mean(values * values, axis=-1, keepdims=True) + EPS_NORM)
        normed_ref[pl.ds(at, tile)] = (values * scale * gain_ref[...]).astype(LOW)
        scale_ref[pl.ds(at, tile)] = jnp.broadcast_to(scale, (tile, 128))

    @pl.when(step == 0)
    def _():
        @pl.loop(0, PROMPT_LEN // tile)
        def _(at):
            first = pl.multiple_of(at * tile, tile)
            norm_tile(group_ref[pl.ds(first, tile)], first)

        for at in range(0, CONT, tile):
            norm_tile(own_ref[prompt_rows + at : prompt_rows + at + tile], PROMPT_LEN + at)
        own_normed_ref[:prompt_rows] = normed_ref[pl.ds(start, prompt_rows)]
        own_normed_ref[prompt_rows:] = normed_ref[PROMPT_LEN:]

    def turn(values, cosine, sine_part):
        front, back = values[:, : HD // 2], values[:, HD // 2 :]
        return front * cosine - back * sine_part, back * cosine + front * sine_part

    def project(rows):
        return jnp.dot(rows, weight_ref[...], preferred_element_type=FULL)

    @pl.when(step < HQ)
    def _():
        for first, count, table in ((0, prompt_rows, start), (prompt_rows, CONT, PROMPT_LEN)):
            values = project(own_normed_ref[first : first + count])
            front, back = turn(
                values, cosine_ref[pl.ds(table, count)], sine_ref[pl.ds(table, count)]
            )
            query_ref[first : first + count, : HD // 2] = front.astype(LOW)
            query_ref[first : first + count, HD // 2 :] = back.astype(LOW)

    key_count = PROMPT_LEN + CONT
    part = key_count // 4

    @pl.when((step >= HQ) & (step < HQ + HK))
    def _():
        @pl.loop(0, 4)
        def _(at):
            rows = pl.ds(pl.multiple_of(at * part, 16), part)
            front, back = turn(project(normed_ref[rows]), cosine_ref[rows], sine_ref[rows])
            pair_ref[rows, : HD // 2] = front.astype(LOW)
            pair_ref[rows, HD // 2 :] = back.astype(LOW)

    @pl.when(step >= HQ + HK)
    def _():
        @pl.loop(0, 4)
        def _(at):
            rows = pl.ds(pl.multiple_of(at * part, 16), part)
            pair_ref[rows] = project(normed_ref[rows]).astype(LOW)


VMEM_LIMIT = 60 * 2**20


def project_heads(place, group_rows, own_inputs, gain_row, cosine, sine_part, weights):
    own_rows = own_inputs.shape[0]
    key_count = PROMPT_LEN + CONT
    whole = lambda shape: pl.BlockSpec(shape, lambda j, p: (0, 0))
    return pl.pallas_call(
        project_kernel,
        grid_spec=pltpu.PrefetchScalarGridSpec(
            num_scalar_prefetch=1,
            grid=(HQ + 2 * HK,),
            in_specs=[
                whole((PROMPT_LEN, D)),
                whole((own_rows, D)),
                whole((1, D)),
                whole((key_count, HD // 2)),
                whole((key_count, HD // 2)),
                pl.BlockSpec((D, HD), lambda j, p: (0, j)),
            ],
            out_specs=[
                pl.BlockSpec((own_rows, HD), lambda j, p: (0, jnp.minimum(j, HQ - 1))),
                pl.BlockSpec((key_count, HD), lambda j, p: (0, jnp.maximum(j - HQ, 0))),
                whole((key_count, D)),
                whole((own_rows, D)),
                whole((key_count, 128)),
            ],
        ),
        out_shape=[
            jax.ShapeDtypeStruct((own_rows, HQ * HD), LOW),
            jax.ShapeDtypeStruct((key_count, 2 * HK * HD), LOW),
            jax.ShapeDtypeStruct((key_count, D), LOW),
            jax.ShapeDtypeStruct((own_rows, D), LOW),
            jax.ShapeDtypeStruct((key_count, 128), FULL),
        ],
        compiler_params=pltpu.CompilerParams(vmem_limit_bytes=VMEM_LIMIT),
        name="project_heads",
    )(place, group_rows, own_inputs, gain_row, cosine, sine_part, weights)


def across(left, right):
    return lax.dot_general(left, right, (((1,), (1,)), ((), ())), preferred_element_type=FULL)


def along(left, right):
    return lax.dot_general(left, right, (((0,), (0,)), ((), ())), preferred_element_type=FULL)


def attend_kernel(query_ref, key_ref, value_ref, seen_ref, attended_ref, logsum_ref):
    group_heads = HQ // HK
    for head in range(group_heads):
        columns = slice(head * HD, (head + 1) * HD)
        scores = across(query_ref[:, columns], key_ref[...]) * HD ** (-0.5)
        scores = jnp.where(seen_ref[...] > 0, scores, MASK_FILL)
        peak = jnp.max(scores, axis=-1, keepdims=True)
        unnormed = jnp.exp(scores - peak)
        total = jnp.sum(unnormed, axis=-1, keepdims=True)
        low = (unnormed / total).astype(LOW)
        attended_ref[:, columns] = jnp.dot(
            low, value_ref[...], preferred_element_type=FULL
        ).astype(LOW)
        logsum_ref[:, head * 128 : (head + 1) * 128] = jnp.broadcast_to(
            peak + jnp.log(total), (query_ref.shape[0], 128)
        )


def attend(queries, pairs, seen):
    rows, key_count = seen.shape
    group_heads = HQ // HK
    return pl.pallas_call(
        attend_kernel,
        grid=(HK,),
        in_specs=[
            pl.BlockSpec((rows, group_heads * HD), lambda j: (0, j)),
            pl.BlockSpec((key_count, HD), lambda j: (0, j)),
            pl.BlockSpec((key_count, HD), lambda j: (0, HK + j)),
            pl.BlockSpec((rows, key_count), lambda j: (0, 0)),
        ],
        out_specs=[
            pl.BlockSpec((rows, group_heads * HD), lambda j: (0, j)),
            pl.BlockSpec((rows, group_heads * 128), lambda j: (0, j)),
        ],
        out_shape=[
            jax.ShapeDtypeStruct((rows, HQ * HD), LOW),
            jax.ShapeDtypeStruct((rows, HQ * 128), FULL),
        ],
        compiler_params=pltpu.CompilerParams(vmem_limit_bytes=VMEM_LIMIT),
        name="attend",
    )(queries, pairs, pairs, seen)


def attend_back_kernel(
    place_ref,
    query_ref,
    key_ref,
    value_ref,
    seen_ref,
    logsum_ref,
    grad_ref,
    cosine_ref,
    sine_ref,
    query_out,
    pair_out,
):
    step = pl.program_id(0)
    group_heads = HQ // HK
    rows = query_ref.shape[0]
    prompt_rows = rows - CONT
    start = pl.multiple_of(place_ref[0] * prompt_rows, 16)
    score_scale = HD ** (-0.5)
    key_grad = value_grad = 0.0

    def turn_back(values, cosine, sine_part):
        front, back = values[:, : HD // 2], values[:, HD // 2 :]
        return jnp.concatenate(
            [front * cosine + back * sine_part, back * cosine - front * sine_part], axis=1
        ).astype(LOW)

    for head in range(group_heads):
        columns = slice(head * HD, (head + 1) * HD)
        scores = across(query_ref[:, columns], key_ref[...]) * score_scale
        scores = jnp.where(seen_ref[...] > 0, scores, MASK_FILL)
        probabilities = jnp.exp(scores - logsum_ref[:, head * 128 : head * 128 + 1])
        grads = grad_ref[:, columns]
        probability_grad = across(grads, value_ref[...])
        delta = jnp.sum(probabilities * probability_grad, axis=-1, keepdims=True)
        score_grad = (probabilities * (probability_grad - delta)).astype(LOW)
        query_grad = jnp.dot(score_grad, key_ref[...], preferred_element_type=FULL) * score_scale
        key_grad = key_grad + along(score_grad, query_ref[:, columns])
        value_grad = value_grad + along(probabilities.astype(LOW), grads)
        query_out[:prompt_rows, columns] = turn_back(
            query_grad[:prompt_rows],
            cosine_ref[pl.ds(start, prompt_rows)],
            sine_ref[pl.ds(start, prompt_rows)],
        )
        query_out[prompt_rows:, columns] = turn_back(
            query_grad[prompt_rows:], cosine_ref[PROMPT_LEN:], sine_ref[PROMPT_LEN:]
        )
    pair_out[:, pl.ds(pl.multiple_of(step * HD, HD), HD)] = turn_back(
        key_grad * score_scale, cosine_ref[...], sine_ref[...]
    )
    pair_out[:, pl.ds(pl.multiple_of((HK + step) * HD, HD), HD)] = value_grad.astype(LOW)


def attend_back(place, queries, pairs, seen, logsum, grads, cosine, sine_part):
    rows, key_count = seen.shape
    group_heads = HQ // HK
    whole = lambda shape: pl.BlockSpec(shape, lambda j, p: (0, 0))
    return pl.pallas_call(
        attend_back_kernel,
        grid_spec=pltpu.PrefetchScalarGridSpec(
            num_scalar_prefetch=1,
            grid=(HK,),
            in_specs=[
                pl.BlockSpec((rows, group_heads * HD), lambda j, p: (0, j)),
                pl.BlockSpec((key_count, HD), lambda j, p: (0, j)),
                pl.BlockSpec((key_count, HD), lambda j, p: (0, HK + j)),
                whole((rows, key_count)),
                pl.BlockSpec((rows, group_heads * 128), lambda j, p: (0, j)),
                pl.BlockSpec((rows, group_heads * HD), lambda j, p: (0, j)),
                whole((key_count, HD // 2)),
                whole((key_count, HD // 2)),
            ],
            out_specs=[
                pl.BlockSpec((rows, group_heads * HD), lambda j, p: (0, j)),
                whole((key_count, 2 * HK * HD)),
            ],
        ),
        out_shape=[
            jax.ShapeDtypeStruct((rows, HQ * HD), LOW),
            jax.ShapeDtypeStruct((key_count, 2 * HK * HD), LOW),
        ],
        compiler_params=pltpu.CompilerParams(vmem_limit_bytes=VMEM_LIMIT),
        name="attend_back",
    )(place, queries, pairs, pairs, seen, logsum, grads, cosine, sine_part)


def weights_back_kernel(
    place_ref,
    query_ref,
    pair_ref,
    branch_ref,
    attended_ref,
    normed_ref,
    own_normed_ref,
    group_ref,
    own_ref,
    scale_ref,
    query_weight_ref,
    pair_weight_ref,
    query_term,
    pair_term,
    merge_term,
    back_out,
    pair_back_out,
    gain_out,
):
    rows = query_ref.shape[0]
    prompt_rows = rows - CONT
    start = pl.multiple_of(place_ref[0] * prompt_rows, 16)
    query_term[...] = along(own_normed_ref[...], query_ref[...]).astype(LOW)
    pair_term[...] = along(normed_ref[...], pair_ref[...]).astype(LOW)
    merge_term[...] = along(branch_ref[...], attended_ref[...]).astype(LOW)
    query_back = across(query_ref[...], query_weight_ref[...])
    pair_back = across(pair_ref[...], pair_weight_ref[...])
    own_values = own_ref[prompt_rows:].astype(FULL) * scale_ref[PROMPT_LEN:, :1]
    tail = query_back[prompt_rows:] + pair_back[PROMPT_LEN:]
    group_values = group_ref[...].astype(FULL) * scale_ref[:PROMPT_LEN, :1]
    own_prompt = own_ref[:prompt_rows].astype(FULL) * scale_ref[pl.ds(start, prompt_rows), :1]
    gain_out[...] = (
        jnp.sum(pair_back[:PROMPT_LEN] * group_values, axis=0, keepdims=True)
        + jnp.sum(query_back[:prompt_rows] * own_prompt, axis=0, keepdims=True)
        + jnp.sum(tail * own_values, axis=0, keepdims=True)
    )
    back_out[:prompt_rows] = query_back[:prompt_rows]
    back_out[prompt_rows:] = tail
    pair_back_out[...] = pair_back[:PROMPT_LEN].astype(LOW)


def weights_back(
    place, queries, pairs, branch, attended, normed, own_normed, group_rows, own_inputs, scale, weights
):
    rows, key_count = queries.shape[0], pairs.shape[0]
    wide, tile = HQ * HD, 256
    whole = lambda shape: pl.BlockSpec(shape, lambda j, p: (0, 0))
    tall = lambda count: pl.BlockSpec((count, tile), lambda j, p: (0, j))
    flat = lambda at: pl.BlockSpec((tile, wide), lambda j, p: (j, at))
    return pl.pallas_call(
        weights_back_kernel,
        grid_spec=pltpu.PrefetchScalarGridSpec(
            num_scalar_prefetch=1,
            grid=(D // tile,),
            in_specs=[
                whole((rows, wide)),
                whole((key_count, wide)),
                tall(rows),
                whole((rows, wide)),
                tall(key_count),
                tall(rows),
                tall(PROMPT_LEN),
                tall(rows),
                whole((key_count, 128)),
                flat(0),
                flat(1),
            ],
            out_specs=[flat(0), flat(0), flat(0), tall(rows), tall(PROMPT_LEN), tall(1)],
        ),
        out_shape=[
            jax.ShapeDtypeStruct((D, wide), LOW),
            jax.ShapeDtypeStruct((D, wide), LOW),
            jax.ShapeDtypeStruct((D, wide), LOW),
            jax.ShapeDtypeStruct((rows, D), FULL),
            jax.ShapeDtypeStruct((PROMPT_LEN, D), LOW),
            jax.ShapeDtypeStruct((1, D), FULL),
        ],
        compiler_params=pltpu.CompilerParams(vmem_limit_bytes=VMEM_LIMIT),
        name="weights_back",
    )(
        place,
        queries,
        pairs,
        branch,
        attended,
        normed,
        own_normed,
        group_rows,
        own_inputs,
        scale,
        weights,
        weights,
    )


def forward_back_kernel(
    activated_ref, grad_ref, gate_up_ref, first_ref, second_ref, out_ref, gate_up_grad_ref
):
    own_hidden = activated_ref.shape[1]
    part = first_ref.shape[0] // 4
    piece = own_hidden // 2

    @pl.loop(0, 4)
    def _(at):
        columns = pl.ds(pl.multiple_of(at * part, part), part)
        out_ref[:, columns] = (
            across(activated_ref[:, :piece], first_ref[columns])
            + across(activated_ref[:, piece:], second_ref[columns])
        ).astype(LOW)

    for at, down_ref in enumerate((first_ref, second_ref)):
        columns = slice(at * piece, (at + 1) * piece)
        upper = slice(own_hidden + at * piece, own_hidden + (at + 1) * piece)
        activated_grad = jnp.dot(grad_ref[...], down_ref[...], preferred_element_type=FULL)
        gate_values, up_values = gate_up_ref[:, columns], gate_up_ref[:, upper]
        gate_sigmoid = jax.nn.sigmoid(gate_values)
        gate_grad, up_grad = gate_backward(
            activated_grad, gate_values, up_values, gate_sigmoid, gate_values * gate_sigmoid
        )
        gate_up_grad_ref[:, columns] = gate_grad
        gate_up_grad_ref[:, upper] = up_grad


def forward_back(rows, activated, grads, gate_up, first_down, second_down):
    count, own_hidden = activated.shape
    block = lambda width: pl.BlockSpec((rows, width), lambda j: (j, 0))
    return pl.pallas_call(
        forward_back_kernel,
        grid=(count // rows,),
        in_specs=[
            block(own_hidden),
            block(D),
            block(2 * own_hidden),
            pl.BlockSpec(first_down.shape, lambda j: (0, 0)),
            pl.BlockSpec(second_down.shape, lambda j: (0, 0)),
        ],
        out_specs=[block(D), block(2 * own_hidden)],
        out_shape=[
            jax.ShapeDtypeStruct((count, D), LOW),
            jax.ShapeDtypeStruct((count, 2 * own_hidden), LOW),
        ],
        compiler_params=pltpu.CompilerParams(vmem_limit_bytes=VMEM_LIMIT),
        name="forward_back",
    )(activated, grads, gate_up, first_down, second_down)


def plane_back_kernel(
    plane,
    rows_ref,
    weight_ref,
    down_ref,
    out_ref,
    swapped_ref,
    weight,
    tiles,
    keep,
    give,
    core_in,
    plane_in,
    total,
    load_sem,
    tile_sem,
    core_send,
    core_recv,
    plane_send,
    plane_recv,
    out_sem,
    swap_send,
    swap_recv,
):
    g = lax.axis_index("grp")
    d = lax.axis_index("dp")
    chips = plane // 2
    own_hidden = down_ref.shape[2]
    halves = plane == 8
    order = (3, 1, 2, 0) if halves else tuple(range(chips - 1, -1, -1))
    cut = D // 2
    half_of = (pl.ds(0, cut), pl.ds(cut, D - cut))

    barrier = pltpu.get_barrier_semaphore()
    for offset in range(1, plane):
        pl.semaphore_signal(
            barrier, inc=1, device_id=(g, flip(d, offset)), device_id_type=MESH
        )

    load = pltpu.make_async_copy(weight_ref, weight, load_sem.at[0])
    load.start()

    def tile_copy(turn):
        at = order[turn]
        return pltpu.make_async_copy(
            rows_ref.at[pl.ds(2 * at, 2)], tiles.at[turn % 2], tile_sem.at[turn % 2]
        )

    def core_copy(at):
        return remote(
            give.at[at], core_in.at[at], core_send.at[at], core_recv.at[at], (g, flip(d, 1))
        )

    def plane_copy(at):
        return remote(
            keep.at[at],
            plane_in.at[at],
            plane_send.at[at],
            plane_recv.at[at],
            (g, flip(d, 2 * at)),
        )

    def near_copy(part, relayed):
        there = part + 1
        return remote(
            keep.at[3 if relayed else there, :, half_of[part]],
            plane_in.at[1 if relayed else 0, :, half_of[part]],
            plane_send.at[2 * relayed + part],
            plane_recv.at[2 * relayed + part],
            (g, flip(d, 2 * there)),
        )

    def relay_copy(part):
        there = 2 - part
        return remote(
            keep.at[there, :, half_of[part]],
            plane_in.at[2, :, half_of[part]],
            plane_send.at[4 + part],
            plane_recv.at[4 + part],
            (g, flip(d, 2 * there)),
        )

    def swap_copy(offset):
        there = flip(d, offset)
        return remote(
            down_ref.at[there],
            swapped_ref.at[:, pl.ds(d * own_hidden, own_hidden)],
            swap_send.at[offset],
            swap_recv.at[offset],
            (g, there),
        )

    own_swap = pltpu.make_async_copy(
        down_ref.at[d], swapped_ref.at[:, pl.ds(d * own_hidden, own_hidden)], out_sem.at[1]
    )
    tile_copy(0).start()
    tile_copy(1).start()
    pl.semaphore_wait(barrier, plane - 1)
    for offset in range(1, plane):
        swap_copy(offset).start()
    own_swap.start()
    load.wait()
    part_width = 1024

    def product(turn, which, target):
        @pl.loop(0, D // part_width)
        def _(at):
            columns = pl.ds(pl.multiple_of(at * part_width, part_width), part_width)
            target[order[turn], :, columns] = across(
                tiles[turn % 2, which], weight[columns]
            ).astype(LOW)

    def add_into(at, other, first, count):
        step = 256

        @pl.loop(0, count // step)
        def _(k):
            here = pl.ds(pl.multiple_of(first + k * step, step), step)
            keep[at, :, here] = (
                keep[at, :, here].astype(FULL) + other(here).astype(FULL)
            ).astype(LOW)

    def settle(turn):
        at = order[turn]
        core_copy(at).wait_recv()
        add_into(at, lambda here: core_in[at, :, here], 0, D)
        if halves and at == 3:
            near_copy(0, True).start()
            near_copy(1, True).start()
        elif halves and at:
            near_copy(at - 1, False).start()
        elif at:
            plane_copy(at).start()

    for turn in range(chips):
        tile_copy(turn).wait()
        product(turn, 1, give)
        core_copy(order[turn]).start()
        if turn:
            settle(turn - 1)
        product(turn, 0, keep)
        if turn + 2 < chips:
            tile_copy(turn + 2).start()
        if halves and turn == chips - 1:
            for part in range(2):
                near_copy(part, True).wait_recv()
                add_into(
                    2 - part,
                    lambda here: plane_in[1, :, here],
                    part * cut,
                    cut,
                )
                relay_copy(part).start()
    settle(chips - 1)
    if halves:
        for part in range(2):
            near_copy(part, False).wait_recv()
            relay_copy(part).wait_recv()
        arrived = (0, 2)
    else:
        for at in range(1, chips):
            plane_copy(at).wait_recv()
        arrived = tuple(range(1, chips))

    @pl.loop(0, D // 256)
    def _(k):
        here = pl.ds(pl.multiple_of(k * 256, 256), 256)
        value = keep[0, :, here].astype(FULL)
        for at in arrived:
            value = value + plane_in[at, :, here].astype(FULL)
        total[:, here] = value

    out = pltpu.make_async_copy(total, out_ref, out_sem.at[0])
    out.start()
    for at in range(chips):
        core_copy(at).wait_send()
    if halves:
        for part in range(2):
            near_copy(part, False).wait_send()
            near_copy(part, True).wait_send()
            relay_copy(part).wait_send()
    else:
        for at in range(1, chips):
            plane_copy(at).wait_send()
    for offset in range(1, plane):
        swap_copy(offset).wait()
    own_swap.wait()
    out.wait()


def plane_back(rows, gate_up_grad, gate_weight, down_part):
    plane = lax.axis_size("dp")
    chips = plane // 2
    inner = gate_up_grad.shape[1]
    anywhere = pl.BlockSpec(memory_space=pl.ANY)
    dma = pltpu.SemaphoreType.DMA
    return pl.pallas_call(
        functools.partial(plane_back_kernel, plane),
        out_shape=(
            jax.ShapeDtypeStruct((rows, D), FULL),
            jax.ShapeDtypeStruct((down_part.shape[1], FF), LOW),
        ),
        in_specs=[anywhere] * 3,
        out_specs=(anywhere,) * 2,
        scratch_shapes=[
            pltpu.VMEM((D, inner), LOW),
            pltpu.VMEM((2, 2, rows, inner), LOW),
            pltpu.VMEM((chips, rows, D), LOW),
            pltpu.VMEM((chips, rows, D), LOW),
            pltpu.VMEM((chips, rows, D), LOW),
            pltpu.VMEM((3 if plane == 8 else chips, rows, D), LOW),
            pltpu.VMEM((rows, D), FULL),
            dma((1,)),
            dma((2,)),
            dma((chips,)),
            dma((chips,)),
            dma((max(6, chips),)),
            dma((max(6, chips),)),
            dma((2,)),
            dma((plane,)),
            dma((plane,)),
        ],
        compiler_params=pltpu.CompilerParams(
            collective_id=2, has_side_effects=True, vmem_limit_bytes=VMEM_LIMIT
        ),
        name="plane_back",
    )(gate_up_grad.reshape(plane, rows, inner), gate_weight, down_part)


def plane_swap(block, offset):
    size = lax.axis_size("dp")
    return lax.ppermute(block, "dp", [(i, i ^ offset) for i in range(size)])


def plane_gather(block):
    mine = [block] + [plane_swap(block, o) for o in range(2, lax.axis_size("dp"), 2)]
    pairs = [(one, plane_swap(one, 1)) for one in mine]
    return jnp.concatenate([one for pair in pairs for one in pair], axis=0)


def line_scatter(term):
    return lax.psum_scatter(term, "grp", scatter_dimension=0, tiled=True)


def finish_kernel(
    lines,
    plane,
    query_ref,
    pair_ref,
    merge_ref,
    gain_ref,
    gate_ref,
    down_ref,
    a_out,
    m_out,
    gain_out,
    f_out,
    mine,
    core_in,
    plane_in,
    line_in,
    owned,
    gain_made,
    mine_sem,
    core_send,
    core_recv,
    plane_send,
    plane_recv,
    line_send,
    line_recv,
    swap_send,
    swap_recv,
    own_sem,
    out_sem,
):
    g = lax.axis_index("grp")
    d = lax.axis_index("dp")
    chips = plane // 2
    chip, core = lax.div(d, 2), lax.rem(d, 2)
    partner = d + 1 - 2 * core
    own_hidden = gate_ref.shape[2] // 2
    width = core_in.shape[3]
    a_width, m_width = a_out.shape[1], m_out.shape[1]
    parts, begin = [], 0
    for ref in (query_ref, pair_ref, merge_ref, gain_ref):
        parts.append((ref, pl.ds(begin, ref.shape[4])))
        begin += ref.shape[4]

    barrier = pltpu.get_barrier_semaphore()
    for step in range(1, plane):
        there = lax.rem(d + step, plane)
        pl.semaphore_signal(barrier, inc=1, device_id=(g, there), device_id_type=MESH)
    for step in range(1, lines):
        there = lax.rem(g + step, lines)
        pl.semaphore_signal(barrier, inc=1, device_id=(there, d), device_id_type=MESH)
    pl.semaphore_wait(barrier, plane + lines - 2)

    def line_at(turn):
        return lax.rem(g + turn + 1, lines)

    def core_copy(turn, part):
        line = line_at(turn)
        ref, columns = parts[part]
        return remote(
            ref.at[line, :, 1 - core],
            core_in.at[line, :, :, columns],
            core_send.at[turn, part],
            core_recv.at[turn, part],
            (g, partner),
        )

    def mine_copy(turn, part):
        line = line_at(turn)
        ref, columns = parts[part]
        return pltpu.make_async_copy(
            ref.at[line, :, core], mine.at[turn % 2, :, :, columns], mine_sem.at[turn, part]
        )

    cut = width // 256 * 128
    columns_of = (pl.ds(0, cut), pl.ds(cut, width - cut))

    def plane_copy(turn, step):
        line = line_at(turn)
        there = lax.rem(chip + step, chips)
        return remote(
            core_in.at[line, there],
            plane_in.at[line, chip],
            plane_send.at[turn, step],
            plane_recv.at[turn, step],
            (g, 2 * there + core),
        )

    def near_copy(turn, part, relayed):
        line = line_at(turn)
        there = flip(chip, part + 1)
        owner = flip(chip, 3) if relayed else there
        return remote(
            core_in.at[line, owner, :, columns_of[part]],
            plane_in.at[line, 1 if relayed else 0, :, columns_of[part]],
            plane_send.at[turn, 2 * relayed + part],
            plane_recv.at[turn, 2 * relayed + part],
            (g, 2 * there + core),
        )

    def relay_copy(turn, part):
        line = line_at(turn)
        there = flip(chip, 2 - part)
        return remote(
            core_in.at[line, there, :, columns_of[part]],
            plane_in.at[line, 2, :, columns_of[part]],
            plane_send.at[turn, 4 + part],
            plane_recv.at[turn, 4 + part],
            (g, 2 * there + core),
        )

    def line_copy(turn):
        line = line_at(turn)
        return remote(
            core_in.at[line, chip],
            line_in.at[g],
            line_send.at[turn],
            line_recv.at[turn],
            (line, d),
        )

    def swap_source(owner, part):
        return gate_ref.at[owner, :, pl.ds(part * own_hidden, own_hidden)]

    def swap_place(part):
        return f_out.at[:, pl.ds(part * FF + d * own_hidden, own_hidden)]

    def swap_copy(step, part):
        there = lax.rem(d + step, plane)
        return remote(
            swap_source(there, part),
            swap_place(part),
            swap_send.at[step, part],
            swap_recv.at[step, part],
            (g, there),
        )

    own_swap = [
        pltpu.make_async_copy(swap_source(d, part), swap_place(part), own_sem.at[part])
        for part in range(2)
    ] + [pltpu.make_async_copy(down_ref, f_out.at[:, pl.ds(2 * FF, FF)], own_sem.at[2])]

    every = range(len(parts))
    for turn in range(lines):
        for part in every:
            core_copy(turn, part).start()
            if turn < 2:
                mine_copy(turn, part).start()
    tile = 896 if width % 896 == 0 else 128
    halves = plane == 8

    def add_into(line, there, other, columns=None):
        first, count = (0, width) if columns is None else columns
        step = tile if columns is None else 128

        @pl.loop(0, count // step)
        def _(at):
            here = pl.ds(pl.multiple_of(first + at * step, 128), step)
            total = core_in[line, there, :, here].astype(FULL) + other(here).astype(FULL)
            core_in[line, there, :, here] = total.astype(LOW)

    def near_start(turn):
        if halves:
            for relayed in (True, False):
                for part in range(2):
                    near_copy(turn, part, relayed).start()
        else:
            for step in range(1, chips):
                plane_copy(turn, step).start()

    for turn in range(lines):
        line = line_at(turn)
        for part in every:
            core_copy(turn, part).wait_recv()
            mine_copy(turn, part).wait()
        for step in range(1, chips + 1):
            there = lax.rem(chip + step, chips)
            add_into(
                line, there, lambda here, there=there, turn=turn: mine[turn % 2, there, :, here]
            )
        if turn + 2 < lines:
            for part in every:
                mine_copy(turn + 2, part).start()
        if turn < 2:
            near_start(turn)

    def pass_on(turn):
        line = line_at(turn)
        for part, columns in enumerate(((0, cut), (cut, width - cut))):
            near_copy(turn, part, True).wait_recv()
            add_into(
                line,
                flip(chip, 2 - part),
                lambda here, line=line: plane_in[line, 1, :, here],
                columns,
            )
            relay_copy(turn, part).start()

    def near_done(turn):
        if halves:
            pass_on(turn)
            for part in range(2):
                near_copy(turn, part, False).wait_recv()
        else:
            for step in range(1, chips):
                plane_copy(turn, step).wait_recv()
        if turn + 2 < lines:
            near_start(turn + 2)

    def line_done(turn):
        line = line_at(turn)
        if halves:
            for part in range(2):
                relay_copy(turn, part).wait_recv()
            arrived = (0, 2)
        else:
            arrived = tuple(lax.rem(chip + step, chips) for step in range(1, chips))

        @pl.loop(0, width // tile)
        def _(at):
            columns = pl.ds(pl.multiple_of(at * tile, tile), tile)
            total = core_in[line, chip, :, columns].astype(FULL)
            for block in arrived:
                total = total + plane_in[line, block, :, columns].astype(FULL)
            core_in[line, chip, :, columns] = total.astype(LOW)

        if turn < lines - 1:
            line_copy(turn).start()

    near_done(0)
    for turn in range(1, lines):
        near_done(turn)
        line_done(turn - 1)
        if turn == lines - 2:
            for step in range(1, plane):
                for part in range(2):
                    swap_copy(step, part).start()
            for one in own_swap:
                one.start()
    line_done(lines - 1)
    for turn in range(lines - 1):
        line_copy(turn).wait_recv()

    def total_of(columns):
        total = core_in[g, chip, :, columns].astype(FULL)
        for step in range(1, lines):
            total = total + line_in[lax.rem(g + step, lines), :, columns].astype(FULL)
        return total

    @pl.loop(0, (a_width + m_width) // 256)
    def _(at):
        columns = pl.ds(pl.multiple_of(at * 256, 256), 256)
        owned[:, columns] = total_of(columns)

    gain_made[...] = total_of(pl.ds(a_width + m_width, GAIN_PAD)).T[:8]
    outs = (
        pltpu.make_async_copy(owned.at[:, pl.ds(0, a_width)], a_out, out_sem.at[0]),
        pltpu.make_async_copy(owned.at[:, pl.ds(a_width, m_width)], m_out, out_sem.at[1]),
        pltpu.make_async_copy(gain_made, gain_out, out_sem.at[2]),
    )
    for one in outs:
        one.start()
    for turn in range(lines):
        for part in every:
            core_copy(turn, part).wait_send()
        if halves:
            for part in range(2):
                near_copy(turn, part, False).wait_send()
                near_copy(turn, part, True).wait_send()
                relay_copy(turn, part).wait_send()
        else:
            for step in range(1, chips):
                plane_copy(turn, step).wait_send()
        if turn < lines - 1:
            line_copy(turn).wait_send()
    for step in range(1, plane):
        for part in range(2):
            swap_copy(step, part).wait()
    for one in own_swap:
        one.wait()
    for one in outs:
        one.wait()


def finish(terms, gate_part, down_swapped):
    lines, plane = lax.axis_size("grp"), lax.axis_size("dp")
    chips = plane // 2
    rows = D // (lines * plane)
    m_width = terms[2].shape[1]
    a_width = terms[0].shape[1] + terms[1].shape[1]
    width = a_width + m_width + GAIN_PAD
    anywhere = pl.BlockSpec(memory_space=pl.ANY)
    dma = pltpu.SemaphoreType.DMA
    vmem = pltpu.VMEM
    return pl.pallas_call(
        functools.partial(finish_kernel, lines, plane),
        out_shape=(
            jax.ShapeDtypeStruct((rows, a_width), FULL),
            jax.ShapeDtypeStruct((rows, m_width), FULL),
            jax.ShapeDtypeStruct((8, rows), FULL),
            jax.ShapeDtypeStruct((rows, 3 * FF), LOW),
        ),
        in_specs=[anywhere] * 6,
        out_specs=(anywhere,) * 4,
        scratch_shapes=[
            vmem((2, chips, rows, width), LOW),
            vmem((lines, chips, rows, width), LOW),
            vmem((lines, 3 if plane == 8 else chips, rows, width), LOW),
            vmem((lines, rows, width), LOW),
            vmem((rows, a_width + m_width), FULL),
            vmem((8, rows), FULL),
            dma((lines, 4)),
            dma((lines, 4)),
            dma((lines, 4)),
            dma((lines, max(6, chips))),
            dma((lines, max(6, chips))),
            dma((lines,)),
            dma((lines,)),
            dma((plane, 2)),
            dma((plane, 2)),
            dma((3,)),
            dma((3,)),
        ],
        compiler_params=pltpu.CompilerParams(
            collective_id=1, has_side_effects=True, vmem_limit_bytes=VMEM_LIMIT
        ),
        name="finish",
    )(
        *(term.reshape(lines, chips, 2, rows, term.shape[1]) for term in terms),
        gate_part.reshape(plane, rows, -1),
        down_swapped,
    )


def body(
    hidden,
    cotangent,
    segment_ids,
    continuation_prompt,
    gain_master,
    gain_first,
    gain_second,
    attention_master,
    attention_first,
    attention_second,
    merge_master,
    merge_first,
    merge_second,
    feedforward_master,
    feedforward_first,
    feedforward_second,
):
    group_index = lax.axis_index("grp")
    dp_size = lax.axis_size("dp")
    row_count = hidden.shape[2]
    prompt_rows = row_count - CONT
    qkv_width = (HQ + 2 * HK) * HD
    own_rows = feedforward_master.shape[0]
    own_hidden = FF // dp_size
    own_inputs = hidden.reshape(row_count, D)

    gain_columns = jnp.pad(gain_master.T, ((0, 0), (0, GAIN_PAD - 2)))
    weight_low = jnp.concatenate(
        [attention_master.astype(LOW), merge_master.astype(LOW), gain_columns.astype(LOW)], axis=1
    )
    weights, group_rows, gate_rows, first_rows, second_rows = gather_start(
        weight_low, own_inputs, feedforward_master.astype(LOW)
    )
    weights, late_cotangent = lax.optimization_barrier((weights, cotangent))
    weights = weights.reshape(D, -1)
    merge_weight = weights[:, qkv_width : qkv_width + D]
    gain_float = weights[:, qkv_width + D : qkv_width + D + 2].astype(FULL).T
    gate_weight = lax.all_gather(
        gate_rows.reshape(dp_size * own_rows, 2 * own_hidden), "grp", axis=0, tiled=True
    )
    gate_weight, second_rows = lax.optimization_barrier((gate_weight, second_rows))
    first_down = first_rows.reshape(D, own_hidden // 2)
    second_down = lax.all_gather(
        second_rows.reshape(dp_size * own_rows, own_hidden // 2), "grp", axis=0, tiled=True
    )
    down_grad = plane_gather(late_cotangent.reshape(row_count, D))

    segment_row = segment_ids[0]
    source_row = continuation_prompt[0]
    prompt_positions, follow_positions = segment_positions(segment_row, source_row)
    cosine, sine_part = angle_table(jnp.concatenate([prompt_positions, follow_positions[0]]))

    place = jnp.reshape(group_index, (1,)).astype(jnp.int32)
    group_rows = group_rows.reshape(PROMPT_LEN, D)
    queries, pairs, key_normed, normed, key_scale = project_heads(
        place, group_rows, own_inputs, gain_float[:1], cosine, sine_part, weights
    )
    inputs = own_inputs.astype(FULL)
    first_scale = norm_scale(inputs)

    row_index = jnp.arange(row_count, dtype=jnp.int32)
    is_prompt = row_index < prompt_rows
    global_row = group_index * prompt_rows + jnp.minimum(row_index, prompt_rows - 1)
    own_segment = lax.dynamic_slice_in_dim(segment_row, group_index * prompt_rows, prompt_rows)
    query_segment = jnp.concatenate([own_segment, jnp.broadcast_to(source_row, (CONT,))])
    key_index = jnp.arange(PROMPT_LEN, dtype=jnp.int32)
    prompt_seen = (segment_row[None, :] == query_segment[:, None]) & (
        (key_index[None, :] <= global_row[:, None]) | ~is_prompt[:, None]
    )
    follow_seen = (~is_prompt)[:, None] & (
        jnp.arange(CONT, dtype=jnp.int32)[None, :] <= (row_index - prompt_rows)[:, None]
    )
    visible = jnp.concatenate([prompt_seen, follow_seen], axis=1)
    seen = visible.astype(FULL)
    attended, row_logsum = attend(queries, pairs, seen)
    middle = inputs + contract(attended, merge_weight, 1, 1)
    second_scale = norm_scale(middle)
    normed_two = (middle * second_scale * gain_float[1]).astype(LOW)
    grad_rows = cotangent.reshape(row_count, D).astype(FULL)

    normed_two, down_grad = lax.optimization_barrier((normed_two, down_grad))
    normed_all = plane_gather(normed_two)
    gate_up = jnp.dot(normed_all, gate_weight, preferred_element_type=FULL)
    gate_values = gate_up[:, :own_hidden]
    up_values = gate_up[:, own_hidden:]
    gate_sigmoid, gate_silu, activated = gate_parts(gate_values, up_values)
    down_term = contract(down_grad, activated, 0, 0).astype(LOW)
    down_term, second_down = lax.optimization_barrier((down_term, second_down))
    out_term, gate_up_grad = forward_back(
        row_count, activated, down_grad, gate_up, first_down, second_down
    )
    down_part = line_scatter(down_term)
    gate_term = contract(normed_all, gate_up_grad, 0, 0).astype(LOW)
    gate_up_grad, gate_term, down_part = lax.optimization_barrier(
        (gate_up_grad, gate_term, down_part)
    )
    gate_part = line_scatter(gate_term)
    normed_two_grad, down_swapped = plane_back(
        row_count, gate_up_grad, gate_weight, down_part.reshape(dp_size, own_rows, own_hidden)
    )
    normed_two_grad, out_term = lax.optimization_barrier((normed_two_grad, out_term))
    out_chunks = out_term.reshape(dp_size, row_count, D)
    out_swapped = [plane_swap(out_chunks[offset + 1], 1) for offset in range(0, dp_size, 2)]
    middle_grad = grad_rows + norm_back(middle, second_scale, gain_float[1], normed_two_grad)
    gain_two_part = jnp.sum(normed_two_grad * middle * second_scale, axis=0)
    branch_grad = middle_grad.astype(LOW)
    attended_grad = contract(branch_grad, merge_weight, 1, 0).astype(LOW)
    attended_grad, out_swapped = lax.optimization_barrier((attended_grad, out_swapped))
    out_sums = [
        out_chunks[2 * at].astype(FULL) + one.astype(FULL) for at, one in enumerate(out_swapped)
    ]
    out_low = [one.astype(LOW) for one in out_sums[1:]]
    attended_grad, out_low = lax.optimization_barrier((attended_grad, out_low))
    out_arrived = [plane_swap(one, 2 * at + 2) for at, one in enumerate(out_low)]
    query_project, pair_project = attend_back(
        place, queries, pairs, seen, row_logsum, attended_grad, cosine, sine_part
    )
    query_term, pair_term, merge_term, normed_grad, pair_back, gain_one_part = weights_back(
        place,
        query_project,
        pair_project,
        branch_grad,
        attended,
        key_normed,
        normed,
        group_rows,
        own_inputs,
        key_scale,
        weights,
    )
    gain_term = jnp.pad(
        jnp.stack([gain_one_part[0], gain_two_part], axis=1), ((0, 0), (0, GAIN_PAD - 2))
    )
    pair_back, gate_part, out_arrived = lax.optimization_barrier(
        (pair_back, gate_part, out_arrived)
    )
    result = middle + out_sums[0]
    for one in out_arrived:
        result = result + one.astype(FULL)
    block_output, query_term = lax.optimization_barrier((result.astype(LOW), query_term))
    block_output = block_output.reshape(hidden.shape)
    pair_sum = line_scatter(pair_back)
    attention_grad, merge_grad, gain_sums, forward_low = finish(
        (query_term, pair_term, merge_term, gain_term.astype(LOW)),
        gate_part,
        down_swapped,
    )
    gain_grad = gain_sums[:2]
    pair_sum, gain_grad = lax.optimization_barrier((pair_sum, gain_grad))
    pair_sum = pair_sum.astype(FULL)
    normed_grad = normed_grad + jnp.pad(pair_sum, ((0, CONT), (0, 0)))
    input_grad = (middle_grad + norm_back(inputs, first_scale, gain_float[0], normed_grad)).reshape(
        hidden.shape
    )
    feedforward_grad = forward_low.astype(FULL)
    gain_new = adam_step(gain_master, gain_first, gain_second, gain_grad, 0.0)
    attention_new = adam_step(
        attention_master, attention_first, attention_second, attention_grad, WEIGHT_DECAY
    )
    merge_new = adam_step(merge_master, merge_first, merge_second, merge_grad, WEIGHT_DECAY)
    feedforward_new = adam_step(
        feedforward_master, feedforward_first, feedforward_second, feedforward_grad, WEIGHT_DECAY
    )
    return (
        block_output,
        input_grad,
        gain_grad,
        *gain_new,
        attention_grad,
        *attention_new,
        merge_grad,
        *merge_new,
        feedforward_grad,
        *feedforward_new,
    )


def solution(mesh):
    tokens = P("dp", "grp", None, None)
    gains = P(None, ("grp", "dp"))
    matrix = P(("grp", "dp"), None)
    return jax.shard_map(
        body,
        mesh=mesh,
        in_specs=(tokens, tokens, P("dp", None), P("dp", "grp")) + (gains,) * 3 + (matrix,) * 9,
        out_specs=(tokens, tokens) + (gains,) * 4 + (matrix,) * 12,
        check_vma=False,
    )
```
